32 devices in a mesh: seq: 8 (over y, x, core), head: 4 (over z).
Axes of the slice: x: 2, y: 2, z: 4, core: 2. Of those that a mesh axis runs over, the one named last changes fastest.
Arguments:
- tokens: bfloat16 [16384, 1024], P('seq'), may hold values from -6 to 6
- start_flags: int32 [16384], P('seq'), may hold values from 0 to 1, as said below
- in_gain: float32 [1024], replicated, may hold values from 0.5 to 1.5
- proj_zx: bfloat16 [1024, 2, 2048], P(None, None, 'head'), may hold values from -0.1875 to 0.1875
- proj_bc: bfloat16 [1024, 256], P(None, 'head'), may hold values from -0.1875 to 0.1875
- proj_dt: bfloat16 [1024, 32], P(None, 'head'), may hold values from -0.1875 to 0.1875
- conv_x_weight: bfloat16 [4, 2048], P(None, 'head'), may hold values from -3 to 3
- conv_x_bias: float32 [2048], P('head'), may hold values from -3 to 3
- conv_bc_weight: bfloat16 [4, 256], P(None, 'head'), may hold values from -3 to 3
- conv_bc_bias: float32 [256], P('head'), may hold values from -3 to 3
- dt_bias: float32 [32], P('head'), may hold values from -14 to -3
- a_log: float32 [32], P('head'), may hold values from 0 to 1.4
- skip_scale: float32 [32], P('head'), may hold values from 0.5 to 1.5
- norm_gain: float32 [2048], P('head'), may hold values from 0.5 to 1.5
- out_proj: bfloat16 [2048, 1024], P('head'), may hold values from -0.125 to 0.125
- cotangent: bfloat16 [16384, 1024], P('seq'), may hold values from -6 to 6
Outputs:
- mixed_out: bfloat16 [16384, 1024], P('seq')
- grad_tokens: float32 [16384, 1024], P('seq')
- grad_in_gain: float32 [1024], replicated
- grad_proj_zx: float32 [1024, 2, 2048], P(None, None, 'head')
- grad_proj_bc: float32 [1024, 256], P(None, 'head')
- grad_proj_dt: float32 [1024, 32], P(None, 'head')
- grad_conv_x_weight: float32 [4, 2048], P(None, 'head')
- grad_conv_x_bias: float32 [2048], P('head')
- grad_conv_bc_weight: float32 [4, 256], P(None, 'head')
- grad_conv_bc_bias: float32 [256], P('head')
- grad_dt_bias: float32 [32], P('head')
- grad_a_log: float32 [32], P('head')
- grad_skip_scale: float32 [32], P('head')
- grad_norm_gain: float32 [2048], P('head')
- grad_out_proj: float32 [2048, 1024], P('head')
The draws below stay inside these ranges and needn't reach their ends.
Inputs may be any that keep to these rules, and one draw needn't show every extreme that they name: `start_flags`: position 0 starts a sequence; there are at most two other starts among positions 1 to 2047 and at most two among the last 2047 positions, and none elsewhere, so one sequence runs from the first device of seq to the last.
All inputs are finite; a program needn't handle non-finite values.
Results may differ from the reference program's by a relative error of at most 0.011.
Values may be sent and summed in bfloat16 or wider, within the bound.
A program may use at most 192 MiB of HBM per device.

```python
import math
import jax
import jax.numpy as jnp
from jax import lax

D = 1024
HEADS = 32
HEADDIM = 64
NSTATE = 128
CONV = 4
GROUP = 256
TOK_DEV = 2048
INNER = 2048
TOKENS = 16384


def draw_start_flags(key, part):
    key = jax.random.fold_in(key, 11)
    early_key, late_key = jax.random.split(key)
    early_starts = jax.random.randint(early_key, (2,), 1, TOK_DEV)
    late_starts = jax.random.randint(late_key, (2,), TOKENS - TOK_DEV + 1, TOKENS)
    chosen = jnp.concatenate([jnp.zeros((1,), jnp.int32), early_starts.astype(jnp.int32), late_starts.astype(jnp.int32)])
    places = jnp.arange(TOKENS, dtype=jnp.int32)
    return jnp.any(places[:, None] == chosen[None, :], axis=1).astype(jnp.int32)


def draw_dt_bias(key, part):
    key = jax.random.fold_in(key, 23)
    pick_key, slow_key, fast_key = jax.random.split(key, 3)
    slow_share = 0.5
    slow_heads = jax.random.uniform(pick_key, (HEADS,)) < slow_share
    slow_steps = jnp.exp(jax.random.uniform(slow_key, (HEADS,), minval=math.log(0.1), maxval=math.log(0.35))) / TOKENS
    fast_steps = jnp.exp(jax.random.uniform(fast_key, (HEADS,), minval=math.log(0.01), maxval=math.log(0.03)))
    target = jnp.where(slow_heads, slow_steps, fast_steps)
    return jnp.log(jnp.expm1(target)).astype(jnp.float32)


def block_levels(stream_key, extent, cuts, low, top_value):
    def one(axis_at, parts):
        heights = jax.random.uniform(jax.random.fold_in(jax.random.fold_in(stream_key, 6), axis_at), (parts,), jnp.float32, low / len(cuts), top_value / len(cuts))
        return jnp.repeat(jnp.exp(heights), extent[axis_at] // parts).reshape((-1,) + (1,) * (len(extent) - axis_at - 1))

    level = one(*cuts[0])
    for cut in cuts[1:]:
        level = level * one(*cut)
    return level


def gaussian(rng, dims, scale, most, cuts=(), kind=jnp.bfloat16):
    gain = block_levels(rng, dims, cuts, -0.22, 0.18) if cuts else 1.0
    array = jax.random.normal(rng, dims, jnp.float32) * scale * gain
    return jnp.minimum(jnp.maximum(array, -most), most).astype(kind)


def setup_inputs(seed: int = 0) -> dict:
    key_of = jax.random.split(jax.random.key(seed), 17)
    return {
        "tokens": gaussian(key_of[0], (TOKENS, D), 1.0, 6.0, ((0, 8),)),
        "start_flags": draw_start_flags(jax.random.fold_in(key_of[16], 71), 0),
        "in_gain": jnp.clip(1.0 + 0.1 * jax.random.normal(key_of[2], (D,), jnp.float32), 0.5, 1.5),
        "proj_zx": gaussian(key_of[3], (D, 2, INNER), D ** -0.5, 0.1875, ((2, 4),)),
        "proj_bc": gaussian(key_of[4], (D, 2 * NSTATE), D ** -0.5, 0.1875, ((1, 4),)),
        "proj_dt": gaussian(key_of[5], (D, HEADS), D ** -0.5, 0.1875, ((1, 4),)),
        "conv_x_weight": gaussian(key_of[6], (CONV, INNER), CONV ** -0.5, 3.0, ((1, 4),)),
        "conv_x_bias": gaussian(key_of[7], (INNER,), 0.5, 3.0, ((0, 4),), jnp.float32),
        "conv_bc_weight": gaussian(key_of[8], (CONV, 2 * NSTATE), CONV ** -0.5, 3.0, ((1, 4),)),
        "conv_bc_bias": gaussian(key_of[9], (2 * NSTATE,), 0.5, 3.0, ((0, 4),), jnp.float32),
        "dt_bias": draw_dt_bias(jax.random.fold_in(key_of[16], 71), 0),
        "a_log": jnp.clip(1.4 * jax.random.uniform(key_of[11], (HEADS,), jnp.float32) ** block_levels(key_of[11], (HEADS,), ((0, 4),), -0.2, 0.2), 0.0, 1.4),
        "skip_scale": jnp.clip(0.5 + 1.0 * jax.random.uniform(key_of[12], (HEADS,), jnp.float32) ** block_levels(key_of[12], (HEADS,), ((0, 4),), -0.2, 0.2), 0.5, 1.5),
        "norm_gain": jnp.clip(1.0 + 0.1 * jax.random.normal(key_of[13], (INNER,), jnp.float32), 0.5, 1.5),
        "out_proj": gaussian(key_of[14], (INNER, D), INNER ** -0.5, 0.125, ((0, 4),)),
        "cotangent": gaussian(key_of[15], (TOKENS, D), 1.0, 6.0, ((0, 8),)),
    }


@jax.custom_vjp
def low(v):
    return lax.optimization_barrier(v.astype(jnp.bfloat16)).astype(jnp.float32)

@jax.custom_vjp
def low_back(v):
    return v

def low_keep(v):
    return (low(v), None)

def low_pass(kept, grad):
    return (grad,)

def back_keep(v):
    return (v, None)

def back_low(kept, grad):
    return (low(grad),)
low.defvjp(low_keep, low_pass)
low_back.defvjp(back_keep, back_low)
epsilon = 1e-05
highest = lax.Precision.HIGHEST

def lower_ones(length):
    order = jnp.arange(length)
    return (order[:, None] >= order[None, :]).astype(jnp.float32)

def group_prefix(log_decay, group_flags):
    triangle = lower_ones(group_flags.shape[0])
    running = jnp.dot(triangle, log_decay, precision=highest)
    segment = jnp.dot(triangle, group_flags, precision=highest)
    return (running, segment)

def group_state(x_heads, b_proj, log_decay, step_size, group_flags):
    running, segment = group_prefix(log_decay, group_flags)
    same_seg = (segment == segment[-1]).astype(jnp.float32)
    weights = jnp.exp(running[-1][None, :] - running) * same_seg[:, None] * step_size
    end_state = jnp.einsum('sh,shp,sn->hpn', weights, x_heads, b_proj, precision=highest)
    carry_decay = jnp.exp(running[-1]) * (segment[-1] == 0.0).astype(jnp.float32)
    return (end_state, carry_decay)

def group_output(x_heads, b_proj, c_proj, log_decay, step_size, group_flags, start):
    running, segment = group_prefix(log_decay, group_flags)
    order = jnp.arange(group_flags.shape[0])
    same_seg = (segment[:, None] == segment[None, :]) & (order[:, None] >= order[None, :])
    pair_mask = same_seg[:, :, None]
    log_gap = running[:, None, :] - running[None, :, :]
    decays = jnp.where(pair_mask, jnp.exp(jnp.where(pair_mask, log_gap, 0.0)), 0.0)
    scores = jnp.dot(c_proj, b_proj.T, precision=highest)
    weights = scores[:, :, None] * decays * step_size[None, :, :]
    inner_part = jnp.einsum('tsh,shp->thp', weights, x_heads, precision=highest)
    entry_decay = jnp.exp(running) * (segment == 0.0).astype(jnp.float32)[:, None]
    outer_part = jnp.einsum('tn,hpn->thp', c_proj, start, precision=highest) * entry_decay[:, :, None]
    return inner_part + outer_part

def mamba_layer(tokens_f, in_gain, proj_zx, proj_bc, proj_dt, conv_x_weight, conv_x_bias, conv_bc_weight, conv_bc_bias, dt_bias, a_log, skip_scale, norm_gain, out_proj, flag_values):
    length = tokens_f.shape[0]
    normed = low(tokens_f * lax.rsqrt(lax.optimization_barrier(jnp.mean(tokens_f * tokens_f, axis=1, keepdims=True)) + epsilon) * in_gain)
    gate_z = low_back(jnp.dot(normed, proj_zx[:, 0], precision=highest))
    x_raw = low_back(jnp.dot(normed, proj_zx[:, 1], precision=highest))
    bc_raw = low_back(jnp.dot(normed, proj_bc, precision=highest))
    step_raw = low_back(jnp.dot(normed, proj_dt, precision=highest))
    conv_in = low(jnp.concatenate([x_raw, bc_raw], axis=1))
    conv_weight = jnp.concatenate([conv_x_weight, conv_bc_weight], axis=1)
    conv_bias = jnp.concatenate([conv_x_bias, conv_bc_bias])
    segment = jnp.cumsum(flag_values)
    halo_rows = CONV - 1
    padded = jnp.concatenate([jnp.zeros((halo_rows, conv_in.shape[1]), jnp.float32), conv_in])
    padded_seg = jnp.concatenate([jnp.full((halo_rows,), -1.0, jnp.float32), segment])
    summed = conv_bias[None, :] + jnp.zeros_like(conv_in)
    for offset in range(CONV):
        keep_mask = (padded_seg[halo_rows - offset:halo_rows - offset + length] == segment).astype(jnp.float32)
        summed = summed + conv_weight[offset] * padded[halo_rows - offset:halo_rows - offset + length] * keep_mask[:, None]
    active = jax.nn.silu(summed)
    inner_width = HEADS * HEADDIM
    x_heads = active[:, :inner_width].reshape(length, HEADS, HEADDIM)
    b_proj = low(active[:, inner_width:inner_width + NSTATE])
    c_proj = low(active[:, inner_width + NSTATE:])
    step_size = jax.nn.softplus(step_raw + dt_bias)
    log_decay = -step_size * jnp.exp(a_log)
    group_count = length // GROUP
    pieces = (x_heads.reshape(group_count, GROUP, HEADS, HEADDIM), b_proj.reshape(group_count, GROUP, NSTATE), c_proj.reshape(group_count, GROUP, NSTATE), log_decay.reshape(group_count, GROUP, HEADS), step_size.reshape(group_count, GROUP, HEADS), flag_values.reshape(group_count, GROUP))

    def advance(carried, group_piece):
        x_part, b_part, c_part, decay_part, step_part, flag_part = group_piece
        result = group_output(x_part, b_part, c_part, decay_part, step_part, flag_part, carried)
        end_state, carry_decay = group_state(x_part, b_part, decay_part, step_part, flag_part)
        return (carry_decay[:, None, None] * carried + end_state, result)
    initial = jnp.zeros((HEADS, HEADDIM, NSTATE), jnp.float32)
    _, outputs = lax.scan(jax.checkpoint(advance), initial, pieces)
    mixed_ssm = outputs.reshape(length, HEADS, HEADDIM) + skip_scale[None, :, None] * x_heads
    gated_out = mixed_ssm.reshape(length, inner_width) * jax.nn.silu(gate_z)
    inv_rms = lax.rsqrt(lax.optimization_barrier(jnp.mean(gated_out * gated_out, axis=1, keepdims=True)) + epsilon)
    normed_out = low(gated_out * inv_rms * norm_gain)
    return tokens_f + jnp.dot(normed_out, out_proj, precision=highest)

def reference(tokens, start_flags, in_gain, proj_zx, proj_bc, proj_dt, conv_x_weight, conv_x_bias, conv_bc_weight, conv_bc_bias, dt_bias, a_log, skip_scale, norm_gain, out_proj, cotangent):
    flag_values = start_flags.astype(jnp.float32)
    params = (tokens, in_gain, proj_zx, proj_bc, proj_dt, conv_x_weight, conv_x_bias, conv_bc_weight, conv_bc_bias, dt_bias, a_log, skip_scale, norm_gain, out_proj)
    floats = tuple((member.astype(jnp.float32) for member in params))

    def closed(*values):
        return mamba_layer(*values, flag_values)
    result, pullback = jax.vjp(closed, *floats)
    gradients = pullback(cotangent.astype(jnp.float32))
    return (result.astype(jnp.bfloat16), gradients[0], gradients[1], gradients[2], gradients[3], gradients[4], gradients[5], gradients[6], gradients[7], gradients[8], gradients[9], gradients[10], gradients[11], gradients[12], gradients[13])
```

```python
import functools
import jax
import jax.numpy as jnp
from jax import lax
from jax.experimental import pallas as pl
from jax.experimental.pallas import tpu as pltpu
from jax.sharding import PartitionSpec as P

GROUP = 256
MESH = pl.DeviceIdType.MESH
f32 = jnp.float32
bf16 = jnp.bfloat16


def rows_of(ref, start, size):
    return ref.at[pl.ds(pl.multiple_of(start, size), size)]


def greet(pairs):
    barrier = pltpu.get_barrier_semaphore()
    for live, where in pairs:
        @pl.when(live)
        def _():
            pl.semaphore_signal(barrier, inc=1, device_id=where, device_id_type=MESH)
    pl.semaphore_wait(barrier, sum(live.astype(jnp.int32) for live, _ in pairs))


def greet_axis(axis):
    barrier = pltpu.get_barrier_semaphore()
    size, mine = lax.axis_size(axis), lax.axis_index(axis)

    @pl.loop(1, size)
    def _(k):
        pl.semaphore_signal(
            barrier, inc=1, device_id={axis: lax.rem(mine + k, size)}, device_id_type=MESH
        )
    pl.semaphore_wait(barrier, size - 1)


class LineSum:
    def __init__(self, own, out, acc, rin, rx, sems, block):
        self.own, self.out, self.acc, self.rin, self.rx = own, out, acc, rin, rx
        self.send1, self.got_in, self.got_x, self.got_out, self.send2 = (
            sems.at[0], sems.at[1], sems.at[2], sems.at[3], sems.at[4])
        self.block = block
        size, me = lax.axis_size("head"), lax.axis_index("head")
        half = size // 2
        self.size = size
        left = me < half
        self.mid = (me == half - 1) | (me == half)
        self.has_outer = (me > 0) & (me < size - 1)
        self.inner = jnp.where(left, me + 1, me - 1)
        outer = jnp.where(left, me - 1, me + 1)
        self.outer = jnp.clip(outer, 0, size - 1)
        self.lag = max(1, half - 1)

    def pairs(self):
        return [(self.inner >= 0, {"head": self.inner}), (self.has_outer, {"head": self.outer})]

    def copy(self, src, dst, b, send, recv, to):
        return pltpu.make_async_remote_copy(
            src_ref=rows_of(src, b * self.block, self.block),
            dst_ref=rows_of(dst, b * self.block, self.block),
            send_sem=send.at[b], recv_sem=recv.at[b],
            device_id={"head": to}, device_id_type=MESH)

    def inward(self, b):
        rows = pl.ds(pl.multiple_of(b * self.block, self.block), self.block)

        @pl.when(self.has_outer)
        def _():
            self.copy(self.acc, self.rin, b, self.send1, self.got_in, self.outer).wait_recv()
            self.acc[rows] = (self.rin[rows].astype(f32) + self.own[rows].astype(f32)).astype(bf16)

        @pl.when(jnp.logical_not(self.has_outer))
        def _():
            self.acc[rows] = self.own[rows]

        @pl.when(self.mid)
        def _():
            self.copy(self.acc, self.rx, b, self.send1, self.got_x, self.inner).start()

        @pl.when(jnp.logical_not(self.mid))
        def _():
            self.copy(self.acc, self.rin, b, self.send1, self.got_in, self.inner).start()

    def outward(self, b, done=None):
        rows = pl.ds(pl.multiple_of(b * self.block, self.block), self.block)

        @pl.when(self.mid)
        def _():
            self.copy(self.acc, self.rx, b, self.send1, self.got_x, self.inner).wait_recv()
            total = self.acc[rows].astype(f32) + self.rx[rows].astype(f32)
            if done is not None:
                total = done(rows, total)
            self.out[rows] = total.astype(bf16)

        @pl.when(jnp.logical_not(self.mid))
        def _():
            self.copy(self.out, self.out, b, self.send2, self.got_out, self.inner).wait_recv()

        @pl.when(self.has_outer)
        def _():
            self.copy(self.out, self.out, b, self.send2, self.got_out, self.outer).start()

    def drain(self, count):
        @pl.loop(0, count)
        def _(b):
            self.copy(self.acc, self.rin, b, self.send1, self.got_in, self.inner).wait_send()

            @pl.when(self.has_outer)
            def _():
                self.copy(self.out, self.out, b, self.send2, self.got_out, self.outer).wait_send()

    def run(self, first, last, count, done=None):
        @pl.loop(first, last)
        def _(b):
            @pl.when(b < count)
            def _():
                self.inward(b)

            @pl.when(b >= self.lag)
            def _():
                self.outward(b - self.lag, done)


class PlaneSum:
    def __init__(self, own, slots, res, sems, owners):
        self.own, self.slots, self.res = own, slots, res
        self.rs_send, self.rs_got, self.ag_send, self.ag_got = (
            sems.at[0], sems.at[1], sems.at[2], sems.at[3])
        self.owners = owners
        self.size, self.me = lax.axis_size("seq"), lax.axis_index("seq")
        self.piece = own.shape[0] // owners

    def part(self, ref, k):
        return rows_of(ref, k * self.piece, self.piece)

    def scatter_copy(self, to, source):
        return pltpu.make_async_remote_copy(
            src_ref=self.part(self.own, to), dst_ref=self.slots.at[source],
            send_sem=self.rs_send.at[to], recv_sem=self.rs_got.at[source],
            device_id={"seq": to}, device_id_type=MESH)

    def gather_copy(self, owner, to):
        return pltpu.make_async_remote_copy(
            src_ref=self.part(self.res, owner), dst_ref=self.part(self.res, owner),
            send_sem=self.ag_send.at[to], recv_sem=self.ag_got.at[owner],
            device_id={"seq": to}, device_id_type=MESH)

    def scatter(self):
        @pl.loop(1, self.size)
        def _(k):
            to = lax.rem(self.me + k, self.size)

            @pl.when(to < self.owners)
            def _():
                self.scatter_copy(to, self.me).start()

    def reduce(self):
        @pl.when(self.me < self.owners)
        def _():
            @pl.loop(1, self.size)
            def _(k):
                source = lax.rem(self.me + k, self.size)
                self.scatter_copy(self.me, source).wait_recv()
            mine = pl.ds(pl.multiple_of(self.me * self.piece, self.piece), self.piece)
            self.slots[self.me] = self.own[mine]
            total = self.slots[0].astype(f32)
            for k in range(1, self.size):
                total = total + self.slots[k].astype(f32)
            self.res[mine] = total.astype(self.res.dtype)

            @pl.loop(1, self.size)
            def _(k):
                self.gather_copy(self.me, lax.rem(self.me + k, self.size)).start()

    def finish(self):
        @pl.loop(1, self.size)
        def _(k):
            other = lax.rem(self.me + k, self.size)

            @pl.when(other < self.owners)
            def _():
                self.gather_copy(other, self.me).wait_recv()
                self.scatter_copy(other, self.me).wait_send()

        @pl.when(self.me < self.owners)
        def _():
            @pl.loop(1, self.size)
            def _(k):
                self.gather_copy(self.me, lax.rem(self.me + k, self.size)).wait_send()


def line_sum_kernel(block, own, out, acc, rin, rx, sems):
    line = LineSum(own, out, acc, rin, rx, sems, block)
    greet(line.pairs())
    count = own.shape[0] // block
    line.run(0, count + line.lag, count)
    line.drain(count)


VMEM = pl.BlockSpec(memory_space=pltpu.VMEM)


def line_sum(part, block=128):
    rows, width = part.shape
    slot = pltpu.VMEM((rows, width), bf16)
    return pl.pallas_call(
        functools.partial(line_sum_kernel, block),
        out_shape=jax.ShapeDtypeStruct((rows, width), bf16),
        in_specs=[VMEM], out_specs=VMEM,
        scratch_shapes=[slot, slot, slot, pltpu.SemaphoreType.DMA((5, rows // block))],
        compiler_params=pltpu.CompilerParams(
            collective_id=1, has_side_effects=True, vmem_limit_bytes=48 * 2**20),
        name="line_sum",
    )(part)


def tail_kernel(block, owners, part, zx, op, bc, small,
                out, zx_out, op_out, bc_out, small_out,
                acc, rin, rx, zx_slots, op_slots, bc_slots, bc_z, small_slots, small_z,
                line_sems, zx_sems, op_sems, bc_sems, bcz_sems, small_sems, smallz_sems):
    seq, heads = lax.axis_size("seq"), lax.axis_size("head")
    me, my_head = lax.axis_index("seq"), lax.axis_index("head")
    line = LineSum(part, out, acc, rin, rx, line_sems, block)
    sums = [PlaneSum(zx, zx_slots, zx_out, zx_sems, owners[0]),
            PlaneSum(op, op_slots, op_out, op_sems, owners[1])]
    barrier = pltpu.get_barrier_semaphore()
    for axis, size, mine in (("seq", seq, me), ("head", heads, my_head)):
        @pl.loop(1, size)
        def _(k):
            pl.semaphore_signal(barrier, inc=1, device_id={axis: lax.rem(mine + k, size)},
                                device_id_type=MESH)
    pl.semaphore_wait(barrier, seq + heads - 2)

    piece = bc.shape[1] // owners[2]

    def bc_scatter(to, source):
        return pltpu.make_async_remote_copy(
            src_ref=bc.at[:, pl.ds(pl.multiple_of(to * piece, piece), piece)],
            dst_ref=bc_slots.at[source], send_sem=bc_sems.at[0, to], recv_sem=bc_sems.at[1, source],
            device_id={"seq": to}, device_id_type=MESH)

    def bc_gather(owner, to):
        rows = pl.ds(pl.multiple_of(owner * piece, piece), piece)
        return pltpu.make_async_remote_copy(
            src_ref=bc_out.at[rows], dst_ref=bc_out.at[rows],
            send_sem=bc_sems.at[2, to], recv_sem=bc_sems.at[3, owner],
            device_id={"seq": to}, device_id_type=MESH)

    def bc_swap(to, source):
        return pltpu.make_async_remote_copy(
            src_ref=bc_slots.at[me, to], dst_ref=bc_z.at[source],
            send_sem=bcz_sems.at[0, to], recv_sem=bcz_sems.at[1, source],
            device_id={"head": to}, device_id_type=MESH)

    def small_send(to, source):
        return pltpu.make_async_remote_copy(
            src_ref=small, dst_ref=small_slots.at[source],
            send_sem=small_sems.at[0, to], recv_sem=small_sems.at[1, source],
            device_id={"seq": to}, device_id_type=MESH)

    both = small_z.shape[1]
    lone = small.shape[0] - both

    def small_swap(to, source):
        return pltpu.make_async_remote_copy(
            src_ref=small_z.at[my_head], dst_ref=small_z.at[source],
            send_sem=smallz_sems.at[0, to], recv_sem=smallz_sems.at[1, source],
            device_id={"head": to}, device_id_type=MESH)

    for each in sums:
        each.scatter()

    @pl.loop(1, seq)
    def _(k):
        to = lax.rem(me + k, seq)

        @pl.when(to < owners[2])
        def _():
            bc_scatter(to, me).start()
        small_send(to, me).start()

    count = part.shape[0] // block
    steps = count + line.lag
    cut1, cut2 = (steps * 7) // 16, (steps * 10) // 16
    line.run(0, cut1, count)

    for each in sums:
        each.reduce()

    @pl.loop(1, seq)
    def _(k):
        small_send(me, lax.rem(me + k, seq)).wait_recv()
    small_slots[me] = small[...]
    total = small_slots[0]
    for k in range(1, seq):
        total = total + small_slots[k]
    small_out[0:lone] = total[0:lone]
    small_z[my_head] = total[lone:]

    @pl.when(me < owners[2])
    def _():
        @pl.loop(1, seq)
        def _(k):
            bc_scatter(me, lax.rem(me + k, seq)).wait_recv()
        bc_slots[me] = bc[:, pl.ds(pl.multiple_of(me * piece, piece), piece)]
        total = bc_slots[0]
        for k in range(1, seq):
            total = total + bc_slots[k]
        bc_slots[me] = total
        bc_z[my_head] = bc_slots[me, my_head]

    @pl.loop(1, heads)
    def _(k):
        to = lax.rem(my_head + k, heads)
        small_swap(to, my_head).start()

        @pl.when(me < owners[2])
        def _():
            bc_swap(to, my_head).start()

    line.run(cut1, cut2, count)

    @pl.loop(1, heads)
    def _(k):
        source = lax.rem(my_head + k, heads)
        small_swap(my_head, source).wait_recv()

        @pl.when(me < owners[2])
        def _():
            bc_swap(my_head, source).wait_recv()
    total = small_z[0]
    for k in range(1, heads):
        total = total + small_z[k]
    small_out[lone:] = total

    @pl.when(me < owners[2])
    def _():
        total = bc_z[0]
        for k in range(1, heads):
            total = total + bc_z[k]
        bc_out[pl.ds(pl.multiple_of(me * piece, piece), piece)] = total

        @pl.loop(1, seq)
        def _(k):
            bc_gather(me, lax.rem(me + k, seq)).start()

    line.run(cut2, steps, count)
    line.drain(count)
    for each in sums:
        each.finish()

    @pl.loop(1, seq)
    def _(k):
        other = lax.rem(me + k, seq)
        small_send(other, me).wait_send()

        @pl.when(other < owners[2])
        def _():
            bc_gather(other, me).wait_recv()
            bc_scatter(other, me).wait_send()

        @pl.when(me < owners[2])
        def _():
            bc_gather(me, other).wait_send()

    @pl.loop(1, heads)
    def _(k):
        to = lax.rem(my_head + k, heads)
        small_swap(to, my_head).wait_send()

        @pl.when(me < owners[2])
        def _():
            bc_swap(to, my_head).wait_send()


def tail(part, zx, op, bc, small, both, block=128):
    seq, heads = lax.axis_size("seq"), lax.axis_size("head")
    rows, width = part.shape
    owners = (min(seq, zx.shape[0] // 16), min(seq, op.shape[0] // 16), min(seq, bc.shape[1] // 8))
    slot = pltpu.VMEM((rows, width), bf16)
    dma = pltpu.SemaphoreType.DMA
    piece = bc.shape[1] // owners[2]
    return pl.pallas_call(
        functools.partial(tail_kernel, block, owners),
        out_shape=(jax.ShapeDtypeStruct((rows, width), bf16),
                   jax.ShapeDtypeStruct(zx.shape, bf16), jax.ShapeDtypeStruct(op.shape, bf16),
                   jax.ShapeDtypeStruct(bc.shape[1:], f32), jax.ShapeDtypeStruct(small.shape, f32)),
        in_specs=[VMEM] * 5, out_specs=(VMEM,) * 5,
        scratch_shapes=[
            slot, slot, slot,
            pltpu.VMEM((seq, zx.shape[0] // owners[0], zx.shape[1]), bf16),
            pltpu.VMEM((seq, op.shape[0] // owners[1], op.shape[1]), bf16),
            pltpu.VMEM((seq, heads, piece, bc.shape[2]), f32),
            pltpu.VMEM((heads, piece, bc.shape[2]), f32),
            pltpu.VMEM((seq,) + small.shape, f32),
            pltpu.VMEM((heads, both, small.shape[1]), f32),
            dma((5, rows // block)), dma((4, seq)), dma((4, seq)), dma((4, seq)),
            dma((2, heads)), dma((2, seq)), dma((2, heads)),
        ],
        compiler_params=pltpu.CompilerParams(
            collective_id=2, has_side_effects=True, vmem_limit_bytes=56 * 2**20),
        name="tail",
    )(part, zx, op, bc, small)


epsilon = 1e-05
highest = lax.Precision.HIGHEST


def shifted(shard, axis, by):
    size = lax.axis_size(axis)
    pairs = [(i, i + by) for i in range(size) if 0 <= i + by < size]
    return lax.ppermute(shard, axis, pairs)


def carried_in(value, axis, join, neutral, backward):
    count, mine = (lax.axis_size(axis), lax.axis_index(axis))
    pieces = jax.tree.map(lambda part: lax.all_gather(part, axis), value)
    if backward:
        pieces = jax.tree.map(lambda part: part[::-1], pieces)
        mine = count - 1 - mine
    running = jax.tree.map(
        lambda part, zero: jnp.full_like(part, 0) + jnp.asarray(zero, part.dtype), value, neutral
    )

    def lap(position, running):
        longer = join(running, jax.tree.map(lambda part: part[position], pieces))
        return jax.tree.map(lambda new, old: jnp.where(position < mine, new, old), longer, running)

    return lax.fori_loop(0, count - 1, lap, running)


def lower_ones(length):
    order = jnp.arange(length)
    return (order[:, None] >= order[None, :]).astype(jnp.float32)


def group_prefix(log_decay, group_flags):
    triangle = lower_ones(group_flags.shape[0])
    running = jnp.dot(triangle, log_decay, precision=highest)
    segment = jnp.dot(triangle, group_flags, precision=highest)
    return (running, segment)


def group_state(x_heads, b_proj, log_decay, step_size, group_flags):
    running, segment = group_prefix(log_decay, group_flags)
    same_seg = (segment == segment[-1]).astype(jnp.float32)
    weights = jnp.exp(running[-1][None, :] - running) * same_seg[:, None] * step_size
    end_state = jnp.einsum("sh,shp,sn->hpn", weights, x_heads, b_proj, precision=highest)
    carry_decay = jnp.exp(running[-1]) * (segment[-1] == 0.0).astype(jnp.float32)
    return (end_state, carry_decay)


def group_output(x_heads, b_proj, c_proj, log_decay, step_size, group_flags, start):
    running, segment = group_prefix(log_decay, group_flags)
    order = jnp.arange(group_flags.shape[0])
    same_seg = (segment[:, None] == segment[None, :]) & (order[:, None] >= order[None, :])
    pair_mask = same_seg[:, :, None]
    log_gap = running[:, None, :] - running[None, :, :]
    decays = jnp.where(pair_mask, jnp.exp(jnp.where(pair_mask, log_gap, 0.0)), 0.0)
    scores = jnp.dot(c_proj, b_proj.T, precision=highest)
    weights = scores[:, :, None] * decays * step_size[None, :, :]
    inner_part = jnp.einsum("tsh,shp->thp", weights, x_heads, precision=highest)
    entry_decay = jnp.exp(running) * (segment == 0.0).astype(jnp.float32)[:, None]
    outer_part = (
        jnp.einsum("tn,hpn->thp", c_proj, start, precision=highest) * entry_decay[:, :, None]
    )
    return inner_part + outer_part


def in_norm(token_rows, gain_vec):
    return (
        token_rows
        * lax.rsqrt(jnp.mean(token_rows * token_rows, axis=1, keepdims=True) + epsilon)
        * gain_vec
    )


def conv_front(
    extended, weight_x, weight_bc, bias_x, bias_bc, step_raw, dt_bias, a_log, keep_masks
):
    conv_weight = jnp.concatenate([weight_x, weight_bc], axis=1)
    conv_bias = jnp.concatenate([bias_x, bias_bc])
    halo_rows = conv_weight.shape[0] - 1
    length = step_raw.shape[0]
    summed = jnp.broadcast_to(conv_bias[None, :], (length, conv_bias.shape[0]))
    for offset in range(conv_weight.shape[0]):
        summed = (
            summed
            + conv_weight[offset]
            * extended[halo_rows - offset : halo_rows - offset + length]
            * keep_masks[offset][:, None]
        )
    step_size = jax.nn.softplus(step_raw + dt_bias)
    log_decay = -step_size * jnp.exp(a_log)
    return (jax.nn.silu(summed), step_size, log_decay)


def mix_gate(ssm_out, x_heads, skip_scale, gate_z):
    mixed = ssm_out + skip_scale[None, :, None] * x_heads
    return mixed.reshape(gate_z.shape) * jax.nn.silu(gate_z)


def group_starts(group_states, group_carries, incoming):
    starts = []
    current = incoming
    for position in range(group_states.shape[0]):
        starts.append(current)
        current = group_carries[position][:, None, None] * current + group_states[position]
    return jnp.stack(starts)


def device_total(group_states, group_carries):
    current = jnp.zeros_like(group_states[0])
    product = jnp.ones_like(group_carries[0])
    for position in range(group_states.shape[0]):
        current = group_carries[position][:, None, None] * current + group_states[position]
        product = product * group_carries[position]
    return (product, current)


def combine_forward(earlier, later):
    return (earlier[0] * later[0], later[0][:, None, None] * earlier[1] + later[1])


def combine_backward(earlier, later):
    return (later[0] * earlier[0], later[1] + later[0][:, None, None] * earlier[1])


def shards(
    tokens,
    start_flags,
    in_gain,
    proj_zx,
    proj_bc,
    proj_dt,
    conv_x_weight,
    conv_x_bias,
    conv_bc_weight,
    conv_bc_bias,
    dt_bias,
    a_log,
    skip_scale,
    norm_gain,
    out_proj,
    cotangent,
):
    length = tokens.shape[0]
    local_heads = a_log.shape[0]
    local_inner = proj_zx.shape[2]
    head_dim = local_inner // local_heads
    halo_rows = conv_x_weight.shape[0] - 1
    group_count = length // GROUP
    head_count = lax.axis_size("head")
    tokens_f = tokens.astype(jnp.float32)
    flag_values = start_flags.astype(jnp.float32)
    normed = in_norm(tokens_f, in_gain)
    normed_low = normed.astype(jnp.bfloat16)
    zx_raw = jnp.einsum("td,dkc->tkc", normed_low, proj_zx, preferred_element_type=jnp.float32)
    gate_z = zx_raw[:, 0]
    bc_raw = jnp.dot(normed_low, proj_bc, preferred_element_type=jnp.float32)
    step_raw = jnp.dot(normed_low, proj_dt, preferred_element_type=jnp.float32)
    conv_in = jnp.concatenate([zx_raw[:, 1], bc_raw], axis=1).astype(jnp.bfloat16)
    tail_rows, tail_flags = shifted(
        (conv_in[length - halo_rows :], flag_values[length - halo_rows :].astype(jnp.bfloat16)),
        "seq",
        1,
    )
    extended = jnp.concatenate([tail_rows, conv_in]).astype(jnp.float32)
    ext_segment = jnp.cumsum(jnp.concatenate([tail_flags.astype(jnp.float32), flag_values]))
    keep_masks = jnp.stack(
        [
            (
                ext_segment[halo_rows - offset : halo_rows - offset + length]
                == ext_segment[halo_rows:]
            ).astype(jnp.float32)
            for offset in range(halo_rows + 1)
        ]
    )
    front_values, front_pull = jax.vjp(
        lambda ext_rows, weight_x, weight_bc, bias_x, bias_bc, raw_steps, bias_steps, log_rates: conv_front(
            ext_rows,
            weight_x,
            weight_bc,
            bias_x,
            bias_bc,
            raw_steps,
            bias_steps,
            log_rates,
            keep_masks,
        ),
        extended,
        conv_x_weight.astype(jnp.float32),
        conv_bc_weight.astype(jnp.float32),
        conv_x_bias,
        conv_bc_bias,
        step_raw,
        dt_bias,
        a_log,
    )
    active, step_size, log_decay = front_values
    bc_full = lax.all_gather(
        active[:, local_inner:].astype(jnp.bfloat16), "head", axis=1, tiled=True
    ).astype(jnp.float32)
    state_dim = bc_full.shape[1] // 2
    x_heads = active[:, :local_inner].reshape(length, local_heads, head_dim)
    x_groups = x_heads.reshape(group_count, GROUP, local_heads, head_dim)
    b_groups = bc_full[:, :state_dim].reshape(group_count, GROUP, state_dim)
    c_groups = bc_full[:, state_dim:].reshape(group_count, GROUP, state_dim)
    decay_groups = log_decay.reshape(group_count, GROUP, local_heads)
    step_groups = step_size.reshape(group_count, GROUP, local_heads)
    flag_groups = flag_values.reshape(group_count, GROUP)

    def states_fn(x_part, b_part, decay_part, step_part):
        return jax.vmap(group_state)(x_part, b_part, decay_part, step_part, flag_groups)

    def outputs_fn(x_part, b_part, c_part, decay_part, step_part, start_part):
        return jax.vmap(group_output)(
            x_part, b_part, c_part, decay_part, step_part, flag_groups, start_part
        )

    (group_states, group_carries), states_pull = jax.vjp(
        states_fn, x_groups, b_groups, decay_groups, step_groups
    )
    (dev_decay, dev_state), total_pull = jax.vjp(device_total, group_states, group_carries)
    _, incoming = carried_in(
        (dev_decay, dev_state),
        "seq",
        combine_forward,
        (jnp.ones_like(dev_decay), jnp.zeros_like(dev_state)),
        False,
    )
    starts, starts_pull = jax.vjp(group_starts, group_states, group_carries, incoming)
    ssm_groups, outputs_pull = jax.vjp(
        outputs_fn, x_groups, b_groups, c_groups, decay_groups, step_groups, starts
    )
    gated_out, gate_pull = jax.vjp(
        mix_gate, ssm_groups.reshape(length, local_heads, head_dim), x_heads, skip_scale, gate_z
    )
    inner_total = local_inner * head_count
    square_sum = lax.psum(jnp.sum(gated_out * gated_out, axis=1), "head")
    inv_rms = lax.rsqrt(square_sum / inner_total + epsilon)[:, None]
    normed_out = (gated_out * inv_rms * norm_gain).astype(jnp.bfloat16)
    partial_out = jnp.dot(normed_out, out_proj, preferred_element_type=jnp.float32)
    mixed_out = (tokens_f + line_sum(partial_out.astype(jnp.bfloat16)).astype(jnp.float32)).astype(jnp.bfloat16)
    d_normed_out = jnp.einsum("td,cd->tc", cotangent, out_proj, preferred_element_type=jnp.float32)
    grad_out_proj = jnp.einsum(
        "tc,td->cd", normed_out, cotangent, preferred_element_type=jnp.float32
    )
    weighted = d_normed_out * norm_gain
    cross_sum = lax.psum(jnp.sum(weighted * gated_out, axis=1), "head")
    d_gated = weighted * inv_rms - gated_out * inv_rms**3 * (cross_sum / inner_total)[:, None]
    grad_norm_gain = jnp.sum(d_normed_out * gated_out * inv_rms, axis=0)
    d_ssm, d_skip_x, grad_skip_scale, d_gate_z = gate_pull(d_gated)
    d_x_out, d_b_out, d_c_out, d_decay_out, d_step_out, d_starts = outputs_pull(
        d_ssm.reshape(ssm_groups.shape)
    )
    d_states_a, d_carries_a, d_incoming = starts_pull(d_starts)
    _, d_dev_state = carried_in(
        (dev_decay, d_incoming),
        "seq",
        combine_backward,
        (jnp.ones_like(dev_decay), jnp.zeros_like(d_incoming)),
        True,
    )
    d_dev_decay = jnp.sum(d_dev_state * incoming, axis=(1, 2))
    d_states_b, d_carries_b = total_pull((d_dev_decay, d_dev_state))
    d_x_state, d_b_state, d_decay_state, d_step_state = states_pull(
        (d_states_a + d_states_b, d_carries_a + d_carries_b)
    )
    d_b_total = (d_b_out + d_b_state).reshape(length, state_dim)
    d_c_total = d_c_out.reshape(length, state_dim)
    d_bc_slice = lax.psum_scatter(
        jnp.concatenate([d_b_total, d_c_total], axis=1), "head", scatter_dimension=1, tiled=True
    )
    d_x_total = (d_x_out + d_x_state).reshape(length, local_inner) + d_skip_x.reshape(
        length, local_inner
    )
    d_active = jnp.concatenate([d_x_total, d_bc_slice], axis=1)
    d_step_total = (d_step_out + d_step_state).reshape(length, local_heads)
    d_decay_total = (d_decay_out + d_decay_state).reshape(length, local_heads)
    (
        d_ext,
        grad_conv_x_weight,
        grad_conv_bc_weight,
        grad_conv_x_bias,
        grad_conv_bc_bias,
        d_step_raw,
        grad_dt_bias,
        grad_a_log,
    ) = front_pull((d_active, d_step_total, d_decay_total))
    back_rows = shifted(d_ext[:halo_rows], "seq", -1)
    d_conv_in = d_ext[halo_rows:] + jnp.concatenate(
        [jnp.zeros((length - halo_rows, d_ext.shape[1]), jnp.float32), back_rows]
    )
    d_bc_low = d_conv_in[:, local_inner:].astype(jnp.bfloat16)
    d_zx = jnp.stack(
        [d_gate_z.astype(jnp.bfloat16), d_conv_in[:, :local_inner].astype(jnp.bfloat16)], axis=1
    )
    d_step_low = d_step_raw.astype(jnp.bfloat16)
    grad_proj_zx = jnp.einsum("td,tkc->dkc", normed_low, d_zx, preferred_element_type=jnp.float32)
    grad_proj_bc = jnp.einsum("td,tc->dc", normed_low, d_bc_low, preferred_element_type=jnp.float32)
    grad_proj_dt = jnp.einsum(
        "td,th->dh", normed_low, d_step_low, preferred_element_type=jnp.float32
    )
    d_normed_part = jnp.einsum("tkc,dkc->td", d_zx, proj_zx, preferred_element_type=jnp.float32)
    d_normed_part = d_normed_part + jnp.einsum(
        "tc,dc->td", d_bc_low, proj_bc, preferred_element_type=jnp.float32
    )
    d_normed_part = d_normed_part + jnp.einsum(
        "th,dh->td", d_step_low, proj_dt, preferred_element_type=jnp.float32
    )
    _, norm_pull = jax.vjp(in_norm, tokens_f, in_gain)
    _, grad_in_gain = norm_pull(d_normed_part)
    width = tokens.shape[1]
    small = [grad_conv_x_weight, grad_conv_x_bias, grad_dt_bias, grad_a_log, grad_skip_scale, grad_norm_gain]
    flat = jnp.concatenate([grad_proj_dt.T.reshape(-1)] + [each.reshape(-1) for each in small])
    lone = -(-flat.shape[0] // (8 * width)) * 8
    flat = jnp.pad(flat, (0, lone * width - flat.shape[0])).reshape(lone, width)
    head_at = lax.axis_index("head")
    bc_width = conv_bc_bias.shape[0]
    def spread(piece):
        return lax.dynamic_update_slice(jnp.zeros(piece.shape[:-1] + (bc_width * head_count,), jnp.float32), piece, (0,) * (piece.ndim - 1) + (head_at * bc_width,))
    flat_both = jnp.concatenate([grad_in_gain, spread(grad_conv_bc_weight).reshape(-1), spread(grad_conv_bc_bias)])
    flat_both = jnp.pad(flat_both, (0, 8 * width - flat_both.shape[0])).reshape(8, width)
    bc_part = lax.dynamic_update_slice(jnp.zeros((head_count, bc_width, width), jnp.float32), grad_proj_bc.T[None], (head_at, 0, 0))
    d_normed, zx_sum, op_sum, bc_sum, small_sum = tail(
        d_normed_part.astype(jnp.bfloat16),
        grad_proj_zx.reshape(width, -1).astype(jnp.bfloat16),
        grad_out_proj.astype(jnp.bfloat16), bc_part, jnp.concatenate([flat, flat_both]), 8)
    d_tokens, _ = norm_pull(d_normed.astype(jnp.float32))
    grad_tokens = cotangent.astype(jnp.float32) + d_tokens
    at = 0
    found = []
    flat = small_sum[:lone].reshape(-1)
    for like in [grad_proj_dt.T] + small:
        found.append(flat[at : at + like.size].reshape(like.shape))
        at += like.size
    both = small_sum[lone:].reshape(-1)
    taps = conv_bc_weight.shape[0]
    bc_all = bc_width * head_count
    bc_w = lax.dynamic_slice(both[width : width + taps * bc_all].reshape(taps, bc_all), (0, head_at * bc_width), (taps, bc_width))
    bc_b = lax.dynamic_slice(both[width + taps * bc_all : width + (taps + 1) * bc_all], (head_at * bc_width,), (bc_width,))
    return (
        mixed_out,
        grad_tokens,
        both[:width],
        zx_sum.astype(jnp.float32).reshape(grad_proj_zx.shape),
        bc_sum.T,
        found[0].T,
        found[1],
        found[2],
        bc_w,
        bc_b,
        found[3],
        found[4],
        found[5],
        found[6],
        op_sum.astype(jnp.float32),
    )


def solution(mesh):
    in_specs = (
        P("seq", None),
        P("seq"),
        P(),
        P(None, None, "head"),
        P(None, "head"),
        P(None, "head"),
        P(None, "head"),
        P("head"),
        P(None, "head"),
        P("head"),
        P("head"),
        P("head"),
        P("head"),
        P("head"),
        P("head", None),
        P("seq", None),
    )
    out_specs = (
        P("seq", None),
        P("seq", None),
        P(),
        P(None, None, "head"),
        P(None, "head"),
        P(None, "head"),
        P(None, "head"),
        P("head"),
        P(None, "head"),
        P("head"),
        P("head"),
        P("head"),
        P("head"),
        P("head"),
        P("head", None),
    )
    return jax.shard_map(shards, mesh=mesh, in_specs=in_specs, out_specs=out_specs, check_vma=False)
```

```python
import functools

import jax
import jax.numpy as jnp
from jax import lax
from jax.experimental import pallas as pl
from jax.experimental.pallas import tpu as pltpu
from jax.sharding import PartitionSpec as P

MESH = pl.DeviceIdType.MESH
f32 = jnp.float32
bf16 = jnp.bfloat16


def rows_of(ref, start, size):
    return ref.at[pl.ds(pl.multiple_of(start, size), size)]


def greet(pairs):
    barrier = pltpu.get_barrier_semaphore()
    for live, where in pairs:
        @pl.when(live)
        def _():
            pl.semaphore_signal(barrier, inc=1, device_id=where, device_id_type=MESH)
    pl.semaphore_wait(barrier, sum(live.astype(jnp.int32) for live, _ in pairs))


def greet_axis(axis):
    barrier = pltpu.get_barrier_semaphore()
    size, mine = lax.axis_size(axis), lax.axis_index(axis)

    @pl.loop(1, size)
    def _(k):
        pl.semaphore_signal(
            barrier, inc=1, device_id={axis: lax.rem(mine + k, size)}, device_id_type=MESH
        )
    pl.semaphore_wait(barrier, size - 1)


class LineSum:
    def __init__(self, own, out, acc, rin, rx, sems, block):
        self.own, self.out, self.acc, self.rin, self.rx = own, out, acc, rin, rx
        self.send1, self.got_in, self.got_x, self.got_out, self.send2 = (
            sems.at[0], sems.at[1], sems.at[2], sems.at[3], sems.at[4])
        self.block = block
        size, me = lax.axis_size("head"), lax.axis_index("head")
        half = size // 2
        self.size = size
        left = me < half
        self.mid = (me == half - 1) | (me == half)
        self.has_outer = (me > 0) & (me < size - 1)
        self.inner = jnp.where(left, me + 1, me - 1)
        outer = jnp.where(left, me - 1, me + 1)
        self.outer = jnp.clip(outer, 0, size - 1)
        self.lag = max(2, half)

    def pairs(self):
        return [(self.inner >= 0, {"head": self.inner}), (self.has_outer, {"head": self.outer})]

    def copy(self, src, dst, b, send, recv, to):
        return pltpu.make_async_remote_copy(
            src_ref=rows_of(src, b * self.block, self.block),
            dst_ref=rows_of(dst, b * self.block, self.block),
            send_sem=send.at[b], recv_sem=recv.at[b],
            device_id={"head": to}, device_id_type=MESH)

    def inward(self, b):
        rows = pl.ds(pl.multiple_of(b * self.block, self.block), self.block)

        @pl.when(self.has_outer)
        def _():
            self.copy(self.acc, self.rin, b, self.send1, self.got_in, self.outer).wait_recv()
            self.acc[rows] = (self.rin[rows].astype(f32) + self.own[rows].astype(f32)).astype(bf16)

        @pl.when(jnp.logical_not(self.has_outer))
        def _():
            self.acc[rows] = self.own[rows]

        @pl.when(self.mid)
        def _():
            self.copy(self.acc, self.rx, b, self.send1, self.got_x, self.inner).start()

        @pl.when(jnp.logical_not(self.mid))
        def _():
            self.copy(self.acc, self.rin, b, self.send1, self.got_in, self.inner).start()

    def outward(self, b, done=None):
        rows = pl.ds(pl.multiple_of(b * self.block, self.block), self.block)

        @pl.when(self.mid)
        def _():
            self.copy(self.acc, self.rx, b, self.send1, self.got_x, self.inner).wait_recv()
            total = self.acc[rows].astype(f32) + self.rx[rows].astype(f32)
            if done is not None:
                total = done(rows, total)
            self.out[rows] = total.astype(bf16)

        @pl.when(jnp.logical_not(self.mid))
        def _():
            self.copy(self.out, self.out, b, self.send2, self.got_out, self.inner).wait_recv()

        @pl.when(self.has_outer)
        def _():
            self.copy(self.out, self.out, b, self.send2, self.got_out, self.outer).start()

    def drain(self, count):
        @pl.loop(0, count)
        def _(b):
            self.copy(self.acc, self.rin, b, self.send1, self.got_in, self.inner).wait_send()

            @pl.when(self.has_outer)
            def _():
                self.copy(self.out, self.out, b, self.send2, self.got_out, self.outer).wait_send()

    def run(self, first, last, count, done=None):
        if first == 0:
            @pl.when(jnp.logical_not(self.has_outer))
            def _():
                @pl.loop(0, count)
                def _(b):
                    self.inward(b)

        @pl.loop(first, last)
        def _(b):
            @pl.when((b < count) & self.has_outer)
            def _():
                self.inward(b)

            @pl.when(b >= self.lag)
            def _():
                self.outward(b - self.lag, done)


class PlaneSum:
    def __init__(self, own, slots, res, sems, owners):
        self.own, self.slots, self.res = own, slots, res
        self.rs_send, self.rs_got, self.ag_send, self.ag_got = (
            sems.at[0], sems.at[1], sems.at[2], sems.at[3])
        self.owners = owners
        self.size, self.me = lax.axis_size("seq"), lax.axis_index("seq")
        self.piece = own.shape[0] // owners

    def part(self, ref, k):
        return rows_of(ref, k * self.piece, self.piece)

    def scatter_copy(self, to, source):
        return pltpu.make_async_remote_copy(
            src_ref=self.part(self.own, to), dst_ref=self.slots.at[source],
            send_sem=self.rs_send.at[to], recv_sem=self.rs_got.at[source],
            device_id={"seq": to}, device_id_type=MESH)

    def gather_copy(self, owner, to):
        return pltpu.make_async_remote_copy(
            src_ref=self.part(self.res, owner), dst_ref=self.part(self.res, owner),
            send_sem=self.ag_send.at[to], recv_sem=self.ag_got.at[owner],
            device_id={"seq": to}, device_id_type=MESH)

    def scatter(self):
        @pl.loop(1, self.size)
        def _(k):
            to = lax.rem(self.me + k, self.size)

            @pl.when(to < self.owners)
            def _():
                self.scatter_copy(to, self.me).start()

    def reduce(self):
        @pl.when(self.me < self.owners)
        def _():
            @pl.loop(1, self.size)
            def _(k):
                source = lax.rem(self.me + k, self.size)
                self.scatter_copy(self.me, source).wait_recv()
            mine = pl.ds(pl.multiple_of(self.me * self.piece, self.piece), self.piece)
            self.slots[self.me] = self.own[mine]
            total = self.slots[0].astype(f32)
            for k in range(1, self.size):
                total = total + self.slots[k].astype(f32)
            self.res[mine] = total.astype(self.res.dtype)

            @pl.loop(1, self.size)
            def _(k):
                self.gather_copy(self.me, lax.rem(self.me + k, self.size)).start()

    def finish(self):
        @pl.loop(1, self.size)
        def _(k):
            other = lax.rem(self.me + k, self.size)

            @pl.when(other < self.owners)
            def _():
                self.gather_copy(other, self.me).wait_recv()
                self.scatter_copy(other, self.me).wait_send()

        @pl.when(self.me < self.owners)
        def _():
            @pl.loop(1, self.size)
            def _(k):
                self.gather_copy(self.me, lax.rem(self.me + k, self.size)).wait_send()


def line_sum_kernel(block, own, out, acc, rin, rx, sems):
    line = LineSum(own, out, acc, rin, rx, sems, block)
    greet(line.pairs())
    count = own.shape[0] // block
    line.run(0, count + line.lag, count)
    line.drain(count)


VMEM = pl.BlockSpec(memory_space=pltpu.VMEM)


def line_sum(part, block=128):
    rows, width = part.shape
    slot = pltpu.VMEM((rows, width), bf16)
    return pl.pallas_call(
        functools.partial(line_sum_kernel, block),
        out_shape=jax.ShapeDtypeStruct((rows, width), bf16),
        in_specs=[VMEM], out_specs=VMEM,
        scratch_shapes=[slot, slot, slot, pltpu.SemaphoreType.DMA((5, rows // block))],
        compiler_params=pltpu.CompilerParams(
            collective_id=1, has_side_effects=True, vmem_limit_bytes=48 * 2**20),
        name="line_sum",
    )(part)


def tail_kernel(block, owners, part, zx, op, bc, small,
                out, zx_out, op_out, bc_out, small_out,
                acc, rin, rx, zx_slots, op_slots, bc_slots, bc_z, small_slots, small_z,
                line_sems, zx_sems, op_sems, bc_sems, bcz_sems, small_sems, smallz_sems):
    seq, heads = lax.axis_size("seq"), lax.axis_size("head")
    me, my_head = lax.axis_index("seq"), lax.axis_index("head")
    line = LineSum(part, out, acc, rin, rx, line_sems, block)
    sums = [PlaneSum(zx, zx_slots, zx_out, zx_sems, owners[0]),
            PlaneSum(op, op_slots, op_out, op_sems, owners[1])]
    barrier = pltpu.get_barrier_semaphore()
    for axis, size, mine in (("seq", seq, me), ("head", heads, my_head)):
        @pl.loop(1, size)
        def _(k):
            pl.semaphore_signal(barrier, inc=1, device_id={axis: lax.rem(mine + k, size)},
                                device_id_type=MESH)
    pl.semaphore_wait(barrier, seq + heads - 2)

    piece = bc.shape[1] // owners[2]

    def bc_scatter(to, source):
        return pltpu.make_async_remote_copy(
            src_ref=bc.at[:, pl.ds(pl.multiple_of(to * piece, piece), piece)],
            dst_ref=bc_slots.at[source], send_sem=bc_sems.at[0, to], recv_sem=bc_sems.at[1, source],
            device_id={"seq": to}, device_id_type=MESH)

    def bc_gather(owner, to):
        rows = pl.ds(pl.multiple_of(owner * piece, piece), piece)
        return pltpu.make_async_remote_copy(
            src_ref=bc_out.at[rows], dst_ref=bc_out.at[rows],
            send_sem=bc_sems.at[2, to], recv_sem=bc_sems.at[3, owner],
            device_id={"seq": to}, device_id_type=MESH)

    def bc_swap(to, source):
        return pltpu.make_async_remote_copy(
            src_ref=bc_slots.at[me, to], dst_ref=bc_z.at[source],
            send_sem=bcz_sems.at[0, to], recv_sem=bcz_sems.at[1, source],
            device_id={"head": to}, device_id_type=MESH)

    def small_send(to, source):
        return pltpu.make_async_remote_copy(
            src_ref=small, dst_ref=small_slots.at[source],
            send_sem=small_sems.at[0, to], recv_sem=small_sems.at[1, source],
            device_id={"seq": to}, device_id_type=MESH)

    both = small_z.shape[1]
    lone = small.shape[0] - both

    def small_swap(to, source):
        return pltpu.make_async_remote_copy(
            src_ref=small_z.at[my_head], dst_ref=small_z.at[source],
            send_sem=smallz_sems.at[0, to], recv_sem=smallz_sems.at[1, source],
            device_id={"head": to}, device_id_type=MESH)

    for each in sums:
        each.scatter()

    @pl.loop(1, seq)
    def _(k):
        to = lax.rem(me + k, seq)

        @pl.when(to < owners[2])
        def _():
            bc_scatter(to, me).start()
        small_send(to, me).start()

    count = part.shape[0] // block
    steps = count + line.lag
    cut1, cut2 = (steps * 7) // 16, (steps * 10) // 16
    line.run(0, cut1, count)

    for each in sums:
        each.reduce()

    @pl.loop(1, seq)
    def _(k):
        small_send(me, lax.rem(me + k, seq)).wait_recv()
    small_slots[me] = small[...]
    total = small_slots[0]
    for k in range(1, seq):
        total = total + small_slots[k]
    small_out[0:lone] = total[0:lone]
    small_z[my_head] = total[lone:]

    @pl.when(me < owners[2])
    def _():
        @pl.loop(1, seq)
        def _(k):
            bc_scatter(me, lax.rem(me + k, seq)).wait_recv()
        bc_slots[me] = bc[:, pl.ds(pl.multiple_of(me * piece, piece), piece)]
        total = bc_slots[0]
        for k in range(1, seq):
            total = total + bc_slots[k]
        bc_slots[me] = total
        bc_z[my_head] = bc_slots[me, my_head]

    @pl.loop(1, heads)
    def _(k):
        to = lax.rem(my_head + k, heads)
        small_swap(to, my_head).start()

        @pl.when(me < owners[2])
        def _():
            bc_swap(to, my_head).start()

    line.run(cut1, cut2, count)

    @pl.loop(1, heads)
    def _(k):
        source = lax.rem(my_head + k, heads)
        small_swap(my_head, source).wait_recv()

        @pl.when(me < owners[2])
        def _():
            bc_swap(my_head, source).wait_recv()
    total = small_z[0]
    for k in range(1, heads):
        total = total + small_z[k]
    small_out[lone:] = total

    @pl.when(me < owners[2])
    def _():
        total = bc_z[0]
        for k in range(1, heads):
            total = total + bc_z[k]
        bc_out[pl.ds(pl.multiple_of(me * piece, piece), piece)] = total

        @pl.loop(1, seq)
        def _(k):
            bc_gather(me, lax.rem(me + k, seq)).start()

    line.run(cut2, steps, count)
    line.drain(count)
    for each in sums:
        each.finish()

    @pl.loop(1, seq)
    def _(k):
        other = lax.rem(me + k, seq)
        small_send(other, me).wait_send()

        @pl.when(other < owners[2])
        def _():
            bc_gather(other, me).wait_recv()
            bc_scatter(other, me).wait_send()

        @pl.when(me < owners[2])
        def _():
            bc_gather(me, other).wait_send()

    @pl.loop(1, heads)
    def _(k):
        to = lax.rem(my_head + k, heads)
        small_swap(to, my_head).wait_send()

        @pl.when(me < owners[2])
        def _():
            bc_swap(to, my_head).wait_send()


def tail(part, zx, op, bc, small, both, block=128):
    seq, heads = lax.axis_size("seq"), lax.axis_size("head")
    rows, width = part.shape
    owners = (min(seq, zx.shape[0] // 16), min(seq, op.shape[0] // 16), min(seq, bc.shape[1] // 8))
    slot = pltpu.VMEM((rows, width), bf16)
    dma = pltpu.SemaphoreType.DMA
    piece = bc.shape[1] // owners[2]
    return pl.pallas_call(
        functools.partial(tail_kernel, block, owners),
        out_shape=(jax.ShapeDtypeStruct((rows, width), bf16),
                   jax.ShapeDtypeStruct(zx.shape, bf16), jax.ShapeDtypeStruct(op.shape, bf16),
                   jax.ShapeDtypeStruct(bc.shape[1:], f32), jax.ShapeDtypeStruct(small.shape, f32)),
        in_specs=[VMEM] * 5, out_specs=(VMEM,) * 5,
        scratch_shapes=[
            slot, slot, slot,
            pltpu.VMEM((seq, zx.shape[0] // owners[0], zx.shape[1]), bf16),
            pltpu.VMEM((seq, op.shape[0] // owners[1], op.shape[1]), bf16),
            pltpu.VMEM((seq, heads, piece, bc.shape[2]), f32),
            pltpu.VMEM((heads, piece, bc.shape[2]), f32),
            pltpu.VMEM((seq,) + small.shape, f32),
            pltpu.VMEM((heads, both, small.shape[1]), f32),
            dma((5, rows // block)), dma((4, seq)), dma((4, seq)), dma((4, seq)),
            dma((2, heads)), dma((2, seq)), dma((2, heads)),
        ],
        compiler_params=pltpu.CompilerParams(
            collective_id=2, has_side_effects=True, vmem_limit_bytes=56 * 2**20),
        name="tail",
    )(part, zx, op, bc, small)


GROUP = 256
STRIP = 128
GAP = 200.0
epsilon = 1e-05
LIMIT = 56 * 2**20


def dot(a, b):
    return jnp.dot(a, b, preferred_element_type=f32)


def dot_nt(a, b):
    return lax.dot_general(a, b, (((1,), (1,)), ((), ())), preferred_element_type=f32)


def dot_tn(a, b):
    return lax.dot_general(a, b, (((0,), (0,)), ((), ())), preferred_element_type=f32)


def split3(v):
    one = v.astype(bf16)
    rest = v - one.astype(f32)
    two = rest.astype(bf16)
    return one, two, (rest - two.astype(f32)).astype(bf16)


def exact_left(ones, v):
    width = v.shape[1]
    out = dot(ones, jnp.concatenate(split3(v), axis=1))
    return out[:, :width] + out[:, width : 2 * width] + out[:, 2 * width :]


def head_sum(v, group_ones):
    high = v.astype(bf16)
    low = (v - high.astype(f32)).astype(bf16)
    return dot(high, group_ones) + dot(low, group_ones)


def sigmoid(v):
    return 1.0 / (1.0 + jnp.exp(-v))


def softplus(v):
    return jnp.maximum(v, 0.0) + jnp.log1p(jnp.exp(-jnp.abs(v)))


def spread(cols, first, heads, head_dim):
    rows = cols.shape[0]
    per = 128 // head_dim
    lane = lax.broadcasted_iota(jnp.int32, (rows, 128), 1)
    tiles = []
    for at in range(0, heads, per):
        tile = cols[:, first + at : first + at + 1]
        for k in range(1, per):
            tile = jnp.where(lane < k * head_dim, tile, cols[:, first + at + k : first + at + k + 1])
        tiles.append(jnp.broadcast_to(tile, (rows, 128)))
    return jnp.concatenate(tiles, axis=1)


def norm_rows(block, gain):
    value = block.astype(f32)
    inv = lax.rsqrt(jnp.mean(value * value, axis=1, keepdims=True) + epsilon)
    return (value * inv * gain).astype(bf16)


def lane_groups(rows, *parts):
    lane = lax.broadcasted_iota(jnp.int32, (rows, 128), 1)
    out = parts[-1]
    for k in range(len(parts) - 2, -1, -1):
        out = jnp.where(lane < 8 * (k + 1), parts[k], out)
    return out


RAW, STEP, CUM, DEV = 0, 8, 16, 24


def front_kernel(heads, head_dim, state_dim,
                 normed, halo, weights, flags, conv_w, params,
                 gate_out, conv_in_out, conv_out_out, heads_out, state_out, decay_out, halo_out,
                 carry, ext, state, running):
    at = pl.program_id(0)
    rows = normed.shape[0]
    inner = heads * head_dim
    width = inner + 2 * state_dim

    @pl.when(at == 0)
    def _():
        ahead = dot(halo[...], weights[:, inner : inner + width]).astype(bf16)
        halo_out[...] = ahead
        carry[...] = ahead[8:].astype(f32)
        state[...] = jnp.zeros_like(state)
        running[...] = jnp.zeros_like(running)

    raw = dot(normed[...], weights[...])
    gate_out[...] = raw[:, :inner]
    conv_in = raw[:, inner : inner + width].astype(bf16)
    conv_in_out[...] = conv_in
    current = conv_in.astype(f32)
    ext[0:8] = carry[...]
    ext[8:] = current
    carry[...] = ext[rows:]
    keep = 1.0 - flags[...]
    total = conv_w[4:5] + conv_w[0:1] * current
    for j in range(1, 4):
        total = total + conv_w[j : j + 1] * ext[pl.ds(8 - j, rows)] * keep[:, j : j + 1]
    conv_out_out[...] = total
    active = total * sigmoid(total)

    step_raw = raw[:, inner + width :]
    step = softplus(step_raw + params[0:1])
    log_decay = step * params[1:2] - GAP * flags[:, 1:2]
    order_r = lax.broadcasted_iota(jnp.int32, (rows, rows), 0)
    order_c = lax.broadcasted_iota(jnp.int32, (rows, rows), 1)
    cum = exact_left((order_r >= order_c).astype(bf16), log_decay)
    heads_out[...] = lane_groups(rows, step_raw, step, cum, cum + running[0:1])
    end = cum[rows - 1 : rows]
    running[...] = running[...] + end
    weight = step * jnp.exp(end - cum)
    scaled = (active[:, :inner] * spread(weight, 0, heads, head_dim)).astype(bf16)
    b_proj = active[:, inner : inner + state_dim].astype(bf16)
    state[...] = state[...] * spread(jnp.exp(end), 0, heads, head_dim) + dot_tn(b_proj, scaled)

    @pl.when(at == pl.num_programs(0) - 1)
    def _():
        state_out[...] = state[...]
        decay_out[...] = spread(jnp.exp(running[...]), 0, heads, head_dim)


def params_of(name, grid=1):
    return pltpu.CompilerParams(dimension_semantics=("arbitrary",) * grid, vmem_limit_bytes=LIMIT)


def whole(shape):
    return pl.BlockSpec(shape, lambda g: (0,) * len(shape))


def front(normed, halo, weights, flags, conv_w, params, heads, head_dim, state_dim):
    length, width = normed.shape
    count = length // GROUP
    inner = heads * head_dim
    conv = inner + 2 * state_dim

    def by(cols):
        return pl.BlockSpec((GROUP, cols), lambda g: (g, 0))
    shape = jax.ShapeDtypeStruct
    return pl.pallas_call(
        functools.partial(front_kernel, heads, head_dim, state_dim),
        grid=(count,),
        out_shape=(shape((length, inner), f32), shape((length, conv), bf16), shape((length, conv), f32),
                   shape((length, 128), f32), shape((state_dim, inner), f32), shape((8, inner), f32),
                   shape((16, conv), bf16)),
        in_specs=[by(width), whole(halo.shape), whole(weights.shape), by(8), whole(conv_w.shape),
                  whole(params.shape)],
        out_specs=(by(inner), by(conv), by(conv), by(128), whole((state_dim, inner)),
                   whole((8, inner)), whole((16, conv))),
        scratch_shapes=[pltpu.VMEM((8, conv), f32), pltpu.VMEM((GROUP + 8, conv), f32),
                        pltpu.VMEM((state_dim, inner), f32), pltpu.VMEM((8, 128), f32)],
        compiler_params=params_of("front"), name="front",
    )(normed, halo, weights, flags, conv_w, params)


def scan_kernel(backward, own, decay, out, total, fade, lead, got, got_fade, sent, sent_fade, sems):
    size, me = lax.axis_size("seq"), lax.axis_index("seq")
    barrier = pltpu.get_barrier_semaphore()
    rounds = size.bit_length() - 1
    for k in range(rounds):
        pl.semaphore_signal(barrier, inc=1, device_id={"seq": jnp.bitwise_xor(me, 1 << k)},
                            device_id_type=MESH)
    pl.semaphore_wait(barrier, rounds)
    total[...] = own[...]
    fade[...] = decay[...]
    out[...] = jnp.zeros_like(out)
    lead[...] = jnp.ones_like(lead)
    for k in range(rounds):
        sent[k] = total[...].astype(bf16)
        sent_fade[k] = fade[...]
        copies = [
            pltpu.make_async_remote_copy(
                src_ref=src.at[k], dst_ref=dst.at[k], send_sem=sems.at[i, k], recv_sem=sems.at[i + 1, k],
                device_id={"seq": jnp.bitwise_xor(me, 1 << k)}, device_id_type=MESH)
            for src, dst, i in ((sent, got, 0), (sent_fade, got_fade, 2))]
        for copy in copies:
            copy.start()
        for copy in copies:
            copy.wait()
        later = lax.rem(me // (1 << k), 2) == (0 if backward else 1)

        @pl.when(later)
        def _():
            theirs = got[k].astype(f32)
            out[...] = out[...] + lead[0:1] * theirs
            total[...] = total[...] + fade[0:1] * theirs

        @pl.when(jnp.logical_not(later))
        def _():
            total[...] = got[k].astype(f32) + got_fade[k, 0:1] * total[...]

        @pl.when(later)
        def _():
            lead[...] = lead[...] * got_fade[k]
        fade[...] = fade[...] * got_fade[k]


def device_scan(state, decay, backward):
    rounds = lax.axis_size("seq").bit_length() - 1
    return pl.pallas_call(
        functools.partial(scan_kernel, backward),
        out_shape=jax.ShapeDtypeStruct(state.shape, f32),
        in_specs=[VMEM, VMEM], out_specs=VMEM,
        scratch_shapes=[
            pltpu.VMEM(state.shape, f32), pltpu.VMEM(decay.shape, f32), pltpu.VMEM(decay.shape, f32),
            pltpu.VMEM((rounds,) + state.shape, bf16), pltpu.VMEM((rounds,) + decay.shape, f32),
            pltpu.VMEM((rounds,) + state.shape, bf16), pltpu.VMEM((rounds,) + decay.shape, f32),
            pltpu.SemaphoreType.DMA((4, rounds))],
        compiler_params=pltpu.CompilerParams(
            collective_id=4 if backward else 3, has_side_effects=True, vmem_limit_bytes=16 * 2**20),
        name="scan_back" if backward else "scan_ahead",
    )(state, decay)


def strips(rows):
    return [(lo, lo + STRIP) for lo in range(0, rows, STRIP)]


def mix_kernel(heads, head_dim, state_dim,
               conv_out, heads_in, gate, cot, out_proj, gains, entering,
               ssm_out, d_normed_out, partial_out, sums_out, starts_out,
               state):
    at = pl.program_id(0)
    rows = conv_out.shape[0]
    inner = heads * head_dim
    per = 128 // head_dim

    @pl.when(at == 0)
    def _():
        state[...] = entering[...]

    values = conv_out[...]
    active = values * sigmoid(values)
    x = active[:, :inner]
    b_proj = active[:, inner : inner + state_dim].astype(bf16)
    c_proj = active[:, inner + state_dim :].astype(bf16)
    info = heads_in[...]
    flipped = info.T
    stepped = x * spread(info, STEP, heads, head_dim)
    low = stepped.astype(bf16)
    scores = dot_nt(c_proj, b_proj)
    lane = lax.broadcasted_iota(jnp.int32, (rows, 128), 1)
    tiles = []
    for pair in range(heads // per):
        tile = low[:, pair * 128 : (pair + 1) * 128]
        parts = [None] * (rows // STRIP)
        for k in range(per):
            head = pair * per + k
            masked = jnp.where((lane >= k * head_dim) & (lane < (k + 1) * head_dim), tile, jnp.zeros_like(tile))
            for n, (lo, hi) in enumerate(strips(rows)):
                gap = info[lo:hi, CUM + head : CUM + head + 1] - flipped[CUM + head : CUM + head + 1, :hi]
                ok = (lax.broadcasted_iota(jnp.int32, (STRIP, hi), 0) + lo
                      >= lax.broadcasted_iota(jnp.int32, (STRIP, hi), 1))
                weight = jnp.exp(jnp.where(ok, gap, -1e30)) * scores[lo:hi, :hi]
                part = dot(weight.astype(bf16), masked[:hi])
                parts[n] = part if parts[n] is None else parts[n] + part
        tiles.append(jnp.concatenate(parts, axis=0))
    inside = jnp.concatenate(tiles, axis=1)
    cum = info[:, CUM : CUM + 8]
    end = info[rows - 1 : rows]
    start = state[...]
    starts_out[0] = start.astype(bf16)
    grown = spread(jnp.exp(info), CUM, heads, head_dim)
    result = inside + grown * dot(c_proj, start.astype(bf16)) + gains[1:2] * x
    fade = spread(jnp.exp(end - info), CUM, heads, head_dim)
    state[...] = start * spread(jnp.exp(end), CUM, heads, head_dim) + dot_tn(b_proj, (stepped * fade).astype(bf16))
    ssm_out[...] = result
    z = gate[...]
    gated = result * (z * sigmoid(z))
    d_normed = dot_nt(cot[...], out_proj[...])
    d_normed_out[...] = d_normed
    scaled = gated * gains[0:1]
    partial_out[...] = dot(scaled.astype(bf16), out_proj[...]).astype(bf16)
    squares = jnp.sum(gated * gated, axis=1, keepdims=True)
    cross = jnp.sum(d_normed * scaled, axis=1, keepdims=True)
    turned = jnp.where(lane == 0, squares, cross).T
    sums_out[0, pl.ds(at, 1)] = turned[0:1]
    sums_out[1, pl.ds(at, 1)] = turned[1:2]


def mix(conv_out, heads_in, gate, cot, out_proj, gains, entering, heads, head_dim, state_dim):
    length = conv_out.shape[0]
    count = length // GROUP
    inner = heads * head_dim
    width = cot.shape[1]

    def by(cols):
        return pl.BlockSpec((GROUP, cols), lambda g: (g, 0))
    shape = jax.ShapeDtypeStruct
    return pl.pallas_call(
        functools.partial(mix_kernel, heads, head_dim, state_dim),
        grid=(count,),
        out_shape=(shape((length, inner), f32), shape((length, inner), f32), shape((length, width), bf16),
                   shape((2, count, GROUP), f32), shape((count, state_dim, inner), bf16)),
        in_specs=[by(conv_out.shape[1]), by(128), by(inner), by(width), whole(out_proj.shape),
                  whole(gains.shape), whole(entering.shape)],
        out_specs=(by(inner), by(inner), by(width), whole((2, count, GROUP)),
                   pl.BlockSpec((1, state_dim, inner), lambda g: (g, 0, 0))),
        scratch_shapes=[pltpu.VMEM((state_dim, inner), f32)],
        compiler_params=params_of("mix"), name="mix",
    )(conv_out, heads_in, gate, cot, out_proj, gains, entering)


def gate_kernel(heads, head_dim, state_dim, all_channels,
                ssm, gate, d_normed, sums, conv_out, heads_in, cot, gains,
                d_ssm_out, d_gate_out, grad_out, rows_out, total_out):
    at = pl.program_id(0)
    rows = ssm.shape[0]
    inner = heads * head_dim

    @pl.when(at == 0)
    def _():
        grad_out[...] = jnp.zeros_like(grad_out)
        rows_out[...] = jnp.zeros_like(rows_out)
        total_out[...] = jnp.zeros_like(total_out)

    tall = jnp.concatenate([sums[0, pl.ds(at, 1)], sums[1, pl.ds(at, 1)], jnp.zeros((126, rows), f32)], axis=0).T
    inv = lax.rsqrt(tall[:, 0:1] / all_channels + epsilon)
    cross = tall[:, 1:2] / all_channels
    z = gate[...]
    s = sigmoid(z)
    y = ssm[...]
    gated = y * (z * s)
    gain = gains[0:1]
    back = d_normed[...]
    unit = gated * inv
    d_gated = inv * (back * gain - unit * (inv * cross))
    grad_out[...] += dot_tn((unit * gain).astype(bf16), cot[...])
    d_ssm = d_gated * (z * s)
    d_ssm_out[...] = d_ssm
    d_gate_out[...] = (d_gated * y * (s * (1.0 + z * (1.0 - s)))).astype(bf16)
    values = conv_out[...]
    active = values * sigmoid(values)
    rows_out[0:1] += jnp.sum(back * unit, axis=0, keepdims=True)
    rows_out[1:2] += jnp.sum(d_ssm * active[:, :inner], axis=0, keepdims=True)
    c_proj = active[:, inner + state_dim :].astype(bf16)
    grown = spread(jnp.exp(heads_in[...]), DEV, heads, head_dim)
    total_out[...] += dot_tn(c_proj, (grown * d_ssm).astype(bf16))


def gate_back(ssm, gate, d_normed, sums, conv_out, heads_in, cot, gains, heads, head_dim, state_dim, all_channels):
    length, inner = ssm.shape
    width = cot.shape[1]

    def by(cols):
        return pl.BlockSpec((GROUP, cols), lambda g: (g, 0))
    shape = jax.ShapeDtypeStruct
    return pl.pallas_call(
        functools.partial(gate_kernel, heads, head_dim, state_dim, all_channels),
        grid=(length // GROUP,),
        out_shape=(shape((length, inner), f32), shape((length, inner), bf16), shape((inner, width), f32),
                   shape((8, inner), f32), shape((state_dim, inner), f32)),
        in_specs=[by(inner), by(inner), by(inner), whole(sums.shape), by(conv_out.shape[1]), by(128),
                  by(width), whole(gains.shape)],
        out_specs=(by(inner), by(inner), whole((inner, width)), whole((8, inner)),
                   whole((state_dim, inner))),
        compiler_params=params_of("gate_back"), name="gate_back",
    )(ssm, gate, d_normed, sums, conv_out, heads_in, cot, gains)


def back_kernel(heads, head_dim, state_dim,
                d_ssm, conv_out, conv_in, heads_in, starts, entering, flags, conv_w, params, skip, conv_halo,
                d_conv_in_out, d_step_out, conv_grads, head_grads, halo_out,
                lam, shift1, shift2, shift3):
    at = pl.program_id(0)
    rows = d_ssm.shape[0]
    inner = heads * head_dim
    per = 128 // head_dim
    shifts = (shift1, shift2, shift3)

    @pl.when(at == 0)
    def _():
        lam[...] = entering[...]
        conv_grads[...] = jnp.zeros_like(conv_grads)
        head_grads[...] = jnp.zeros_like(head_grads)
        for each in shifts:
            each[rows:] = jnp.zeros((8, each.shape[1]), f32)

    values = conv_out[...]
    gates = sigmoid(values)
    active = values * gates
    x = active[:, :inner]
    b_proj = active[:, inner : inner + state_dim].astype(bf16)
    c_proj = active[:, inner + state_dim :].astype(bf16)
    info = heads_in[...]
    flipped = info.T
    step = spread(info, STEP, heads, head_dim)
    stepped = x * step
    low = stepped.astype(bf16)
    dy = d_ssm[...]
    dy_low = dy.astype(bf16)
    scores = dot_nt(b_proj, c_proj)
    lane = lax.broadcasted_iota(jnp.int32, (rows, 128), 1)
    lane_one = lax.broadcasted_iota(jnp.int32, (STRIP, 128), 1)
    cuts = strips(rows)
    d_scores = [jnp.zeros((STRIP, rows - lo), f32) for lo, _ in cuts]
    d_rows = []
    d_cols = [jnp.zeros((STRIP, 128), f32) for _ in cuts]
    tiles = []
    for pair in range(heads // per):
        tile = low[:, pair * 128 : (pair + 1) * 128]
        dy_tile = dy_low[:, pair * 128 : (pair + 1) * 128]
        parts = [None] * len(cuts)
        for k in range(per):
            head = pair * per + k
            own = (lane >= k * head_dim) & (lane < (k + 1) * head_dim)
            masked = jnp.where(own, tile, jnp.zeros_like(tile))
            dy_masked = jnp.where(own, dy_tile, jnp.zeros_like(dy_tile))
            row_total = jnp.zeros((1, rows), f32)
            for n, (lo, hi) in enumerate(cuts):
                gap = flipped[CUM + head : CUM + head + 1, lo:] - info[lo:hi, CUM + head : CUM + head + 1]
                ok = (lax.broadcasted_iota(jnp.int32, (STRIP, rows - lo), 1)
                      >= lax.broadcasted_iota(jnp.int32, (STRIP, rows - lo), 0))
                decay = jnp.exp(jnp.where(ok, gap, -1e30))
                weight = decay * scores[lo:hi, lo:]
                part = dot(weight.astype(bf16), dy_masked[lo:])
                parts[n] = part if parts[n] is None else parts[n] + part
                pairs = dot_nt(masked[lo:hi], dy_tile[lo:])
                d_scores[n] = d_scores[n] + pairs * decay
                moved = pairs * weight
                d_cols[n] = d_cols[n] - jnp.where(lane_one == head, jnp.sum(moved, axis=1, keepdims=True), 0.0)
                col = jnp.sum(moved, axis=0, keepdims=True)
                if lo:
                    col = jnp.concatenate([jnp.zeros((1, lo), f32), col], axis=1)
                row_total = row_total + col
            d_rows.append(row_total)
        tiles.append(jnp.concatenate(parts, axis=0))
    d_stepped = jnp.concatenate(tiles, axis=1)
    d_cum = jnp.concatenate(d_cols, axis=0)
    d_cum = d_cum + jnp.concatenate(d_rows + [jnp.zeros((128 - heads, rows), f32)], axis=0).T
    full = jnp.concatenate(
        [jnp.concatenate([jnp.zeros((STRIP, lo), f32), part], axis=1) if lo else part
         for part, (lo, _) in zip(d_scores, cuts)], axis=0).astype(bf16)
    d_b = dot(full, c_proj)
    d_c = dot_tn(full, b_proj)

    group_ones = (lax.broadcasted_iota(jnp.int32, (inner, 128), 0) // head_dim
                  == lax.broadcasted_iota(jnp.int32, (inner, 128), 1)).astype(bf16)
    start = starts[0]
    after = lam[...]
    after_low = after.astype(bf16)
    end = info[rows - 1 : rows]
    grown = spread(jnp.exp(info), CUM, heads, head_dim)
    fade = spread(jnp.exp(end - info), CUM, heads, head_dim)
    end_grown = spread(jnp.exp(end), CUM, heads, head_dim)
    from_after = fade * dot(b_proj, after_low)
    d_stepped = d_stepped + from_after
    grown_dy = grown * dy
    grown_low = grown_dy.astype(bf16)
    to_cum = head_sum(grown_dy * dot(c_proj, start), group_ones)
    left = head_sum(stepped * from_after, group_ones)
    kept = jnp.sum(after * start.astype(f32), axis=0, keepdims=True) * end_grown
    kept = head_sum(jnp.broadcast_to(kept, (8, inner)), group_ones)[0:1]
    last = kept + jnp.sum(left, axis=0, keepdims=True)
    row_id = lax.broadcasted_iota(jnp.int32, (rows, 128), 0)
    d_cum = d_cum + to_cum - left + jnp.where(row_id == rows - 1, last, 0.0)
    d_c = d_c + dot_nt(grown_low, start)
    d_b = d_b + dot_nt((fade * stepped).astype(bf16), after_low)
    lam[...] = end_grown * after + dot_tn(c_proj, grown_low)
    d_step = head_sum(d_stepped * x, group_ones)
    d_x = step * d_stepped + skip[0:1] * dy

    order_r = lax.broadcasted_iota(jnp.int32, (rows, rows), 0)
    order_c = lax.broadcasted_iota(jnp.int32, (rows, rows), 1)
    free = 1.0 - flags[...]
    d_decay = exact_left((order_r <= order_c).astype(bf16), d_cum) * free[:, 1:2]
    rate = params[1:2]
    real = lane < heads
    step_raw = jnp.where(real, info, 0.0) + params[0:1]
    slope = sigmoid(step_raw)
    d_pre = jnp.where(real, (d_step + d_decay * rate) * slope, 0.0)
    d_step_out[...] = d_pre.astype(bf16)
    head_grads[0:1] += jnp.sum(d_pre, axis=0, keepdims=True)
    head_grads[1:2] += jnp.sum(jnp.where(real, d_decay * softplus(step_raw) * rate, 0.0), axis=0, keepdims=True)

    d_active = jnp.concatenate([d_x, d_b, d_c], axis=1)
    d_conv = d_active * (gates * (1.0 + values * (1.0 - gates)))
    taken = conv_in[...].astype(f32)
    total = d_conv * conv_w[0:1]
    conv_grads[0:1] += jnp.sum(d_conv * taken, axis=0, keepdims=True)
    conv_grads[4:5] += jnp.sum(d_conv, axis=0, keepdims=True)
    for j in range(1, 4):
        ref = shifts[j - 1]
        ref[0:rows] = d_conv * free[:, j : j + 1]
        moved = ref[pl.ds(j, rows)]
        total = total + moved * conv_w[j : j + 1]
        conv_grads[j : j + 1] += jnp.sum(moved * taken, axis=0, keepdims=True)
    d_conv_in_out[...] = total.astype(bf16)

    @pl.when(at == pl.num_programs(0) - 1)
    def _():
        ahead = conv_halo[...].astype(f32)
        halo_out[...] = jnp.zeros_like(halo_out)
        for j in range(1, 4):
            first = shifts[j - 1][0:8]
            for t in range(j):
                row = 16 + t - j
                conv_grads[j : j + 1] += first[t : t + 1] * ahead[row : row + 1]
                halo_out[row - 8 : row - 7] += first[t : t + 1] * conv_w[j : j + 1]
    for each in shifts:
        each[rows:] = each[0:8]


def back(d_ssm, conv_out, conv_in, heads_in, starts, entering, flags, conv_w, params, skip, conv_halo,
         heads, head_dim, state_dim):
    length, inner = d_ssm.shape
    count = length // GROUP
    conv = conv_out.shape[1]

    def by(cols):
        return pl.BlockSpec((GROUP, cols), lambda g: (count - 1 - g, 0))
    shape = jax.ShapeDtypeStruct
    return pl.pallas_call(
        functools.partial(back_kernel, heads, head_dim, state_dim),
        grid=(count,),
        out_shape=(shape((length, conv), bf16), shape((length, 128), bf16), shape((8, conv), f32),
                   shape((8, 128), f32), shape((8, conv), f32)),
        in_specs=[by(inner), by(conv), by(conv), by(128),
                  pl.BlockSpec((1, state_dim, inner), lambda g: (count - 1 - g, 0, 0)),
                  whole(entering.shape), by(8), whole(conv_w.shape), whole(params.shape),
                  whole(skip.shape), whole(conv_halo.shape)],
        out_specs=(by(conv), by(128), whole((8, conv)), whole((8, 128)), whole((8, conv))),
        scratch_shapes=[pltpu.VMEM((state_dim, inner), f32)] + [pltpu.VMEM((GROUP + 8, conv), f32)] * 3,
        compiler_params=params_of("back"), name="back",
    )(d_ssm, conv_out, conv_in, heads_in, starts, entering, flags, conv_w, params, skip, conv_halo)


def project_kernel(count, normed, tokens, d_gate, d_conv, d_step, d_back, weights,
                   partial_out, grad_zx, grad_bc, grad_gain):
    at = pl.program_id(0)
    inner = d_gate.shape[1]

    @pl.when(at == 0)
    def _():
        grad_zx[...] = jnp.zeros_like(grad_zx)
        grad_bc[...] = jnp.zeros_like(grad_bc)
        grad_gain[...] = jnp.zeros_like(grad_gain)

    def add(block, source, d_rows, skipped):
        d_normed = dot_nt(d_rows, weights[:, skipped:])
        grad_zx[:, skipped:] += dot_tn(block, d_rows[:, : 2 * inner - skipped])
        grad_bc[...] += dot_tn(d_rows[:, 2 * inner - skipped :], block)
        value = source.astype(f32)
        inv = lax.rsqrt(jnp.mean(value * value, axis=1, keepdims=True) + epsilon)
        grad_gain[0:1] += jnp.sum(d_normed * (value * inv), axis=0, keepdims=True)
        return d_normed
    d_rows = jnp.concatenate([d_gate[...], d_conv[...], d_step[...]], axis=1)
    partial_out[...] = add(normed[...], tokens[...], d_rows, 0).astype(bf16)

    @pl.when(at == count - 1)
    def _():
        extra = add(normed[GROUP - 16 :], tokens[GROUP - 16 :], d_back[...], inner)
        partial_out[GROUP - 16 :] = (partial_out[GROUP - 16 :].astype(f32) + extra).astype(bf16)


def project_back(normed, tokens, d_gate, d_conv, d_step, d_back, weights):
    length, width = normed.shape
    inner, conv = d_gate.shape[1], d_conv.shape[1]
    count = length // GROUP
    rest = weights.shape[1] - 2 * inner

    def by(cols):
        return pl.BlockSpec((GROUP, cols), lambda g: (g, 0))
    shape = jax.ShapeDtypeStruct
    return pl.pallas_call(
        functools.partial(project_kernel, count),
        grid=(count,),
        out_shape=(shape((length, width), bf16), shape((width, 2 * inner), f32), shape((rest, width), f32),
                   shape((8, width), f32)),
        in_specs=[by(width), by(width), by(inner), by(conv), by(128), whole(d_back.shape),
                  whole(weights.shape)],
        out_specs=(by(width), whole((width, 2 * inner)), whole((rest, width)), whole((8, width))),
        compiler_params=params_of("project_back"), name="project_back",
    )(normed, tokens, d_gate, d_conv, d_step, d_back, weights)


def swap_kernel(own, out, slots, sems):
    size, me = lax.axis_size("head"), lax.axis_index("head")
    greet_axis("head")

    def copy(to, source):
        return pltpu.make_async_remote_copy(
            src_ref=own, dst_ref=slots.at[source], send_sem=sems.at[0, to], recv_sem=sems.at[1, source],
            device_id={"head": to}, device_id_type=MESH)

    @pl.loop(1, size)
    def _(k):
        copy(lax.rem(me + k, size), me).start()
    slots[me] = own[...]

    @pl.loop(1, size)
    def _(k):
        copy(me, lax.rem(me + k, size)).wait_recv()
    total = slots[0]
    for k in range(1, size):
        total = total + slots[k]
    out[...] = total

    @pl.loop(1, size)
    def _(k):
        copy(lax.rem(me + k, size), me).wait_send()


def head_total(sums):
    size = lax.axis_size("head")
    return pl.pallas_call(
        swap_kernel, out_shape=jax.ShapeDtypeStruct(sums.shape, f32),
        in_specs=[VMEM], out_specs=VMEM,
        scratch_shapes=[pltpu.VMEM((size,) + sums.shape, f32), pltpu.SemaphoreType.DMA((2, size))],
        compiler_params=pltpu.CompilerParams(collective_id=5, has_side_effects=True),
        name="head_total",
    )(sums)


def begin_kernel(tokens, gain, tail_rows, proj_bc, conv_bc,
                 normed, halo, proj_all, conv_all, landed, sems, seq_sems):
    heads, my_head = lax.axis_size("head"), lax.axis_index("head")
    seq, me = lax.axis_size("seq"), lax.axis_index("seq")
    before, after = lax.rem(me + seq - 1, seq), lax.rem(me + 1, seq)
    barrier = pltpu.get_barrier_semaphore()

    @pl.loop(1, heads)
    def _(k):
        pl.semaphore_signal(barrier, inc=1, device_id={"head": lax.rem(my_head + k, heads)},
                            device_id_type=MESH)
    for to in (before, after):
        pl.semaphore_signal(barrier, inc=1, device_id={"seq": to}, device_id_type=MESH)
    pl.semaphore_wait(barrier, heads + 1)

    def copies(to, source):
        return [pltpu.make_async_remote_copy(
            src_ref=src, dst_ref=dst.at[source], send_sem=sems.at[i, to], recv_sem=sems.at[i + 1, source],
            device_id={"head": to}, device_id_type=MESH)
            for src, dst, i in ((proj_bc, proj_all, 0), (conv_bc, conv_all, 2))]
    row_copy = pltpu.make_async_remote_copy(
        src_ref=tail_rows, dst_ref=landed, send_sem=seq_sems.at[0], recv_sem=seq_sems.at[1],
        device_id={"seq": after}, device_id_type=MESH)
    row_copy.start()

    @pl.loop(1, heads)
    def _(k):
        for copy in copies(lax.rem(my_head + k, heads), my_head):
            copy.start()
    proj_all[my_head] = proj_bc[...]
    conv_all[my_head] = conv_bc[...]
    count = tokens.shape[0] // 128

    @pl.loop(0, count)
    def _(b):
        rows = pl.ds(pl.multiple_of(b * 128, 128), 128)
        normed[rows] = norm_rows(tokens[rows], gain[0:1])
    row_copy.wait()
    halo[...] = jnp.where(me > 0, norm_rows(landed[...], gain[0:1]), jnp.zeros(halo.shape, bf16))

    @pl.loop(1, heads)
    def _(k):
        other = lax.rem(my_head + k, heads)
        for copy in copies(my_head, other):
            copy.wait_recv()
        for copy in copies(other, my_head):
            copy.wait_send()


def begin(tokens, gain, tail_rows, proj_bc, conv_bc):
    heads = lax.axis_size("head")
    shape = jax.ShapeDtypeStruct
    return pl.pallas_call(
        begin_kernel,
        out_shape=(shape(tokens.shape, bf16), shape(tail_rows.shape, bf16),
                   shape((heads,) + proj_bc.shape, bf16), shape((heads,) + conv_bc.shape, f32)),
        in_specs=[VMEM] * 5, out_specs=(VMEM,) * 4,
        scratch_shapes=[pltpu.VMEM(tail_rows.shape, bf16), pltpu.SemaphoreType.DMA((4, heads)),
                        pltpu.SemaphoreType.DMA((2,))],
        compiler_params=pltpu.CompilerParams(
            collective_id=6, has_side_effects=True, vmem_limit_bytes=32 * 2**20),
        name="begin",
    )(tokens, gain, tail_rows, proj_bc, conv_bc)


def halo_kernel(own, out, sems):
    seq, me = lax.axis_size("seq"), lax.axis_index("seq")
    before, after = lax.rem(me + seq - 1, seq), lax.rem(me + 1, seq)
    barrier = pltpu.get_barrier_semaphore()
    for to in (before, after):
        pl.semaphore_signal(barrier, inc=1, device_id={"seq": to}, device_id_type=MESH)
    pl.semaphore_wait(barrier, 2)
    copy = pltpu.make_async_remote_copy(
        src_ref=own, dst_ref=out, send_sem=sems.at[0], recv_sem=sems.at[1],
        device_id={"seq": before}, device_id_type=MESH)
    copy.start()
    copy.wait()


def to_before(rows):
    return pl.pallas_call(
        halo_kernel, out_shape=jax.ShapeDtypeStruct(rows.shape, rows.dtype),
        in_specs=[VMEM], out_specs=VMEM, scratch_shapes=[pltpu.SemaphoreType.DMA((2,))],
        compiler_params=pltpu.CompilerParams(collective_id=7, has_side_effects=True),
        name="to_before",
    )(rows)


def padded(block, rows, cols):
    return jnp.pad(block, ((0, rows - block.shape[0]), (0, cols - block.shape[1])))


def shards(
    tokens, start_flags, in_gain, proj_zx, proj_bc, proj_dt, conv_x_weight, conv_x_bias,
    conv_bc_weight, conv_bc_bias, dt_bias, a_log, skip_scale, norm_gain, out_proj, cotangent,
):
    length, width = tokens.shape
    heads = a_log.shape[0]
    inner = proj_zx.shape[2]
    head_dim = inner // heads
    taps = conv_x_weight.shape[0]
    head_count = lax.axis_size("head")
    bc_part = conv_bc_bias.shape[0]
    bc_width = bc_part * head_count
    state_dim = bc_width // 2
    my_head = lax.axis_index("head")

    flag = start_flags.astype(f32)
    free = 1.0 - flag
    free1 = jnp.pad(free, (1, 0), constant_values=1.0)[:length]
    free2 = jnp.pad(free, (2, 0), constant_values=1.0)[:length]
    flags = jnp.pad(jnp.stack([flag, 1.0 - free * free1, 1.0 - free * free1 * free2], axis=1), ((0, 0), (1, 4)))
    last = jnp.stack([free[length - 1] * free[length - 2], free[length - 1], jnp.ones((), f32)])
    tail_mask = jnp.pad(last, (13, 0))[:, None]
    tail_rows = (tokens[length - 16 :].astype(f32) * tail_mask).astype(bf16)
    gain8 = jnp.broadcast_to(in_gain[None], (8, width))
    conv_bc = padded(jnp.concatenate([conv_bc_weight.astype(f32), conv_bc_bias[None]]), 8, bc_part)

    normed, halo, proj_all, conv_all = begin(tokens, gain8, tail_rows, proj_bc, conv_bc)

    eight = jnp.pad(proj_dt, ((0, 0), (0, 8 - heads)))
    weights = jnp.concatenate(
        [proj_zx[:, 0], proj_zx[:, 1], jnp.moveaxis(proj_all, 0, 1).reshape(width, bc_width)]
        + [eight] * 16, axis=1)
    conv_x = padded(jnp.concatenate([conv_x_weight.astype(f32), conv_x_bias[None]]), 8, inner)
    conv_w = jnp.concatenate([conv_x, jnp.moveaxis(conv_all, 0, 1).reshape(8, bc_width)], axis=1)
    head_rows = jnp.pad(jnp.stack([dt_bias, -jnp.exp(a_log)]), ((0, 6), (0, 8 - heads)))
    params = jnp.tile(head_rows, (1, 16))
    skip = jnp.repeat(skip_scale, head_dim)
    gains = jnp.pad(jnp.stack([norm_gain, skip]), ((0, 6), (0, 0)))
    skip8 = jnp.broadcast_to(skip[None], (8, inner))

    gate, conv_in, conv_out, info, state, decay, conv_halo = front(
        normed, halo, weights, flags, conv_w, params, heads, head_dim, state_dim)
    entering = device_scan(state, decay, False)
    ssm, d_normed_out, partial, sums, starts = mix(
        conv_out, info, gate, cotangent, out_proj, gains, entering, heads, head_dim, state_dim)
    sums = head_total(sums)
    mixed = line_sum(partial, 64)
    all_channels = inner * head_count
    inv_rms = lax.rsqrt(sums[0].reshape(length, 1) / all_channels + epsilon)
    mixed_out = (tokens.astype(f32) + mixed.astype(f32) * inv_rms).astype(bf16)
    d_ssm, d_gate, grad_out, gate_rows, d_total = gate_back(
        ssm, gate, d_normed_out, sums, conv_out, info, cotangent, gains, heads, head_dim, state_dim,
        all_channels)
    leaving = device_scan(d_total, decay, True)
    d_conv, d_step, conv_grads, head_grads, back_rows = back(
        d_ssm, conv_out, conv_in, info, starts, leaving, flags, conv_w, params, skip8, conv_halo,
        heads, head_dim, state_dim)
    landed = to_before(back_rows)
    last_device = lax.axis_index("seq") == lax.axis_size("seq") - 1
    landed = jnp.where(last_device, 0.0, landed * tail_mask[8:])
    d_back = jnp.pad(landed.astype(bf16), ((8, 0), (0, 128)))
    part, grad_zx, grad_bc, grad_gain = project_back(
        normed, tokens, d_gate, d_conv, d_step, d_back, weights)

    right = jnp.concatenate([gate_rows[:2], padded(head_grads[:2], 6, inner)])
    small = jnp.concatenate([
        grad_bc[bc_width : bc_width + 8],
        padded(jnp.concatenate([conv_grads[:, :inner], right], axis=1), 8, width),
        grad_gain[:1], padded(conv_grads[: taps + 1, inner:], 7, width)])
    d_normed, zx_sum, op_sum, bc_sum, small_sum = tail(
        part, grad_zx.astype(bf16), grad_out.astype(bf16),
        grad_bc[:bc_width].reshape(head_count, bc_part, width), small, 8, 64)

    tokens_f = tokens.astype(f32)
    inv = lax.rsqrt(jnp.mean(tokens_f * tokens_f, axis=1, keepdims=True) + epsilon)
    xhat = tokens_f * inv
    scaled = d_normed.astype(f32) * in_gain
    grad_tokens = cotangent.astype(f32) + inv * (
        scaled - xhat * jnp.mean(scaled * xhat, axis=1, keepdims=True))
    conv_bc_sum = lax.dynamic_slice(small_sum, (17, my_head * bc_part), (taps + 1, bc_part))
    return (
        mixed_out,
        grad_tokens,
        small_sum[16],
        zx_sum.astype(f32).reshape(width, 2, inner),
        bc_sum.T,
        small_sum[:heads].T,
        small_sum[8 : 8 + taps, :inner],
        small_sum[8 + taps, :inner],
        conv_bc_sum[:taps],
        conv_bc_sum[taps],
        small_sum[10, inner : inner + heads],
        small_sum[11, inner : inner + heads],
        small_sum[9, inner : 2 * inner].reshape(heads, head_dim).sum(axis=1),
        small_sum[8, inner : 2 * inner],
        op_sum.astype(f32),
    )


def solution(mesh):
    in_specs = (
        P("seq", None),
        P("seq"),
        P(),
        P(None, None, "head"),
        P(None, "head"),
        P(None, "head"),
        P(None, "head"),
        P("head"),
        P(None, "head"),
        P("head"),
        P("head"),
        P("head"),
        P("head"),
        P("head"),
        P("head", None),
        P("seq", None),
    )
    out_specs = (
        P("seq", None),
        P("seq", None),
        P(),
        P(None, None, "head"),
        P(None, "head"),
        P(None, "head"),
        P(None, "head"),
        P("head"),
        P(None, "head"),
        P("head"),
        P("head"),
        P("head"),
        P("head"),
        P("head"),
        P("head", None),
    )
    return jax.shard_map(shards, mesh=mesh, in_specs=in_specs, out_specs=out_specs, check_vma=False)
```

```python
import functools

import jax
import jax.numpy as jnp
from jax import lax
from jax.experimental import pallas as pl
from jax.experimental.pallas import tpu as pltpu
from jax.sharding import PartitionSpec as P

MESH = pl.DeviceIdType.MESH
f32 = jnp.float32
bf16 = jnp.bfloat16
VMEM = pl.BlockSpec(memory_space=pltpu.VMEM)
HBM = pl.BlockSpec(memory_space=pl.ANY)
DMA = pltpu.SemaphoreType.DMA


def rows_of(ref, start, size):
    return ref.at[pl.ds(pl.multiple_of(start, size), size)]


def other_of(axis, k):
    size = lax.axis_size(axis)
    return lax.rem(lax.axis_index(axis) + k, size)


def greet(*axes):
    barrier = pltpu.get_barrier_semaphore()
    count = 0
    for axis in axes:
        size = lax.axis_size(axis)
        count += size - 1

        @pl.loop(1, size)
        def _(k):
            pl.semaphore_signal(barrier, inc=1, device_id={axis: other_of(axis, k)}, device_id_type=MESH)
    pl.semaphore_wait(barrier, count)


class LineSum:
    AHEAD = 3

    def __init__(self, own, got, total, out, sems, block):
        self.own, self.got, self.total, self.out = own, got, total, out
        self.send1, self.got_in, self.got_total, self.send2, self.stored = (sems.at[i] for i in range(5))
        self.block = block
        self.count = own.shape[0] // block
        size, me = lax.axis_size("head"), lax.axis_index("head")
        half = size // 2
        left = me < half
        self.mid = (me == half - 1) | (me == half)
        self.has_outer = (me > 0) & (me < size - 1)
        self.inner = jnp.where(left, me + 1, me - 1)
        self.outer = jnp.clip(jnp.where(left, me - 1, me + 1), 0, size - 1)

    @staticmethod
    def sems(rows, block):
        return DMA((5, rows // block))

    def rows(self, b):
        return pl.ds(pl.multiple_of(b * self.block, self.block), self.block)

    def copy(self, src, dst, b, send, recv, to):
        return pltpu.make_async_remote_copy(
            src_ref=src.at[self.rows(b)], dst_ref=dst.at[self.rows(b)],
            send_sem=send.at[b], recv_sem=recv.at[b], device_id={"head": to}, device_id_type=MESH)

    def store(self, b):
        return pltpu.make_async_copy(
            self.total.at[self.rows(b)], self.out.at[self.rows(b)], self.stored.at[b])

    def inward(self, b):
        rows = self.rows(b)

        @pl.when(self.has_outer)
        def _():
            self.copy(self.own, self.got, b, self.send1, self.got_in, self.outer).wait_recv()
            self.own[rows] = (self.got[rows].astype(f32) + self.own[rows].astype(f32)).astype(bf16)

        @pl.when(self.mid)
        def _():
            self.copy(self.own, self.total, b, self.send1, self.got_total, self.inner).start()

        @pl.when(jnp.logical_not(self.mid))
        def _():
            self.copy(self.own, self.got, b, self.send1, self.got_in, self.inner).start()

    def outward(self, b):
        rows = self.rows(b)
        self.copy(self.own, self.total, b, self.send1, self.got_total, self.inner).wait_recv()

        @pl.when(self.mid)
        def _():
            self.total[rows] = (self.own[rows].astype(f32) + self.total[rows].astype(f32)).astype(bf16)

        @pl.when(self.has_outer)
        def _():
            self.copy(self.total, self.total, b, self.send2, self.got_total, self.outer).start()
        self.store(b).start()

    def serve(self, first, last, lag):
        @pl.when(self.has_outer)
        def _():
            @pl.loop(first, last)
            def _(b):
                @pl.when(b < self.count)
                def _():
                    self.inward(b)

                @pl.when(b >= lag)
                def _():
                    self.outward(b - lag)

    def send(self, first, last):
        @pl.when(jnp.logical_not(self.has_outer))
        def _():
            @pl.loop(first, last)
            def _(b):
                @pl.when(b >= self.AHEAD)
                def _():
                    self.copy(self.own, self.got, b - self.AHEAD, self.send1, self.got_in, self.inner).wait_send()
                self.inward(b)

    def finish(self):
        @pl.when(jnp.logical_not(self.has_outer))
        def _():
            pl.loop(0, self.count)(self.outward)

        @pl.loop(0, self.count)
        def _(b):
            @pl.when(self.has_outer | (b >= self.count - self.AHEAD))
            def _():
                self.copy(self.own, self.got, b, self.send1, self.got_in, self.inner).wait_send()
            self.store(b).wait()

            @pl.when(self.has_outer)
            def _():
                self.copy(self.total, self.total, b, self.send2, self.got_total, self.outer).wait_send()


class PlaneSum:
    def __init__(self, own, slots, res, sems, owners):
        self.own, self.slots, self.res = own, slots, res
        self.rs_send, self.rs_got, self.ag_send, self.ag_got = (sems.at[i] for i in range(4))
        self.owners = owners
        self.size, self.me = lax.axis_size("seq"), lax.axis_index("seq")
        self.piece = own.shape[0] // owners

    def part(self, ref, k):
        return rows_of(ref, k * self.piece, self.piece)

    def scatter_copy(self, to, source):
        return pltpu.make_async_remote_copy(
            src_ref=self.part(self.own, to), dst_ref=self.slots.at[source],
            send_sem=self.rs_send.at[to], recv_sem=self.rs_got.at[source],
            device_id={"seq": to}, device_id_type=MESH)

    def gather_copy(self, owner, to):
        return pltpu.make_async_remote_copy(
            src_ref=self.part(self.res, owner), dst_ref=self.part(self.res, owner),
            send_sem=self.ag_send.at[to], recv_sem=self.ag_got.at[owner],
            device_id={"seq": to}, device_id_type=MESH)

    def scatter(self):
        @pl.loop(1, self.size)
        def _(k):
            to = other_of("seq", k)

            @pl.when(to < self.owners)
            def _():
                self.scatter_copy(to, self.me).start()

    def reduce(self):
        @pl.when(self.me < self.owners)
        def _():
            @pl.loop(1, self.size)
            def _(k):
                self.scatter_copy(self.me, other_of("seq", k)).wait_recv()
            mine = pl.ds(pl.multiple_of(self.me * self.piece, self.piece), self.piece)
            self.slots[self.me] = self.own[mine]
            total = self.slots[0].astype(f32)
            for k in range(1, self.size):
                total = total + self.slots[k].astype(f32)
            self.res[mine] = total.astype(self.res.dtype)

            @pl.loop(1, self.size)
            def _(k):
                self.gather_copy(self.me, other_of("seq", k)).start()

    def finish(self):
        @pl.loop(1, self.size)
        def _(k):
            other = other_of("seq", k)

            @pl.when(other < self.owners)
            def _():
                self.gather_copy(other, self.me).wait_recv()
                self.scatter_copy(other, self.me).wait_send()

        @pl.when(self.me < self.owners)
        def _():
            @pl.loop(1, self.size)
            def _(k):
                self.gather_copy(self.me, other_of("seq", k)).wait_send()


class Swap:
    def __init__(self, axis, own, slots, sems):
        self.axis, self.own, self.slots = axis, own, slots
        self.send, self.got = sems.at[0], sems.at[1]
        self.size, self.me = lax.axis_size(axis), lax.axis_index(axis)

    def copy(self, to, source):
        return pltpu.make_async_remote_copy(
            src_ref=self.own, dst_ref=self.slots.at[source],
            send_sem=self.send.at[to], recv_sem=self.got.at[source],
            device_id={self.axis: to}, device_id_type=MESH)

    def start(self):
        @pl.loop(1, self.size)
        def _(k):
            self.copy(other_of(self.axis, k), self.me).start()
        self.slots[self.me] = self.own[...]

    def wait(self):
        @pl.loop(1, self.size)
        def _(k):
            self.copy(self.me, other_of(self.axis, k)).wait_recv()

    def total(self):
        out = self.slots[0]
        for k in range(1, self.size):
            out = out + self.slots[k]
        return out

    def finish(self):
        @pl.loop(1, self.size)
        def _(k):
            self.copy(other_of(self.axis, k), self.me).wait_send()


class DeviceScan:
    def __init__(self, backward, total, fade, lead, out, got, got_fade, sent, sent_fade, sems):
        self.backward, self.total, self.fade, self.lead, self.out = backward, total, fade, lead, out
        self.got, self.got_fade, self.sent, self.sent_fade, self.sems = got, got_fade, sent, sent_fade, sems
        self.me = lax.axis_index("seq")
        self.rounds = lax.axis_size("seq").bit_length() - 1

    @staticmethod
    def scratch(state, fade):
        rounds = lax.axis_size("seq").bit_length() - 1
        return [pltpu.VMEM(fade, f32), pltpu.VMEM(fade, f32)] + [
            pltpu.VMEM((rounds,) + state, bf16), pltpu.VMEM((rounds,) + fade, f32)] * 2 + [DMA((4, rounds))]

    def copies(self, k):
        return [
            pltpu.make_async_remote_copy(
                src_ref=src.at[k], dst_ref=dst.at[k],
                send_sem=self.sems.at[i, k], recv_sem=self.sems.at[i + 1, k],
                device_id={"seq": jnp.bitwise_xor(self.me, 1 << k)}, device_id_type=MESH)
            for src, dst, i in ((self.sent, self.got, 0), (self.sent_fade, self.got_fade, 2))]

    def begin(self, decay):
        self.fade[...] = decay
        self.out[...] = jnp.zeros_like(self.out)
        self.lead[...] = jnp.ones_like(self.lead)

    def start(self, k):
        self.sent[k] = self.total[...].astype(bf16)
        self.sent_fade[k] = self.fade[...]
        for copy in self.copies(k):
            copy.start()

    def finish(self, k):
        for copy in self.copies(k):
            copy.wait()
        later = lax.rem(self.me // (1 << k), 2) == (0 if self.backward else 1)

        @pl.when(later)
        def _():
            theirs = self.got[k].astype(f32)
            self.out[...] = self.out[...] + self.lead[0:1] * theirs
            self.total[...] = self.total[...] + self.fade[0:1] * theirs
            self.lead[...] = self.lead[...] * self.got_fade[k]

        @pl.when(jnp.logical_not(later))
        def _():
            self.total[...] = self.got[k].astype(f32) + self.got_fade[k, 0:1] * self.total[...]
        self.fade[...] = self.fade[...] * self.got_fade[k]

    def run(self, between=None):
        for k in range(self.rounds):
            self.start(k)
            if between is not None:
                between(k)
            self.finish(k)


GROUP = 256
STRIP = 128
GAP = 200.0
epsilon = 1e-05
LIMIT = 56 * 2**20


def dot(a, b):
    return jnp.dot(a, b, preferred_element_type=f32)


def dot_nt(a, b):
    return lax.dot_general(a, b, (((1,), (1,)), ((), ())), preferred_element_type=f32)


def dot_tn(a, b):
    return lax.dot_general(a, b, (((0,), (0,)), ((), ())), preferred_element_type=f32)


def split3(v):
    one = v.astype(bf16)
    rest = v - one.astype(f32)
    two = rest.astype(bf16)
    return one, two, (rest - two.astype(f32)).astype(bf16)


def exact_left(ones, v):
    width = v.shape[1]
    out = dot(ones, jnp.concatenate(split3(v), axis=1))
    return out[:, :width] + out[:, width : 2 * width] + out[:, 2 * width :]


def head_sum(v, group_ones):
    high = v.astype(bf16)
    low = (v - high.astype(f32)).astype(bf16)
    return dot(high, group_ones) + dot(low, group_ones)


def sigmoid(v):
    return 1.0 / (1.0 + jnp.exp(-v))


def softplus(v):
    return jnp.maximum(v, 0.0) + jnp.log1p(jnp.exp(-jnp.abs(v)))


def spread(cols, first, heads, head_dim):
    rows = cols.shape[0]
    per = 128 // head_dim
    lane = lax.broadcasted_iota(jnp.int32, (rows, 128), 1)
    tiles = []
    for at in range(0, heads, per):
        tile = cols[:, first + at : first + at + 1]
        for k in range(1, per):
            tile = jnp.where(lane < k * head_dim, tile, cols[:, first + at + k : first + at + k + 1])
        tiles.append(jnp.broadcast_to(tile, (rows, 128)))
    return jnp.concatenate(tiles, axis=1)


def norm_rows(block, gain):
    value = block.astype(f32)
    inv = lax.rsqrt(jnp.mean(value * value, axis=1, keepdims=True) + epsilon)
    return (value * inv * gain).astype(bf16)


def whole(shape):
    return pl.BlockSpec(shape, lambda g: (0,) * len(shape))


def lane_groups(rows, *parts):
    lane = lax.broadcasted_iota(jnp.int32, (rows, 128), 1)
    out = parts[-1]
    for k in range(len(parts) - 2, -1, -1):
        out = jnp.where(lane < 8 * (k + 1), parts[k], out)
    return out


RAW, STEP, CUM, DEV = 0, 8, 16, 24


def front_kernel(heads, head_dim, state_dim, count,
                 tokens, zx, dt, flags, gain, tail_rows, proj_bc, conv_bc, conv_x, params,
                 normed_out, gate_out, conv_in_out, conv_out_out, heads_out, entering, decay_out,
                 halo_out, weights_out, conv_w_out,
                 normed, taken, landed, proj_all, conv_all, carry, ext, state, running, lead, fade,
                 scan_got, scan_got_fade, scan_sent, scan_sent_fade, scan_sems, proj_sems, conv_sems, row_sems):
    at = pl.program_id(0)
    rows = tokens.shape[0]
    inner = heads * head_dim
    bc_width = 2 * state_dim
    seq, me = lax.axis_size("seq"), lax.axis_index("seq")
    block = lax.rem(at, count)
    mine = pl.ds(pl.multiple_of(block * rows, rows), rows)
    swaps = [Swap("head", proj_bc, proj_all, proj_sems), Swap("head", conv_bc, conv_all, conv_sems)]
    row_copy = pltpu.make_async_remote_copy(
        src_ref=tail_rows, dst_ref=landed, send_sem=row_sems.at[0], recv_sem=row_sems.at[1],
        device_id={"seq": lax.rem(me + 1, seq)}, device_id_type=MESH)

    @pl.when(at == 0)
    def _():
        greet("head", "seq")
        row_copy.start()
        for each in swaps:
            each.start()

    @pl.when(at < count)
    def _():
        low = norm_rows(tokens[...], gain[0:1])
        normed[mine] = low
        normed_out[...] = low
        raw = dot(low, zx[...])
        gate_out[...] = raw[:, :inner]
        taken[mine] = raw[:, inner:].astype(bf16)

    @pl.when(at == count)
    def _():
        row_copy.wait()
        for each in swaps:
            each.wait()
            each.finish()
        heads_there = proj_all.shape[0]
        weights_out[:, :bc_width] = jnp.concatenate([proj_all[k] for k in range(heads_there)], axis=1)
        weights_out[:, bc_width:] = dt[...]
        conv_w_out[...] = jnp.concatenate([conv_x[...]] + [conv_all[k] for k in range(heads_there)], axis=1)
        head_rows = norm_rows(landed[...], gain[0:1])
        ahead = jnp.concatenate([dot(head_rows, zx[:, inner:]), dot(head_rows, weights_out[:, :bc_width])], axis=1)
        ahead = jnp.where(me > 0, ahead, 0.0).astype(bf16)
        halo_out[...] = ahead
        carry[...] = ahead[8:].astype(f32)
        state[...] = jnp.zeros_like(state)
        running[...] = jnp.zeros_like(running)

    @pl.when(at >= count)
    def _():
        raw = dot(normed[mine], weights_out[...])
        conv_in = jnp.concatenate([taken[mine], raw[:, :bc_width].astype(bf16)], axis=1)
        conv_in_out[...] = conv_in
        current = conv_in.astype(f32)
        ext[0:8] = carry[...]
        ext[8:] = current
        carry[...] = ext[rows:]
        keep = 1.0 - flags[...]
        total = conv_w_out[4:5] + conv_w_out[0:1] * current
        for j in range(1, 4):
            total = total + conv_w_out[j : j + 1] * ext[pl.ds(8 - j, rows)] * keep[:, j : j + 1]
        conv_out_out[...] = total
        active = total * sigmoid(total)

        step_raw = raw[:, bc_width:]
        step = softplus(step_raw + params[0:1])
        log_decay = step * params[1:2] - GAP * flags[:, 1:2]
        order_r = lax.broadcasted_iota(jnp.int32, (rows, rows), 0)
        order_c = lax.broadcasted_iota(jnp.int32, (rows, rows), 1)
        cum = exact_left((order_r >= order_c).astype(bf16), log_decay)
        heads_out[...] = lane_groups(rows, step_raw, step, cum, cum + running[0:1])
        end = cum[rows - 1 : rows]
        running[...] = running[...] + end
        weight = step * jnp.exp(end - cum)
        scaled = (active[:, :inner] * spread(weight, 0, heads, head_dim)).astype(bf16)
        b_proj = active[:, inner : inner + state_dim].astype(bf16)
        state[...] = state[...] * spread(jnp.exp(end), 0, heads, head_dim) + dot_tn(b_proj, scaled)

    @pl.when(at == 2 * count - 1)
    def _():
        decay = spread(jnp.exp(running[...]), 0, heads, head_dim)
        decay_out[...] = decay
        scan = DeviceScan(False, state, fade, lead, entering, scan_got, scan_got_fade, scan_sent,
                          scan_sent_fade, scan_sems)
        scan.begin(decay)
        scan.run()


def front(tokens, zx, dt, flags, gain, tail_rows, proj_bc, conv_bc, conv_x, params, heads, head_dim, state_dim):
    length, width = tokens.shape
    count = length // GROUP
    inner = heads * head_dim
    conv = inner + 2 * state_dim
    head_count = lax.axis_size("head")

    def early(cols):
        return pl.BlockSpec((GROUP, cols), lambda g: (jnp.minimum(g, count - 1), 0))

    def late(cols):
        return pl.BlockSpec((GROUP, cols), lambda g: (jnp.maximum(g - count, 0), 0))
    shape = jax.ShapeDtypeStruct
    state, fade = (state_dim, inner), (8, inner)
    return pl.pallas_call(
        functools.partial(front_kernel, heads, head_dim, state_dim, count),
        grid=(2 * count,),
        out_shape=(shape((length, width), bf16), shape((length, inner), f32), shape((length, conv), bf16),
                   shape((length, conv), f32), shape((length, 128), f32), shape(state, f32),
                   shape(fade, f32), shape((16, conv), bf16), shape((width, 2 * state_dim + 128), bf16),
                   shape((8, conv), f32)),
        in_specs=[early(width), whole(zx.shape), whole(dt.shape), late(8), VMEM, VMEM, VMEM, VMEM, VMEM, VMEM],
        out_specs=(early(width), early(inner), late(conv), late(conv), late(128), whole(state), whole(fade),
                   whole((16, conv)), whole((width, 2 * state_dim + 128)), whole((8, conv))),
        scratch_shapes=[
            pltpu.VMEM((length, width), bf16), pltpu.VMEM((length, inner), bf16),
            pltpu.VMEM(tail_rows.shape, bf16), pltpu.VMEM((head_count,) + proj_bc.shape, bf16),
            pltpu.VMEM((head_count,) + conv_bc.shape, f32), pltpu.VMEM((8, conv), f32),
            pltpu.VMEM((GROUP + 8, conv), f32), pltpu.VMEM(state, f32), pltpu.VMEM((8, 128), f32)]
        + DeviceScan.scratch(state, fade) + [DMA((2, head_count)), DMA((2, head_count)), DMA((2,))],
        compiler_params=pltpu.CompilerParams(
            dimension_semantics=("arbitrary",), collective_id=3, has_side_effects=True,
            vmem_limit_bytes=LIMIT),
        name="front",
    )(tokens, zx, dt, flags, gain, tail_rows, proj_bc, conv_bc, conv_x, params)


def strips(rows):
    return [(lo, lo + STRIP) for lo in range(0, rows, STRIP)]


def mix_step(heads, head_dim, state_dim, at,
             conv_out, heads_in, gate, cot, out_proj, gains, entering,
             ssm_out, d_normed_out, partial_out, sums_out, starts_out, state):
    rows = conv_out.shape[0]
    inner = heads * head_dim
    per = 128 // head_dim

    @pl.when(at == 0)
    def _():
        state[...] = entering[...]

    values = conv_out[...]
    active = values * sigmoid(values)
    x = active[:, :inner]
    b_proj = active[:, inner : inner + state_dim].astype(bf16)
    c_proj = active[:, inner + state_dim :].astype(bf16)
    info = heads_in[...]
    flipped = info.T
    stepped = x * spread(info, STEP, heads, head_dim)
    low = stepped.astype(bf16)
    scores = dot_nt(c_proj, b_proj)
    lane = lax.broadcasted_iota(jnp.int32, (rows, 128), 1)
    tiles = []
    for pair in range(heads // per):
        tile = low[:, pair * 128 : (pair + 1) * 128]
        parts = [None] * (rows // STRIP)
        for k in range(per):
            head = pair * per + k
            masked = jnp.where((lane >= k * head_dim) & (lane < (k + 1) * head_dim), tile, jnp.zeros_like(tile))
            for n, (lo, hi) in enumerate(strips(rows)):
                gap = info[lo:hi, CUM + head : CUM + head + 1] - flipped[CUM + head : CUM + head + 1, :hi]
                ok = (lax.broadcasted_iota(jnp.int32, (STRIP, hi), 0) + lo
                      >= lax.broadcasted_iota(jnp.int32, (STRIP, hi), 1))
                weight = jnp.exp(jnp.where(ok, gap, -1e30)) * scores[lo:hi, :hi]
                part = dot(weight.astype(bf16), masked[:hi])
                parts[n] = part if parts[n] is None else parts[n] + part
        tiles.append(jnp.concatenate(parts, axis=0))
    inside = jnp.concatenate(tiles, axis=1)
    cum = info[:, CUM : CUM + 8]
    end = info[rows - 1 : rows]
    start = state[...]
    starts_out[at] = start.astype(bf16)
    grown = spread(jnp.exp(info), CUM, heads, head_dim)
    result = inside + grown * dot(c_proj, start.astype(bf16)) + gains[1:2] * x
    fade = spread(jnp.exp(end - info), CUM, heads, head_dim)
    state[...] = start * spread(jnp.exp(end), CUM, heads, head_dim) + dot_tn(b_proj, (stepped * fade).astype(bf16))
    ssm_out[...] = result
    z = gate[...]
    gated = result * (z * sigmoid(z))
    d_normed = dot_nt(cot[...], out_proj[...])
    d_normed_out[...] = d_normed
    scaled = gated * gains[0:1]
    partial_out[...] = dot(scaled.astype(bf16), out_proj[...]).astype(bf16)
    squares = jnp.sum(gated * gated, axis=1, keepdims=True)
    cross = jnp.sum(d_normed * scaled, axis=1, keepdims=True)
    turned = jnp.where(lane == 0, squares, cross).T
    sums_out[0, pl.ds(at, 1)] = turned[0:1]
    sums_out[1, pl.ds(at, 1)] = turned[1:2]


def gate_step(heads, head_dim, state_dim, all_channels, at,
              ssm, gate, d_normed, sums, conv_out, heads_in, cot, gains,
              d_ssm_out, d_gate_out, grad_out, rows_out, total_out):
    rows = ssm.shape[0]
    inner = heads * head_dim

    @pl.when(at == 0)
    def _():
        grad_out[...] = jnp.zeros_like(grad_out)
        rows_out[...] = jnp.zeros_like(rows_out)
        total_out[...] = jnp.zeros_like(total_out)

    tall = jnp.concatenate([sums[0, pl.ds(at, 1)], sums[1, pl.ds(at, 1)], jnp.zeros((126, rows), f32)], axis=0).T
    inv = lax.rsqrt(tall[:, 0:1] / all_channels + epsilon)
    cross = tall[:, 1:2] / all_channels
    z = gate[...]
    s = sigmoid(z)
    y = ssm[...]
    gated = y * (z * s)
    gain = gains[0:1]
    back = d_normed[...]
    unit = gated * inv
    d_gated = inv * (back * gain - unit * (inv * cross))
    grad_out[...] += dot_tn((unit * gain).astype(bf16), cot[...])
    d_ssm = d_gated * (z * s)
    d_ssm_out[...] = d_ssm
    d_gate_out[...] = (d_gated * y * (s * (1.0 + z * (1.0 - s)))).astype(bf16)
    values = conv_out[...]
    active = values * sigmoid(values)
    rows_out[0:1] += jnp.sum(back * unit, axis=0, keepdims=True)
    rows_out[1:2] += jnp.sum(d_ssm * active[:, :inner], axis=0, keepdims=True)
    c_proj = active[:, inner + state_dim :].astype(bf16)
    grown = spread(jnp.exp(heads_in[...]), DEV, heads, head_dim)
    total_out[...] += dot_tn(c_proj, (grown * d_ssm).astype(bf16))


def back_step(heads, head_dim, state_dim, first_step, last_step,
              d_ssm, conv_out, conv_in, heads_in, start, entering, flags, conv_w, params, skip, conv_halo,
              d_conv_in_out, d_step_out, conv_grads, head_grads, halo_out,
              lam, shift1, shift2, shift3, between):
    rows = d_ssm.shape[0]
    inner = heads * head_dim
    per = 128 // head_dim
    shifts = (shift1, shift2, shift3)

    @pl.when(first_step)
    def _():
        lam[...] = entering[...]
        conv_grads[...] = jnp.zeros_like(conv_grads)
        head_grads[...] = jnp.zeros_like(head_grads)
        for each in shifts:
            each[rows:] = jnp.zeros((8, each.shape[1]), f32)

    values = conv_out[...]
    gates = sigmoid(values)
    active = values * gates
    x = active[:, :inner]
    b_proj = active[:, inner : inner + state_dim].astype(bf16)
    c_proj = active[:, inner + state_dim :].astype(bf16)
    info = heads_in[...]
    flipped = info.T
    step = spread(info, STEP, heads, head_dim)
    stepped = x * step
    low = stepped.astype(bf16)
    dy = d_ssm[...]
    dy_low = dy.astype(bf16)
    scores = dot_nt(b_proj, c_proj)
    lane = lax.broadcasted_iota(jnp.int32, (rows, 128), 1)
    lane_one = lax.broadcasted_iota(jnp.int32, (STRIP, 128), 1)
    cuts = strips(rows)
    d_scores = [jnp.zeros((STRIP, rows - lo), f32) for lo, _ in cuts]
    d_rows = []
    d_cols = [jnp.zeros((STRIP, 128), f32) for _ in cuts]
    tiles = []
    for pair in range(heads // per):
        tile = low[:, pair * 128 : (pair + 1) * 128]
        dy_tile = dy_low[:, pair * 128 : (pair + 1) * 128]
        parts = [None] * len(cuts)
        for k in range(per):
            head = pair * per + k
            own = (lane >= k * head_dim) & (lane < (k + 1) * head_dim)
            masked = jnp.where(own, tile, jnp.zeros_like(tile))
            dy_masked = jnp.where(own, dy_tile, jnp.zeros_like(dy_tile))
            row_total = jnp.zeros((1, rows), f32)
            for n, (lo, hi) in enumerate(cuts):
                gap = flipped[CUM + head : CUM + head + 1, lo:] - info[lo:hi, CUM + head : CUM + head + 1]
                ok = (lax.broadcasted_iota(jnp.int32, (STRIP, rows - lo), 1)
                      >= lax.broadcasted_iota(jnp.int32, (STRIP, rows - lo), 0))
                decay = jnp.exp(jnp.where(ok, gap, -1e30))
                weight = decay * scores[lo:hi, lo:]
                part = dot(weight.astype(bf16), dy_masked[lo:])
                parts[n] = part if parts[n] is None else parts[n] + part
                pairs = dot_nt(masked[lo:hi], dy_tile[lo:])
                d_scores[n] = d_scores[n] + pairs * decay
                moved = pairs * weight
                d_cols[n] = d_cols[n] - jnp.where(lane_one == head, jnp.sum(moved, axis=1, keepdims=True), 0.0)
                col = jnp.sum(moved, axis=0, keepdims=True)
                if lo:
                    col = jnp.concatenate([jnp.zeros((1, lo), f32), col], axis=1)
                row_total = row_total + col
            d_rows.append(row_total)
        tiles.append(jnp.concatenate(parts, axis=0))
    between()
    d_stepped = jnp.concatenate(tiles, axis=1)
    d_cum = jnp.concatenate(d_cols, axis=0)
    d_cum = d_cum + jnp.concatenate(d_rows + [jnp.zeros((128 - heads, rows), f32)], axis=0).T
    full = jnp.concatenate(
        [jnp.concatenate([jnp.zeros((STRIP, lo), f32), part], axis=1) if lo else part
         for part, (lo, _) in zip(d_scores, cuts)], axis=0).astype(bf16)
    d_b = dot(full, c_proj)
    d_c = dot_tn(full, b_proj)

    group_ones = (lax.broadcasted_iota(jnp.int32, (inner, 128), 0) // head_dim
                  == lax.broadcasted_iota(jnp.int32, (inner, 128), 1)).astype(bf16)
    after = lam[...]
    after_low = after.astype(bf16)
    end = info[rows - 1 : rows]
    grown = spread(jnp.exp(info), CUM, heads, head_dim)
    fade = spread(jnp.exp(end - info), CUM, heads, head_dim)
    end_grown = spread(jnp.exp(end), CUM, heads, head_dim)
    from_after = fade * dot(b_proj, after_low)
    d_stepped = d_stepped + from_after
    grown_dy = grown * dy
    grown_low = grown_dy.astype(bf16)
    to_cum = head_sum(grown_dy * dot(c_proj, start), group_ones)
    left = head_sum(stepped * from_after, group_ones)
    kept = jnp.sum(after * start.astype(f32), axis=0, keepdims=True) * end_grown
    kept = head_sum(jnp.broadcast_to(kept, (8, inner)), group_ones)[0:1]
    last = kept + jnp.sum(left, axis=0, keepdims=True)
    row_id = lax.broadcasted_iota(jnp.int32, (rows, 128), 0)
    d_cum = d_cum + to_cum - left + jnp.where(row_id == rows - 1, last, 0.0)
    d_c = d_c + dot_nt(grown_low, start)
    d_b = d_b + dot_nt((fade * stepped).astype(bf16), after_low)
    lam[...] = end_grown * after + dot_tn(c_proj, grown_low)
    d_step = head_sum(d_stepped * x, group_ones)
    d_x = step * d_stepped + skip[0:1] * dy

    order_r = lax.broadcasted_iota(jnp.int32, (rows, rows), 0)
    order_c = lax.broadcasted_iota(jnp.int32, (rows, rows), 1)
    free = 1.0 - flags[...]
    d_decay = exact_left((order_r <= order_c).astype(bf16), d_cum) * free[:, 1:2]
    rate = params[1:2]
    real = lane < heads
    step_raw = jnp.where(real, info, 0.0) + params[0:1]
    slope = sigmoid(step_raw)
    d_pre = jnp.where(real, (d_step + d_decay * rate) * slope, 0.0)
    d_step_out[...] = d_pre.astype(bf16)
    head_grads[0:1] += jnp.sum(d_pre, axis=0, keepdims=True)
    head_grads[1:2] += jnp.sum(jnp.where(real, d_decay * softplus(step_raw) * rate, 0.0), axis=0, keepdims=True)

    d_active = jnp.concatenate([d_x, d_b, d_c], axis=1)
    d_conv = d_active * (gates * (1.0 + values * (1.0 - gates)))
    taken = conv_in[...].astype(f32)
    total = d_conv * conv_w[0:1]
    conv_grads[0:1] += jnp.sum(d_conv * taken, axis=0, keepdims=True)
    conv_grads[4:5] += jnp.sum(d_conv, axis=0, keepdims=True)
    for j in range(1, 4):
        ref = shifts[j - 1]
        ref[0:rows] = d_conv * free[:, j : j + 1]
        moved = ref[pl.ds(j, rows)]
        total = total + moved * conv_w[j : j + 1]
        conv_grads[j : j + 1] += jnp.sum(moved * taken, axis=0, keepdims=True)
    d_conv_in_out[...] = total.astype(bf16)

    @pl.when(last_step)
    def _():
        ahead = conv_halo[...].astype(f32)
        halo_out[...] = jnp.zeros_like(halo_out)
        for j in range(1, 4):
            first = shifts[j - 1][0:8]
            for t in range(j):
                row = 16 + t - j
                conv_grads[j : j + 1] += first[t : t + 1] * ahead[row : row + 1]
                halo_out[row - 8 : row - 7] += first[t : t + 1] * conv_w[j : j + 1]
    for each in shifts:
        each[rows:] = each[0:8]


def paced(times, pace, behind, most):
    return [max(0, min(most, int((time - behind) / pace))) for time in times]


def at_point(counts):
    def count(point):
        if isinstance(point, int):
            return counts[point] if point >= 0 else 0
        out = jnp.int32(0)
        for k, value in enumerate(counts):
            more = value - (counts[k - 1] if k else 0)
            if more:
                out = out + more * (point >= k).astype(jnp.int32)
        return out
    return count


def layer_kernel(heads, head_dim, state_dim, all_channels, count, block, lag, plans,
                 conv_out, conv_in, heads_in, gate, cot, flags, out_proj, gains, entering, decay, conv_w,
                 params, conv_halo,
                 line_out, d_gate_out, d_conv_out, d_step_out, grad_out_out, gate_rows, conv_grads, head_grads,
                 halo_out, sums_out,
                 own, got, total, ssm, d_normed, starts, state, leaving, shift1, shift2, shift3, sums, sum_slots,
                 grad_out, grad_low, grad_slots, grad_res, lead, fade,
                 scan_got, scan_got_fade, scan_sent, scan_sent_fade, scan_sems, line_sems, sum_sems, grad_sems):
    at = pl.program_id(0)
    rows = conv_out.shape[0]
    seq = lax.axis_size("seq")
    line = LineSum(own, got, total, line_out, line_sems, block)
    swap = Swap("head", sums, sum_slots, sum_sems)
    scan = DeviceScan(True, state, fade, lead, leaving, scan_got, scan_got_fade, scan_sent, scan_sent_fade,
                      scan_sems)
    grad_sum = PlaneSum(grad_low, grad_slots, grad_res, grad_sems, min(seq, grad_low.shape[0] // 16))
    served, sent = at_point(plans[0]), at_point(plans[1])

    def serve(point):
        line.send(sent(point - 1), sent(point))
        line.serve(served(point - 1), served(point), lag)

    @pl.when(at == 0)
    def _():
        greet("head", "seq")
        state[...] = entering[...]

    serve(2 * at)

    @pl.when(at < count)
    def _():
        mine = pl.ds(pl.multiple_of(at * rows, rows), rows)
        mix_step(heads, head_dim, state_dim, at, conv_out, heads_in, gate, cot, out_proj, gains, entering,
                 ssm.at[mine], d_normed.at[mine], own.at[mine], sums, starts, state)

    @pl.when(at == count - 1)
    def _():
        swap.start()

    @pl.when(at == count)
    def _():
        swap.wait()
        sums_out[...] = swap.total()
        swap.finish()
        grad_out[...] = jnp.zeros_like(grad_out)
        gate_rows[...] = jnp.zeros_like(gate_rows)
        state[...] = jnp.zeros_like(state)

    @pl.when((at >= count) & (at < 2 * count))
    def _():
        here = at - count
        mine = pl.ds(pl.multiple_of(here * rows, rows), rows)
        gate_step(heads, head_dim, state_dim, all_channels, here,
                  ssm.at[mine], gate, d_normed.at[mine], sums_out, conv_out, heads_in, cot, gains,
                  ssm.at[mine], d_gate_out, grad_out, gate_rows, state)

    @pl.when(at == 2 * count)
    def _():
        grad_low[...] = grad_out[...].astype(bf16)
        scan.begin(decay[...])
        scan.run()
        grad_sum.scatter()

    @pl.when(at >= 2 * count)
    def _():
        here = 3 * count - 1 - at
        mine = pl.ds(pl.multiple_of(here * rows, rows), rows)
        back_step(heads, head_dim, state_dim, at == 2 * count, at == 3 * count - 1,
                  ssm.at[mine], conv_out, conv_in, heads_in, starts[here], leaving, flags, conv_w, params,
                  gains[1:2], conv_halo, d_conv_out, d_step_out, conv_grads, head_grads, halo_out,
                  state, shift1, shift2, shift3, lambda: serve(2 * at + 1))

    @pl.when(at == 2 * count + count // 2)
    def _():
        grad_sum.reduce()

    @pl.when(at == 3 * count - 1)
    def _():
        grad_sum.finish()
        grad_out_out[...] = grad_res[...]
        serve(6 * count)
        line.finish()


def layer(conv_out, conv_in, heads_in, gate, cot, flags, out_proj, gains, entering, decay, conv_w, params,
          conv_halo, heads, head_dim, state_dim, all_channels):
    length, conv = conv_out.shape
    count = length // GROUP
    inner = heads * head_dim
    width = cot.shape[1]
    seq, head_count = lax.axis_size("seq"), lax.axis_size("head")
    block = 64
    blocks = length // block
    lag = max(2, head_count // 2)
    steps = [MIX] * count + [GATE] * count + [BACK] * count
    times, now = [], 0.0
    for k, step in enumerate(steps):
        now += SWAP if k == count else 0.0
        half = SCAN + step / 2 if k == 2 * count else step / 2 if k > 2 * count else 0.0
        times += [now, now + half]
        now += step + (SCAN if k == 2 * count else 0.0)
    made = [min(blocks, (k // 2) * (GROUP // block)) for k in range(6 * count)]
    plans = (paced(times, PACE, LATE, blocks) + [blocks + lag],
             [min(a, b) for a, b in zip(made, paced(times, PACE, EARLY, blocks))] + [blocks])

    def by(cols, first, step):
        def index(g):
            ahead = jnp.where(g < count, g, jnp.where(g < 2 * count, g - count, 3 * count - 1 - g))
            if first == 2:
                ahead = jnp.where(g < 2 * count, count - 1, ahead)
            if first == 1:
                ahead = jnp.where(g < count, 0, ahead)
            if step == 1:
                ahead = jnp.where(g < 2 * count, ahead, count - 1)
            return (ahead, 0)
        return pl.BlockSpec((GROUP, cols), index)
    shape = jax.ShapeDtypeStruct
    state, fade = (state_dim, inner), (8, inner)
    owners = min(seq, inner // 16)
    return pl.pallas_call(
        functools.partial(layer_kernel, heads, head_dim, state_dim, all_channels, count, block, lag, plans),
        grid=(3 * count,),
        out_shape=(shape((length, width), bf16), shape((length, inner), bf16), shape((length, conv), bf16),
                   shape((length, 128), bf16), shape((inner, width), bf16), shape((8, inner), f32),
                   shape((8, conv), f32), shape((8, 128), f32), shape((8, conv), f32),
                   shape((2, count, GROUP), f32)),
        in_specs=[by(conv, 0, 2), by(conv, 2, 2), by(128, 0, 2), by(inner, 0, 1), by(width, 0, 1), by(8, 2, 2)]
        + [VMEM] * 7,
        out_specs=(HBM, by(inner, 1, 1), by(conv, 2, 2), by(128, 2, 2)) + (VMEM,) * 6,
        scratch_shapes=[pltpu.VMEM((length, width), bf16)] * 3 + [pltpu.VMEM((length, inner), f32)] * 2 + [
            pltpu.VMEM((count,) + state, bf16), pltpu.VMEM(state, f32), pltpu.VMEM(state, f32)]
        + [pltpu.VMEM((GROUP + 8, conv), f32)] * 3 + [
            pltpu.VMEM((2, count, GROUP), f32), pltpu.VMEM((head_count, 2, count, GROUP), f32),
            pltpu.VMEM((inner, width), f32), pltpu.VMEM((inner, width), bf16),
            pltpu.VMEM((seq, inner // owners, width), bf16), pltpu.VMEM((inner, width), bf16)]
        + DeviceScan.scratch(state, fade) + [LineSum.sems(length, block), DMA((2, head_count)), DMA((4, seq))],
        compiler_params=pltpu.CompilerParams(
            dimension_semantics=("arbitrary",), collective_id=4, has_side_effects=True,
            vmem_limit_bytes=LIMIT),
        name="layer",
    )(conv_out, conv_in, heads_in, gate, cot, flags, out_proj, gains, entering, decay, conv_w, params, conv_halo)


PACE = 2.9
MIX, SWAP, GATE, SCAN, BACK = 2.7, 3.0, 2.0, 10.0, 6.6
EARLY, LATE = -2.0, 5.0
PROJECT, CUTS = 2.6, (17, 21)


def tail_kernel(count, block, lag, plans, cuts, owners, last_rows,
                normed, d_gate, d_conv, d_step, zx, weights, gain, back_rows, tail_mask, small_in,
                line_out, zx_out, bc_out, small_out,
                own, got, total, grad_zx, grad_low, zx_slots, zx_res, grad_bc, bc_part, bc_slots, bc_z, bc_res, small, small_slots,
                small_own, small_z, landed,
                line_sems, zx_sems, bc_sems, bcz_sems, small_sems, smallz_sems, row_sems):
    at = pl.program_id(0)
    rows, width = normed.shape
    inner = d_gate.shape[1]
    seq, heads = lax.axis_size("seq"), lax.axis_size("head")
    me, my_head = lax.axis_index("seq"), lax.axis_index("head")
    bc_width = bc_part.shape[0] * bc_part.shape[1]
    line = LineSum(own, got, total, line_out, line_sems, block)
    zx_sum = PlaneSum(grad_low, zx_slots, zx_res, zx_sems, owners[0])
    small_swap = Swap("seq", small, small_slots, small_sems)
    both_swap = Swap("head", small_own, small_z, smallz_sems)
    row_copy = pltpu.make_async_remote_copy(
        src_ref=back_rows, dst_ref=landed, send_sem=row_sems.at[0], recv_sem=row_sems.at[1],
        device_id={"seq": lax.rem(me + seq - 1, seq)}, device_id_type=MESH)
    served, sent = at_point(plans[0]), at_point(plans[1])

    @pl.when(at == 0)
    def _():
        greet("head", "seq")
        row_copy.start()
        grad_zx[...] = jnp.zeros_like(grad_zx)
        grad_bc[...] = jnp.zeros_like(grad_bc)
        small[...] = small_in[...]

    line.send(sent(at - 1), sent(at))
    line.serve(served(at - 1), served(at), lag)

    block_low = normed[...]
    gate_low, conv_low, step_low = d_gate[...], d_conv[...], d_step[...]
    rest_low = jnp.concatenate([conv_low[:, inner:], step_low], axis=1)
    d_normed = (dot_nt(gate_low, zx[:, :inner]) + dot_nt(conv_low[:, :inner], zx[:, inner:])
                + dot_nt(rest_low, weights[...]))
    grad_zx[:, :inner] += dot_tn(block_low, gate_low)
    grad_zx[:, inner:] += dot_tn(block_low, conv_low[:, :inner])
    grad_bc[...] += dot_tn(rest_low, block_low)
    small[16:17] += jnp.sum(d_normed * block_low.astype(f32), axis=0, keepdims=True) / gain[0:1]
    mine = pl.ds(pl.multiple_of(at * rows, rows), rows)
    own[mine] = d_normed.astype(bf16)

    @pl.when(at == count - 1)
    def _():
        row_copy.wait()
        extra = jnp.where(me < seq - 1, landed[...] * tail_mask[...], 0.0)
        extra = jnp.concatenate([jnp.zeros_like(extra), extra], axis=0).astype(bf16)
        tail_low = normed[rows - 16 :]
        more = dot_nt(extra[:, :inner], zx[:, inner:]) + dot_nt(extra[:, inner:], weights[:, :bc_width])
        grad_zx[:, inner:] += dot_tn(tail_low, extra[:, :inner])
        grad_bc[:bc_width] += dot_tn(extra[:, inner:], tail_low)
        small[16:17] += jnp.sum(more * tail_low.astype(f32), axis=0, keepdims=True) / gain[0:1]
        own[last_rows:] = (own[last_rows:].astype(f32) + more).astype(bf16)

    piece = bc_part.shape[1] // owners[1]

    def bc_scatter(to, source):
        return pltpu.make_async_remote_copy(
            src_ref=bc_part.at[:, pl.ds(pl.multiple_of(to * piece, piece), piece)],
            dst_ref=bc_slots.at[source], send_sem=bc_sems.at[0, to], recv_sem=bc_sems.at[1, source],
            device_id={"seq": to}, device_id_type=MESH)

    def bc_gather(owner, to):
        rows = pl.ds(pl.multiple_of(owner * piece, piece), piece)
        return pltpu.make_async_remote_copy(
            src_ref=bc_res.at[rows], dst_ref=bc_res.at[rows],
            send_sem=bc_sems.at[2, to], recv_sem=bc_sems.at[3, owner],
            device_id={"seq": to}, device_id_type=MESH)

    def bc_swap(to, source):
        return pltpu.make_async_remote_copy(
            src_ref=bc_slots.at[me, to], dst_ref=bc_z.at[source],
            send_sem=bcz_sems.at[0, to], recv_sem=bcz_sems.at[1, source],
            device_id={"head": to}, device_id_type=MESH)

    @pl.when(at == count - 1)
    def _():
        grad_low[...] = grad_zx[...].astype(bf16)
        zx_sum.scatter()
        small[0:8] += grad_bc[bc_width : bc_width + 8]
        small_swap.start()
        for k in range(heads):
            bc_part[k] = grad_bc[k * bc_part.shape[1] : (k + 1) * bc_part.shape[1]]

        @pl.loop(1, seq)
        def _(k):
            to = other_of("seq", k)

            @pl.when(to < owners[1])
            def _():
                bc_scatter(to, me).start()

        last = count - 1

        def go(first, until, sent_first, sent_until):
            line.send(sent_first, sent_until)
            line.serve(first, until, lag)
        go(served(last), cuts[0], sent(last), cuts[0] + 2)
        zx_sum.reduce()
        small_swap.wait()
        sums = small_swap.total()
        lone = small.shape[0] - small_own.shape[0]
        small_out[:lone] = sums[:lone]
        small_own[...] = sums[lone:]
        both_swap.start()

        @pl.when(me < owners[1])
        def _():
            @pl.loop(1, seq)
            def _(k):
                bc_scatter(me, other_of("seq", k)).wait_recv()
            bc_slots[me] = bc_part[:, pl.ds(pl.multiple_of(me * piece, piece), piece)]
            sums = bc_slots[0]
            for k in range(1, seq):
                sums = sums + bc_slots[k]
            bc_slots[me] = sums
            bc_z[my_head] = bc_slots[me, my_head]

            @pl.loop(1, heads)
            def _(k):
                bc_swap(other_of("head", k), my_head).start()

        go(cuts[0], cuts[1], cuts[0] + 2, cuts[1] + 2)
        both_swap.wait()
        small_out[lone:] = both_swap.total()

        @pl.when(me < owners[1])
        def _():
            @pl.loop(1, heads)
            def _(k):
                bc_swap(my_head, other_of("head", k)).wait_recv()
            sums = bc_z[0]
            for k in range(1, heads):
                sums = sums + bc_z[k]
            bc_res[pl.ds(pl.multiple_of(me * piece, piece), piece)] = sums

            @pl.loop(1, seq)
            def _(k):
                bc_gather(me, other_of("seq", k)).start()

        go(cuts[1], line.count + lag, cuts[1] + 2, line.count)
        line.finish()
        zx_sum.finish()
        zx_out[...] = zx_res[...]
        small_swap.finish()
        both_swap.finish()

        @pl.loop(1, seq)
        def _(k):
            other = other_of("seq", k)

            @pl.when(other < owners[1])
            def _():
                bc_gather(other, me).wait_recv()
                bc_scatter(other, me).wait_send()

            @pl.when(me < owners[1])
            def _():
                bc_gather(me, other).wait_send()
        bc_out[...] = bc_res[...]

        @pl.when(me < owners[1])
        def _():
            @pl.loop(1, heads)
            def _(k):
                bc_swap(other_of("head", k), my_head).wait_send()


def tail(normed, d_gate, d_conv, d_step, zx, weights, gain, back_rows, tail_mask, small_in, both):
    length, width = normed.shape
    inner, conv = d_gate.shape[1], d_conv.shape[1]
    count = length // GROUP
    seq, heads = lax.axis_size("seq"), lax.axis_size("head")
    bc_rows = (conv - inner) // heads
    owners = (min(seq, width // 16), min(seq, bc_rows // 8))
    piece = bc_rows // owners[1]
    block = 64
    blocks = length // block
    lag = max(2, heads // 2)
    made = [k * (GROUP // block) for k in range(count)]
    times = [PROJECT * k for k in range(count)]
    plans = (paced(times, PACE, LATE, blocks), [min(a, b) for a, b in zip(made, paced(times, PACE, EARLY, blocks))])
    cuts = ((blocks * CUTS[0]) // 32, (blocks * CUTS[1]) // 32)

    def by(cols):
        return pl.BlockSpec((GROUP, cols), lambda g: (g, 0))
    shape = jax.ShapeDtypeStruct
    return pl.pallas_call(
        functools.partial(tail_kernel, count, block, lag, plans, cuts, owners, length - 16),
        grid=(count,),
        out_shape=(shape((length, width), bf16), shape((width, 2 * inner), bf16), shape((bc_rows, width), f32),
                   shape(small_in.shape, f32)),
        in_specs=[by(width), by(inner), by(conv), by(128)] + [VMEM] * 6,
        out_specs=(HBM, VMEM, VMEM, VMEM),
        scratch_shapes=[pltpu.VMEM((length, width), bf16)] * 3 + [
            pltpu.VMEM((width, 2 * inner), f32), pltpu.VMEM((width, 2 * inner), bf16),
            pltpu.VMEM((seq, width // owners[0], 2 * inner), bf16), pltpu.VMEM((width, 2 * inner), bf16),
            pltpu.VMEM((conv - inner + 128, width), f32), pltpu.VMEM((heads, bc_rows, width), f32),
            pltpu.VMEM((seq, heads, piece, width), f32), pltpu.VMEM((heads, piece, width), f32),
            pltpu.VMEM((bc_rows, width), f32), pltpu.VMEM(small_in.shape, f32), pltpu.VMEM((seq,) + small_in.shape, f32),
            pltpu.VMEM((both, width), f32), pltpu.VMEM((heads, both, width), f32),
            pltpu.VMEM(back_rows.shape, f32),
            LineSum.sems(length, block), DMA((4, seq)), DMA((4, seq)), DMA((2, heads)), DMA((2, seq)),
            DMA((2, heads)), DMA((2,))],
        compiler_params=pltpu.CompilerParams(
            dimension_semantics=("arbitrary",), collective_id=5, has_side_effects=True,
            vmem_limit_bytes=LIMIT),
        name="tail",
    )(normed, d_gate, d_conv, d_step, zx, weights, gain, back_rows, tail_mask, small_in)


def padded(block, rows, cols):
    return jnp.pad(block, ((0, rows - block.shape[0]), (0, cols - block.shape[1])))


def shards(
    tokens, start_flags, in_gain, proj_zx, proj_bc, proj_dt, conv_x_weight, conv_x_bias,
    conv_bc_weight, conv_bc_bias, dt_bias, a_log, skip_scale, norm_gain, out_proj, cotangent,
):
    length, width = tokens.shape
    heads = a_log.shape[0]
    inner = proj_zx.shape[2]
    head_dim = inner // heads
    taps = conv_x_weight.shape[0]
    head_count = lax.axis_size("head")
    bc_part = conv_bc_bias.shape[0]
    bc_width = bc_part * head_count
    state_dim = bc_width // 2
    my_head = lax.axis_index("head")

    flag = start_flags.astype(f32)
    free = 1.0 - flag
    free1 = jnp.pad(free, (1, 0), constant_values=1.0)[:length]
    free2 = jnp.pad(free, (2, 0), constant_values=1.0)[:length]
    flags = jnp.pad(jnp.stack([flag, 1.0 - free * free1, 1.0 - free * free1 * free2], axis=1), ((0, 0), (1, 4)))
    last = jnp.stack([free[length - 1] * free[length - 2], free[length - 1], jnp.ones((), f32)])
    tail_mask = jnp.pad(last, (13, 0))[:, None]
    tail_rows = (tokens[length - 16 :].astype(f32) * tail_mask).astype(bf16)
    gain8 = jnp.broadcast_to(in_gain[None], (8, width))
    conv_bc = padded(jnp.concatenate([conv_bc_weight.astype(f32), conv_bc_bias[None]]), 8, bc_part)

    conv_x = padded(jnp.concatenate([conv_x_weight.astype(f32), conv_x_bias[None]]), 8, inner)
    head_rows = jnp.pad(jnp.stack([dt_bias, -jnp.exp(a_log)]), ((0, 6), (0, 8 - heads)))
    params = jnp.tile(head_rows, (1, 16))
    gains = jnp.pad(jnp.stack([norm_gain, jnp.repeat(skip_scale, head_dim)]), ((0, 6), (0, 0)))
    zx = proj_zx.reshape(width, 2 * inner)
    dt = jnp.tile(jnp.pad(proj_dt, ((0, 0), (0, 8 - heads))), (1, 16))

    normed, gate, conv_in, conv_out, info, entering, decay, conv_halo, weights, conv_w = front(
        tokens, zx, dt, flags, gain8, tail_rows, proj_bc, conv_bc, conv_x, params, heads, head_dim, state_dim)
    all_channels = inner * head_count
    mixed, d_gate, d_conv, d_step, op_sum, gate_rows, conv_grads, head_grads, back_rows, sums = layer(
        conv_out, conv_in, info, gate, cotangent, flags, out_proj, gains, entering, decay, conv_w, params,
        conv_halo, heads, head_dim, state_dim, all_channels)
    inv_rms = lax.rsqrt(sums[0].reshape(length, 1) / all_channels + epsilon)
    mixed_out = (tokens.astype(f32) + mixed.astype(f32) * inv_rms).astype(bf16)

    right = jnp.concatenate([gate_rows[:2], padded(head_grads[:2], 6, inner)])
    small = jnp.concatenate([
        jnp.zeros((8, width), f32),
        padded(jnp.concatenate([conv_grads[:, :inner], right], axis=1), 8, width),
        jnp.zeros((1, width), f32), padded(conv_grads[: taps + 1, inner:], 7, width)])
    d_normed, zx_sum, bc_sum, small_sum = tail(
        normed, d_gate, d_conv, d_step, zx, weights, gain8, back_rows, tail_mask[8:], small, 8)

    tokens_f = tokens.astype(f32)
    inv = lax.rsqrt(jnp.mean(tokens_f * tokens_f, axis=1, keepdims=True) + epsilon)
    xhat = tokens_f * inv
    scaled = d_normed.astype(f32) * in_gain
    grad_tokens = cotangent.astype(f32) + inv * (
        scaled - xhat * jnp.mean(scaled * xhat, axis=1, keepdims=True))
    conv_bc_sum = lax.dynamic_slice(small_sum, (17, my_head * bc_part), (taps + 1, bc_part))
    return (
        mixed_out,
        grad_tokens,
        small_sum[16],
        zx_sum.astype(f32).reshape(width, 2, inner),
        bc_sum.T,
        small_sum[:heads].T,
        small_sum[8 : 8 + taps, :inner],
        small_sum[8 + taps, :inner],
        conv_bc_sum[:taps],
        conv_bc_sum[taps],
        small_sum[10, inner : inner + heads],
        small_sum[11, inner : inner + heads],
        small_sum[9, inner : 2 * inner].reshape(heads, head_dim).sum(axis=1),
        small_sum[8, inner : 2 * inner],
        op_sum.astype(f32),
    )


def solution(mesh):
    in_specs = (
        P("seq", None),
        P("seq"),
        P(),
        P(None, None, "head"),
        P(None, "head"),
        P(None, "head"),
        P(None, "head"),
        P("head"),
        P(None, "head"),
        P("head"),
        P("head"),
        P("head"),
        P("head"),
        P("head"),
        P("head", None),
        P("seq", None),
    )
    out_specs = (
        P("seq", None),
        P("seq", None),
        P(),
        P(None, None, "head"),
        P(None, "head"),
        P(None, "head"),
        P(None, "head"),
        P("head"),
        P(None, "head"),
        P("head"),
        P("head"),
        P("head"),
        P("head"),
        P("head"),
        P("head", None),
    )
    return jax.shard_map(shards, mesh=mesh, in_specs=in_specs, out_specs=out_specs, check_vma=False)
```

```python
import functools

import jax
import jax.numpy as jnp
from jax import lax
from jax.experimental import pallas as pl
from jax.experimental.pallas import tpu as pltpu
from jax.sharding import PartitionSpec as P

MESH = pl.DeviceIdType.MESH
f32 = jnp.float32
bf16 = jnp.bfloat16
VMEM = pl.BlockSpec(memory_space=pltpu.VMEM)
HBM = pl.BlockSpec(memory_space=pl.ANY)
DMA = pltpu.SemaphoreType.DMA


def rows_of(ref, start, size):
    return ref.at[pl.ds(pl.multiple_of(start, size), size)]


def other_of(axis, k):
    size = lax.axis_size(axis)
    return lax.rem(lax.axis_index(axis) + k, size)


def greet(*axes):
    barrier = pltpu.get_barrier_semaphore()
    count = 0
    for axis in axes:
        size = lax.axis_size(axis)
        count += size - 1

        @pl.loop(1, size)
        def _(k):
            pl.semaphore_signal(barrier, inc=1, device_id={axis: other_of(axis, k)}, device_id_type=MESH)
    pl.semaphore_wait(barrier, count)


class LineSum:
    AHEAD = 3

    def __init__(self, own, got, total, out, sems, block):
        self.own, self.got, self.total, self.out = own, got, total, out
        self.send1, self.got_in, self.got_total, self.send2, self.stored = (sems.at[i] for i in range(5))
        self.block = block
        self.count = own.shape[0] // block
        size, me = lax.axis_size("head"), lax.axis_index("head")
        half = size // 2
        left = me < half
        self.mid = (me == half - 1) | (me == half)
        self.has_outer = (me > 0) & (me < size - 1)
        self.inner = jnp.where(left, me + 1, me - 1)
        self.outer = jnp.clip(jnp.where(left, me - 1, me + 1), 0, size - 1)

    @staticmethod
    def sems(rows, block):
        return DMA((5, rows // block))

    def rows(self, b):
        return pl.ds(pl.multiple_of(b * self.block, self.block), self.block)

    def copy(self, src, dst, b, send, recv, to):
        return pltpu.make_async_remote_copy(
            src_ref=src.at[self.rows(b)], dst_ref=dst.at[self.rows(b)],
            send_sem=send.at[b], recv_sem=recv.at[b], device_id={"head": to}, device_id_type=MESH)

    def store(self, b):
        return pltpu.make_async_copy(
            self.total.at[self.rows(b)], self.out.at[self.rows(b)], self.stored.at[b])

    def inward(self, b):
        rows = self.rows(b)

        @pl.when(self.has_outer)
        def _():
            self.copy(self.own, self.got, b, self.send1, self.got_in, self.outer).wait_recv()
            self.own[rows] = (self.got[rows].astype(f32) + self.own[rows].astype(f32)).astype(bf16)

        @pl.when(self.mid)
        def _():
            self.copy(self.own, self.total, b, self.send1, self.got_total, self.inner).start()

        @pl.when(jnp.logical_not(self.mid))
        def _():
            self.copy(self.own, self.got, b, self.send1, self.got_in, self.inner).start()

    def outward(self, b):
        rows = self.rows(b)
        self.copy(self.own, self.total, b, self.send1, self.got_total, self.inner).wait_recv()

        @pl.when(self.mid)
        def _():
            self.total[rows] = (self.own[rows].astype(f32) + self.total[rows].astype(f32)).astype(bf16)

        @pl.when(self.has_outer)
        def _():
            self.copy(self.total, self.total, b, self.send2, self.got_total, self.outer).start()
        self.store(b).start()

    def serve(self, first, last, lag):
        @pl.when(self.has_outer)
        def _():
            @pl.loop(first, last)
            def _(b):
                @pl.when(b < self.count)
                def _():
                    self.inward(b)

                @pl.when(b >= lag)
                def _():
                    self.outward(b - lag)

    def send(self, first, last):
        @pl.when(jnp.logical_not(self.has_outer))
        def _():
            @pl.loop(first, last)
            def _(b):
                @pl.when(b >= self.AHEAD)
                def _():
                    self.copy(self.own, self.got, b - self.AHEAD, self.send1, self.got_in, self.inner).wait_send()
                self.inward(b)

    def finish(self):
        @pl.when(jnp.logical_not(self.has_outer))
        def _():
            pl.loop(0, self.count)(self.outward)

        @pl.loop(0, self.count)
        def _(b):
            @pl.when(self.has_outer | (b >= self.count - self.AHEAD))
            def _():
                self.copy(self.own, self.got, b, self.send1, self.got_in, self.inner).wait_send()
            self.store(b).wait()

            @pl.when(self.has_outer)
            def _():
                self.copy(self.total, self.total, b, self.send2, self.got_total, self.outer).wait_send()


class PlaneSum:
    def __init__(self, own, slots, res, sems, owners):
        self.own, self.slots, self.res = own, slots, res
        self.rs_send, self.rs_got, self.ag_send, self.ag_got = (sems.at[i] for i in range(4))
        self.owners = owners
        self.size, self.me = lax.axis_size("seq"), lax.axis_index("seq")
        self.piece = own.shape[0] // owners

    def part(self, ref, k):
        return rows_of(ref, k * self.piece, self.piece)

    def scatter_copy(self, to, source):
        return pltpu.make_async_remote_copy(
            src_ref=self.part(self.own, to), dst_ref=self.slots.at[source],
            send_sem=self.rs_send.at[to], recv_sem=self.rs_got.at[source],
            device_id={"seq": to}, device_id_type=MESH)

    def gather_copy(self, owner, to):
        return pltpu.make_async_remote_copy(
            src_ref=self.part(self.res, owner), dst_ref=self.part(self.res, owner),
            send_sem=self.ag_send.at[to], recv_sem=self.ag_got.at[owner],
            device_id={"seq": to}, device_id_type=MESH)

    def scatter(self):
        @pl.loop(1, self.size)
        def _(k):
            to = other_of("seq", k)

            @pl.when(to < self.owners)
            def _():
                self.scatter_copy(to, self.me).start()

    def reduce(self):
        @pl.when(self.me < self.owners)
        def _():
            @pl.loop(1, self.size)
            def _(k):
                self.scatter_copy(self.me, other_of("seq", k)).wait_recv()
            mine = pl.ds(pl.multiple_of(self.me * self.piece, self.piece), self.piece)
            self.slots[self.me] = self.own[mine]
            total = self.slots[0].astype(f32)
            for k in range(1, self.size):
                total = total + self.slots[k].astype(f32)
            self.res[mine] = total.astype(self.res.dtype)

            @pl.loop(1, self.size)
            def _(k):
                self.gather_copy(self.me, other_of("seq", k)).start()

    def finish(self):
        @pl.loop(1, self.size)
        def _(k):
            other = other_of("seq", k)

            @pl.when(other < self.owners)
            def _():
                self.gather_copy(other, self.me).wait_recv()
                self.scatter_copy(other, self.me).wait_send()

        @pl.when(self.me < self.owners)
        def _():
            @pl.loop(1, self.size)
            def _(k):
                self.gather_copy(self.me, other_of("seq", k)).wait_send()


class Swap:
    def __init__(self, axis, own, slots, sems):
        self.axis, self.own, self.slots = axis, own, slots
        self.send, self.got = sems.at[0], sems.at[1]
        self.size, self.me = lax.axis_size(axis), lax.axis_index(axis)

    def copy(self, to, source):
        return pltpu.make_async_remote_copy(
            src_ref=self.own, dst_ref=self.slots.at[source],
            send_sem=self.send.at[to], recv_sem=self.got.at[source],
            device_id={self.axis: to}, device_id_type=MESH)

    def start(self):
        @pl.loop(1, self.size)
        def _(k):
            self.copy(other_of(self.axis, k), self.me).start()
        self.slots[self.me] = self.own[...]

    def wait(self):
        @pl.loop(1, self.size)
        def _(k):
            self.copy(self.me, other_of(self.axis, k)).wait_recv()

    def total(self):
        out = self.slots[0]
        for k in range(1, self.size):
            out = out + self.slots[k]
        return out

    def finish(self):
        @pl.loop(1, self.size)
        def _(k):
            self.copy(other_of(self.axis, k), self.me).wait_send()


class DeviceScan:
    def __init__(self, backward, total, fade, lead, out, got, got_fade, sent, sent_fade, sems):
        self.backward, self.total, self.fade, self.lead, self.out = backward, total, fade, lead, out
        self.got, self.got_fade, self.sent, self.sent_fade, self.sems = got, got_fade, sent, sent_fade, sems
        self.me = lax.axis_index("seq")
        self.rounds = lax.axis_size("seq").bit_length() - 1

    @staticmethod
    def scratch(state, fade):
        rounds = lax.axis_size("seq").bit_length() - 1
        return [pltpu.VMEM(fade, f32), pltpu.VMEM(fade, f32)] + [
            pltpu.VMEM((rounds,) + state, bf16), pltpu.VMEM((rounds,) + fade, f32)] * 2 + [DMA((4, rounds))]

    def copies(self, k):
        return [
            pltpu.make_async_remote_copy(
                src_ref=src.at[k], dst_ref=dst.at[k],
                send_sem=self.sems.at[i, k], recv_sem=self.sems.at[i + 1, k],
                device_id={"seq": jnp.bitwise_xor(self.me, 1 << k)}, device_id_type=MESH)
            for src, dst, i in ((self.sent, self.got, 0), (self.sent_fade, self.got_fade, 2))]

    def begin(self, decay):
        self.fade[...] = decay
        self.out[...] = jnp.zeros_like(self.out)
        self.lead[...] = jnp.ones_like(self.lead)

    def start(self, k):
        self.sent[k] = self.total[...].astype(bf16)
        self.sent_fade[k] = self.fade[...]
        for copy in self.copies(k):
            copy.start()

    def finish(self, k):
        for copy in self.copies(k):
            copy.wait()
        later = lax.rem(self.me // (1 << k), 2) == (0 if self.backward else 1)

        @pl.when(later)
        def _():
            theirs = self.got[k].astype(f32)
            self.out[...] = self.out[...] + self.lead[0:1] * theirs
            self.total[...] = self.total[...] + self.fade[0:1] * theirs
            self.lead[...] = self.lead[...] * self.got_fade[k]

        @pl.when(jnp.logical_not(later))
        def _():
            self.total[...] = self.got[k].astype(f32) + self.got_fade[k, 0:1] * self.total[...]
        self.fade[...] = self.fade[...] * self.got_fade[k]

    def run(self, between=None):
        for k in range(self.rounds):
            self.start(k)
            if between is not None:
                between(k)
            self.finish(k)


GROUP = 256
STRIP = 128
GAP = 200.0
epsilon = 1e-05
LIMIT = 56 * 2**20


def dot(a, b):
    return jnp.dot(a, b, preferred_element_type=f32)


def dot_nt(a, b):
    return lax.dot_general(a, b, (((1,), (1,)), ((), ())), preferred_element_type=f32)


def dot_tn(a, b):
    return lax.dot_general(a, b, (((0,), (0,)), ((), ())), preferred_element_type=f32)


def split3(v):
    one = v.astype(bf16)
    rest = v - one.astype(f32)
    two = rest.astype(bf16)
    return one, two, (rest - two.astype(f32)).astype(bf16)


def exact_left(ones, v):
    width = v.shape[1]
    out = dot(ones, jnp.concatenate(split3(v), axis=1))
    return out[:, :width] + out[:, width : 2 * width] + out[:, 2 * width :]


def head_sum(v, group_ones):
    high = v.astype(bf16)
    low = (v - high.astype(f32)).astype(bf16)
    return dot(high, group_ones) + dot(low, group_ones)


def sigmoid(v):
    return 1.0 / (1.0 + jnp.exp(-v))


def softplus(v):
    return jnp.maximum(v, 0.0) + jnp.log1p(jnp.exp(-jnp.abs(v)))


def spread(cols, first, heads, head_dim):
    rows = cols.shape[0]
    per = 128 // head_dim
    lane = lax.broadcasted_iota(jnp.int32, (rows, 128), 1)
    tiles = []
    for at in range(0, heads, per):
        tile = cols[:, first + at : first + at + 1]
        for k in range(1, per):
            tile = jnp.where(lane < k * head_dim, tile, cols[:, first + at + k : first + at + k + 1])
        tiles.append(jnp.broadcast_to(tile, (rows, 128)))
    return jnp.concatenate(tiles, axis=1)


def norm_rows(block, gain):
    value = block.astype(f32)
    inv = lax.rsqrt(jnp.mean(value * value, axis=1, keepdims=True) + epsilon)
    return (value * inv * gain).astype(bf16)


def whole(shape):
    return pl.BlockSpec(shape, lambda g: (0,) * len(shape))


def lane_groups(rows, *parts):
    lane = lax.broadcasted_iota(jnp.int32, (rows, 128), 1)
    out = parts[-1]
    for k in range(len(parts) - 2, -1, -1):
        out = jnp.where(lane < 8 * (k + 1), parts[k], out)
    return out


RAW, STEP, CUM, DEV, KEEP = 0, 8, 16, 24, 32


def head_lanes(row, heads, lane):
    out = jnp.zeros(lane.shape, f32)
    for k in range(heads):
        out = jnp.where(lane % 8 == k, row[:, k : k + 1], out)
    return out


def front_kernel(heads, head_dim, state_dim, count,
                 tokens, last_tokens, zx, flags, gain, proj_bc, proj_dt, conv_x_weight, conv_x_bias,
                 conv_bc_weight, conv_bc_bias, dt_bias, a_log, skip, norm_gain,
                 normed_out, gate_out, conv_in_out, conv_out_out, heads_out, entering, decay_out,
                 halo_out, weights_out, conv_w_out, params, gains_out, mask_out,
                 normed, taken, tail_rows, landed, proj_all, conv_bc, conv_all, flag_cols, flag_ext,
                 carry, ext, state, running, lead, fade,
                 scan_got, scan_got_fade, scan_sent, scan_sent_fade, scan_sems, proj_sems, conv_sems, row_sems):
    at = pl.program_id(0)
    rows = tokens.shape[0]
    inner = heads * head_dim
    bc_width = 2 * state_dim
    bc_part = proj_bc.shape[0]
    seq, me = lax.axis_size("seq"), lax.axis_index("seq")
    block = lax.rem(at, count)
    mine = pl.ds(pl.multiple_of(block * rows, rows), rows)
    swaps = [Swap("head", proj_bc, proj_all, proj_sems), Swap("head", conv_bc, conv_all, conv_sems)]
    row_copy = pltpu.make_async_remote_copy(
        src_ref=tail_rows, dst_ref=landed, send_sem=row_sems.at[0], recv_sem=row_sems.at[1],
        device_id={"seq": lax.rem(me + 1, seq)}, device_id_type=MESH)
    lane_row = lax.broadcasted_iota(jnp.int32, (1, 128), 1)

    @pl.when(at == 0)
    def _():
        final = 1.0 - flags[flags.shape[0] - 1 :].astype(f32)
        one, two = final[:, 127:128], final[:, 126:127]
        row = lax.broadcasted_iota(jnp.int32, (16, 128), 0)
        mask = jnp.where(row == 15, 1.0, jnp.where(row == 14, one, jnp.where(row == 13, one * two, 0.0)))
        mask_out[...] = mask
        tail_rows[...] = (last_tokens[...].astype(f32) * mask[:, 0:1]).astype(bf16)
        conv_bc[...] = jnp.zeros_like(conv_bc)
        conv_bc[0:4, :bc_part] = conv_bc_weight[...].astype(f32)
        conv_bc[4:5, :bc_part] = conv_bc_bias[...]
        greet("head", "seq")
        row_copy.start()
        for each in swaps:
            each.start()
        params[...] = jnp.zeros_like(params)
        params[0:1] = head_lanes(dt_bias[...], heads, lane_row)
        params[1:2] = -jnp.exp(head_lanes(a_log[...], heads, lane_row))
        gains_out[...] = jnp.zeros_like(gains_out)
        gains_out[0:1] = norm_gain[...]
        gains_out[1:2] = spread(head_lanes(skip[...], heads, lane_row), 0, heads, head_dim)
        flat = flags[...].astype(f32)
        turned = jnp.concatenate([flat, jnp.zeros((128 - flat.shape[0], 128), f32)], axis=0).T
        for k in range(flat.shape[0]):
            flag_cols[k * 128 : (k + 1) * 128] = jnp.broadcast_to(turned[:, k : k + 1], (128, 128))

    @pl.when(at < count)
    def _():
        low = norm_rows(tokens[...], gain[...])
        normed[mine] = low
        normed_out[...] = low
        raw = dot(low, zx[...])
        gate_out[...] = raw[:, :inner]
        taken[mine] = raw[:, inner:].astype(bf16)

    @pl.when(at == count)
    def _():
        row_copy.wait()
        for each in swaps:
            each.wait()
            each.finish()
        heads_there = proj_all.shape[0]
        for k in range(heads_there):
            weights_out[k * bc_part : (k + 1) * bc_part] = proj_all[k]
        eight = jnp.concatenate([proj_dt[...].astype(f32)] + (
            [jnp.zeros((8 - heads, proj_dt.shape[1]), f32)] if heads < 8 else []), axis=0)
        weights_out[bc_width:] = jnp.concatenate([eight] * 16, axis=0).astype(bf16)
        conv_w_out[...] = jnp.zeros_like(conv_w_out)
        conv_w_out[0:4, :inner] = conv_x_weight[...].astype(f32)
        conv_w_out[4:5, :inner] = conv_x_bias[...]
        conv_w_out[:, inner:] = jnp.concatenate([conv_all[k, :, :bc_part] for k in range(heads_there)], axis=1)
        head_rows = norm_rows(landed[...], gain[...])
        ahead = jnp.concatenate([dot(head_rows, zx[:, inner:]), dot_nt(head_rows, weights_out[:bc_width])], axis=1)
        ahead = jnp.where(me > 0, ahead, 0.0).astype(bf16)
        halo_out[...] = ahead
        carry[...] = ahead[8:].astype(f32)
        state[...] = jnp.zeros_like(state)
        running[...] = jnp.zeros_like(running)
        flag_ext[0:8] = jnp.zeros((8, 128), f32)

    @pl.when(at >= count)
    def _():
        raw = dot_nt(normed[mine], weights_out[...])
        conv_in = jnp.concatenate([taken[mine], raw[:, :bc_width].astype(bf16)], axis=1)
        conv_in_out[...] = conv_in
        current = conv_in.astype(f32)
        ext[0:8] = carry[...]
        ext[8:] = current
        carry[...] = ext[rows:]
        flag = flag_cols[mine]
        flag_ext[8:] = flag
        keep1 = 1.0 - flag
        keep2 = keep1 * (1.0 - flag_ext[7 : 7 + rows])
        keep3 = keep2 * (1.0 - flag_ext[6 : 6 + rows])
        flag_ext[0:8] = flag_ext[rows:]
        keep = (None, keep1, keep2, keep3)
        total = conv_w_out[4:5] + conv_w_out[0:1] * current
        for j in range(1, 4):
            total = total + conv_w_out[j : j + 1] * ext[pl.ds(8 - j, rows)] * keep[j][:, 0:1]
        conv_out_out[...] = total
        active = total * sigmoid(total)

        step_raw = raw[:, bc_width:]
        step = softplus(step_raw + params[0:1])
        log_decay = step * params[1:2] - GAP * flag
        order_r = lax.broadcasted_iota(jnp.int32, (rows, rows), 0)
        order_c = lax.broadcasted_iota(jnp.int32, (rows, rows), 1)
        cum = exact_left((order_r >= order_c).astype(bf16), log_decay)
        lane = lax.broadcasted_iota(jnp.int32, (rows, 128), 1)
        keeps = jnp.where(lane < KEEP + 1, keep1, jnp.where(lane < KEEP + 2, keep2, keep3))
        heads_out[...] = lane_groups(rows, step_raw, step, cum, cum + running[0:1], keeps)
        end = cum[rows - 1 : rows]
        running[...] = running[...] + end
        weight = step * jnp.exp(end - cum)
        scaled = (active[:, :inner] * spread(weight, 0, heads, head_dim)).astype(bf16)
        b_proj = active[:, inner : inner + state_dim].astype(bf16)
        state[...] = state[...] * spread(jnp.exp(end), 0, heads, head_dim) + dot_tn(b_proj, scaled)

    @pl.when(at == 2 * count - 1)
    def _():
        decay = spread(jnp.exp(running[...]), 0, heads, head_dim)
        decay_out[...] = decay
        scan = DeviceScan(False, state, fade, lead, entering, scan_got, scan_got_fade, scan_sent,
                          scan_sent_fade, scan_sems)
        scan.begin(decay)
        scan.run()


def front(tokens, zx, flags, gain, proj_bc, proj_dt, conv_x_weight, conv_x_bias, conv_bc_weight, conv_bc_bias,
          dt_bias, a_log, skip, norm_gain, heads, head_dim, state_dim):
    length, width = tokens.shape
    count = length // GROUP
    inner = heads * head_dim
    conv = inner + 2 * state_dim
    head_count = lax.axis_size("head")

    def early(cols):
        return pl.BlockSpec((GROUP, cols), lambda g: (jnp.minimum(g, count - 1), 0))

    def late(cols):
        return pl.BlockSpec((GROUP, cols), lambda g: (jnp.maximum(g - count, 0), 0))
    shape = jax.ShapeDtypeStruct
    state, fade = (state_dim, inner), (8, inner)
    rest = 2 * state_dim + 128
    return pl.pallas_call(
        functools.partial(front_kernel, heads, head_dim, state_dim, count),
        grid=(2 * count,),
        out_shape=(shape((length, width), bf16), shape((length, inner), f32), shape((length, conv), bf16),
                   shape((length, conv), f32), shape((length, 128), f32), shape(state, f32),
                   shape(fade, f32), shape((16, conv), bf16), shape((rest, width), bf16),
                   shape((8, conv), f32), shape((8, 128), f32), shape((8, inner), f32), shape((16, 128), f32)),
        in_specs=[early(width), pl.BlockSpec((16, width), lambda g: (length // 16 - 1, 0))] + [VMEM] * 13,
        out_specs=(early(width), early(inner), late(conv), late(conv), late(128)) + (VMEM,) * 8,
        scratch_shapes=[
            pltpu.VMEM((length, width), bf16), pltpu.VMEM((length, inner), bf16),
            pltpu.VMEM((16, width), bf16), pltpu.VMEM((16, width), bf16),
            pltpu.VMEM((head_count,) + proj_bc.shape, bf16), pltpu.VMEM((8, 128), f32),
            pltpu.VMEM((head_count, 8, 128), f32), pltpu.VMEM((length, 128), f32),
            pltpu.VMEM((GROUP + 8, 128), f32), pltpu.VMEM((8, conv), f32),
            pltpu.VMEM((GROUP + 8, conv), f32), pltpu.VMEM(state, f32), pltpu.VMEM((8, 128), f32)]
        + DeviceScan.scratch(state, fade) + [DMA((2, head_count)), DMA((2, head_count)), DMA((2,))],
        compiler_params=pltpu.CompilerParams(
            dimension_semantics=("arbitrary",), collective_id=3, has_side_effects=True,
            vmem_limit_bytes=LIMIT),
        name="front",
    )(tokens, tokens, zx, flags, gain, proj_bc, proj_dt, conv_x_weight, conv_x_bias, conv_bc_weight,
      conv_bc_bias, dt_bias, a_log, skip, norm_gain)


def strips(rows):
    return [(lo, lo + STRIP) for lo in range(0, rows, STRIP)]


def mix_step(heads, head_dim, state_dim, at,
             conv_out, heads_in, gate, cot, out_proj, gains, entering,
             ssm_out, d_normed_out, partial_out, sums_out, starts_out, state):
    rows = conv_out.shape[0]
    inner = heads * head_dim
    per = 128 // head_dim

    @pl.when(at == 0)
    def _():
        state[...] = entering[...]

    values = conv_out[...]
    active = values * sigmoid(values)
    x = active[:, :inner]
    b_proj = active[:, inner : inner + state_dim].astype(bf16)
    c_proj = active[:, inner + state_dim :].astype(bf16)
    info = heads_in[...]
    flipped = info.T
    stepped = x * spread(info, STEP, heads, head_dim)
    low = stepped.astype(bf16)
    scores = dot_nt(c_proj, b_proj)
    lane = lax.broadcasted_iota(jnp.int32, (rows, 128), 1)
    tiles = []
    for pair in range(heads // per):
        tile = low[:, pair * 128 : (pair + 1) * 128]
        parts = [None] * (rows // STRIP)
        for k in range(per):
            head = pair * per + k
            masked = jnp.where((lane >= k * head_dim) & (lane < (k + 1) * head_dim), tile, jnp.zeros_like(tile))
            for n, (lo, hi) in enumerate(strips(rows)):
                gap = info[lo:hi, CUM + head : CUM + head + 1] - flipped[CUM + head : CUM + head + 1, :hi]
                ok = (lax.broadcasted_iota(jnp.int32, (STRIP, hi), 0) + lo
                      >= lax.broadcasted_iota(jnp.int32, (STRIP, hi), 1))
                weight = jnp.exp(jnp.where(ok, gap, -1e30)) * scores[lo:hi, :hi]
                part = dot(weight.astype(bf16), masked[:hi])
                parts[n] = part if parts[n] is None else parts[n] + part
        tiles.append(jnp.concatenate(parts, axis=0))
    inside = jnp.concatenate(tiles, axis=1)
    cum = info[:, CUM : CUM + 8]
    end = info[rows - 1 : rows]
    start = state[...]
    starts_out[at] = start.astype(bf16)
    grown = spread(jnp.exp(info), CUM, heads, head_dim)
    result = inside + grown * dot(c_proj, start.astype(bf16)) + gains[1:2] * x
    fade = spread(jnp.exp(end - info), CUM, heads, head_dim)
    state[...] = start * spread(jnp.exp(end), CUM, heads, head_dim) + dot_tn(b_proj, (stepped * fade).astype(bf16))
    ssm_out[...] = result
    z = gate[...]
    gated = result * (z * sigmoid(z))
    d_normed = dot_nt(cot[...], out_proj[...])
    d_normed_out[...] = d_normed
    scaled = gated * gains[0:1]
    partial_out[...] = dot(scaled.astype(bf16), out_proj[...]).astype(bf16)
    squares = jnp.sum(gated * gated, axis=1, keepdims=True)
    cross = jnp.sum(d_normed * scaled, axis=1, keepdims=True)
    turned = jnp.where(lane == 0, squares, cross).T
    sums_out[0, pl.ds(at, 1)] = turned[0:1]
    sums_out[1, pl.ds(at, 1)] = turned[1:2]


def gate_step(heads, head_dim, state_dim, all_channels, at,
              ssm, gate, d_normed, sums, conv_out, heads_in, cot, gains,
              d_ssm_out, d_gate_out, grad_out, rows_out, total_out):
    rows = ssm.shape[0]
    inner = heads * head_dim

    @pl.when(at == 0)
    def _():
        grad_out[...] = jnp.zeros_like(grad_out)
        rows_out[...] = jnp.zeros_like(rows_out)
        total_out[...] = jnp.zeros_like(total_out)

    tall = jnp.concatenate([sums[0, pl.ds(at, 1)], sums[1, pl.ds(at, 1)], jnp.zeros((126, rows), f32)], axis=0).T
    inv = lax.rsqrt(tall[:, 0:1] / all_channels + epsilon)
    cross = tall[:, 1:2] / all_channels
    z = gate[...]
    s = sigmoid(z)
    y = ssm[...]
    gated = y * (z * s)
    gain = gains[0:1]
    back = d_normed[...]
    unit = gated * inv
    d_gated = inv * (back * gain - unit * (inv * cross))
    grad_out[...] += dot_tn((unit * gain).astype(bf16), cot[...])
    d_ssm = d_gated * (z * s)
    d_ssm_out[...] = d_ssm
    d_gate_out[...] = (d_gated * y * (s * (1.0 + z * (1.0 - s)))).astype(bf16)
    values = conv_out[...]
    active = values * sigmoid(values)
    rows_out[0:1] += jnp.sum(back * unit, axis=0, keepdims=True)
    rows_out[1:2] += jnp.sum(d_ssm * active[:, :inner], axis=0, keepdims=True)
    c_proj = active[:, inner + state_dim :].astype(bf16)
    grown = spread(jnp.exp(heads_in[...]), DEV, heads, head_dim)
    total_out[...] += dot_tn(c_proj, (grown * d_ssm).astype(bf16))


def back_step(heads, head_dim, state_dim, first_step, last_step,
              d_ssm, conv_out, conv_in, heads_in, start, entering, conv_w, params, skip, conv_halo,
              d_conv_in_out, d_step_out, conv_grads, head_grads, halo_out,
              lam, shift1, shift2, shift3, between):
    rows = d_ssm.shape[0]
    inner = heads * head_dim
    per = 128 // head_dim
    shifts = (shift1, shift2, shift3)

    @pl.when(first_step)
    def _():
        lam[...] = entering[...]
        conv_grads[...] = jnp.zeros_like(conv_grads)
        head_grads[...] = jnp.zeros_like(head_grads)
        for each in shifts:
            each[rows:] = jnp.zeros((8, each.shape[1]), f32)

    values = conv_out[...]
    gates = sigmoid(values)
    active = values * gates
    x = active[:, :inner]
    b_proj = active[:, inner : inner + state_dim].astype(bf16)
    c_proj = active[:, inner + state_dim :].astype(bf16)
    info = heads_in[...]
    flipped = info.T
    step = spread(info, STEP, heads, head_dim)
    stepped = x * step
    low = stepped.astype(bf16)
    dy = d_ssm[...]
    dy_low = dy.astype(bf16)
    scores = dot_nt(b_proj, c_proj)
    lane = lax.broadcasted_iota(jnp.int32, (rows, 128), 1)
    lane_one = lax.broadcasted_iota(jnp.int32, (STRIP, 128), 1)
    cuts = strips(rows)
    d_scores = [jnp.zeros((STRIP, rows - lo), f32) for lo, _ in cuts]
    d_rows = []
    d_cols = [jnp.zeros((STRIP, 128), f32) for _ in cuts]
    tiles = []
    for pair in range(heads // per):
        tile = low[:, pair * 128 : (pair + 1) * 128]
        dy_tile = dy_low[:, pair * 128 : (pair + 1) * 128]
        parts = [None] * len(cuts)
        for k in range(per):
            head = pair * per + k
            own = (lane >= k * head_dim) & (lane < (k + 1) * head_dim)
            masked = jnp.where(own, tile, jnp.zeros_like(tile))
            dy_masked = jnp.where(own, dy_tile, jnp.zeros_like(dy_tile))
            row_total = jnp.zeros((1, rows), f32)
            for n, (lo, hi) in enumerate(cuts):
                gap = flipped[CUM + head : CUM + head + 1, lo:] - info[lo:hi, CUM + head : CUM + head + 1]
                ok = (lax.broadcasted_iota(jnp.int32, (STRIP, rows - lo), 1)
                      >= lax.broadcasted_iota(jnp.int32, (STRIP, rows - lo), 0))
                decay = jnp.exp(jnp.where(ok, gap, -1e30))
                weight = decay * scores[lo:hi, lo:]
                part = dot(weight.astype(bf16), dy_masked[lo:])
                parts[n] = part if parts[n] is None else parts[n] + part
                pairs = dot_nt(masked[lo:hi], dy_tile[lo:])
                d_scores[n] = d_scores[n] + pairs * decay
                moved = pairs * weight
                d_cols[n] = d_cols[n] - jnp.where(lane_one == head, jnp.sum(moved, axis=1, keepdims=True), 0.0)
                col = jnp.sum(moved, axis=0, keepdims=True)
                if lo:
                    col = jnp.concatenate([jnp.zeros((1, lo), f32), col], axis=1)
                row_total = row_total + col
            d_rows.append(row_total)
        tiles.append(jnp.concatenate(parts, axis=0))
    between()
    d_stepped = jnp.concatenate(tiles, axis=1)
    d_cum = jnp.concatenate(d_cols, axis=0)
    d_cum = d_cum + jnp.concatenate(d_rows + [jnp.zeros((128 - heads, rows), f32)], axis=0).T
    full = jnp.concatenate(
        [jnp.concatenate([jnp.zeros((STRIP, lo), f32), part], axis=1) if lo else part
         for part, (lo, _) in zip(d_scores, cuts)], axis=0).astype(bf16)
    d_b = dot(full, c_proj)
    d_c = dot_tn(full, b_proj)

    group_ones = (lax.broadcasted_iota(jnp.int32, (inner, 128), 0) // head_dim
                  == lax.broadcasted_iota(jnp.int32, (inner, 128), 1)).astype(bf16)
    after = lam[...]
    after_low = after.astype(bf16)
    end = info[rows - 1 : rows]
    grown = spread(jnp.exp(info), CUM, heads, head_dim)
    fade = spread(jnp.exp(end - info), CUM, heads, head_dim)
    end_grown = spread(jnp.exp(end), CUM, heads, head_dim)
    from_after = fade * dot(b_proj, after_low)
    d_stepped = d_stepped + from_after
    grown_dy = grown * dy
    grown_low = grown_dy.astype(bf16)
    to_cum = head_sum(grown_dy * dot(c_proj, start), group_ones)
    left = head_sum(stepped * from_after, group_ones)
    kept = jnp.sum(after * start.astype(f32), axis=0, keepdims=True) * end_grown
    kept = head_sum(jnp.broadcast_to(kept, (8, inner)), group_ones)[0:1]
    last = kept + jnp.sum(left, axis=0, keepdims=True)
    row_id = lax.broadcasted_iota(jnp.int32, (rows, 128), 0)
    d_cum = d_cum + to_cum - left + jnp.where(row_id == rows - 1, last, 0.0)
    d_c = d_c + dot_nt(grown_low, start)
    d_b = d_b + dot_nt((fade * stepped).astype(bf16), after_low)
    lam[...] = end_grown * after + dot_tn(c_proj, grown_low)
    d_step = head_sum(d_stepped * x, group_ones)
    d_x = step * d_stepped + skip[0:1] * dy

    order_r = lax.broadcasted_iota(jnp.int32, (rows, rows), 0)
    order_c = lax.broadcasted_iota(jnp.int32, (rows, rows), 1)
    d_decay = exact_left((order_r <= order_c).astype(bf16), d_cum) * info[:, KEEP : KEEP + 1]
    rate = params[1:2]
    real = lane < heads
    step_raw = jnp.where(real, info, 0.0) + params[0:1]
    slope = sigmoid(step_raw)
    d_pre = jnp.where(real, (d_step + d_decay * rate) * slope, 0.0)
    d_step_out[...] = d_pre.astype(bf16)
    head_grads[0:1] += jnp.sum(d_pre, axis=0, keepdims=True)
    head_grads[1:2] += jnp.sum(jnp.where(real, d_decay * softplus(step_raw) * rate, 0.0), axis=0, keepdims=True)

    d_active = jnp.concatenate([d_x, d_b, d_c], axis=1)
    d_conv = d_active * (gates * (1.0 + values * (1.0 - gates)))
    taken = conv_in[...].astype(f32)
    total = d_conv * conv_w[0:1]
    conv_grads[0:1] += jnp.sum(d_conv * taken, axis=0, keepdims=True)
    conv_grads[4:5] += jnp.sum(d_conv, axis=0, keepdims=True)
    for j in range(1, 4):
        ref = shifts[j - 1]
        ref[0:rows] = d_conv * info[:, KEEP + j - 1 : KEEP + j]
        moved = ref[pl.ds(j, rows)]
        total = total + moved * conv_w[j : j + 1]
        conv_grads[j : j + 1] += jnp.sum(moved * taken, axis=0, keepdims=True)
    d_conv_in_out[...] = total.astype(bf16)

    @pl.when(last_step)
    def _():
        ahead = conv_halo[...].astype(f32)
        halo_out[...] = jnp.zeros_like(halo_out)
        for j in range(1, 4):
            first = shifts[j - 1][0:8]
            for t in range(j):
                row = 16 + t - j
                conv_grads[j : j + 1] += first[t : t + 1] * ahead[row : row + 1]
                halo_out[row - 8 : row - 7] += first[t : t + 1] * conv_w[j : j + 1]
    for each in shifts:
        each[rows:] = each[0:8]


def paced(times, pace, behind, most):
    return [max(0, min(most, int((time - behind) / pace))) for time in times]


def at_point(counts):
    def count(point):
        if isinstance(point, int):
            return counts[point] if point >= 0 else 0
        out = jnp.int32(0)
        for k, value in enumerate(counts):
            more = value - (counts[k - 1] if k else 0)
            if more:
                out = out + more * (point >= k).astype(jnp.int32)
        return out
    return count


def layer_kernel(heads, head_dim, state_dim, all_channels, count, block, lag, plans,
                 conv_out, conv_in, heads_in, gate, cot, out_proj, gains, entering, decay, conv_w,
                 params, conv_halo,
                 line_out, d_gate_out, d_conv_out, d_step_out, grad_out_out, gate_rows, conv_grads, head_grads,
                 halo_out, sums_out,
                 own, got, total, ssm, d_normed, starts, state, leaving, shift1, shift2, shift3, sums, sum_slots,
                 grad_out, grad_low, grad_slots, grad_res, lead, fade,
                 scan_got, scan_got_fade, scan_sent, scan_sent_fade, scan_sems, line_sems, sum_sems, grad_sems):
    at = pl.program_id(0)
    rows = conv_out.shape[0]
    seq = lax.axis_size("seq")
    line = LineSum(own, got, total, line_out, line_sems, block)
    swap = Swap("head", sums, sum_slots, sum_sems)
    scan = DeviceScan(True, state, fade, lead, leaving, scan_got, scan_got_fade, scan_sent, scan_sent_fade,
                      scan_sems)
    grad_sum = PlaneSum(grad_low, grad_slots, grad_res, grad_sems, min(seq, grad_low.shape[0] // 16))
    served, sent = at_point(plans[0]), at_point(plans[1])

    def serve(point):
        line.send(sent(point - 1), sent(point))
        line.serve(served(point - 1), served(point), lag)

    @pl.when(at == 0)
    def _():
        greet("head", "seq")
        state[...] = entering[...]

    serve(2 * at)

    @pl.when(at < count)
    def _():
        mine = pl.ds(pl.multiple_of(at * rows, rows), rows)
        mix_step(heads, head_dim, state_dim, at, conv_out, heads_in, gate, cot, out_proj, gains, entering,
                 ssm.at[mine], d_normed.at[mine], own.at[mine], sums, starts, state)

    @pl.when(at == count - 1)
    def _():
        swap.start()

    @pl.when(at == count)
    def _():
        swap.wait()
        sums_out[...] = swap.total()
        swap.finish()
        grad_out[...] = jnp.zeros_like(grad_out)
        gate_rows[...] = jnp.zeros_like(gate_rows)
        state[...] = jnp.zeros_like(state)

    @pl.when((at >= count) & (at < 2 * count))
    def _():
        here = at - count
        mine = pl.ds(pl.multiple_of(here * rows, rows), rows)
        gate_step(heads, head_dim, state_dim, all_channels, here,
                  ssm.at[mine], gate, d_normed.at[mine], sums_out, conv_out, heads_in, cot, gains,
                  ssm.at[mine], d_gate_out, grad_out, gate_rows, state)

    @pl.when(at == 2 * count)
    def _():
        grad_low[...] = grad_out[...].astype(bf16)
        scan.begin(decay[...])
        scan.run()
        grad_sum.scatter()

    @pl.when(at >= 2 * count)
    def _():
        here = 3 * count - 1 - at
        mine = pl.ds(pl.multiple_of(here * rows, rows), rows)
        back_step(heads, head_dim, state_dim, at == 2 * count, at == 3 * count - 1,
                  ssm.at[mine], conv_out, conv_in, heads_in, starts[here], leaving, conv_w, params,
                  gains[1:2], conv_halo, d_conv_out, d_step_out, conv_grads, head_grads, halo_out,
                  state, shift1, shift2, shift3, lambda: serve(2 * at + 1))

    @pl.when(at == 2 * count + count // 2)
    def _():
        grad_sum.reduce()

    @pl.when(at == 3 * count - 1)
    def _():
        grad_sum.finish()
        grad_out_out[...] = grad_res[...]
        serve(6 * count)
        line.finish()


def layer(conv_out, conv_in, heads_in, gate, cot, out_proj, gains, entering, decay, conv_w, params,
          conv_halo, heads, head_dim, state_dim, all_channels):
    length, conv = conv_out.shape
    count = length // GROUP
    inner = heads * head_dim
    width = cot.shape[1]
    seq, head_count = lax.axis_size("seq"), lax.axis_size("head")
    block = 64
    blocks = length // block
    lag = max(2, head_count // 2)
    steps = [MIX] * count + [GATE] * count + [BACK] * count
    times, now = [], 0.0
    for k, step in enumerate(steps):
        now += SWAP if k == count else 0.0
        half = SCAN + step / 2 if k == 2 * count else step / 2 if k > 2 * count else 0.0
        times += [now, now + half]
        now += step + (SCAN if k == 2 * count else 0.0)
    made = [min(blocks, (k // 2) * (GROUP // block)) for k in range(6 * count)]
    plans = (paced(times, PACE, LATE, blocks) + [blocks + lag],
             [min(a, b) for a, b in zip(made, paced(times, PACE, EARLY, blocks))] + [blocks])

    def by(cols, first, step):
        def index(g):
            ahead = jnp.where(g < count, g, jnp.where(g < 2 * count, g - count, 3 * count - 1 - g))
            if first == 2:
                ahead = jnp.where(g < 2 * count, count - 1, ahead)
            if first == 1:
                ahead = jnp.where(g < count, 0, ahead)
            if step == 1:
                ahead = jnp.where(g < 2 * count, ahead, count - 1)
            return (ahead, 0)
        return pl.BlockSpec((GROUP, cols), index)
    shape = jax.ShapeDtypeStruct
    state, fade = (state_dim, inner), (8, inner)
    owners = min(seq, inner // 16)
    return pl.pallas_call(
        functools.partial(layer_kernel, heads, head_dim, state_dim, all_channels, count, block, lag, plans),
        grid=(3 * count,),
        out_shape=(shape((length, width), bf16), shape((length, inner), bf16), shape((length, conv), bf16),
                   shape((length, 128), bf16), shape((inner, width), bf16), shape((8, inner), f32),
                   shape((8, conv), f32), shape((8, 128), f32), shape((8, conv), f32),
                   shape((2, count, GROUP), f32)),
        in_specs=[by(conv, 0, 2), by(conv, 2, 2), by(128, 0, 2), by(inner, 0, 1), by(width, 0, 1)]
        + [VMEM] * 7,
        out_specs=(HBM, by(inner, 1, 1), by(conv, 2, 2), by(128, 2, 2)) + (VMEM,) * 6,
        scratch_shapes=[pltpu.VMEM((length, width), bf16)] * 3 + [pltpu.VMEM((length, inner), f32)] * 2 + [
            pltpu.VMEM((count,) + state, bf16), pltpu.VMEM(state, f32), pltpu.VMEM(state, f32)]
        + [pltpu.VMEM((GROUP + 8, conv), f32)] * 3 + [
            pltpu.VMEM((2, count, GROUP), f32), pltpu.VMEM((head_count, 2, count, GROUP), f32),
            pltpu.VMEM((inner, width), f32), pltpu.VMEM((inner, width), bf16),
            pltpu.VMEM((seq, inner // owners, width), bf16), pltpu.VMEM((inner, width), bf16)]
        + DeviceScan.scratch(state, fade) + [LineSum.sems(length, block), DMA((2, head_count)), DMA((4, seq))],
        compiler_params=pltpu.CompilerParams(
            dimension_semantics=("arbitrary",), collective_id=4, has_side_effects=True,
            vmem_limit_bytes=LIMIT),
        name="layer",
    )(conv_out, conv_in, heads_in, gate, cot, out_proj, gains, entering, decay, conv_w, params, conv_halo)


PACE = 2.9
MIX, SWAP, GATE, SCAN, BACK = 2.7, 3.0, 2.0, 10.0, 6.6
EARLY, LATE = -2.0, 5.0
PROJECT, CUTS = 2.6, (17, 21)


def tail_kernel(count, block, lag, plans, cuts, owners, last_rows, taps,
                normed, d_gate, d_conv, d_step, zx, weights, gain, back_rows, tail_mask, gate_rows, conv_grads,
                head_grads, line_out, zx_out, bc_out, small_out,
                own, got, total, grad_zx, grad_low, zx_slots, zx_res, grad_bc, bc_part, bc_slots, bc_z, bc_res, small, small_slots,
                small_own, small_z, landed,
                line_sems, zx_sems, bc_sems, bcz_sems, small_sems, smallz_sems, row_sems):
    at = pl.program_id(0)
    rows, width = normed.shape
    inner = d_gate.shape[1]
    seq, heads = lax.axis_size("seq"), lax.axis_size("head")
    me, my_head = lax.axis_index("seq"), lax.axis_index("head")
    bc_width = bc_part.shape[0] * bc_part.shape[1]
    line = LineSum(own, got, total, line_out, line_sems, block)
    zx_sum = PlaneSum(grad_low, zx_slots, zx_res, zx_sems, owners[0])
    small_swap = Swap("seq", small, small_slots, small_sems)
    both_swap = Swap("head", small_own, small_z, smallz_sems)
    row_copy = pltpu.make_async_remote_copy(
        src_ref=back_rows, dst_ref=landed, send_sem=row_sems.at[0], recv_sem=row_sems.at[1],
        device_id={"seq": lax.rem(me + seq - 1, seq)}, device_id_type=MESH)
    served, sent = at_point(plans[0]), at_point(plans[1])

    @pl.when(at == 0)
    def _():
        greet("head", "seq")
        row_copy.start()
        grad_zx[...] = jnp.zeros_like(grad_zx)
        grad_bc[...] = jnp.zeros_like(grad_bc)
        small[...] = jnp.zeros_like(small)
        small[8 : 9 + taps, :inner] = conv_grads[: taps + 1, :inner]
        small[8:10, inner : 2 * inner] = gate_rows[0:2]
        small[10:12, inner : inner + 128] = head_grads[0:2]
        small[17 : 18 + taps, :bc_width] = conv_grads[: taps + 1, inner:]

    line.send(sent(at - 1), sent(at))
    line.serve(served(at - 1), served(at), lag)

    block_low = normed[...]
    gate_low, conv_low, step_low = d_gate[...], d_conv[...], d_step[...]
    rest_low = jnp.concatenate([conv_low[:, inner:], step_low], axis=1)
    d_normed = (dot_nt(gate_low, zx[:, :inner]) + dot_nt(conv_low[:, :inner], zx[:, inner:])
                + dot(rest_low, weights[...]))
    grad_zx[:, :inner] += dot_tn(block_low, gate_low)
    grad_zx[:, inner:] += dot_tn(block_low, conv_low[:, :inner])
    grad_bc[...] += dot_tn(rest_low, block_low)
    small[16:17] += jnp.sum(d_normed * block_low.astype(f32), axis=0, keepdims=True) / gain[...]
    mine = pl.ds(pl.multiple_of(at * rows, rows), rows)
    own[mine] = d_normed.astype(bf16)

    @pl.when(at == count - 1)
    def _():
        row_copy.wait()
        extra = jnp.where(me < seq - 1, landed[...] * tail_mask[8:, 0:1], 0.0)
        extra = jnp.concatenate([jnp.zeros_like(extra), extra], axis=0).astype(bf16)
        tail_low = normed[rows - 16 :]
        more = dot_nt(extra[:, :inner], zx[:, inner:]) + dot(extra[:, inner:], weights[:bc_width])
        grad_zx[:, inner:] += dot_tn(tail_low, extra[:, :inner])
        grad_bc[:bc_width] += dot_tn(extra[:, inner:], tail_low)
        small[16:17] += jnp.sum(more * tail_low.astype(f32), axis=0, keepdims=True) / gain[...]
        own[last_rows:] = (own[last_rows:].astype(f32) + more).astype(bf16)

    piece = bc_part.shape[1] // owners[1]

    def bc_scatter(to, source):
        return pltpu.make_async_remote_copy(
            src_ref=bc_part.at[:, pl.ds(pl.multiple_of(to * piece, piece), piece)],
            dst_ref=bc_slots.at[source], send_sem=bc_sems.at[0, to], recv_sem=bc_sems.at[1, source],
            device_id={"seq": to}, device_id_type=MESH)

    def bc_gather(owner, to):
        rows = pl.ds(pl.multiple_of(owner * piece, piece), piece)
        return pltpu.make_async_remote_copy(
            src_ref=bc_res.at[rows], dst_ref=bc_res.at[rows],
            send_sem=bc_sems.at[2, to], recv_sem=bc_sems.at[3, owner],
            device_id={"seq": to}, device_id_type=MESH)

    def bc_swap(to, source):
        return pltpu.make_async_remote_copy(
            src_ref=bc_slots.at[me, to], dst_ref=bc_z.at[source],
            send_sem=bcz_sems.at[0, to], recv_sem=bcz_sems.at[1, source],
            device_id={"head": to}, device_id_type=MESH)

    @pl.when(at == count - 1)
    def _():
        grad_low[...] = grad_zx[...].astype(bf16)
        zx_sum.scatter()
        small[0:8] += grad_bc[bc_width : bc_width + 8]
        small_swap.start()
        for k in range(heads):
            bc_part[k] = grad_bc[k * bc_part.shape[1] : (k + 1) * bc_part.shape[1]]

        @pl.loop(1, seq)
        def _(k):
            to = other_of("seq", k)

            @pl.when(to < owners[1])
            def _():
                bc_scatter(to, me).start()

        last = count - 1

        def go(first, until, sent_first, sent_until):
            line.send(sent_first, sent_until)
            line.serve(first, until, lag)
        go(served(last), cuts[0], sent(last), cuts[0] + 2)
        zx_sum.reduce()
        small_swap.wait()
        sums = small_swap.total()
        lone = small.shape[0] - small_own.shape[0]
        small_out[:lone] = sums[:lone]
        small_own[...] = sums[lone:]
        both_swap.start()

        @pl.when(me < owners[1])
        def _():
            @pl.loop(1, seq)
            def _(k):
                bc_scatter(me, other_of("seq", k)).wait_recv()
            bc_slots[me] = bc_part[:, pl.ds(pl.multiple_of(me * piece, piece), piece)]
            sums = bc_slots[0]
            for k in range(1, seq):
                sums = sums + bc_slots[k]
            bc_slots[me] = sums
            bc_z[my_head] = bc_slots[me, my_head]

            @pl.loop(1, heads)
            def _(k):
                bc_swap(other_of("head", k), my_head).start()

        go(cuts[0], cuts[1], cuts[0] + 2, cuts[1] + 2)
        both_swap.wait()
        small_out[lone:] = both_swap.total()

        @pl.when(me < owners[1])
        def _():
            @pl.loop(1, heads)
            def _(k):
                bc_swap(my_head, other_of("head", k)).wait_recv()
            sums = bc_z[0]
            for k in range(1, heads):
                sums = sums + bc_z[k]
            bc_res[pl.ds(pl.multiple_of(me * piece, piece), piece)] = sums

            @pl.loop(1, seq)
            def _(k):
                bc_gather(me, other_of("seq", k)).start()

        go(cuts[1], line.count + lag, cuts[1] + 2, line.count)
        line.finish()
        zx_sum.finish()
        zx_out[...] = zx_res[...]
        small_swap.finish()
        both_swap.finish()

        @pl.loop(1, seq)
        def _(k):
            other = other_of("seq", k)

            @pl.when(other < owners[1])
            def _():
                bc_gather(other, me).wait_recv()
                bc_scatter(other, me).wait_send()

            @pl.when(me < owners[1])
            def _():
                bc_gather(me, other).wait_send()
        bc_out[...] = bc_res[...]

        @pl.when(me < owners[1])
        def _():
            @pl.loop(1, heads)
            def _(k):
                bc_swap(other_of("head", k), my_head).wait_send()


def tail(normed, d_gate, d_conv, d_step, zx, weights, gain, back_rows, tail_mask, gate_rows, conv_grads,
         head_grads, taps):
    length, width = normed.shape
    inner, conv = d_gate.shape[1], d_conv.shape[1]
    count = length // GROUP
    seq, heads = lax.axis_size("seq"), lax.axis_size("head")
    bc_rows = (conv - inner) // heads
    owners = (min(seq, width // 16), min(seq, bc_rows // 8))
    piece = bc_rows // owners[1]
    block = 64
    blocks = length // block
    lag = max(2, heads // 2)
    made = [k * (GROUP // block) for k in range(count)]
    times = [PROJECT * k for k in range(count)]
    plans = (paced(times, PACE, LATE, blocks), [min(a, b) for a, b in zip(made, paced(times, PACE, EARLY, blocks))])
    cuts = ((blocks * CUTS[0]) // 32, (blocks * CUTS[1]) // 32)

    def by(cols):
        return pl.BlockSpec((GROUP, cols), lambda g: (g, 0))
    shape = jax.ShapeDtypeStruct
    return pl.pallas_call(
        functools.partial(tail_kernel, count, block, lag, plans, cuts, owners, length - 16, taps),
        grid=(count,),
        out_shape=(shape((length, width), bf16), shape((width, 2 * inner), bf16), shape((bc_rows, width), f32),
                   shape((24, width), f32)),
        in_specs=[by(width), by(inner), by(conv), by(128)] + [VMEM] * 8,
        out_specs=(HBM, VMEM, VMEM, VMEM),
        scratch_shapes=[pltpu.VMEM((length, width), bf16)] * 3 + [
            pltpu.VMEM((width, 2 * inner), f32), pltpu.VMEM((width, 2 * inner), bf16),
            pltpu.VMEM((seq, width // owners[0], 2 * inner), bf16), pltpu.VMEM((width, 2 * inner), bf16),
            pltpu.VMEM((conv - inner + 128, width), f32), pltpu.VMEM((heads, bc_rows, width), f32),
            pltpu.VMEM((seq, heads, piece, width), f32), pltpu.VMEM((heads, piece, width), f32),
            pltpu.VMEM((bc_rows, width), f32), pltpu.VMEM((24, width), f32), pltpu.VMEM((seq, 24, width), f32),
            pltpu.VMEM((8, width), f32), pltpu.VMEM((heads, 8, width), f32),
            pltpu.VMEM(back_rows.shape, f32),
            LineSum.sems(length, block), DMA((4, seq)), DMA((4, seq)), DMA((2, heads)), DMA((2, seq)),
            DMA((2, heads)), DMA((2,))],
        compiler_params=pltpu.CompilerParams(
            dimension_semantics=("arbitrary",), collective_id=5, has_side_effects=True,
            vmem_limit_bytes=LIMIT),
        name="tail",
    )(normed, d_gate, d_conv, d_step, zx, weights, gain, back_rows, tail_mask, gate_rows, conv_grads, head_grads)


def finish_kernel(heads, head_dim, all_channels, taps,
                  tokens, cot, mixed, d_normed, sums, gain, zx, op, bc, small,
                  mixed_out, tokens_out, zx_out, op_out, bc_out, dt_out, gain_out, conv_w_out, conv_b_out,
                  bc_w_out, bc_b_out, bias_out, rate_out, skip_out, norm_out):
    at = pl.program_id(0)
    rows = tokens.shape[0]
    inner = heads * head_dim
    value = tokens[...].astype(f32)
    tall = jnp.concatenate([sums[0, pl.ds(at, 1)], jnp.zeros((127, rows), f32)], axis=0).T
    inv_rms = lax.rsqrt(tall[:, 0:1] / all_channels + epsilon)
    mixed_out[...] = (value + mixed[...].astype(f32) * inv_rms).astype(bf16)
    inv = lax.rsqrt(jnp.mean(value * value, axis=1, keepdims=True) + epsilon)
    xhat = value * inv
    scaled = d_normed[...].astype(f32) * gain[...]
    tokens_out[...] = cot[...].astype(f32) + inv * (
        scaled - xhat * jnp.mean(scaled * xhat, axis=1, keepdims=True))
    sums_zx = zx[...].astype(f32)
    zx_out[:, 0, :] = sums_zx[:, :inner]
    zx_out[:, 1, :] = sums_zx[:, inner:]
    op_out[...] = op[...].astype(f32)
    cols = bc.shape[1]
    mine = pl.ds(pl.multiple_of(at * cols, cols), cols)
    bc_out[...] = bc[...].T
    dt_out[...] = small[0:8, mine].T[:, :heads]

    @pl.when(at == 0)
    def _():
        gain_out[...] = small[16:17]
        conv_w_out[...] = small[8 : 8 + taps, :inner]
        conv_b_out[...] = small[8 + taps : 9 + taps, :inner]
        bias_out[...] = small[10:11, inner : inner + heads]
        rate_out[...] = small[11:12, inner : inner + heads]
        norm_out[...] = small[8:9, inner : 2 * inner]
        group_ones = (lax.broadcasted_iota(jnp.int32, (inner, 128), 0) // head_dim
                      == lax.broadcasted_iota(jnp.int32, (inner, 128), 1)).astype(bf16)
        skips = jnp.broadcast_to(small[9:10, inner : 2 * inner], (8, inner))
        total = sum(dot(part, group_ones) for part in split3(skips))
        skip_out[...] = total[0:1, :heads]
        part = bc_w_out.shape[1]
        mine_bc = small[17 : 18 + taps, : part * lax.axis_size("head")]
        chosen = mine_bc[:, :part]
        for k in range(1, lax.axis_size("head")):
            chosen = jnp.where(lax.axis_index("head") == k, mine_bc[:, k * part : (k + 1) * part], chosen)
        bc_w_out[...] = chosen[:taps]
        bc_b_out[...] = chosen[taps : taps + 1]


def finish(tokens, cot, mixed, d_normed, sums, gain, zx, op, bc, small, heads, head_dim, taps):
    length, width = tokens.shape
    count = length // GROUP
    inner = heads * head_dim
    part = bc.shape[0]

    def by(rows, cols):
        return pl.BlockSpec((rows, cols), lambda g: (g, 0))
    shape = jax.ShapeDtypeStruct
    tall = by(GROUP, width)
    lone = [(1, width), (taps, inner), (1, inner), (taps, part), (1, part), (1, heads), (1, heads), (1, heads),
            (1, inner)]
    cols = width // count
    return pl.pallas_call(
        functools.partial(finish_kernel, heads, head_dim, inner * lax.axis_size("head"), taps),
        grid=(count,),
        out_shape=(shape((length, width), bf16), shape((length, width), f32), shape((width, 2, inner), f32),
                   shape((inner, width), f32), shape((width, part), f32), shape((width, heads), f32))
        + tuple(shape(each, f32) for each in lone),
        in_specs=[tall] * 4 + [VMEM, VMEM, by(cols, 2 * inner), by(inner // count, width),
                               pl.BlockSpec((part, cols), lambda g: (0, g)), VMEM],
        out_specs=(tall, tall, pl.BlockSpec((cols, 2, inner), lambda g: (g, 0, 0)), by(inner // count, width),
                   by(cols, part), by(cols, heads)) + (VMEM,) * len(lone),
        compiler_params=pltpu.CompilerParams(dimension_semantics=("arbitrary",), vmem_limit_bytes=LIMIT),
        name="finish",
    )(tokens, cot, mixed, d_normed, sums, gain, zx, op, bc, small)


def shards(
    tokens, start_flags, in_gain, proj_zx, proj_bc, proj_dt, conv_x_weight, conv_x_bias,
    conv_bc_weight, conv_bc_bias, dt_bias, a_log, skip_scale, norm_gain, out_proj, cotangent,
):
    length, width = tokens.shape
    heads = a_log.shape[0]
    inner = proj_zx.shape[2]
    head_dim = inner // heads
    taps = conv_x_weight.shape[0]
    head_count = lax.axis_size("head")
    bc_part = conv_bc_bias.shape[0]
    bc_width = bc_part * head_count
    state_dim = bc_width // 2
    zx = proj_zx.reshape(width, 2 * inner)
    gain = in_gain[None]
    (normed, gate, conv_in, conv_out, info, entering, decay, conv_halo, weights, conv_w, params, gains,
     tail_mask) = front(
        tokens, zx, start_flags.reshape(length // 128, 128), gain, proj_bc.T, proj_dt.T, conv_x_weight,
        conv_x_bias[None], conv_bc_weight, conv_bc_bias[None], dt_bias[None], a_log[None], skip_scale[None],
        norm_gain[None], heads, head_dim, state_dim)
    all_channels = inner * head_count
    mixed, d_gate, d_conv, d_step, op_sum, gate_rows, conv_grads, head_grads, back_rows, sums = layer(
        conv_out, conv_in, info, gate, cotangent, out_proj, gains, entering, decay, conv_w, params,
        conv_halo, heads, head_dim, state_dim, all_channels)
    d_normed, zx_sum, bc_sum, small_sum = tail(
        normed, d_gate, d_conv, d_step, zx, weights, gain, back_rows, tail_mask, gate_rows, conv_grads,
        head_grads, taps)
    (mixed_out, grad_tokens, grad_zx, grad_op, grad_bc, grad_dt, grad_gain, grad_conv_w, grad_conv_b,
     grad_bc_w, grad_bc_b, grad_bias, grad_rate, grad_skip, grad_norm) = finish(
        tokens, cotangent, mixed, d_normed, sums, gain, zx_sum, op_sum, bc_sum, small_sum, heads, head_dim, taps)
    return (
        mixed_out, grad_tokens, grad_gain[0], grad_zx, grad_bc, grad_dt, grad_conv_w, grad_conv_b[0],
        grad_bc_w, grad_bc_b[0], grad_bias[0], grad_rate[0], grad_skip[0], grad_norm[0], grad_op,
    )


def solution(mesh):
    in_specs = (
        P("seq", None),
        P("seq"),
        P(),
        P(None, None, "head"),
        P(None, "head"),
        P(None, "head"),
        P(None, "head"),
        P("head"),
        P(None, "head"),
        P("head"),
        P("head"),
        P("head"),
        P("head"),
        P("head"),
        P("head", None),
        P("seq", None),
    )
    out_specs = (
        P("seq", None),
        P("seq", None),
        P(),
        P(None, None, "head"),
        P(None, "head"),
        P(None, "head"),
        P(None, "head"),
        P("head"),
        P(None, "head"),
        P("head"),
        P("head"),
        P("head"),
        P("head"),
        P("head"),
        P("head", None),
    )
    return jax.shard_map(shards, mesh=mesh, in_specs=in_specs, out_specs=out_specs, check_vma=False)
```

```python
import functools

import jax
import jax.numpy as jnp
from jax import lax
from jax.experimental import pallas as pl
from jax.experimental.pallas import tpu as pltpu
from jax.sharding import PartitionSpec as P

MESH = pl.DeviceIdType.MESH
f32 = jnp.float32
bf16 = jnp.bfloat16
VMEM = pl.BlockSpec(memory_space=pltpu.VMEM)
HBM = pl.BlockSpec(memory_space=pl.ANY)
DMA = pltpu.SemaphoreType.DMA


def rows_of(ref, start, size):
    return ref.at[pl.ds(pl.multiple_of(start, size), size)]


def other_of(axis, k):
    size = lax.axis_size(axis)
    return lax.rem(lax.axis_index(axis) + k, size)


def greet(*axes):
    barrier = pltpu.get_barrier_semaphore()
    count = 0
    for axis in axes:
        size = lax.axis_size(axis)
        count += size - 1

        @pl.loop(1, size)
        def _(k):
            pl.semaphore_signal(barrier, inc=1, device_id={axis: other_of(axis, k)}, device_id_type=MESH)
    pl.semaphore_wait(barrier, count)


class Pace:
    def __init__(self, phases, pace, behind, most):
        self.phases, self.pace, self.behind, self.most = phases, pace, behind, most
        self.before = [0]
        for n, (points, _, _) in enumerate(phases):
            self.before.append(self.count(n, points - 1) if points else self.before[-1])

    def count(self, phase, k):
        _, start, step = self.phases[phase]
        low, top = self.before[phase], self.most
        value = (start + k * step - self.behind) // self.pace
        if isinstance(value, int):
            return max(low, min(top, value))
        return jnp.clip(value, low, top)

    def span(self, phase, k):
        if isinstance(k, int):
            return (self.count(phase, k - 1) if k else self.before[phase]), self.count(phase, k)
        return jnp.where(k == 0, self.before[phase], self.count(phase, k - 1)), self.count(phase, k)


class LineSum:
    AHEAD = 3

    def __init__(self, own, got, total, outs, place, sems, block):
        self.own, self.got, self.total, self.outs, self.place = own, got, total, outs, place
        self.send1, self.got_in, self.got_total, self.send2, self.stored = (sems.at[i] for i in range(5))
        self.block = block
        self.half = own.shape[0] // block
        self.count = 2 * self.half
        size, me = lax.axis_size("head"), lax.axis_index("head")
        left = me < size // 2
        self.mid = (me == size // 2 - 1) | (me == size // 2)
        self.has_outer = (me > 0) & (me < size - 1)
        self.inner = jnp.where(left, me + 1, me - 1)
        self.outer = jnp.clip(jnp.where(left, me - 1, me + 1), 0, size - 1)

    @staticmethod
    def sems(rows, block):
        return DMA((5, 2 * rows // block))

    def rows(self, b):
        return pl.ds(pl.multiple_of(b * self.block, self.block), self.block)

    def slot(self, b):
        return self.rows(lax.rem(b, self.half))

    def in_copy(self, b, to):
        return pltpu.make_async_remote_copy(
            src_ref=self.own.at[self.slot(b)], dst_ref=self.got.at[self.slot(b)],
            send_sem=self.send1.at[b], recv_sem=self.got_in.at[b], device_id={"head": to}, device_id_type=MESH)

    def cross_copy(self, b):
        return pltpu.make_async_remote_copy(
            src_ref=self.own.at[self.slot(b)], dst_ref=self.total.at[self.rows(b)],
            send_sem=self.send1.at[b], recv_sem=self.got_total.at[b],
            device_id={"head": self.inner}, device_id_type=MESH)

    def out_copy(self, b, to):
        return pltpu.make_async_remote_copy(
            src_ref=self.total.at[self.rows(b)], dst_ref=self.total.at[self.rows(b)],
            send_sem=self.send2.at[b], recv_sem=self.got_total.at[b],
            device_id={"head": to}, device_id_type=MESH)

    def store(self, b, do):
        for n, out in enumerate(self.outs):
            @pl.when(b // self.half == n)
            def _():
                do(pltpu.make_async_copy(self.total.at[self.rows(b)],
                                         out.at[self.rows(self.place(n, lax.rem(b, self.half)))],
                                         self.stored.at[b]))

    def inward(self, b):
        rows = self.slot(b)
        self.in_copy(b, self.outer).wait_recv()
        self.own[rows] = (self.got[rows].astype(f32) + self.own[rows].astype(f32)).astype(bf16)

        @pl.when(self.mid)
        def _():
            self.cross_copy(b).start()

        @pl.when(jnp.logical_not(self.mid))
        def _():
            self.in_copy(b, self.inner).start()

    def outward(self, b):
        rows = self.rows(b)
        self.cross_copy(b).wait_recv()

        @pl.when(self.has_outer)
        def _():
            self.cross_copy(b).wait_send()

        @pl.when(self.mid)
        def _():
            self.total[rows] = (self.own[self.slot(b)].astype(f32) + self.total[rows].astype(f32)).astype(bf16)

        @pl.when(self.has_outer)
        def _():
            self.out_copy(b, self.outer).start()
        self.store(b, lambda copy: copy.start())

    def serve(self, first, last, lag):
        @pl.when(self.has_outer)
        def _():
            @pl.loop(first, last)
            def _(b):
                @pl.when(b < self.count)
                def _():
                    self.inward(b)

                @pl.when(b >= lag)
                def _():
                    self.outward(b - lag)

    def send(self, first, last):
        @pl.when(jnp.logical_not(self.has_outer))
        def _():
            @pl.loop(first, last)
            def _(b):
                @pl.when(b >= self.AHEAD)
                def _():
                    self.in_copy(b - self.AHEAD, self.inner).wait_send()

                @pl.when(b >= self.half)
                def _():
                    self.outward(b - self.half)
                self.in_copy(b, self.inner).start()

    def finish(self):
        @pl.when(jnp.logical_not(self.has_outer))
        def _():
            pl.loop(self.half, self.count)(self.outward)

            @pl.loop(self.count - self.AHEAD, self.count)
            def _(b):
                self.in_copy(b, self.inner).wait_send()

        @pl.loop(0, self.count)
        def _(b):
            self.store(b, lambda copy: copy.wait())

            @pl.when(self.has_outer)
            def _():
                self.out_copy(b, self.outer).wait_send()


class PairedSum:
    def __init__(self, own, pair, mine, slots, theirs, sems):
        self.own, self.pair, self.mine, self.slots, self.theirs = own, pair, mine, slots, theirs
        self.sems = sems
        self.me = lax.axis_index("seq")
        self.chip, self.odd = self.me // 2, lax.rem(self.me, 2)
        self.partner = self.me + 1 - 2 * self.odd
        self.chips, self.piece = own.shape[0], own.shape[1] // 2

    @staticmethod
    def scratch(rows, width):
        seq = lax.axis_size("seq")
        piece = max(16, rows // seq)
        part = pltpu.VMEM((seq // 2, piece, width), bf16)
        return [pltpu.VMEM((seq // 2, 2 * piece, width), bf16)] + [part] * 4 + [DMA((6, seq // 2))]

    def half(self, odd):
        return pl.ds(pl.multiple_of(odd * self.piece, self.piece), self.piece)

    def swap_copy(self):
        return pltpu.make_async_remote_copy(
            src_ref=self.own.at[:, self.half(1 - self.odd)], dst_ref=self.pair,
            send_sem=self.sems.at[0, 0], recv_sem=self.sems.at[1, 0],
            device_id={"seq": self.partner}, device_id_type=MESH)

    def back_copy(self):
        return pltpu.make_async_remote_copy(
            src_ref=self.pair, dst_ref=self.theirs,
            send_sem=self.sems.at[0, 1], recv_sem=self.sems.at[1, 1],
            device_id={"seq": self.partner}, device_id_type=MESH)

    def scatter_copy(self, to, source):
        return pltpu.make_async_remote_copy(
            src_ref=self.mine.at[to], dst_ref=self.slots.at[source],
            send_sem=self.sems.at[2, to], recv_sem=self.sems.at[3, source],
            device_id={"seq": 2 * to + self.odd}, device_id_type=MESH)

    def gather_copy(self, owner, to):
        return pltpu.make_async_remote_copy(
            src_ref=self.pair.at[owner], dst_ref=self.pair.at[owner],
            send_sem=self.sems.at[4, to], recv_sem=self.sems.at[5, owner],
            device_id={"seq": 2 * to + self.odd}, device_id_type=MESH)

    def release(self, free):
        pl.semaphore_signal(free, inc=1, device_id={"seq": self.partner}, device_id_type=MESH)

    def others(self, do):
        @pl.loop(1, self.chips)
        def _(k):
            do(lax.rem(self.chip + k, self.chips))

    def swap(self):
        self.swap_copy().start()

    def scatter(self):
        self.swap_copy().wait()
        self.mine[...] = (self.own[:, self.half(self.odd)].astype(f32) + self.pair[...].astype(f32)).astype(bf16)
        self.others(lambda other: self.scatter_copy(other, self.chip).start())

    def gather(self):
        self.others(lambda other: self.scatter_copy(self.chip, other).wait_recv())
        self.others(lambda other: self.scatter_copy(other, self.chip).wait_send())
        self.slots[self.chip] = self.mine[self.chip]
        total = self.slots[0].astype(f32)
        for k in range(1, self.chips):
            total = total + self.slots[k].astype(f32)
        self.pair[self.chip] = total.astype(bf16)
        self.others(lambda other: self.gather_copy(self.chip, other).start())

    def back(self):
        self.others(lambda other: self.gather_copy(other, self.chip).wait_recv())
        self.back_copy().start()

    def finish(self, out):
        self.back_copy().wait()
        self.others(lambda other: self.gather_copy(self.chip, other).wait_send())
        for k in range(min(self.chips, out.shape[0] // (2 * self.piece))):
            for odd, ref in ((self.odd, self.pair), (1 - self.odd, self.theirs)):
                start = pl.multiple_of((2 * k + odd) * self.piece, self.piece)
                out[pl.ds(start, self.piece)] = ref[k]


class Swap:
    def __init__(self, axis, own, slots, sems):
        self.axis, self.own, self.slots = axis, own, slots
        self.send, self.got = sems.at[0], sems.at[1]
        self.size, self.me = lax.axis_size(axis), lax.axis_index(axis)

    def copy(self, to, source):
        return pltpu.make_async_remote_copy(
            src_ref=self.own, dst_ref=self.slots.at[source],
            send_sem=self.send.at[to], recv_sem=self.got.at[source],
            device_id={self.axis: to}, device_id_type=MESH)

    def start(self):
        @pl.loop(1, self.size)
        def _(k):
            self.copy(other_of(self.axis, k), self.me).start()
        self.slots[self.me] = self.own[...]

    def wait(self):
        @pl.loop(1, self.size)
        def _(k):
            self.copy(self.me, other_of(self.axis, k)).wait_recv()

    def total(self):
        out = self.slots[0]
        for k in range(1, self.size):
            out = out + self.slots[k]
        return out

    def finish(self):
        @pl.loop(1, self.size)
        def _(k):
            self.copy(other_of(self.axis, k), self.me).wait_send()


class DeviceScan:
    def __init__(self, backward, total, fade, lead, out, got, got_fade, sent, sent_fade, sems):
        self.backward, self.total, self.fade, self.lead, self.out = backward, total, fade, lead, out
        self.got, self.got_fade, self.sent, self.sent_fade, self.sems = got, got_fade, sent, sent_fade, sems
        self.me = lax.axis_index("seq")
        self.rounds = lax.axis_size("seq").bit_length() - 1

    @staticmethod
    def scratch(state, fade):
        rounds = lax.axis_size("seq").bit_length() - 1
        return [pltpu.VMEM(fade, f32), pltpu.VMEM(fade, f32)] + [
            pltpu.VMEM((rounds,) + state, bf16), pltpu.VMEM((rounds,) + fade, f32)] * 2 + [DMA((4, rounds))]

    def copies(self, k):
        return [
            pltpu.make_async_remote_copy(
                src_ref=src.at[k], dst_ref=dst.at[k],
                send_sem=self.sems.at[i, k], recv_sem=self.sems.at[i + 1, k],
                device_id={"seq": jnp.bitwise_xor(self.me, 1 << k)}, device_id_type=MESH)
            for src, dst, i in ((self.sent, self.got, 0), (self.sent_fade, self.got_fade, 2))]

    def begin(self, decay):
        self.fade[...] = decay
        self.out[...] = jnp.zeros_like(self.out)
        self.lead[...] = jnp.ones_like(self.lead)

    def start(self, k):
        self.sent[k] = self.total[...].astype(bf16)
        self.sent_fade[k] = self.fade[...]
        for copy in self.copies(k):
            copy.start()

    def finish(self, k):
        for copy in self.copies(k):
            copy.wait()
        later = lax.rem(self.me // (1 << k), 2) == (0 if self.backward else 1)

        @pl.when(later)
        def _():
            theirs = self.got[k].astype(f32)
            self.out[...] = self.out[...] + self.lead[0:1] * theirs
            self.total[...] = self.total[...] + self.fade[0:1] * theirs
            self.lead[...] = self.lead[...] * self.got_fade[k]

        @pl.when(jnp.logical_not(later))
        def _():
            self.total[...] = self.got[k].astype(f32) + self.got_fade[k, 0:1] * self.total[...]
        self.fade[...] = self.fade[...] * self.got_fade[k]

    def run(self, between=None):
        for k in range(self.rounds):
            self.start(k)
            if between is not None:
                between(k)
            self.finish(k)


GROUP = 256
STRIP = 128
GAP = 200.0
epsilon = 1e-05
LIMIT = 56 * 2**20


def dot(a, b):
    return jnp.dot(a, b, preferred_element_type=f32)


def dot_nt(a, b):
    return lax.dot_general(a, b, (((1,), (1,)), ((), ())), preferred_element_type=f32)


def dot_tn(a, b):
    return lax.dot_general(a, b, (((0,), (0,)), ((), ())), preferred_element_type=f32)


def split3(v):
    one = v.astype(bf16)
    rest = v - one.astype(f32)
    two = rest.astype(bf16)
    return one, two, (rest - two.astype(f32)).astype(bf16)


def exact_left(ones, v):
    width = v.shape[1]
    out = dot(ones, jnp.concatenate(split3(v), axis=1))
    return out[:, :width] + out[:, width : 2 * width] + out[:, 2 * width :]


def head_sum(v, group_ones):
    high = v.astype(bf16)
    low = (v - high.astype(f32)).astype(bf16)
    return dot(high, group_ones) + dot(low, group_ones)


def sigmoid(v):
    return 1.0 / (1.0 + jnp.exp(-v))


def softplus(v):
    return jnp.maximum(v, 0.0) + jnp.log1p(jnp.exp(-jnp.abs(v)))


def spread(cols, first, heads, head_dim):
    rows = cols.shape[0]
    per = 128 // head_dim
    lane = lax.broadcasted_iota(jnp.int32, (rows, 128), 1)
    tiles = []
    for at in range(0, heads, per):
        tile = cols[:, first + at : first + at + 1]
        for k in range(1, per):
            tile = jnp.where(lane < k * head_dim, tile, cols[:, first + at + k : first + at + k + 1])
        tiles.append(jnp.broadcast_to(tile, (rows, 128)))
    return jnp.concatenate(tiles, axis=1)


def norm_rows(block, gain):
    value = block.astype(f32)
    inv = lax.rsqrt(jnp.mean(value * value, axis=1, keepdims=True) + epsilon)
    return (value * inv * gain).astype(bf16)


def whole(shape):
    return pl.BlockSpec(shape, lambda g: (0,) * len(shape))


def lane_groups(rows, *parts):
    lane = lax.broadcasted_iota(jnp.int32, (rows, 128), 1)
    out = parts[-1]
    for k in range(len(parts) - 2, -1, -1):
        out = jnp.where(lane < 8 * (k + 1), parts[k], out)
    return out


RAW, STEP, CUM, DEV, KEEP = 0, 8, 16, 24, 32


def head_lanes(row, heads, lane):
    out = jnp.zeros(lane.shape, f32)
    for k in range(heads):
        out = jnp.where(lane % 8 == k, row[:, k : k + 1], out)
    return out


def front_kernel(heads, head_dim, state_dim, count,
                 tokens, last_tokens, zx, flags, gain, proj_bc, proj_dt, conv_x_weight, conv_x_bias,
                 conv_bc_weight, conv_bc_bias, dt_bias, a_log, skip, norm_gain,
                 normed_out, gate_out, conv_in_out, conv_out_out, heads_out, entering, decay_out,
                 halo_out, weights_out, conv_w_out, params, gains_out, mask_out,
                 normed, taken, tail_rows, landed, proj_all, conv_bc, conv_all, flag_cols, flag_ext,
                 carry, ext, state, running, lead, fade,
                 scan_got, scan_got_fade, scan_sent, scan_sent_fade, scan_sems, proj_sems, conv_sems, row_sems):
    at = pl.program_id(0)
    rows = tokens.shape[0]
    inner = heads * head_dim
    bc_width = 2 * state_dim
    bc_part = proj_bc.shape[0]
    seq, me = lax.axis_size("seq"), lax.axis_index("seq")
    block = lax.rem(at, count)
    mine = pl.ds(pl.multiple_of(block * rows, rows), rows)
    swaps = [Swap("head", proj_bc, proj_all, proj_sems), Swap("head", conv_bc, conv_all, conv_sems)]
    row_copy = pltpu.make_async_remote_copy(
        src_ref=tail_rows, dst_ref=landed, send_sem=row_sems.at[0], recv_sem=row_sems.at[1],
        device_id={"seq": lax.rem(me + 1, seq)}, device_id_type=MESH)
    lane_row = lax.broadcasted_iota(jnp.int32, (1, 128), 1)

    @pl.when(at == 0)
    def _():
        final = 1.0 - flags[flags.shape[0] - 1 :].astype(f32)
        one, two = final[:, 127:128], final[:, 126:127]
        row = lax.broadcasted_iota(jnp.int32, (16, 128), 0)
        mask = jnp.where(row == 15, 1.0, jnp.where(row == 14, one, jnp.where(row == 13, one * two, 0.0)))
        mask_out[...] = mask
        tail_rows[...] = (last_tokens[...].astype(f32) * mask[:, 0:1]).astype(bf16)
        conv_bc[...] = jnp.zeros_like(conv_bc)
        conv_bc[0:4, :bc_part] = conv_bc_weight[...].astype(f32)
        conv_bc[4:5, :bc_part] = conv_bc_bias[...]
        greet("head", "seq")
        row_copy.start()
        for each in swaps:
            each.start()
        params[...] = jnp.zeros_like(params)
        params[0:1] = head_lanes(dt_bias[...], heads, lane_row)
        params[1:2] = -jnp.exp(head_lanes(a_log[...], heads, lane_row))
        gains_out[...] = jnp.zeros_like(gains_out)
        gains_out[0:1] = norm_gain[...]
        gains_out[1:2] = spread(head_lanes(skip[...], heads, lane_row), 0, heads, head_dim)
        flat = flags[...].astype(f32)
        turned = jnp.concatenate([flat, jnp.zeros((128 - flat.shape[0], 128), f32)], axis=0).T
        for k in range(flat.shape[0]):
            flag_cols[k * 128 : (k + 1) * 128] = jnp.broadcast_to(turned[:, k : k + 1], (128, 128))

    @pl.when(at < count)
    def _():
        low = norm_rows(tokens[...], gain[...])
        normed[mine] = low
        normed_out[...] = low
        raw = dot(low, zx[...])
        gate_out[...] = raw[:, :inner]
        taken[mine] = raw[:, inner:].astype(bf16)

    @pl.when(at == count)
    def _():
        row_copy.wait()
        for each in swaps:
            each.wait()
            each.finish()
        heads_there = proj_all.shape[0]
        for k in range(heads_there):
            weights_out[k * bc_part : (k + 1) * bc_part] = proj_all[k]
        eight = jnp.concatenate([proj_dt[...].astype(f32)] + (
            [jnp.zeros((8 - heads, proj_dt.shape[1]), f32)] if heads < 8 else []), axis=0)
        weights_out[bc_width:] = jnp.concatenate([eight] * 16, axis=0).astype(bf16)
        conv_w_out[...] = jnp.zeros_like(conv_w_out)
        conv_w_out[0:4, :inner] = conv_x_weight[...].astype(f32)
        conv_w_out[4:5, :inner] = conv_x_bias[...]
        conv_w_out[:, inner:] = jnp.concatenate([conv_all[k, :, :bc_part] for k in range(heads_there)], axis=1)
        head_rows = norm_rows(landed[...], gain[...])
        ahead = jnp.concatenate([dot(head_rows, zx[:, inner:]), dot_nt(head_rows, weights_out[:bc_width])], axis=1)
        ahead = jnp.where(me > 0, ahead, 0.0).astype(bf16)
        halo_out[...] = ahead
        carry[...] = ahead[8:].astype(f32)
        state[...] = jnp.zeros_like(state)
        running[...] = jnp.zeros_like(running)
        flag_ext[0:8] = jnp.zeros((8, 128), f32)

    @pl.when(at >= count)
    def _():
        raw = dot_nt(normed[mine], weights_out[...])
        conv_in = jnp.concatenate([taken[mine], raw[:, :bc_width].astype(bf16)], axis=1)
        conv_in_out[...] = conv_in
        current = conv_in.astype(f32)
        ext[0:8] = carry[...]
        ext[8:] = current
        carry[...] = ext[rows:]
        flag = flag_cols[mine]
        flag_ext[8:] = flag
        keep1 = 1.0 - flag
        keep2 = keep1 * (1.0 - flag_ext[7 : 7 + rows])
        keep3 = keep2 * (1.0 - flag_ext[6 : 6 + rows])
        flag_ext[0:8] = flag_ext[rows:]
        keep = (None, keep1, keep2, keep3)
        total = conv_w_out[4:5] + conv_w_out[0:1] * current
        for j in range(1, 4):
            total = total + conv_w_out[j : j + 1] * ext[pl.ds(8 - j, rows)] * keep[j][:, 0:1]
        conv_out_out[...] = total
        active = total * sigmoid(total)

        step_raw = raw[:, bc_width:]
        step = softplus(step_raw + params[0:1])
        log_decay = step * params[1:2] - GAP * flag
        order_r = lax.broadcasted_iota(jnp.int32, (rows, rows), 0)
        order_c = lax.broadcasted_iota(jnp.int32, (rows, rows), 1)
        cum = exact_left((order_r >= order_c).astype(bf16), log_decay)
        lane = lax.broadcasted_iota(jnp.int32, (rows, 128), 1)
        keeps = jnp.where(lane < KEEP + 1, keep1, jnp.where(lane < KEEP + 2, keep2, keep3))
        heads_out[...] = lane_groups(rows, step_raw, step, cum, cum + running[0:1], keeps)
        end = cum[rows - 1 : rows]
        running[...] = running[...] + end
        weight = step * jnp.exp(end - cum)
        scaled = (active[:, :inner] * spread(weight, 0, heads, head_dim)).astype(bf16)
        b_proj = active[:, inner : inner + state_dim].astype(bf16)
        state[...] = state[...] * spread(jnp.exp(end), 0, heads, head_dim) + dot_tn(b_proj, scaled)

    @pl.when(at == 2 * count - 1)
    def _():
        decay = spread(jnp.exp(running[...]), 0, heads, head_dim)
        decay_out[...] = decay
        scan = DeviceScan(False, state, fade, lead, entering, scan_got, scan_got_fade, scan_sent,
                          scan_sent_fade, scan_sems)
        scan.begin(decay)
        scan.run()


def front(tokens, zx, flags, gain, proj_bc, proj_dt, conv_x_weight, conv_x_bias, conv_bc_weight, conv_bc_bias,
          dt_bias, a_log, skip, norm_gain, heads, head_dim, state_dim):
    length, width = tokens.shape
    count = length // GROUP
    inner = heads * head_dim
    conv = inner + 2 * state_dim
    head_count = lax.axis_size("head")

    def early(cols):
        return pl.BlockSpec((GROUP, cols), lambda g: (jnp.minimum(g, count - 1), 0))

    def late(cols):
        return pl.BlockSpec((GROUP, cols), lambda g: (jnp.maximum(g - count, 0), 0))
    shape = jax.ShapeDtypeStruct
    state, fade = (state_dim, inner), (8, inner)
    rest = 2 * state_dim + 128
    return pl.pallas_call(
        functools.partial(front_kernel, heads, head_dim, state_dim, count),
        grid=(2 * count,),
        out_shape=(shape((length, width), bf16), shape((length, inner), f32), shape((length, conv), bf16),
                   shape((length, conv), f32), shape((length, 128), f32), shape(state, f32),
                   shape(fade, f32), shape((16, conv), bf16), shape((rest, width), bf16),
                   shape((8, conv), f32), shape((8, 128), f32), shape((8, inner), f32), shape((16, 128), f32)),
        in_specs=[early(width), pl.BlockSpec((16, width), lambda g: (length // 16 - 1, 0))] + [VMEM] * 13,
        out_specs=(early(width), early(inner), late(conv), late(conv), late(128)) + (VMEM,) * 8,
        scratch_shapes=[
            pltpu.VMEM((length, width), bf16), pltpu.VMEM((length, inner), bf16),
            pltpu.VMEM((16, width), bf16), pltpu.VMEM((16, width), bf16),
            pltpu.VMEM((head_count,) + proj_bc.shape, bf16), pltpu.VMEM((8, 128), f32),
            pltpu.VMEM((head_count, 8, 128), f32), pltpu.VMEM((length, 128), f32),
            pltpu.VMEM((GROUP + 8, 128), f32), pltpu.VMEM((8, conv), f32),
            pltpu.VMEM((GROUP + 8, conv), f32), pltpu.VMEM(state, f32), pltpu.VMEM((8, 128), f32)]
        + DeviceScan.scratch(state, fade) + [DMA((2, head_count)), DMA((2, head_count)), DMA((2,))],
        compiler_params=pltpu.CompilerParams(
            dimension_semantics=("arbitrary",), collective_id=3, has_side_effects=True,
            vmem_limit_bytes=LIMIT),
        name="front",
    )(tokens, tokens, zx, flags, gain, proj_bc, proj_dt, conv_x_weight, conv_x_bias, conv_bc_weight,
      conv_bc_bias, dt_bias, a_log, skip, norm_gain)


def strips(rows):
    return [(lo, lo + STRIP) for lo in range(0, rows, STRIP)]


def mix_step(heads, head_dim, state_dim, at,
             conv_out, heads_in, gate, cot, out_proj, gains, entering,
             ssm_out, d_normed_out, partial_out, sums_out, starts_out, state, between):
    rows = conv_out.shape[0]
    inner = heads * head_dim
    per = 128 // head_dim

    @pl.when(at == 0)
    def _():
        state[...] = entering[...]

    values = conv_out[...]
    active = values * sigmoid(values)
    x = active[:, :inner]
    b_proj = active[:, inner : inner + state_dim].astype(bf16)
    c_proj = active[:, inner + state_dim :].astype(bf16)
    info = heads_in[...]
    flipped = info.T
    stepped = x * spread(info, STEP, heads, head_dim)
    low = stepped.astype(bf16)
    scores = dot_nt(c_proj, b_proj)
    lane = lax.broadcasted_iota(jnp.int32, (rows, 128), 1)
    tiles = []
    for pair in range(heads // per):
        tile = low[:, pair * 128 : (pair + 1) * 128]
        weights, masked = [], []
        for k in range(per):
            head = pair * per + k
            masked.append(jnp.where((lane >= k * head_dim) & (lane < (k + 1) * head_dim), tile,
                                    jnp.zeros_like(tile)))
            parts = []
            for lo, hi in strips(rows):
                gap = info[lo:hi, CUM + head : CUM + head + 1] - flipped[CUM + head : CUM + head + 1, :hi]
                ok = (lax.broadcasted_iota(jnp.int32, (STRIP, hi), 0) + lo
                      >= lax.broadcasted_iota(jnp.int32, (STRIP, hi), 1))
                part = (jnp.exp(jnp.where(ok, gap, -1e30)) * scores[lo:hi, :hi]).astype(bf16)
                if hi < rows:
                    part = jnp.concatenate([part, jnp.zeros((STRIP, rows - hi), bf16)], axis=1)
                parts.append(part)
            weights.append(jnp.concatenate(parts, axis=0))
        tiles.append(dot(jnp.concatenate(weights, axis=1), jnp.concatenate(masked, axis=0)))
        if pair == heads // per // 2 - 1:
            between()
    inside = jnp.concatenate(tiles, axis=1)
    cum = info[:, CUM : CUM + 8]
    end = info[rows - 1 : rows]
    start = state[...]
    starts_out[at] = start.astype(bf16)
    grown = spread(jnp.exp(info), CUM, heads, head_dim)
    result = inside + grown * dot(c_proj, start.astype(bf16)) + gains[1:2] * x
    fade = spread(jnp.exp(end - info), CUM, heads, head_dim)
    state[...] = start * spread(jnp.exp(end), CUM, heads, head_dim) + dot_tn(b_proj, (stepped * fade).astype(bf16))
    ssm_out[...] = result
    z = gate[...]
    gated = result * (z * sigmoid(z))
    d_normed = dot_nt(cot[...], out_proj[...])
    d_normed_out[...] = d_normed.astype(bf16)
    scaled = gated * gains[0:1]
    partial_out[...] = dot(scaled.astype(bf16), out_proj[...]).astype(bf16)
    squares = jnp.sum(gated * gated, axis=1, keepdims=True)
    cross = jnp.sum(d_normed * scaled, axis=1, keepdims=True)
    turned = jnp.where(lane == 0, squares, cross).T
    sums_out[0, pl.ds(at, 1)] = turned[0:1]
    sums_out[1, pl.ds(at, 1)] = turned[1:2]


def gate_step(heads, head_dim, state_dim, all_channels, at,
              ssm, gate, d_normed, sums, conv_out, heads_in, cot, gains,
              d_ssm_out, d_gate_out, grad_out, rows_out, total_out):
    rows = ssm.shape[0]
    inner = heads * head_dim

    @pl.when(at == 0)
    def _():
        grad_out[...] = jnp.zeros_like(grad_out)
        rows_out[...] = jnp.zeros_like(rows_out)
        total_out[...] = jnp.zeros_like(total_out)

    tall = jnp.concatenate([sums[0, pl.ds(at, 1)], sums[1, pl.ds(at, 1)], jnp.zeros((126, rows), f32)], axis=0).T
    inv = lax.rsqrt(tall[:, 0:1] / all_channels + epsilon)
    cross = tall[:, 1:2] / all_channels
    z = gate[...]
    s = sigmoid(z)
    y = ssm[...]
    gated = y * (z * s)
    gain = gains[0:1]
    back = d_normed[...].astype(f32)
    unit = gated * inv
    d_gated = inv * (back * gain - unit * (inv * cross))
    grad_out[:, : cot.shape[1]] += dot_tn((unit * gain).astype(bf16), cot[...])
    d_ssm = d_gated * (z * s)
    d_ssm_out[...] = d_ssm
    d_gate_out[...] = (d_gated * y * (s * (1.0 + z * (1.0 - s)))).astype(bf16)
    values = conv_out[...]
    active = values * sigmoid(values)
    rows_out[0:1] += jnp.sum(back * unit, axis=0, keepdims=True)
    rows_out[1:2] += jnp.sum(d_ssm * active[:, :inner], axis=0, keepdims=True)
    c_proj = active[:, inner + state_dim :].astype(bf16)
    grown = spread(jnp.exp(heads_in[...]), DEV, heads, head_dim)
    total_out[...] += dot_tn(c_proj, (grown * d_ssm).astype(bf16))


def back_step(heads, head_dim, state_dim, first_step, last_step,
              d_ssm, conv_out, conv_in, heads_in, start, entering, conv_w, params, skip, conv_halo,
              d_conv_in_out, d_step_out, conv_grads, head_grads, halo_out,
              lam, later, later_info, between):
    rows = d_ssm.shape[0]
    inner = heads * head_dim
    per = 128 // head_dim

    @pl.when(first_step)
    def _():
        lam[...] = entering[...]
        conv_grads[...] = jnp.zeros_like(conv_grads)
        head_grads[...] = jnp.zeros_like(head_grads)
        for each in (later, later_info):
            each[rows:] = jnp.zeros((8, each.shape[1]), f32)

    values = conv_out[...]
    gates = sigmoid(values)
    active = values * gates
    x = active[:, :inner]
    b_proj = active[:, inner : inner + state_dim].astype(bf16)
    c_proj = active[:, inner + state_dim :].astype(bf16)
    info = heads_in[...]
    flipped = info.T
    step = spread(info, STEP, heads, head_dim)
    stepped = x * step
    low = stepped.astype(bf16)
    dy = d_ssm[...]
    dy_low = dy.astype(bf16)
    scores = dot_nt(b_proj, c_proj)
    lane = lax.broadcasted_iota(jnp.int32, (rows, 128), 1)
    lane_one = lax.broadcasted_iota(jnp.int32, (STRIP, 128), 1)
    cuts = strips(rows)
    d_scores = [jnp.zeros((STRIP, rows - lo), f32) for lo, _ in cuts]
    d_rows = []
    d_cols = [jnp.zeros((STRIP, 128), f32) for _ in cuts]
    tiles = []
    for pair in range(heads // per):
        tile = low[:, pair * 128 : (pair + 1) * 128]
        dy_tile = dy_low[:, pair * 128 : (pair + 1) * 128]
        owns = [(lane >= k * head_dim) & (lane < (k + 1) * head_dim) for k in range(per)]
        stacked = jnp.concatenate([jnp.where(own, tile, jnp.zeros_like(tile)) for own in owns], axis=0)
        all_pairs = dot_nt(stacked, dy_tile)
        weights = []
        for k in range(per):
            head = pair * per + k
            row_total = jnp.zeros((1, rows), f32)
            parts = []
            for n, (lo, hi) in enumerate(cuts):
                gap = flipped[CUM + head : CUM + head + 1, lo:] - info[lo:hi, CUM + head : CUM + head + 1]
                ok = (lax.broadcasted_iota(jnp.int32, (STRIP, rows - lo), 1)
                      >= lax.broadcasted_iota(jnp.int32, (STRIP, rows - lo), 0))
                decay = jnp.exp(jnp.where(ok, gap, -1e30))
                weight = decay * scores[lo:hi, lo:]
                part = weight.astype(bf16)
                if lo:
                    part = jnp.concatenate([jnp.zeros((STRIP, lo), bf16), part], axis=1)
                parts.append(part)
                pairs = all_pairs[k * rows + lo : k * rows + hi, lo:]
                d_scores[n] = d_scores[n] + pairs * decay
                moved = pairs * weight
                d_cols[n] = d_cols[n] - jnp.where(lane_one == head, jnp.sum(moved, axis=1, keepdims=True), 0.0)
                col = jnp.sum(moved, axis=0, keepdims=True)
                if lo:
                    col = jnp.concatenate([jnp.zeros((1, lo), f32), col], axis=1)
                row_total = row_total + col
            weights.append(jnp.concatenate(parts, axis=0))
            d_rows.append(row_total)
        dy_stack = jnp.concatenate([jnp.where(own, dy_tile, jnp.zeros_like(dy_tile)) for own in owns], axis=0)
        tiles.append(dot(jnp.concatenate(weights, axis=1), dy_stack))
        if pair < BACK_POINTS - 1:
            between(pair + 1)
    d_stepped = jnp.concatenate(tiles, axis=1)
    d_cum = jnp.concatenate(d_cols, axis=0)
    d_cum = d_cum + jnp.concatenate(d_rows + [jnp.zeros((128 - heads, rows), f32)], axis=0).T
    full = jnp.concatenate(
        [jnp.concatenate([jnp.zeros((STRIP, lo), f32), part], axis=1) if lo else part
         for part, (lo, _) in zip(d_scores, cuts)], axis=0).astype(bf16)
    d_b = dot(full, c_proj)
    d_c = dot_tn(full, b_proj)

    group_ones = (lax.broadcasted_iota(jnp.int32, (inner, 128), 0) // head_dim
                  == lax.broadcasted_iota(jnp.int32, (inner, 128), 1)).astype(bf16)
    after = lam[...]
    after_low = after.astype(bf16)
    end = info[rows - 1 : rows]
    grown = spread(jnp.exp(info), CUM, heads, head_dim)
    fade = spread(jnp.exp(end - info), CUM, heads, head_dim)
    end_grown = spread(jnp.exp(end), CUM, heads, head_dim)
    from_after = fade * dot(b_proj, after_low)
    d_stepped = d_stepped + from_after
    grown_dy = grown * dy
    grown_low = grown_dy.astype(bf16)
    left = stepped * from_after
    to_cum = head_sum(grown_dy * dot(c_proj, start) - left, group_ones)
    kept = jnp.sum(after * start.astype(f32), axis=0, keepdims=True) * end_grown
    kept = kept + jnp.sum(left, axis=0, keepdims=True)
    last = head_sum(jnp.broadcast_to(kept, (8, inner)), group_ones)[0:1]
    row_id = lax.broadcasted_iota(jnp.int32, (rows, 128), 0)
    d_cum = d_cum + to_cum + jnp.where(row_id == rows - 1, last, 0.0)
    d_c = d_c + dot_nt(grown_low, start)
    d_b = d_b + dot_nt((fade * stepped).astype(bf16), after_low)
    lam[...] = end_grown * after + dot_tn(c_proj, grown_low)
    d_step = dot((d_stepped * x).astype(bf16), group_ones)
    d_x = step * d_stepped + skip[0:1] * dy

    order_r = lax.broadcasted_iota(jnp.int32, (rows, rows), 0)
    order_c = lax.broadcasted_iota(jnp.int32, (rows, rows), 1)
    d_decay = exact_left((order_r <= order_c).astype(bf16), d_cum) * info[:, KEEP : KEEP + 1]
    rate = params[1:2]
    real = lane < heads
    step_raw = jnp.where(real, info, 0.0) + params[0:1]
    slope = sigmoid(step_raw)
    d_pre = jnp.where(real, (d_step + d_decay * rate) * slope, 0.0)
    d_step_out[...] = d_pre.astype(bf16)
    head_grads[0:1] += jnp.sum(d_pre, axis=0, keepdims=True)
    head_grads[1:2] += jnp.sum(jnp.where(real, d_decay * softplus(step_raw) * rate, 0.0), axis=0, keepdims=True)

    d_active = jnp.concatenate([d_x, d_b, d_c], axis=1)
    d_conv = d_active * (gates * (1.0 + values * (1.0 - gates)))
    taken = conv_in[...].astype(f32)
    total = d_conv * conv_w[0:1]
    conv_grads[0:1] += jnp.sum(d_conv * taken, axis=0, keepdims=True)
    conv_grads[4:5] += jnp.sum(d_conv, axis=0, keepdims=True)
    later[0:rows] = d_conv
    later_info[0:rows] = info
    for j in range(1, 4):
        moved = later[pl.ds(j, rows)] * later_info[pl.ds(j, rows)][:, KEEP + j - 1 : KEEP + j]
        total = total + moved * conv_w[j : j + 1]
        conv_grads[j : j + 1] += jnp.sum(moved * taken, axis=0, keepdims=True)
    d_conv_in_out[...] = total.astype(bf16)

    @pl.when(last_step)
    def _():
        ahead = conv_halo[...].astype(f32)
        halo_out[...] = jnp.zeros_like(halo_out)
        for j in range(1, 4):
            first = later[0:8] * later_info[0:8, KEEP + j - 1 : KEEP + j]
            for t in range(j):
                row = 16 + t - j
                conv_grads[j : j + 1] += first[t : t + 1] * ahead[row : row + 1]
                halo_out[row - 8 : row - 7] += first[t : t + 1] * conv_w[j : j + 1]
    for each in (later, later_info):
        each[rows:] = each[0:8]


def block_place(per, blocks):
    def place(n, b):
        if n == 0:
            return b
        late = b - (per - 1)
        group = blocks // per - 2 - late // per
        rest = jnp.where(b == blocks - 1, blocks - 1, group * per + lax.rem(late, per))
        return jnp.where(b < per - 1, blocks - per + b, rest)
    return place


def layer_kernel(heads, head_dim, state_dim, all_channels, count, block, lag, plans, cuts, owners, taps,
                 conv_out, conv_in, heads_in, gate, cot, normed, last_normed, out_proj, gains, entering, decay,
                 conv_w, params, conv_halo, zx, weights, gain, tail_mask,
                 mixed_out, d_normed_out, sums_out, zx_out, op_out, bc_out, small_out,
                 own, got, total, held, ssm, d_normed, starts, state, leaving, later, later_info,
                 sums, sum_slots, lead, fade,
                 scan_got, scan_got_fade, scan_sent, scan_sent_fade, scan_sems,
                 grad, sum_own, sum_pair, sum_mine, sum_slot, sum_theirs, sum_sems, grad_bc,
                 bc_slots, bc_z, bc_res, small, small_slots, small_own, small_z,
                 d_conv, d_step, gate_rows, conv_grads, head_grads, halo_rows, landed,
                 line_sems, swap_sems, bc_sems, bcz_sems, small_sems, smallz_sems, row_sems, free_sem):
    at = pl.program_id(0)
    rows, width = cot.shape
    inner = heads * head_dim
    bc_width = 2 * state_dim
    seq, head_count = lax.axis_size("seq"), lax.axis_size("head")
    me, my_head = lax.axis_index("seq"), lax.axis_index("head")
    per = rows // block
    line = LineSum(own, got, total, (mixed_out, d_normed_out), block_place(per, count * per), line_sems, block)
    swap = Swap("head", sums, sum_slots, swap_sems)
    scan = DeviceScan(True, state, fade, lead, leaving, scan_got, scan_got_fade, scan_sent, scan_sent_fade,
                      scan_sems)
    op_rows = max(16, inner // seq)
    sum_refs = (sum_own, sum_pair, sum_mine, sum_slot, sum_theirs)
    op_sum = PairedSum(*(ref.at[:, : op_rows * (2 if ref is sum_own else 1), :width] for ref in sum_refs),
                       sum_sems.at[0])
    zx_sum = PairedSum(*(ref.at[:, :, : 2 * inner] for ref in sum_refs), sum_sems.at[1])
    small_swap = Swap("seq", small, small_slots, small_sems)
    both_swap = Swap("head", small_own, small_z, smallz_sems)
    row_copy = pltpu.make_async_remote_copy(
        src_ref=halo_rows, dst_ref=landed, send_sem=row_sems.at[0], recv_sem=row_sems.at[1],
        device_id={"seq": lax.rem(me + seq - 1, seq)}, device_id_type=MESH)
    served, sent = plans
    back_at = at - 2 * count - 1
    last_step = back_at == count - 1

    def serve(phase, k):
        line.send(*sent.span(phase, k))
        line.serve(*served.span(phase, k), lag)

    @pl.when(at == 0)
    def _():
        greet("head", "seq")
        state[...] = entering[...]

    @pl.when(at < count)
    def _():
        mine = pl.ds(pl.multiple_of(at * rows, rows), rows)
        serve(0, MIX_POINTS * at)
        mix_step(heads, head_dim, state_dim, at, conv_out, heads_in, gate, cot, out_proj, gains, entering,
                 ssm.at[mine], d_normed.at[mine], own.at[mine], sums, starts, state,
                 lambda: serve(0, MIX_POINTS * at + 1))

    @pl.when(at == count - 1)
    def _():
        swap.start()

    @pl.when((at >= count) & (at < 2 * count))
    def _():
        serve(1, at - count)

    @pl.when(at == count)
    def _():
        swap.wait()
        sums_out[...] = swap.total()
        swap.finish()
        grad[...] = jnp.zeros_like(grad)
        gate_rows[...] = jnp.zeros_like(gate_rows)
        state[...] = jnp.zeros_like(state)

    @pl.when((at >= count) & (at < 2 * count))
    def _():
        here = at - count
        mine = pl.ds(pl.multiple_of(here * rows, rows), rows)
        gate_step(heads, head_dim, state_dim, all_channels, here,
                  ssm.at[mine], gate, d_normed.at[mine], sums_out, conv_out, heads_in, cot, gains,
                  ssm.at[mine], d_normed.at[mine], grad.at[:inner], gate_rows, state)

    @pl.when(at == 2 * count)
    def _():
        for k in range(seq // 2):
            lo, hi = min(inner, k * 2 * op_rows), min(inner, (k + 1) * 2 * op_rows)
            if hi > lo:
                sum_own[k, : hi - lo, :width] = grad[lo:hi, :width].astype(bf16)
        scan.begin(decay[...])
        scan.run(lambda k: serve(2, k))
        op_sum.swap()
        grad[...] = jnp.zeros_like(grad)
        grad_bc[...] = jnp.zeros_like(grad_bc)
        small[...] = jnp.zeros_like(small)

    def project(block_low, gate_low, conv_low, rest_low):
        d_rows = dot_nt(conv_low, zx[:, inner:]) + dot(rest_low, weights[...])
        grad[:, inner : 2 * inner] += dot_tn(block_low, conv_low)
        if gate_low is not None:
            d_rows = d_rows + dot_nt(gate_low, zx[:, :inner])
            grad[:, :inner] += dot_tn(block_low, gate_low)
        grad_bc[...] += dot_tn(rest_low, block_low).reshape(grad_bc.shape)
        small[16:17] += jnp.sum(d_rows * block_low.astype(f32), axis=0, keepdims=True) / gain[...]
        return d_rows

    @pl.when(at > 2 * count)
    def _():
        here = 3 * count - at
        mine = pl.ds(pl.multiple_of(here * rows, rows), rows)
        serve(3, BACK_POINTS * back_at)
        back_step(heads, head_dim, state_dim, back_at == 0, last_step,
                  ssm.at[mine], conv_out, conv_in, heads_in, starts[here], leaving, conv_w, params,
                  gains[1:2], conv_halo, d_conv, d_step, conv_grads, head_grads, halo_rows,
                  state, later, later_info, lambda k: serve(3, BACK_POINTS * back_at + k))

        @pl.when(last_step)
        def _():
            row_copy.start()
        rest_low = jnp.concatenate([d_conv[:, inner:], d_step[...]], axis=1)
        d_rows = project(normed[...], d_normed[mine], d_conv[:, :inner], rest_low).astype(bf16)

        @pl.when(back_at == 0)
        def _():
            own[: rows - block] = d_rows[: rows - block]
            held[...] = d_rows[rows - block :]

        @pl.when(back_at > 0)
        def _():
            start = pl.multiple_of(back_at * rows - block, block)
            own[pl.ds(start, rows)] = d_rows

    @pl.when(back_at == 1)
    def _():
        op_sum.scatter()

    @pl.when(back_at == 3)
    def _():
        op_sum.gather()

    @pl.when(back_at == 5)
    def _():
        op_sum.back()

    piece = grad_bc.shape[1] // owners

    def bc_scatter(to, source):
        return pltpu.make_async_remote_copy(
            src_ref=grad_bc.at[:head_count, pl.ds(pl.multiple_of(to * piece, piece), piece)],
            dst_ref=bc_slots.at[source], send_sem=bc_sems.at[0, to], recv_sem=bc_sems.at[1, source],
            device_id={"seq": to}, device_id_type=MESH)

    def bc_gather(owner, to):
        rows = pl.ds(pl.multiple_of(owner * piece, piece), piece)
        return pltpu.make_async_remote_copy(
            src_ref=bc_res.at[rows], dst_ref=bc_res.at[rows],
            send_sem=bc_sems.at[2, to], recv_sem=bc_sems.at[3, owner],
            device_id={"seq": to}, device_id_type=MESH)

    def bc_swap(to, source):
        return pltpu.make_async_remote_copy(
            src_ref=bc_slots.at[me, to], dst_ref=bc_z.at[source],
            send_sem=bcz_sems.at[0, to], recv_sem=bcz_sems.at[1, source],
            device_id={"head": to}, device_id_type=MESH)

    @pl.when(last_step)
    def _():
        op_sum.finish(op_out)
        op_sum.release(free_sem)
        at_block = [served.count(3, plans[0].phases[3][0] - 1), sent.count(3, plans[0].phases[3][0] - 1)]

        def go(until):
            ahead = max(at_block[1], min(line.count, until + 2))
            line.send(at_block[1], ahead)
            line.serve(at_block[0], until, lag)
            at_block[:] = [until, ahead]
        go(cuts[0])
        row_copy.wait()
        extra = jnp.where(me < seq - 1, landed[...] * tail_mask[8:, 0:1], 0.0)
        extra = jnp.concatenate([jnp.zeros_like(extra), extra], axis=0).astype(bf16)
        extra_rest = jnp.concatenate([extra[:, inner:], jnp.zeros((16, 128), bf16)], axis=1)
        more = project(last_normed[...], None, extra[:, :inner], extra_rest)
        final = held[...].astype(f32) + jnp.concatenate([jnp.zeros((block - 16, width), f32), more], axis=0)
        own[count * rows - block :] = final.astype(bf16)

        pair_rows = sum_own.shape[1]
        for k in range(sum_own.shape[0]):
            sum_own[k, :, : 2 * inner] = grad[k * pair_rows : (k + 1) * pair_rows, : 2 * inner].astype(bf16)
        pl.semaphore_wait(free_sem, 1)
        zx_sum.swap()
        small[0:8] += grad_bc[head_count, 0:8]
        small[8 : 9 + taps, :inner] = conv_grads[: taps + 1, :inner]
        small[8:10, inner : 2 * inner] = gate_rows[0:2]
        small[10:12, inner : inner + 128] = head_grads[0:2]
        small[17 : 18 + taps, :bc_width] = conv_grads[: taps + 1, inner:]
        small_swap.start()

        @pl.loop(1, seq)
        def _(k):
            to = other_of("seq", k)

            @pl.when(to < owners)
            def _():
                bc_scatter(to, me).start()

        go(cuts[1])
        zx_sum.scatter()
        go(cuts[2])
        small_swap.wait()
        sums_small = small_swap.total()
        lone = small.shape[0] - small_own.shape[0]
        small_out[:lone] = sums_small[:lone]
        small_own[...] = sums_small[lone:]
        both_swap.start()

        @pl.when(me < owners)
        def _():
            @pl.loop(1, seq)
            def _(k):
                bc_scatter(me, other_of("seq", k)).wait_recv()
            bc_slots[me] = grad_bc[:head_count, pl.ds(pl.multiple_of(me * piece, piece), piece)]
            sums_bc = bc_slots[0]
            for k in range(1, seq):
                sums_bc = sums_bc + bc_slots[k]
            bc_slots[me] = sums_bc
            bc_z[my_head] = bc_slots[me, my_head]

            @pl.loop(1, head_count)
            def _(k):
                bc_swap(other_of("head", k), my_head).start()

        go(cuts[3])
        zx_sum.gather()
        both_swap.wait()
        small_out[lone:] = both_swap.total()

        @pl.when(me < owners)
        def _():
            @pl.loop(1, head_count)
            def _(k):
                bc_swap(my_head, other_of("head", k)).wait_recv()
            sums_bc = bc_z[0]
            for k in range(1, head_count):
                sums_bc = sums_bc + bc_z[k]
            bc_res[pl.ds(pl.multiple_of(me * piece, piece), piece)] = sums_bc

            @pl.loop(1, seq)
            def _(k):
                bc_gather(me, other_of("seq", k)).start()

        go(cuts[4])
        zx_sum.back()
        go(cuts[5])
        zx_sum.finish(zx_out)
        go(line.count + lag)
        line.finish()
        small_swap.finish()
        both_swap.finish()

        @pl.loop(1, seq)
        def _(k):
            other = other_of("seq", k)

            @pl.when(other < owners)
            def _():
                bc_gather(other, me).wait_recv()
                bc_scatter(other, me).wait_send()

            @pl.when(me < owners)
            def _():
                bc_gather(me, other).wait_send()
        bc_out[...] = bc_res[...]

        @pl.when(me < owners)
        def _():
            @pl.loop(1, head_count)
            def _(k):
                bc_swap(other_of("head", k), my_head).wait_send()


def layer(conv_out, conv_in, heads_in, gate, cot, normed, out_proj, gains, entering, decay, conv_w, params,
          conv_halo, zx, weights, gain, tail_mask, heads, head_dim, state_dim, all_channels, taps):
    length, conv = conv_out.shape
    count = length // GROUP
    inner = heads * head_dim
    width = cot.shape[1]
    seq, head_count = lax.axis_size("seq"), lax.axis_size("head")
    block = BLOCK
    pace = PACE * block // 64
    blocks = length // block
    per = GROUP // block
    lag = max(2, head_count // 2)
    back_points = min(BACK_POINTS, inner // 128)
    gate_at = MIX * count + SWAP
    scan_at = gate_at + GATE * count
    back_start = scan_at + SCAN
    rounds = seq.bit_length() - 1
    phases = [(MIX_POINTS * count, 0, MIX // MIX_POINTS), (count, gate_at, GATE),
              (rounds, scan_at, SCAN // rounds), (back_points * count, back_start, BACK // back_points)]
    served = Pace(phases, pace, LATE, 2 * blocks + lag)
    sent = Pace(phases, pace, EARLY, 2 * blocks)
    for k in range(count):
        point = (k + 1) * back_points - 1
        assert served.count(3, point) >= min(blocks, (k + 1) * per) + lag
        assert sent.count(3, point) >= min(blocks, (k + 1) * per) + LineSum.AHEAD
        for each in (served, sent):
            assert each.count(3, point) <= blocks + max(0, k * per - 1)
    cuts = [2 * blocks - (blocks * (32 - cut)) // 32 for cut in CUTS]

    def by(cols, first, step):
        def index(g):
            ahead = jnp.where(g < count, g, jnp.where(g < 2 * count, g - count, jnp.minimum(3 * count - g, count - 1)))
            if first == 2:
                ahead = jnp.where(g < 2 * count, count - 1, ahead)
            if step == 1:
                ahead = jnp.where(g < 2 * count, ahead, count - 1)
            return (ahead, 0)
        return pl.BlockSpec((GROUP, cols), index)
    shape = jax.ShapeDtypeStruct
    state, fade = (state_dim, inner), (8, inner)
    bc_rows = (conv - inner) // head_count
    owners = min(seq, bc_rows // 8)
    piece = bc_rows // owners
    vm = pltpu.VMEM
    grad_rows = max(width, inner)
    paired = PairedSum.scratch(width, max(width, 2 * inner))
    return pl.pallas_call(
        functools.partial(layer_kernel, heads, head_dim, state_dim, all_channels, count, block, lag,
                          (served, sent), cuts, owners, taps),
        grid=(3 * count + 1,),
        out_shape=(shape((length, width), bf16), shape((length, width), bf16), shape((2, count, GROUP), f32),
                   shape((width, 2 * inner), bf16), shape((inner, width), bf16), shape((bc_rows, width), f32),
                   shape((24, width), f32)),
        in_specs=[by(conv, 0, 2), by(conv, 2, 2), by(128, 0, 2), by(inner, 0, 1), by(width, 0, 1),
                  by(width, 2, 2), pl.BlockSpec((16, width), lambda g: (length // 16 - 1, 0))] + [VMEM] * 11,
        out_specs=(HBM, HBM) + (VMEM,) * 5,
        scratch_shapes=[
            vm((length, width), bf16), vm((length, width), bf16), vm((2 * length, width), bf16),
            vm((block, width), bf16), vm((length, inner), f32), vm((length, inner), bf16),
            vm((count,) + state, bf16), vm(state, f32), vm(state, f32)]
        + [vm((GROUP + 8, conv), f32), vm((GROUP + 8, 128), f32)]
        + [vm((2, count, GROUP), f32), vm((head_count, 2, count, GROUP), f32)]
        + DeviceScan.scratch(state, fade)
        + [vm((grad_rows, max(width, 2 * inner)), f32)] + paired[:-1] + [DMA((2,) + (6, seq // 2))]
        + [vm(((conv - inner + 128) // bc_rows, bc_rows, width), f32),
           vm((seq, head_count, piece, width), f32), vm((head_count, piece, width), f32),
           vm((bc_rows, width), f32), vm((24, width), f32), vm((seq, 24, width), f32),
           vm((8, width), f32), vm((head_count, 8, width), f32),
           vm((GROUP, conv), bf16), vm((GROUP, 128), bf16), vm((8, inner), f32), vm((8, conv), f32),
           vm((8, 128), f32), vm((8, conv), f32), vm((8, conv), f32),
           LineSum.sems(length, block), DMA((2, head_count)), DMA((4, seq)), DMA((2, head_count)),
           DMA((2, seq)), DMA((2, head_count)), DMA((2,)), pltpu.SemaphoreType.REGULAR],
        compiler_params=pltpu.CompilerParams(
            dimension_semantics=("arbitrary",), collective_id=4, has_side_effects=True,
            vmem_limit_bytes=LAYER_LIMIT),
        name="layer",
    )(conv_out, conv_in, heads_in, gate, cot, normed, normed, out_proj, gains, entering, decay, conv_w, params,
      conv_halo, zx, weights, gain, tail_mask)


PACE = 29
MIX, SWAP, GATE, SCAN, BACK = 27, 30, 20, 100, 82
MIX_POINTS, BACK_POINTS = 2, 4
EARLY, LATE = 25, 60
BLOCK = 64
CUTS = (8, 13, 18, 23, 28, 31)
LAYER_LIMIT = 63 * 2**20


def finish_kernel(heads, head_dim, all_channels, taps,
                  tokens, cot, mixed, d_normed, sums, gain, zx, op, bc, small,
                  mixed_out, tokens_out, zx_out, op_out, bc_out, dt_out, gain_out, conv_w_out, conv_b_out,
                  bc_w_out, bc_b_out, bias_out, rate_out, skip_out, norm_out):
    at = pl.program_id(0)
    rows = tokens.shape[0]
    inner = heads * head_dim
    value = tokens[...].astype(f32)
    tall = jnp.concatenate([sums[0, pl.ds(at, 1)], jnp.zeros((127, rows), f32)], axis=0).T
    inv_rms = lax.rsqrt(tall[:, 0:1] / all_channels + epsilon)
    mixed_out[...] = (value + mixed[...].astype(f32) * inv_rms).astype(bf16)
    inv = lax.rsqrt(jnp.mean(value * value, axis=1, keepdims=True) + epsilon)
    xhat = value * inv
    scaled = d_normed[...].astype(f32) * gain[...]
    tokens_out[...] = cot[...].astype(f32) + inv * (
        scaled - xhat * jnp.mean(scaled * xhat, axis=1, keepdims=True))
    sums_zx = zx[...].astype(f32)
    zx_out[:, 0, :] = sums_zx[:, :inner]
    zx_out[:, 1, :] = sums_zx[:, inner:]
    op_out[...] = op[...].astype(f32)
    @pl.when(at == 0)
    def _():
        bc_out[...] = bc[...]
        dt_out[...] = small[0:heads]
        gain_out[...] = small[16:17]
        conv_w_out[...] = small[8 : 8 + taps, :inner]
        conv_b_out[...] = small[8 + taps : 9 + taps, :inner]
        bias_out[...] = small[10:11, inner : inner + heads]
        rate_out[...] = small[11:12, inner : inner + heads]
        norm_out[...] = small[8:9, inner : 2 * inner]
        group_ones = (lax.broadcasted_iota(jnp.int32, (inner, 128), 0) // head_dim
                      == lax.broadcasted_iota(jnp.int32, (inner, 128), 1)).astype(bf16)
        skips = jnp.broadcast_to(small[9:10, inner : 2 * inner], (8, inner))
        total = sum(dot(part, group_ones) for part in split3(skips))
        skip_out[...] = total[0:1, :heads]
        part = bc_w_out.shape[1]
        mine_bc = small[17 : 18 + taps, : part * lax.axis_size("head")]
        chosen = mine_bc[:, :part]
        for k in range(1, lax.axis_size("head")):
            chosen = jnp.where(lax.axis_index("head") == k, mine_bc[:, k * part : (k + 1) * part], chosen)
        bc_w_out[...] = chosen[:taps]
        bc_b_out[...] = chosen[taps : taps + 1]


def finish(tokens, cot, mixed, d_normed, sums, gain, zx, op, bc, small, heads, head_dim, taps):
    length, width = tokens.shape
    count = length // GROUP
    inner = heads * head_dim
    part = bc.shape[0]

    def by(rows, cols):
        return pl.BlockSpec((rows, cols), lambda g: (g, 0))
    shape = jax.ShapeDtypeStruct
    tall = by(GROUP, width)
    lone = [(1, width), (taps, inner), (1, inner), (taps, part), (1, part), (1, heads), (1, heads), (1, heads),
            (1, inner)]
    cols = width // count
    return pl.pallas_call(
        functools.partial(finish_kernel, heads, head_dim, inner * lax.axis_size("head"), taps),
        grid=(count,),
        out_shape=(shape((length, width), bf16), shape((length, width), f32), shape((width, 2, inner), f32),
                   shape((inner, width), f32), shape((part, width), f32), shape((heads, width), f32))
        + tuple(shape(each, f32) for each in lone),
        in_specs=[tall] * 4 + [VMEM, VMEM, by(cols, 2 * inner), by(inner // count, width),
                               VMEM, VMEM],
        out_specs=(tall, tall, pl.BlockSpec((cols, 2, inner), lambda g: (g, 0, 0)), by(inner // count, width),
                   VMEM, VMEM) + (VMEM,) * len(lone),
        compiler_params=pltpu.CompilerParams(dimension_semantics=("arbitrary",), vmem_limit_bytes=LIMIT),
        name="finish",
    )(tokens, cot, mixed, d_normed, sums, gain, zx, op, bc, small)


def shards(
    tokens, start_flags, in_gain, proj_zx, proj_bc, proj_dt, conv_x_weight, conv_x_bias,
    conv_bc_weight, conv_bc_bias, dt_bias, a_log, skip_scale, norm_gain, out_proj, cotangent,
):
    length, width = tokens.shape
    heads = a_log.shape[0]
    inner = proj_zx.shape[2]
    head_dim = inner // heads
    taps = conv_x_weight.shape[0]
    head_count = lax.axis_size("head")
    bc_part = conv_bc_bias.shape[0]
    bc_width = bc_part * head_count
    state_dim = bc_width // 2
    zx = proj_zx.reshape(width, 2 * inner)
    gain = in_gain[None]
    (normed, gate, conv_in, conv_out, info, entering, decay, conv_halo, weights, conv_w, params, gains,
     tail_mask) = front(
        tokens, zx, start_flags.reshape(length // 128, 128), gain, proj_bc.T, proj_dt.T, conv_x_weight,
        conv_x_bias[None], conv_bc_weight, conv_bc_bias[None], dt_bias[None], a_log[None], skip_scale[None],
        norm_gain[None], heads, head_dim, state_dim)
    all_channels = inner * head_count
    mixed, d_normed, sums, zx_sum, op_sum, bc_sum, small_sum = layer(
        conv_out, conv_in, info, gate, cotangent, normed, out_proj, gains, entering, decay, conv_w, params,
        conv_halo, zx, weights, gain, tail_mask, heads, head_dim, state_dim, all_channels, taps)
    (mixed_out, grad_tokens, grad_zx, grad_op, grad_bc, grad_dt, grad_gain, grad_conv_w, grad_conv_b,
     grad_bc_w, grad_bc_b, grad_bias, grad_rate, grad_skip, grad_norm) = finish(
        tokens, cotangent, mixed, d_normed, sums, gain, zx_sum, op_sum, bc_sum, small_sum, heads, head_dim, taps)
    return (
        mixed_out, grad_tokens, grad_gain[0], grad_zx, grad_bc.T, grad_dt.T, grad_conv_w, grad_conv_b[0],
        grad_bc_w, grad_bc_b[0], grad_bias[0], grad_rate[0], grad_skip[0], grad_norm[0], grad_op,
    )


def solution(mesh):
    in_specs = (
        P("seq", None),
        P("seq"),
        P(),
        P(None, None, "head"),
        P(None, "head"),
        P(None, "head"),
        P(None, "head"),
        P("head"),
        P(None, "head"),
        P("head"),
        P("head"),
        P("head"),
        P("head"),
        P("head"),
        P("head", None),
        P("seq", None),
    )
    out_specs = (
        P("seq", None),
        P("seq", None),
        P(),
        P(None, None, "head"),
        P(None, "head"),
        P(None, "head"),
        P(None, "head"),
        P("head"),
        P(None, "head"),
        P("head"),
        P("head"),
        P("head"),
        P("head"),
        P("head"),
        P("head", None),
    )
    return jax.shard_map(shards, mesh=mesh, in_specs=in_specs, out_specs=out_specs, check_vma=False)
```

```python
import functools

import jax
import jax.numpy as jnp
from jax import lax
from jax.experimental import pallas as pl
from jax.experimental.pallas import tpu as pltpu
from jax.sharding import PartitionSpec as P

MESH = pl.DeviceIdType.MESH
f32 = jnp.float32
bf16 = jnp.bfloat16
VMEM = pl.BlockSpec(memory_space=pltpu.VMEM)
HBM = pl.BlockSpec(memory_space=pl.ANY)
DMA = pltpu.SemaphoreType.DMA


def rows_of(ref, start, size):
    return ref.at[pl.ds(pl.multiple_of(start, size), size)]


def other_of(axis, k):
    size = lax.axis_size(axis)
    return lax.rem(lax.axis_index(axis) + k, size)


def greet(*axes):
    barrier = pltpu.get_barrier_semaphore()
    count = 0
    for axis in axes:
        size = lax.axis_size(axis)
        count += size - 1

        @pl.loop(1, size)
        def _(k):
            pl.semaphore_signal(barrier, inc=1, device_id={axis: other_of(axis, k)}, device_id_type=MESH)
    pl.semaphore_wait(barrier, count)


class Pace:
    def __init__(self, phases, pace, behind, most):
        self.phases, self.pace, self.behind, self.most = phases, pace, behind, most
        self.before = [0]
        for n, (points, _, _) in enumerate(phases):
            self.before.append(self.count(n, points - 1) if points else self.before[-1])

    def count(self, phase, k):
        _, start, step = self.phases[phase]
        low, top = self.before[phase], self.most
        value = (start + k * step - self.behind) // self.pace
        if isinstance(value, int):
            return max(low, min(top, value))
        return jnp.clip(value, low, top)

    def span(self, phase, k):
        if isinstance(k, int):
            return (self.count(phase, k - 1) if k else self.before[phase]), self.count(phase, k)
        return jnp.where(k == 0, self.before[phase], self.count(phase, k - 1)), self.count(phase, k)


class LineSum:
    AHEAD = 3

    def __init__(self, own, got, total, outs, place, sems, block):
        self.own, self.got, self.total, self.outs, self.place = own, got, total, outs, place
        self.send1, self.got_in, self.got_total, self.send2, self.stored = (sems.at[i] for i in range(5))
        self.block = block
        self.half = own.shape[0] // block
        self.count = 2 * self.half
        size, me = lax.axis_size("head"), lax.axis_index("head")
        left = me < size // 2
        self.mid = (me == size // 2 - 1) | (me == size // 2)
        self.has_outer = (me > 0) & (me < size - 1)
        self.inner = jnp.where(left, me + 1, me - 1)
        self.outer = jnp.clip(jnp.where(left, me - 1, me + 1), 0, size - 1)

    @staticmethod
    def sems(rows, block):
        return DMA((5, 2 * rows // block))

    def rows(self, b):
        return pl.ds(pl.multiple_of(b * self.block, self.block), self.block)

    def slot(self, b):
        return self.rows(lax.rem(b, self.half))

    def in_copy(self, b, to):
        return pltpu.make_async_remote_copy(
            src_ref=self.own.at[self.slot(b)], dst_ref=self.got.at[self.slot(b)],
            send_sem=self.send1.at[b], recv_sem=self.got_in.at[b], device_id={"head": to}, device_id_type=MESH)

    def cross_copy(self, b):
        return pltpu.make_async_remote_copy(
            src_ref=self.own.at[self.slot(b)], dst_ref=self.total.at[self.rows(b)],
            send_sem=self.send1.at[b], recv_sem=self.got_total.at[b],
            device_id={"head": self.inner}, device_id_type=MESH)

    def out_copy(self, b, to):
        return pltpu.make_async_remote_copy(
            src_ref=self.total.at[self.rows(b)], dst_ref=self.total.at[self.rows(b)],
            send_sem=self.send2.at[b], recv_sem=self.got_total.at[b],
            device_id={"head": to}, device_id_type=MESH)

    def store(self, b, do):
        for n, out in enumerate(self.outs):
            @pl.when(b // self.half == n)
            def _():
                do(pltpu.make_async_copy(self.total.at[self.rows(b)],
                                         out.at[self.rows(self.place(n, lax.rem(b, self.half)))],
                                         self.stored.at[b]))

    def inward(self, b):
        rows = self.slot(b)
        self.in_copy(b, self.outer).wait_recv()
        self.own[rows] = self.got[rows] + self.own[rows]

        @pl.when(self.mid)
        def _():
            self.cross_copy(b).start()

        @pl.when(jnp.logical_not(self.mid))
        def _():
            self.in_copy(b, self.inner).start()

    def outward(self, b):
        rows = self.rows(b)
        self.cross_copy(b).wait_recv()

        @pl.when(self.has_outer)
        def _():
            self.cross_copy(b).wait_send()

        @pl.when(self.mid)
        def _():
            self.total[rows] = self.own[self.slot(b)] + self.total[rows]

        @pl.when(self.has_outer)
        def _():
            self.out_copy(b, self.outer).start()
        self.store(b, lambda copy: copy.start())

    def serve(self, first, last, lag):
        @pl.when(self.has_outer)
        def _():
            @pl.loop(first, last)
            def _(b):
                @pl.when(b < self.count)
                def _():
                    self.inward(b)

                @pl.when(b >= lag)
                def _():
                    self.outward(b - lag)

    def send(self, first, last):
        @pl.when(jnp.logical_not(self.has_outer))
        def _():
            @pl.loop(first, last)
            def _(b):
                @pl.when(b >= self.AHEAD)
                def _():
                    self.in_copy(b - self.AHEAD, self.inner).wait_send()

                @pl.when(b >= self.half)
                def _():
                    self.outward(b - self.half)
                self.in_copy(b, self.inner).start()

    def finish(self):
        @pl.when(jnp.logical_not(self.has_outer))
        def _():
            pl.loop(self.half, self.count)(self.outward)

            @pl.loop(self.count - self.AHEAD, self.count)
            def _(b):
                self.in_copy(b, self.inner).wait_send()

        @pl.loop(0, self.count)
        def _(b):
            self.store(b, lambda copy: copy.wait())

            @pl.when(self.has_outer)
            def _():
                self.out_copy(b, self.outer).wait_send()


class PairedSum:
    def __init__(self, own, pair, mine, slots, theirs, sems):
        self.own, self.pair, self.mine, self.slots, self.theirs = own, pair, mine, slots, theirs
        self.sems = sems
        self.me = lax.axis_index("seq")
        self.chip, self.odd = self.me // 2, lax.rem(self.me, 2)
        self.partner = self.me + 1 - 2 * self.odd
        self.chips, self.piece = own.shape[0], own.shape[1] // 2

    @staticmethod
    def scratch(rows, width):
        seq = lax.axis_size("seq")
        piece = max(16, rows // seq)
        part = pltpu.VMEM((seq // 2, piece, width), bf16)
        return [pltpu.VMEM((seq // 2, 2 * piece, width), bf16)] + [part] * 4 + [DMA((6, seq // 2))]

    def half(self, odd):
        return pl.ds(pl.multiple_of(odd * self.piece, self.piece), self.piece)

    def swap_copy(self):
        return pltpu.make_async_remote_copy(
            src_ref=self.own.at[:, self.half(1 - self.odd)], dst_ref=self.pair,
            send_sem=self.sems.at[0, 0], recv_sem=self.sems.at[1, 0],
            device_id={"seq": self.partner}, device_id_type=MESH)

    def back_copy(self):
        return pltpu.make_async_remote_copy(
            src_ref=self.pair, dst_ref=self.theirs,
            send_sem=self.sems.at[0, 1], recv_sem=self.sems.at[1, 1],
            device_id={"seq": self.partner}, device_id_type=MESH)

    def scatter_copy(self, to, source):
        return pltpu.make_async_remote_copy(
            src_ref=self.mine.at[to], dst_ref=self.slots.at[source],
            send_sem=self.sems.at[2, to], recv_sem=self.sems.at[3, source],
            device_id={"seq": 2 * to + self.odd}, device_id_type=MESH)

    def gather_copy(self, owner, to):
        return pltpu.make_async_remote_copy(
            src_ref=self.pair.at[owner], dst_ref=self.pair.at[owner],
            send_sem=self.sems.at[4, to], recv_sem=self.sems.at[5, owner],
            device_id={"seq": 2 * to + self.odd}, device_id_type=MESH)

    def release(self, free):
        pl.semaphore_signal(free, inc=1, device_id={"seq": self.partner}, device_id_type=MESH)

    def others(self, do):
        @pl.loop(1, self.chips)
        def _(k):
            do(lax.rem(self.chip + k, self.chips))

    def swap(self):
        self.swap_copy().start()

    def scatter(self):
        self.swap_copy().wait()
        self.mine[...] = (self.own[:, self.half(self.odd)].astype(f32) + self.pair[...].astype(f32)).astype(bf16)
        self.others(lambda other: self.scatter_copy(other, self.chip).start())

    def gather(self):
        self.others(lambda other: self.scatter_copy(self.chip, other).wait_recv())
        self.others(lambda other: self.scatter_copy(other, self.chip).wait_send())
        self.slots[self.chip] = self.mine[self.chip]
        total = self.slots[0].astype(f32)
        for k in range(1, self.chips):
            total = total + self.slots[k].astype(f32)
        self.pair[self.chip] = total.astype(bf16)
        self.others(lambda other: self.gather_copy(self.chip, other).start())

    def back(self):
        self.others(lambda other: self.gather_copy(other, self.chip).wait_recv())
        self.back_copy().start()

    def finish(self, out):
        self.back_copy().wait()
        self.others(lambda other: self.gather_copy(self.chip, other).wait_send())
        for k in range(min(self.chips, out.shape[0] // (2 * self.piece))):
            for odd, ref in ((self.odd, self.pair), (1 - self.odd, self.theirs)):
                start = pl.multiple_of((2 * k + odd) * self.piece, self.piece)
                out[pl.ds(start, self.piece)] = ref[k]


class Swap:
    def __init__(self, axis, own, slots, sems):
        self.axis, self.own, self.slots = axis, own, slots
        self.send, self.got = sems.at[0], sems.at[1]
        self.size, self.me = lax.axis_size(axis), lax.axis_index(axis)

    def copy(self, to, source):
        return pltpu.make_async_remote_copy(
            src_ref=self.own, dst_ref=self.slots.at[source],
            send_sem=self.send.at[to], recv_sem=self.got.at[source],
            device_id={self.axis: to}, device_id_type=MESH)

    def start(self):
        @pl.loop(1, self.size)
        def _(k):
            self.copy(other_of(self.axis, k), self.me).start()
        self.slots[self.me] = self.own[...]

    def wait(self):
        @pl.loop(1, self.size)
        def _(k):
            self.copy(self.me, other_of(self.axis, k)).wait_recv()

    def total(self):
        out = self.slots[0]
        for k in range(1, self.size):
            out = out + self.slots[k]
        return out

    def finish(self):
        @pl.loop(1, self.size)
        def _(k):
            self.copy(other_of(self.axis, k), self.me).wait_send()


class DeviceScan:
    def __init__(self, backward, total, fade, lead, out, got, got_fade, sent, sent_fade, sems):
        self.backward, self.total, self.fade, self.lead, self.out = backward, total, fade, lead, out
        self.got, self.got_fade, self.sent, self.sent_fade, self.sems = got, got_fade, sent, sent_fade, sems
        self.me = lax.axis_index("seq")
        self.rounds = lax.axis_size("seq").bit_length() - 1

    @staticmethod
    def scratch(state, fade):
        rounds = lax.axis_size("seq").bit_length() - 1
        return [pltpu.VMEM(fade, f32), pltpu.VMEM(fade, f32)] + [
            pltpu.VMEM((rounds,) + state, bf16), pltpu.VMEM((rounds,) + fade, f32)] * 2 + [DMA((4, rounds))]

    def copies(self, k):
        return [
            pltpu.make_async_remote_copy(
                src_ref=src.at[k], dst_ref=dst.at[k],
                send_sem=self.sems.at[i, k], recv_sem=self.sems.at[i + 1, k],
                device_id={"seq": jnp.bitwise_xor(self.me, 1 << k)}, device_id_type=MESH)
            for src, dst, i in ((self.sent, self.got, 0), (self.sent_fade, self.got_fade, 2))]

    def begin(self, decay):
        self.fade[...] = decay
        self.out[...] = jnp.zeros_like(self.out)
        self.lead[...] = jnp.ones_like(self.lead)

    def start(self, k):
        self.sent[k] = self.total[...].astype(bf16)
        self.sent_fade[k] = self.fade[...]
        for copy in self.copies(k):
            copy.start()

    def finish(self, k):
        for copy in self.copies(k):
            copy.wait()
        later = lax.rem(self.me // (1 << k), 2) == (0 if self.backward else 1)

        @pl.when(later)
        def _():
            theirs = self.got[k].astype(f32)
            self.out[...] = self.out[...] + self.lead[0:1] * theirs
            self.total[...] = self.total[...] + self.fade[0:1] * theirs
            self.lead[...] = self.lead[...] * self.got_fade[k]

        @pl.when(jnp.logical_not(later))
        def _():
            self.total[...] = self.got[k].astype(f32) + self.got_fade[k, 0:1] * self.total[...]
        self.fade[...] = self.fade[...] * self.got_fade[k]

    def run(self, between=None):
        for k in range(self.rounds):
            self.start(k)
            if between is not None:
                between(k)
            self.finish(k)


GROUP = 256
STRIP = 128
GAP = 200.0
epsilon = 1e-05
LIMIT = 56 * 2**20


def dot(a, b):
    return jnp.dot(a, b, preferred_element_type=f32)


def dot_nt(a, b):
    return lax.dot_general(a, b, (((1,), (1,)), ((), ())), preferred_element_type=f32)


def dot_tn(a, b):
    return lax.dot_general(a, b, (((0,), (0,)), ((), ())), preferred_element_type=f32)


def split3(v):
    one = v.astype(bf16)
    rest = v - one.astype(f32)
    two = rest.astype(bf16)
    return one, two, (rest - two.astype(f32)).astype(bf16)


def exact_left(ones, v):
    width = v.shape[1]
    out = dot(ones, jnp.concatenate(split3(v), axis=1))
    return out[:, :width] + out[:, width : 2 * width] + out[:, 2 * width :]


def head_sum(v, group_ones):
    high = v.astype(bf16)
    low = (v - high.astype(f32)).astype(bf16)
    return dot(high, group_ones) + dot(low, group_ones)


def sigmoid(v):
    return 1.0 / (1.0 + jnp.exp(-v))


def softplus(v):
    return jnp.maximum(v, 0.0) + jnp.log1p(jnp.exp(-jnp.abs(v)))


def spread(cols, first, heads, head_dim):
    rows = cols.shape[0]
    per = 128 // head_dim
    lane = lax.broadcasted_iota(jnp.int32, (rows, 128), 1)
    tiles = []
    for at in range(0, heads, per):
        tile = cols[:, first + at : first + at + 1]
        for k in range(1, per):
            tile = jnp.where(lane < k * head_dim, tile, cols[:, first + at + k : first + at + k + 1])
        tiles.append(jnp.broadcast_to(tile, (rows, 128)))
    return jnp.concatenate(tiles, axis=1)


def norm_rows(block, gain):
    value = block.astype(f32)
    inv = lax.rsqrt(jnp.mean(value * value, axis=1, keepdims=True) + epsilon)
    return (value * inv * gain).astype(bf16)


def whole(shape):
    return pl.BlockSpec(shape, lambda g: (0,) * len(shape))


def lane_groups(rows, *parts):
    lane = lax.broadcasted_iota(jnp.int32, (rows, 128), 1)
    out = parts[-1]
    for k in range(len(parts) - 2, -1, -1):
        out = jnp.where(lane < 8 * (k + 1), parts[k], out)
    return out


RAW, STEP, CUM, DEV, KEEP = 0, 8, 16, 24, 32


def head_lanes(row, heads, lane):
    out = jnp.zeros(lane.shape, f32)
    for k in range(heads):
        out = jnp.where(lane % 8 == k, row[:, k : k + 1], out)
    return out


def front_kernel(heads, head_dim, state_dim, count,
                 tokens, last_tokens, zx, flags, gain, proj_bc, proj_dt, conv_x_weight, conv_x_bias,
                 conv_bc_weight, conv_bc_bias, dt_bias, a_log, skip, norm_gain,
                 normed_out, x_in_out, x_conv_out, bc_in_out, bc_conv_out, heads_out, entering, decay_out,
                 halo_out, weights_out, conv_w_out, params, gains_out, mask_out,
                 normed, x_active, tail_rows, landed, head_low, proj_all, conv_bc, conv_all, flag_cols, flag_ext,
                 x_ext, bc_ext, state, running, lead, fade,
                 scan_got, scan_got_fade, scan_sent, scan_sent_fade, scan_sems, proj_sems, conv_sems, row_sems):
    at = pl.program_id(0)
    rows = tokens.shape[0]
    inner = heads * head_dim
    bc_width = 2 * state_dim
    bc_part = proj_bc.shape[0]
    seq, me = lax.axis_size("seq"), lax.axis_index("seq")
    block = lax.rem(at, count)
    mine = pl.ds(pl.multiple_of(block * rows, rows), rows)
    swaps = [Swap("head", proj_bc, proj_all, proj_sems), Swap("head", conv_bc, conv_all, conv_sems)]
    row_copy = pltpu.make_async_remote_copy(
        src_ref=tail_rows, dst_ref=landed, send_sem=row_sems.at[0], recv_sem=row_sems.at[1],
        device_id={"seq": lax.rem(me + 1, seq)}, device_id_type=MESH)
    lane_row = lax.broadcasted_iota(jnp.int32, (1, 128), 1)

    @pl.when(at == 0)
    def _():
        final = 1.0 - flags[flags.shape[0] - 1 :].astype(f32)
        one, two = final[:, 127:128], final[:, 126:127]
        row = lax.broadcasted_iota(jnp.int32, (16, 128), 0)
        mask = jnp.where(row == 15, 1.0, jnp.where(row == 14, one, jnp.where(row == 13, one * two, 0.0)))
        mask_out[...] = mask
        tail_rows[...] = (last_tokens[...].astype(f32) * mask[:, 0:1]).astype(bf16)
        conv_bc[...] = jnp.zeros_like(conv_bc)
        conv_bc[0:4, :bc_part] = conv_bc_weight[...].astype(f32)
        conv_bc[4:5, :bc_part] = conv_bc_bias[...]
        greet("head", "seq")
        row_copy.start()
        for each in swaps:
            each.start()
        params[...] = jnp.zeros_like(params)
        params[0:1] = head_lanes(dt_bias[...], heads, lane_row)
        params[1:2] = -jnp.exp(head_lanes(a_log[...], heads, lane_row))
        gains_out[...] = jnp.zeros_like(gains_out)
        gains_out[0:1] = norm_gain[...]
        gains_out[1:2] = spread(head_lanes(skip[...], heads, lane_row), 0, heads, head_dim)
        flat = flags[...].astype(f32)
        turned = jnp.concatenate([flat, jnp.zeros((128 - flat.shape[0], 128), f32)], axis=0).T
        conv_w_out[...] = jnp.zeros_like(conv_w_out)
        conv_w_out[0:4, :inner] = conv_x_weight[...].astype(f32)
        conv_w_out[4:5, :inner] = conv_x_bias[...]
        for k in range(flat.shape[0]):
            flag_cols[k * 128 : (k + 1) * 128] = jnp.broadcast_to(turned[:, k : k + 1], (128, 128))
        flag_ext[0:8] = jnp.zeros((8, 128), f32)

    def keeps(flag):
        flag_ext[8:] = flag
        one = 1.0 - flag
        two = one * (1.0 - flag_ext[7 : 7 + rows])
        three = two * (1.0 - flag_ext[6 : 6 + rows])
        flag_ext[0:8] = flag_ext[rows:]
        return one, two, three

    def convolve(ext, current, keep, first, last):
        ext[8:] = current
        total = conv_w_out[4:5, first:last] + conv_w_out[0:1, first:last] * current
        for j in range(1, 4):
            total = total + conv_w_out[j : j + 1, first:last] * ext[pl.ds(8 - j, rows)] * keep[j - 1][:, 0:1]
        ext[0:8] = ext[rows:]
        return total

    @pl.when(at < count)
    def _():
        low = norm_rows(tokens[...], gain[...])
        normed[mine] = low
        normed_out[...] = low
        x_in = dot(low, zx[:, inner:]).astype(bf16)
        x_in_out[...] = x_in

        @pl.when(at == 0)
        def _():
            row_copy.wait()
            head_low[...] = norm_rows(landed[...], gain[...])
            ahead = jnp.where(me > 0, dot(head_low[...], zx[:, inner:]), 0.0).astype(bf16)
            halo_out[:, :inner] = ahead
            x_ext[0:8] = ahead[8:].astype(f32)
        total = convolve(x_ext, x_in.astype(f32), keeps(flag_cols[mine]), 0, inner)
        x_conv_out[...] = total
        x_active[mine] = total * sigmoid(total)

    @pl.when(at == count)
    def _():
        for each in swaps:
            each.wait()
            each.finish()
        heads_there = proj_all.shape[0]
        for k in range(heads_there):
            weights_out[k * bc_part : (k + 1) * bc_part] = proj_all[k]
        eight = jnp.concatenate([proj_dt[...].astype(f32)] + (
            [jnp.zeros((8 - heads, proj_dt.shape[1]), f32)] if heads < 8 else []), axis=0)
        weights_out[bc_width:] = jnp.concatenate([eight] * 16, axis=0).astype(bf16)
        conv_w_out[:, inner:] = jnp.concatenate([conv_all[k, :, :bc_part] for k in range(heads_there)], axis=1)
        ahead = jnp.where(me > 0, dot_nt(head_low[...], weights_out[:bc_width]), 0.0).astype(bf16)
        halo_out[:, inner:] = ahead
        bc_ext[0:8] = ahead[8:].astype(f32)
        state[...] = jnp.zeros_like(state)
        running[...] = jnp.zeros_like(running)
        flag_ext[0:8] = jnp.zeros((8, 128), f32)

    @pl.when(at >= count)
    def _():
        raw = dot_nt(normed[mine], weights_out[...])
        bc_in = raw[:, :bc_width].astype(bf16)
        bc_in_out[...] = bc_in
        flag = flag_cols[mine]
        keep = keeps(flag)
        total = convolve(bc_ext, bc_in.astype(f32), keep, inner, inner + bc_width)
        bc_conv_out[...] = total
        b_proj = (total[:, :state_dim] * sigmoid(total[:, :state_dim])).astype(bf16)

        step_raw = raw[:, bc_width:]
        step = softplus(step_raw + params[0:1])
        log_decay = step * params[1:2] - GAP * flag
        order_r = lax.broadcasted_iota(jnp.int32, (rows, rows), 0)
        order_c = lax.broadcasted_iota(jnp.int32, (rows, rows), 1)
        cum = exact_left((order_r >= order_c).astype(bf16), log_decay)
        lane = lax.broadcasted_iota(jnp.int32, (rows, 128), 1)
        kept = jnp.where(lane < KEEP + 1, keep[0], jnp.where(lane < KEEP + 2, keep[1], keep[2]))
        heads_out[...] = lane_groups(rows, step_raw, step, cum, cum + running[0:1], kept)
        end = cum[rows - 1 : rows]
        running[...] = running[...] + end
        weight = step * jnp.exp(end - cum)
        scaled = (x_active[mine] * spread(weight, 0, heads, head_dim)).astype(bf16)
        state[...] = state[...] * spread(jnp.exp(end), 0, heads, head_dim) + dot_tn(b_proj, scaled)

    @pl.when(at == 2 * count - 1)
    def _():
        decay = spread(jnp.exp(running[...]), 0, heads, head_dim)
        decay_out[...] = decay
        scan = DeviceScan(False, state, fade, lead, entering, scan_got, scan_got_fade, scan_sent,
                          scan_sent_fade, scan_sems)
        scan.begin(decay)
        scan.run()


def front(tokens, zx, flags, gain, proj_bc, proj_dt, conv_x_weight, conv_x_bias, conv_bc_weight, conv_bc_bias,
          dt_bias, a_log, skip, norm_gain, heads, head_dim, state_dim):
    length, width = tokens.shape
    count = length // GROUP
    inner = heads * head_dim
    conv = inner + 2 * state_dim
    head_count = lax.axis_size("head")

    def early(cols):
        return pl.BlockSpec((GROUP, cols), lambda g: (jnp.minimum(g, count - 1), 0))

    def late(cols):
        return pl.BlockSpec((GROUP, cols), lambda g: (jnp.maximum(g - count, 0), 0))
    shape = jax.ShapeDtypeStruct
    state, fade = (state_dim, inner), (8, inner)
    rest = 2 * state_dim + 128
    return pl.pallas_call(
        functools.partial(front_kernel, heads, head_dim, state_dim, count),
        grid=(2 * count,),
        out_shape=(shape((length, width), bf16), shape((length, inner), bf16), shape((length, inner), f32),
                   shape((length, conv - inner), bf16), shape((length, conv - inner), f32),
                   shape((length, 128), f32), shape(state, f32),
                   shape(fade, f32), shape((16, conv), bf16), shape((rest, width), bf16),
                   shape((8, conv), f32), shape((8, 128), f32), shape((8, inner), f32), shape((16, 128), f32)),
        in_specs=[early(width), pl.BlockSpec((16, width), lambda g: (length // 16 - 1, 0))] + [VMEM] * 13,
        out_specs=(early(width), early(inner), early(inner), late(conv - inner), late(conv - inner), late(128))
        + (VMEM,) * 8,
        scratch_shapes=[
            pltpu.VMEM((length, width), bf16), pltpu.VMEM((length, inner), f32),
            pltpu.VMEM((16, width), bf16), pltpu.VMEM((16, width), bf16), pltpu.VMEM((16, width), bf16),
            pltpu.VMEM((head_count,) + proj_bc.shape, bf16), pltpu.VMEM((8, 128), f32),
            pltpu.VMEM((head_count, 8, 128), f32), pltpu.VMEM((length, 128), f32),
            pltpu.VMEM((GROUP + 8, 128), f32), pltpu.VMEM((GROUP + 8, inner), f32),
            pltpu.VMEM((GROUP + 8, conv - inner), f32), pltpu.VMEM(state, f32), pltpu.VMEM((8, 128), f32)]
        + DeviceScan.scratch(state, fade) + [DMA((2, head_count)), DMA((2, head_count)), DMA((2,))],
        compiler_params=pltpu.CompilerParams(
            dimension_semantics=("arbitrary",), collective_id=3, has_side_effects=True,
            vmem_limit_bytes=LIMIT),
        name="front",
    )(tokens, tokens, zx, flags, gain, proj_bc, proj_dt, conv_x_weight, conv_x_bias, conv_bc_weight,
      conv_bc_bias, dt_bias, a_log, skip, norm_gain)


def strips(rows):
    return [(lo, lo + STRIP) for lo in range(0, rows, STRIP)]


def mix_step(heads, head_dim, state_dim, at,
             x_conv, bc_conv, heads_in, normed, zx, cot, out_proj, gains, entering,
             ssm_out, d_normed_out, partial_out, sums_out, starts_out, state, between):
    rows = x_conv.shape[0]
    inner = heads * head_dim
    per = 128 // head_dim

    @pl.when(at == 0)
    def _():
        state[...] = entering[...]

    values = jnp.concatenate([x_conv[...], bc_conv[...]], axis=1)
    active = values * sigmoid(values)
    x = active[:, :inner]
    b_proj = active[:, inner : inner + state_dim].astype(bf16)
    c_proj = active[:, inner + state_dim :].astype(bf16)
    info = heads_in[...]
    flipped = info.T
    stepped = x * spread(info, STEP, heads, head_dim)
    low = stepped.astype(bf16)
    scores = dot_nt(c_proj, b_proj)
    lane = lax.broadcasted_iota(jnp.int32, (rows, 128), 1)
    tiles = []
    for pair in range(heads // per):
        tile = low[:, pair * 128 : (pair + 1) * 128]
        weights, masked = [], []
        for k in range(per):
            head = pair * per + k
            masked.append(jnp.where((lane >= k * head_dim) & (lane < (k + 1) * head_dim), tile,
                                    jnp.zeros_like(tile)))
            parts = []
            for lo, hi in strips(rows):
                gap = info[lo:hi, CUM + head : CUM + head + 1] - flipped[CUM + head : CUM + head + 1, :hi]
                ok = (lax.broadcasted_iota(jnp.int32, (STRIP, hi), 0) + lo
                      >= lax.broadcasted_iota(jnp.int32, (STRIP, hi), 1))
                part = (jnp.exp(jnp.where(ok, gap, -1e30)) * scores[lo:hi, :hi]).astype(bf16)
                if hi < rows:
                    part = jnp.concatenate([part, jnp.zeros((STRIP, rows - hi), bf16)], axis=1)
                parts.append(part)
            weights.append(jnp.concatenate(parts, axis=0))
        tiles.append(dot(jnp.concatenate(weights, axis=1), jnp.concatenate(masked, axis=0)))
        if pair == heads // per // 2 - 1:
            between()
    inside = jnp.concatenate(tiles, axis=1)
    cum = info[:, CUM : CUM + 8]
    end = info[rows - 1 : rows]
    start = state[...]
    starts_out[at] = start.astype(bf16)
    grown = spread(jnp.exp(info), CUM, heads, head_dim)
    result = inside + grown * dot(c_proj, start.astype(bf16)) + gains[1:2] * x
    fade = spread(jnp.exp(end - info), CUM, heads, head_dim)
    state[...] = start * spread(jnp.exp(end), CUM, heads, head_dim) + dot_tn(b_proj, (stepped * fade).astype(bf16))
    ssm_out[...] = result
    z = dot(normed[...], zx[:, :inner])
    gated = result * (z * sigmoid(z))
    d_normed = dot_nt(cot[...], out_proj[...])
    d_normed_out[...] = d_normed.astype(bf16)
    scaled = gated * gains[0:1]
    partial_out[...] = dot(scaled.astype(bf16), out_proj[...]).astype(bf16)
    squares = jnp.sum(gated * gated, axis=1, keepdims=True)
    cross = jnp.sum(d_normed * scaled, axis=1, keepdims=True)
    turned = jnp.where(lane == 0, squares, cross).T
    sums_out[0, pl.ds(at, 1)] = turned[0:1]
    sums_out[1, pl.ds(at, 1)] = turned[1:2]


def gate_step(heads, head_dim, state_dim, all_channels, at,
              ssm, d_normed, sums, x_conv, bc_conv, heads_in, normed, zx, cot, gains,
              d_ssm_out, d_gate_out, grad_out, rows_out, total_out):
    rows = ssm.shape[0]
    inner = heads * head_dim

    @pl.when(at == 0)
    def _():
        grad_out[...] = jnp.zeros_like(grad_out)
        rows_out[...] = jnp.zeros_like(rows_out)
        total_out[...] = jnp.zeros_like(total_out)

    tall = jnp.concatenate([sums[0, pl.ds(at, 1)], sums[1, pl.ds(at, 1)], jnp.zeros((126, rows), f32)], axis=0).T
    inv = lax.rsqrt(tall[:, 0:1] / all_channels + epsilon)
    cross = tall[:, 1:2] / all_channels
    z = dot(normed[...], zx[:, :inner])
    s = sigmoid(z)
    y = ssm[...]
    gated = y * (z * s)
    gain = gains[0:1]
    back = d_normed[...].astype(f32)
    unit = gated * inv
    d_gated = inv * (back * gain - unit * (inv * cross))
    grad_out[:, : cot.shape[1]] += dot_tn((unit * gain).astype(bf16), cot[...])
    d_ssm = d_gated * (z * s)
    d_ssm_out[...] = d_ssm
    d_gate_out[...] = (d_gated * y * (s * (1.0 + z * (1.0 - s)))).astype(bf16)
    x_values, c_values = x_conv[...], bc_conv[:, state_dim:]
    rows_out[0:1] += jnp.sum(back * unit, axis=0, keepdims=True)
    rows_out[1:2] += jnp.sum(d_ssm * (x_values * sigmoid(x_values)), axis=0, keepdims=True)
    c_proj = (c_values * sigmoid(c_values)).astype(bf16)
    grown = spread(jnp.exp(heads_in[...]), DEV, heads, head_dim)
    total_out[...] += dot_tn(c_proj, (grown * d_ssm).astype(bf16))


def back_step(heads, head_dim, state_dim, first_step, last_step,
              d_ssm, x_conv, bc_conv, x_in, bc_in, heads_in, start, entering, conv_w, params, skip, conv_halo,
              d_conv_in_out, d_step_out, conv_grads, head_grads, halo_out,
              lam, later, later_info, between):
    rows = d_ssm.shape[0]
    inner = heads * head_dim
    per = 128 // head_dim

    @pl.when(first_step)
    def _():
        lam[...] = entering[...]
        conv_grads[...] = jnp.zeros_like(conv_grads)
        head_grads[...] = jnp.zeros_like(head_grads)
        for each in (later, later_info):
            each[rows:] = jnp.zeros((8, each.shape[1]), f32)

    values = jnp.concatenate([x_conv[...], bc_conv[...]], axis=1)
    gates = sigmoid(values)
    active = values * gates
    x = active[:, :inner]
    b_proj = active[:, inner : inner + state_dim].astype(bf16)
    c_proj = active[:, inner + state_dim :].astype(bf16)
    info = heads_in[...]
    flipped = info.T
    step = spread(info, STEP, heads, head_dim)
    stepped = x * step
    low = stepped.astype(bf16)
    dy = d_ssm[...]
    dy_low = dy.astype(bf16)
    scores = dot_nt(b_proj, c_proj)
    lane = lax.broadcasted_iota(jnp.int32, (rows, 128), 1)
    lane_one = lax.broadcasted_iota(jnp.int32, (STRIP, 128), 1)
    cuts = strips(rows)
    d_scores = [jnp.zeros((STRIP, rows - lo), f32) for lo, _ in cuts]
    d_rows = []
    d_cols = [jnp.zeros((STRIP, 128), f32) for _ in cuts]
    tiles = []
    for pair in range(heads // per):
        tile = low[:, pair * 128 : (pair + 1) * 128]
        dy_tile = dy_low[:, pair * 128 : (pair + 1) * 128]
        owns = [(lane >= k * head_dim) & (lane < (k + 1) * head_dim) for k in range(per)]
        stacked = jnp.concatenate([jnp.where(own, tile, jnp.zeros_like(tile)) for own in owns], axis=0)
        all_pairs = dot_nt(stacked, dy_tile)
        weights = []
        for k in range(per):
            head = pair * per + k
            row_total = jnp.zeros((1, rows), f32)
            parts = []
            for n, (lo, hi) in enumerate(cuts):
                gap = flipped[CUM + head : CUM + head + 1, lo:] - info[lo:hi, CUM + head : CUM + head + 1]
                ok = (lax.broadcasted_iota(jnp.int32, (STRIP, rows - lo), 1)
                      >= lax.broadcasted_iota(jnp.int32, (STRIP, rows - lo), 0))
                decay = jnp.exp(jnp.where(ok, gap, -1e30))
                weight = decay * scores[lo:hi, lo:]
                part = weight.astype(bf16)
                if lo:
                    part = jnp.concatenate([jnp.zeros((STRIP, lo), bf16), part], axis=1)
                parts.append(part)
                pairs = all_pairs[k * rows + lo : k * rows + hi, lo:]
                d_scores[n] = d_scores[n] + pairs * decay
                moved = pairs * weight
                d_cols[n] = d_cols[n] - jnp.where(lane_one == head, jnp.sum(moved, axis=1, keepdims=True), 0.0)
                col = jnp.sum(moved, axis=0, keepdims=True)
                if lo:
                    col = jnp.concatenate([jnp.zeros((1, lo), f32), col], axis=1)
                row_total = row_total + col
            weights.append(jnp.concatenate(parts, axis=0))
            d_rows.append(row_total)
        dy_stack = jnp.concatenate([jnp.where(own, dy_tile, jnp.zeros_like(dy_tile)) for own in owns], axis=0)
        tiles.append(dot(jnp.concatenate(weights, axis=1), dy_stack))
        between(pair + 1)
    d_stepped = jnp.concatenate(tiles, axis=1)
    d_cum = jnp.concatenate(d_cols, axis=0)
    d_cum = d_cum + jnp.concatenate(d_rows + [jnp.zeros((128 - heads, rows), f32)], axis=0).T
    full = jnp.concatenate(
        [jnp.concatenate([jnp.zeros((STRIP, lo), f32), part], axis=1) if lo else part
         for part, (lo, _) in zip(d_scores, cuts)], axis=0).astype(bf16)
    d_b = dot(full, c_proj)
    d_c = dot_tn(full, b_proj)

    group_ones = (lax.broadcasted_iota(jnp.int32, (inner, 128), 0) // head_dim
                  == lax.broadcasted_iota(jnp.int32, (inner, 128), 1)).astype(bf16)
    after = lam[...]
    after_low = after.astype(bf16)
    end = info[rows - 1 : rows]
    grown = spread(jnp.exp(info), CUM, heads, head_dim)
    fade = spread(jnp.exp(end - info), CUM, heads, head_dim)
    end_grown = spread(jnp.exp(end), CUM, heads, head_dim)
    from_after = fade * dot(b_proj, after_low)
    d_stepped = d_stepped + from_after
    grown_dy = grown * dy
    grown_low = grown_dy.astype(bf16)
    left = stepped * from_after
    to_cum = head_sum(grown_dy * dot(c_proj, start) - left, group_ones)
    kept = jnp.sum(after * start.astype(f32), axis=0, keepdims=True) * end_grown
    kept = kept + jnp.sum(left, axis=0, keepdims=True)
    last = head_sum(jnp.broadcast_to(kept, (8, inner)), group_ones)[0:1]
    row_id = lax.broadcasted_iota(jnp.int32, (rows, 128), 0)
    d_cum = d_cum + to_cum + jnp.where(row_id == rows - 1, last, 0.0)
    d_c = d_c + dot_nt(grown_low, start)
    d_b = d_b + dot_nt((fade * stepped).astype(bf16), after_low)
    lam[...] = end_grown * after + dot_tn(c_proj, grown_low)
    d_step = dot((d_stepped * x).astype(bf16), group_ones)
    d_x = step * d_stepped + skip[0:1] * dy
    between(heads // per + 1)

    order_r = lax.broadcasted_iota(jnp.int32, (rows, rows), 0)
    order_c = lax.broadcasted_iota(jnp.int32, (rows, rows), 1)
    d_decay = exact_left((order_r <= order_c).astype(bf16), d_cum) * info[:, KEEP : KEEP + 1]
    rate = params[1:2]
    real = lane < heads
    step_raw = jnp.where(real, info, 0.0) + params[0:1]
    slope = sigmoid(step_raw)
    d_pre = jnp.where(real, (d_step + d_decay * rate) * slope, 0.0)
    d_step_out[...] = d_pre.astype(bf16)
    head_grads[0:1] += jnp.sum(d_pre, axis=0, keepdims=True)
    head_grads[1:2] += jnp.sum(jnp.where(real, d_decay * softplus(step_raw) * rate, 0.0), axis=0, keepdims=True)

    d_active = jnp.concatenate([d_x, d_b, d_c], axis=1)
    d_conv = d_active * (gates * (1.0 + values * (1.0 - gates)))
    taken = jnp.concatenate([x_in[...], bc_in[...]], axis=1).astype(f32)
    total = d_conv * conv_w[0:1]
    conv_grads[0:1] += jnp.sum(d_conv * taken, axis=0, keepdims=True)
    conv_grads[4:5] += jnp.sum(d_conv, axis=0, keepdims=True)
    later[0:rows] = d_conv
    later_info[0:rows] = info
    for j in range(1, 4):
        moved = later[pl.ds(j, rows)] * later_info[pl.ds(j, rows)][:, KEEP + j - 1 : KEEP + j]
        total = total + moved * conv_w[j : j + 1]
        conv_grads[j : j + 1] += jnp.sum(moved * taken, axis=0, keepdims=True)
    d_conv_in_out[...] = total.astype(bf16)

    @pl.when(last_step)
    def _():
        ahead = conv_halo[...].astype(f32)
        halo_out[...] = jnp.zeros_like(halo_out)
        for j in range(1, 4):
            first = later[0:8] * later_info[0:8, KEEP + j - 1 : KEEP + j]
            for t in range(j):
                row = 16 + t - j
                conv_grads[j : j + 1] += first[t : t + 1] * ahead[row : row + 1]
                halo_out[row - 8 : row - 7] += first[t : t + 1] * conv_w[j : j + 1]
    for each in (later, later_info):
        each[rows:] = each[0:8]


def block_place(per, blocks):
    def place(n, b):
        if n == 0:
            return b
        late = b - (per - 1)
        group = blocks // per - 2 - late // per
        rest = jnp.where(b == blocks - 1, blocks - 1, group * per + lax.rem(late, per))
        return jnp.where(b < per - 1, blocks - per + b, rest)
    return place


def layer_kernel(heads, head_dim, state_dim, all_channels, count, block, lag, plans, steps, owners, taps,
                 x_conv, bc_conv, x_in, bc_in, heads_in, cot, normed, last_normed, out_proj, gains, entering, decay,
                 conv_w, params, conv_halo, zx, weights, gain, tail_mask,
                 mixed_out, d_normed_out, sums_out, zx_out, op_out, bc_out, small_out,
                 own, got, total, held, ssm, d_normed, starts, state, leaving, later, later_info,
                 sums, sum_slots, lead, fade,
                 scan_got, scan_got_fade, scan_sent, scan_sent_fade, scan_sems,
                 grad, sum_own, sum_pair, sum_mine, sum_slot, sum_theirs, sum_sems, grad_bc,
                 bc_slots, bc_z, bc_res, small, small_slots, small_own, small_z,
                 d_conv, d_step, gate_rows, conv_grads, head_grads, halo_rows, landed,
                 line_sems, swap_sems, bc_sems, bcz_sems, small_sems, smallz_sems, row_sems, free_sem):
    at = pl.program_id(0)
    rows, width = cot.shape
    inner = heads * head_dim
    bc_width = 2 * state_dim
    seq, head_count = lax.axis_size("seq"), lax.axis_size("head")
    me, my_head = lax.axis_index("seq"), lax.axis_index("head")
    per = rows // block
    line = LineSum(own, got, total, (mixed_out, d_normed_out), block_place(per, count * per), line_sems, block)
    swap = Swap("head", sums, sum_slots, swap_sems)
    scan = DeviceScan(True, state, fade, lead, leaving, scan_got, scan_got_fade, scan_sent, scan_sent_fade,
                      scan_sems)
    op_rows = max(16, inner // seq)
    sum_refs = (sum_own, sum_pair, sum_mine, sum_slot, sum_theirs)
    op_sum = PairedSum(*(ref.at[:, : op_rows * (2 if ref is sum_own else 1), :width] for ref in sum_refs),
                       sum_sems.at[0])
    zx_sum = PairedSum(*(ref.at[:, :, : 2 * inner] for ref in sum_refs), sum_sems.at[1])
    small_swap = Swap("seq", small, small_slots, small_sems)
    both_swap = Swap("head", small_own, small_z, smallz_sems)
    row_copy = pltpu.make_async_remote_copy(
        src_ref=halo_rows, dst_ref=landed, send_sem=row_sems.at[0], recv_sem=row_sems.at[1],
        device_id={"seq": lax.rem(me + seq - 1, seq)}, device_id_type=MESH)
    served, sent = plans
    back_points = inner // 128 + 3
    back_at = at - 2 * count - 1
    last_step = back_at == count - 1

    def serve(phase, k):
        line.send(*sent.span(phase, k))
        line.serve(*served.span(phase, k), lag)

    @pl.when(at == 0)
    def _():
        greet("head", "seq")
        state[...] = entering[...]

    @pl.when(at < count)
    def _():
        mine = pl.ds(pl.multiple_of(at * rows, rows), rows)
        serve(0, MIX_POINTS * at)
        mix_step(heads, head_dim, state_dim, at, x_conv, bc_conv, heads_in, normed, zx, cot, out_proj, gains, entering,
                 ssm.at[mine], d_normed.at[mine], own.at[mine], sums, starts, state,
                 lambda: serve(0, MIX_POINTS * at + 1))

    @pl.when(at == count - 1)
    def _():
        swap.start()

    @pl.when((at >= count) & (at < 2 * count))
    def _():
        serve(1, at - count)

    @pl.when(at == count)
    def _():
        swap.wait()
        sums_out[...] = swap.total()
        swap.finish()
        grad[...] = jnp.zeros_like(grad)
        gate_rows[...] = jnp.zeros_like(gate_rows)
        state[...] = jnp.zeros_like(state)

    @pl.when((at >= count) & (at < 2 * count))
    def _():
        here = at - count
        mine = pl.ds(pl.multiple_of(here * rows, rows), rows)
        gate_step(heads, head_dim, state_dim, all_channels, here,
                  ssm.at[mine], d_normed.at[mine], sums_out, x_conv, bc_conv, heads_in, normed, zx, cot, gains,
                  ssm.at[mine], d_normed.at[mine], grad.at[:inner], gate_rows, state)

    @pl.when(at == 2 * count)
    def _():
        for k in range(seq // 2):
            lo, hi = min(inner, k * 2 * op_rows), min(inner, (k + 1) * 2 * op_rows)
            if hi > lo:
                sum_own[k, : hi - lo, :width] = grad[lo:hi, :width].astype(bf16)
        scan.begin(decay[...])
        scan.run(lambda k: serve(2, k))
        op_sum.swap()
        grad[...] = jnp.zeros_like(grad)
        grad_bc[...] = jnp.zeros_like(grad_bc)
        small[...] = jnp.zeros_like(small)

    def project(block_low, gate_low, conv_low, rest_low):
        d_rows = dot_nt(conv_low, zx[:, inner:]) + dot(rest_low, weights[...])
        grad[:, inner : 2 * inner] += dot_tn(block_low, conv_low)
        if gate_low is not None:
            d_rows = d_rows + dot_nt(gate_low, zx[:, :inner])
            grad[:, :inner] += dot_tn(block_low, gate_low)
        grad_bc[...] += dot_tn(rest_low, block_low).reshape(grad_bc.shape)
        small[16:17] += jnp.sum(d_rows * block_low.astype(f32), axis=0, keepdims=True) / gain[...]
        return d_rows

    @pl.when(at > 2 * count)
    def _():
        here = 3 * count - at
        mine = pl.ds(pl.multiple_of(here * rows, rows), rows)
        serve(3, back_points * back_at)
        back_step(heads, head_dim, state_dim, back_at == 0, last_step,
                  ssm.at[mine], x_conv, bc_conv, x_in, bc_in, heads_in, starts[here], leaving, conv_w, params,
                  gains[1:2], conv_halo, d_conv, d_step, conv_grads, head_grads, halo_rows,
                  state, later, later_info, lambda k: serve(3, back_points * back_at + k))

        @pl.when(last_step)
        def _():
            row_copy.start()
        serve(3, back_points * back_at + back_points - 1)
        rest_low = jnp.concatenate([d_conv[:, inner:], d_step[...]], axis=1)
        d_rows = project(normed[...], d_normed[mine], d_conv[:, :inner], rest_low).astype(bf16)

        @pl.when(back_at == 0)
        def _():
            own[: rows - block] = d_rows[: rows - block]
            held[...] = d_rows[rows - block :]

        @pl.when(back_at > 0)
        def _():
            start = pl.multiple_of(back_at * rows - block, block)
            own[pl.ds(start, rows)] = d_rows

    @pl.when(back_at == 1)
    def _():
        op_sum.scatter()

    @pl.when(back_at == 3)
    def _():
        op_sum.gather()

    @pl.when(back_at == 5)
    def _():
        op_sum.back()

    piece = grad_bc.shape[1] // owners

    def bc_scatter(to, source):
        return pltpu.make_async_remote_copy(
            src_ref=grad_bc.at[:head_count, pl.ds(pl.multiple_of(to * piece, piece), piece)],
            dst_ref=bc_slots.at[source], send_sem=bc_sems.at[0, to], recv_sem=bc_sems.at[1, source],
            device_id={"seq": to}, device_id_type=MESH)

    def bc_gather(owner, to):
        rows = pl.ds(pl.multiple_of(owner * piece, piece), piece)
        return pltpu.make_async_remote_copy(
            src_ref=bc_res.at[rows], dst_ref=bc_res.at[rows],
            send_sem=bc_sems.at[2, to], recv_sem=bc_sems.at[3, owner],
            device_id={"seq": to}, device_id_type=MESH)

    def bc_swap(to, source):
        return pltpu.make_async_remote_copy(
            src_ref=bc_slots.at[me, to], dst_ref=bc_z.at[source],
            send_sem=bcz_sems.at[0, to], recv_sem=bcz_sems.at[1, source],
            device_id={"head": to}, device_id_type=MESH)

    @pl.when(last_step)
    def _():
        op_sum.finish(op_out)
        op_sum.release(free_sem)
        at_block = [served.count(3, plans[0].phases[3][0] - 1), sent.count(3, plans[0].phases[3][0] - 1)]

        def go(more):
            until = min(line.count + lag, at_block[0] + more)
            ahead = max(at_block[1], min(line.count - (0 if filled else 1), until + 2))
            line.send(at_block[1], ahead)
            line.serve(at_block[0], until, lag)
            at_block[:] = [until, ahead]
        filled = False
        go(steps[0])
        row_copy.wait()
        extra = jnp.where(me < seq - 1, landed[...] * tail_mask[8:, 0:1], 0.0)
        extra = jnp.concatenate([jnp.zeros_like(extra), extra], axis=0).astype(bf16)
        extra_rest = jnp.concatenate([extra[:, inner:], jnp.zeros((16, 128), bf16)], axis=1)
        more = project(last_normed[...], None, extra[:, :inner], extra_rest)
        final = held[...].astype(f32) + jnp.concatenate([jnp.zeros((block - 16, width), f32), more], axis=0)
        own[count * rows - block :] = final.astype(bf16)
        filled = True
        go(steps[1])

        pl.semaphore_wait(free_sem, 1)
        pair_rows = sum_own.shape[1]
        for k in range(sum_own.shape[0]):
            sum_own[k, :, : 2 * inner] = grad[k * pair_rows : (k + 1) * pair_rows, : 2 * inner].astype(bf16)
        zx_sum.swap()
        go(steps[2])
        small[0:8] += grad_bc[head_count, 0:8]
        small[8 : 9 + taps, :inner] = conv_grads[: taps + 1, :inner]
        small[8:10, inner : 2 * inner] = gate_rows[0:2]
        small[10:12, inner : inner + 128] = head_grads[0:2]
        small[17 : 18 + taps, :bc_width] = conv_grads[: taps + 1, inner:]
        small_swap.start()

        @pl.loop(1, seq)
        def _(k):
            to = other_of("seq", k)

            @pl.when(to < owners)
            def _():
                bc_scatter(to, me).start()

        go(steps[3])
        zx_sum.scatter()
        go(steps[4])
        small_swap.wait()
        sums_small = small_swap.total()
        lone = small.shape[0] - small_own.shape[0]
        small_out[:lone] = sums_small[:lone]
        small_own[...] = sums_small[lone:]
        both_swap.start()
        go(steps[5])

        @pl.when(me < owners)
        def _():
            @pl.loop(1, seq)
            def _(k):
                bc_scatter(me, other_of("seq", k)).wait_recv()
            bc_slots[me] = grad_bc[:head_count, pl.ds(pl.multiple_of(me * piece, piece), piece)]
            sums_bc = bc_slots[0]
            for k in range(1, seq):
                sums_bc = sums_bc + bc_slots[k]
            bc_slots[me] = sums_bc
            bc_z[my_head] = bc_slots[me, my_head]

            @pl.loop(1, head_count)
            def _(k):
                bc_swap(other_of("head", k), my_head).start()

        go(steps[6])
        zx_sum.gather()
        go(steps[7])
        both_swap.wait()
        small_out[lone:] = both_swap.total()

        @pl.when(me < owners)
        def _():
            @pl.loop(1, head_count)
            def _(k):
                bc_swap(my_head, other_of("head", k)).wait_recv()
            sums_bc = bc_z[0]
            for k in range(1, head_count):
                sums_bc = sums_bc + bc_z[k]
            bc_res[pl.ds(pl.multiple_of(me * piece, piece), piece)] = sums_bc

            @pl.loop(1, seq)
            def _(k):
                bc_gather(me, other_of("seq", k)).start()

        go(steps[8])
        zx_sum.back()
        go(steps[9])
        zx_sum.finish(zx_out)
        go(line.count + lag)
        line.finish()
        small_swap.finish()
        both_swap.finish()

        @pl.loop(1, seq)
        def _(k):
            other = other_of("seq", k)

            @pl.when(other < owners)
            def _():
                bc_gather(other, me).wait_recv()
                bc_scatter(other, me).wait_send()

            @pl.when(me < owners)
            def _():
                bc_gather(me, other).wait_send()
        bc_out[...] = bc_res[...]

        @pl.when(me < owners)
        def _():
            @pl.loop(1, head_count)
            def _(k):
                bc_swap(other_of("head", k), my_head).wait_send()


def layer(x_conv, bc_conv, x_in, bc_in, heads_in, cot, normed, out_proj, gains, entering, decay, conv_w, params,
          conv_halo, zx, weights, gain, tail_mask, heads, head_dim, state_dim, all_channels, taps):
    length, inner = x_conv.shape
    conv = inner + bc_conv.shape[1]
    count = length // GROUP
    width = cot.shape[1]
    seq, head_count = lax.axis_size("seq"), lax.axis_size("head")
    block = BLOCK
    pace = PACE * block // 64
    blocks = length // block
    per = GROUP // block
    lag = max(2, head_count // 2)
    back_points = inner // 128 + 3
    gate_at = MIX * count + SWAP
    scan_at = gate_at + GATE * count
    back_start = scan_at + SCAN
    rounds = seq.bit_length() - 1
    phases = [(MIX_POINTS * count, 0, MIX // MIX_POINTS), (count, gate_at, GATE),
              (rounds, scan_at, SCAN // rounds), (back_points * count, back_start, BACK // back_points)]
    served = Pace(phases, pace, LATE, 2 * blocks + lag)
    sent = Pace(phases, pace, EARLY, 2 * blocks)
    for k in range(count):
        point = (k + 1) * back_points - 1
        assert served.count(3, point) >= min(blocks, (k + 1) * per) + lag
        assert sent.count(3, point) >= min(blocks, (k + 1) * per) + LineSum.AHEAD
        for each in (served, sent):
            assert each.count(3, point) <= blocks + max(0, k * per - 1)
    steps = [step * 64 // block for step in STEPS]

    def by(cols, first, step):
        def index(g):
            ahead = jnp.where(g < count, g, jnp.where(g < 2 * count, g - count, jnp.minimum(3 * count - g, count - 1)))
            if first == 2:
                ahead = jnp.where(g < 2 * count, count - 1, ahead)
            if step == 1:
                ahead = jnp.where(g < 2 * count, ahead, count - 1)
            return (ahead, 0)
        return pl.BlockSpec((GROUP, cols), index)
    shape = jax.ShapeDtypeStruct
    state, fade = (state_dim, inner), (8, inner)
    bc_rows = (conv - inner) // head_count
    owners = min(seq, bc_rows // 8)
    piece = bc_rows // owners
    vm = pltpu.VMEM
    grad_rows = max(width, inner)
    paired = PairedSum.scratch(width, max(width, 2 * inner))
    return pl.pallas_call(
        functools.partial(layer_kernel, heads, head_dim, state_dim, all_channels, count, block, lag,
                          (served, sent), steps, owners, taps),
        grid=(3 * count + 1,),
        out_shape=(shape((length, width), bf16), shape((length, width), bf16), shape((2, count, GROUP), f32),
                   shape((width, 2 * inner), bf16), shape((inner, width), bf16), shape((bc_rows, width), f32),
                   shape((24, width), f32)),
        in_specs=[by(inner, 0, 2), by(conv - inner, 0, 2), by(inner, 2, 2), by(conv - inner, 2, 2),
                  by(128, 0, 2), by(width, 0, 1), by(width, 0, 2), pl.BlockSpec((16, width), lambda g: (length // 16 - 1, 0))] + [VMEM] * 11,
        out_specs=(HBM, HBM) + (VMEM,) * 5,
        scratch_shapes=[
            vm((length, width), bf16), vm((length, width), bf16), vm((2 * length, width), bf16),
            vm((block, width), bf16), vm((length, inner), f32), vm((length, inner), bf16),
            vm((count,) + state, bf16), vm(state, f32), vm(state, f32)]
        + [vm((GROUP + 8, conv), f32), vm((GROUP + 8, 128), f32)]
        + [vm((2, count, GROUP), f32), vm((head_count, 2, count, GROUP), f32)]
        + DeviceScan.scratch(state, fade)
        + [vm((grad_rows, max(width, 2 * inner)), f32)] + paired[:-1] + [DMA((2,) + (6, seq // 2))]
        + [vm(((conv - inner + 128) // bc_rows, bc_rows, width), f32),
           vm((seq, head_count, piece, width), f32), vm((head_count, piece, width), f32),
           vm((bc_rows, width), f32), vm((24, width), f32), vm((seq, 24, width), f32),
           vm((8, width), f32), vm((head_count, 8, width), f32),
           vm((GROUP, conv), bf16), vm((GROUP, 128), bf16), vm((8, inner), f32), vm((8, conv), f32),
           vm((8, 128), f32), vm((8, conv), f32), vm((8, conv), f32),
           LineSum.sems(length, block), DMA((2, head_count)), DMA((4, seq)), DMA((2, head_count)),
           DMA((2, seq)), DMA((2, head_count)), DMA((2,)), pltpu.SemaphoreType.REGULAR],
        compiler_params=pltpu.CompilerParams(
            dimension_semantics=("arbitrary",), collective_id=4, has_side_effects=True,
            vmem_limit_bytes=LAYER_LIMIT),
        name="layer",
    )(x_conv, bc_conv, x_in, bc_in, heads_in, cot, normed, normed, out_proj, gains, entering, decay, conv_w, params,
      conv_halo, zx, weights, gain, tail_mask)


PACE = 29
MIX, SWAP, GATE, SCAN, BACK = 27, 30, 20, 100, 94
MIX_POINTS = 2
EARLY, LATE = -14, 50
BLOCK = 64
STEPS = (1, 1, 1, 1, 5, 1, 2, 1, 5, 1)
LAYER_LIMIT = 63 * 2**20


def finish_kernel(heads, head_dim, all_channels, taps,
                  tokens, cot, mixed, d_normed, sums, gain, zx, op, bc, small,
                  mixed_out, tokens_out, zx_out, op_out, bc_out, dt_out, gain_out, conv_w_out, conv_b_out,
                  bc_w_out, bc_b_out, bias_out, rate_out, skip_out, norm_out):
    at = pl.program_id(0)
    rows = tokens.shape[0]
    inner = heads * head_dim
    value = tokens[...].astype(f32)
    tall = jnp.concatenate([sums[0, pl.ds(at, 1)], jnp.zeros((127, rows), f32)], axis=0).T
    inv_rms = lax.rsqrt(tall[:, 0:1] / all_channels + epsilon)
    mixed_out[...] = (value + mixed[...].astype(f32) * inv_rms).astype(bf16)
    inv = lax.rsqrt(jnp.mean(value * value, axis=1, keepdims=True) + epsilon)
    xhat = value * inv
    scaled = d_normed[...].astype(f32) * gain[...]
    tokens_out[...] = cot[...].astype(f32) + inv * (
        scaled - xhat * jnp.mean(scaled * xhat, axis=1, keepdims=True))
    sums_zx = zx[...].astype(f32)
    zx_out[:, 0, :] = sums_zx[:, :inner]
    zx_out[:, 1, :] = sums_zx[:, inner:]
    op_out[...] = op[...].astype(f32)
    @pl.when(at == 0)
    def _():
        bc_out[...] = bc[...]
        dt_out[...] = small[0:heads]
        gain_out[...] = small[16:17]
        conv_w_out[...] = small[8 : 8 + taps, :inner]
        conv_b_out[...] = small[8 + taps : 9 + taps, :inner]
        bias_out[...] = small[10:11, inner : inner + heads]
        rate_out[...] = small[11:12, inner : inner + heads]
        norm_out[...] = small[8:9, inner : 2 * inner]
        group_ones = (lax.broadcasted_iota(jnp.int32, (inner, 128), 0) // head_dim
                      == lax.broadcasted_iota(jnp.int32, (inner, 128), 1)).astype(bf16)
        skips = jnp.broadcast_to(small[9:10, inner : 2 * inner], (8, inner))
        total = sum(dot(part, group_ones) for part in split3(skips))
        skip_out[...] = total[0:1, :heads]
        part = bc_w_out.shape[1]
        mine_bc = small[17 : 18 + taps, : part * lax.axis_size("head")]
        chosen = mine_bc[:, :part]
        for k in range(1, lax.axis_size("head")):
            chosen = jnp.where(lax.axis_index("head") == k, mine_bc[:, k * part : (k + 1) * part], chosen)
        bc_w_out[...] = chosen[:taps]
        bc_b_out[...] = chosen[taps : taps + 1]


def finish(tokens, cot, mixed, d_normed, sums, gain, zx, op, bc, small, heads, head_dim, taps):
    length, width = tokens.shape
    count = length // GROUP
    inner = heads * head_dim
    part = bc.shape[0]

    def by(rows, cols):
        return pl.BlockSpec((rows, cols), lambda g: (g, 0))
    shape = jax.ShapeDtypeStruct
    tall = by(GROUP, width)
    lone = [(1, width), (taps, inner), (1, inner), (taps, part), (1, part), (1, heads), (1, heads), (1, heads),
            (1, inner)]
    cols = width // count
    return pl.pallas_call(
        functools.partial(finish_kernel, heads, head_dim, inner * lax.axis_size("head"), taps),
        grid=(count,),
        out_shape=(shape((length, width), bf16), shape((length, width), f32), shape((width, 2, inner), f32),
                   shape((inner, width), f32), shape((part, width), f32), shape((heads, width), f32))
        + tuple(shape(each, f32) for each in lone),
        in_specs=[tall] * 4 + [VMEM, VMEM, by(cols, 2 * inner), by(inner // count, width),
                               VMEM, VMEM],
        out_specs=(tall, tall, pl.BlockSpec((cols, 2, inner), lambda g: (g, 0, 0)), by(inner // count, width),
                   VMEM, VMEM) + (VMEM,) * len(lone),
        compiler_params=pltpu.CompilerParams(dimension_semantics=("arbitrary",), vmem_limit_bytes=LIMIT),
        name="finish",
    )(tokens, cot, mixed, d_normed, sums, gain, zx, op, bc, small)


def shards(
    tokens, start_flags, in_gain, proj_zx, proj_bc, proj_dt, conv_x_weight, conv_x_bias,
    conv_bc_weight, conv_bc_bias, dt_bias, a_log, skip_scale, norm_gain, out_proj, cotangent,
):
    length, width = tokens.shape
    heads = a_log.shape[0]
    inner = proj_zx.shape[2]
    head_dim = inner // heads
    taps = conv_x_weight.shape[0]
    head_count = lax.axis_size("head")
    bc_part = conv_bc_bias.shape[0]
    bc_width = bc_part * head_count
    state_dim = bc_width // 2
    zx = proj_zx.reshape(width, 2 * inner)
    gain = in_gain[None]
    (normed, x_in, x_conv, bc_in, bc_conv, info, entering, decay, conv_halo, weights, conv_w, params, gains,
     tail_mask) = front(
        tokens, zx, start_flags.reshape(length // 128, 128), gain, proj_bc.T, proj_dt.T, conv_x_weight,
        conv_x_bias[None], conv_bc_weight, conv_bc_bias[None], dt_bias[None], a_log[None], skip_scale[None],
        norm_gain[None], heads, head_dim, state_dim)
    all_channels = inner * head_count
    mixed, d_normed, sums, zx_sum, op_sum, bc_sum, small_sum = layer(
        x_conv, bc_conv, x_in, bc_in, info, cotangent, normed, out_proj, gains, entering, decay, conv_w, params,
        conv_halo, zx, weights, gain, tail_mask, heads, head_dim, state_dim, all_channels, taps)
    (mixed_out, grad_tokens, grad_zx, grad_op, grad_bc, grad_dt, grad_gain, grad_conv_w, grad_conv_b,
     grad_bc_w, grad_bc_b, grad_bias, grad_rate, grad_skip, grad_norm) = finish(
        tokens, cotangent, mixed, d_normed, sums, gain, zx_sum, op_sum, bc_sum, small_sum, heads, head_dim, taps)
    return (
        mixed_out, grad_tokens, grad_gain[0], grad_zx, grad_bc.T, grad_dt.T, grad_conv_w, grad_conv_b[0],
        grad_bc_w, grad_bc_b[0], grad_bias[0], grad_rate[0], grad_skip[0], grad_norm[0], grad_op,
    )


def solution(mesh):
    in_specs = (
        P("seq", None),
        P("seq"),
        P(),
        P(None, None, "head"),
        P(None, "head"),
        P(None, "head"),
        P(None, "head"),
        P("head"),
        P(None, "head"),
        P("head"),
        P("head"),
        P("head"),
        P("head"),
        P("head"),
        P("head", None),
        P("seq", None),
    )
    out_specs = (
        P("seq", None),
        P("seq", None),
        P(),
        P(None, None, "head"),
        P(None, "head"),
        P(None, "head"),
        P(None, "head"),
        P("head"),
        P(None, "head"),
        P("head"),
        P("head"),
        P("head"),
        P("head"),
        P("head"),
        P("head", None),
    )
    return jax.shard_map(shards, mesh=mesh, in_specs=in_specs, out_specs=out_specs, check_vma=False)
```

```python
import functools

import jax
import jax.numpy as jnp
from jax import lax
from jax.experimental import pallas as pl
from jax.experimental.pallas import tpu as pltpu
from jax.sharding import PartitionSpec as P

MESH = pl.DeviceIdType.MESH
f32 = jnp.float32
bf16 = jnp.bfloat16
VMEM = pl.BlockSpec(memory_space=pltpu.VMEM)
HBM = pl.BlockSpec(memory_space=pl.ANY)
DMA = pltpu.SemaphoreType.DMA


def rows_of(ref, start, size):
    return ref.at[pl.ds(pl.multiple_of(start, size), size)]


def other_of(axis, k):
    size = lax.axis_size(axis)
    return lax.rem(lax.axis_index(axis) + k, size)


def greet(*axes):
    barrier = pltpu.get_barrier_semaphore()
    count = 0
    for axis in axes:
        size = lax.axis_size(axis)
        count += size - 1

        @pl.loop(1, size)
        def _(k):
            pl.semaphore_signal(barrier, inc=1, device_id={axis: other_of(axis, k)}, device_id_type=MESH)
    pl.semaphore_wait(barrier, count)


class Pace:
    def __init__(self, phases, pace, behind, most):
        self.phases, self.pace, self.behind, self.most = phases, pace, behind, most
        self.before = [0]
        for n, (points, _, _) in enumerate(phases):
            self.before.append(self.count(n, points - 1) if points else self.before[-1])

    def count(self, phase, k):
        _, start, step = self.phases[phase]
        low, top = self.before[phase], self.most
        value = (start + k * step - self.behind) // self.pace
        if isinstance(value, int):
            return max(low, min(top, value))
        return jnp.clip(value, low, top)

    def span(self, phase, k):
        if isinstance(k, int):
            return (self.count(phase, k - 1) if k else self.before[phase]), self.count(phase, k)
        return jnp.where(k == 0, self.before[phase], self.count(phase, k - 1)), self.count(phase, k)


class LineSum:
    AHEAD = 3

    def __init__(self, own, got, total, out, place, sems, block):
        self.own, self.got, self.total, self.out, self.place = own, got, total, out, place
        self.send1, self.got_in, self.got_total, self.send2, self.stored = (sems.at[i] for i in range(5))
        self.block = block
        self.half = own.shape[0] // block
        self.count = 2 * self.half
        size, me = lax.axis_size("head"), lax.axis_index("head")
        left = me < size // 2
        self.mid = (me == size // 2 - 1) | (me == size // 2)
        self.has_outer = (me > 0) & (me < size - 1)
        self.inner = jnp.where(left, me + 1, me - 1)
        self.outer = jnp.clip(jnp.where(left, me - 1, me + 1), 0, size - 1)

    @staticmethod
    def sems(rows, block):
        return DMA((5, 2 * rows // block))

    def rows(self, b):
        return pl.ds(pl.multiple_of(b * self.block, self.block), self.block)

    def slot(self, b):
        return self.rows(lax.rem(b, self.half))

    def in_copy(self, b, to):
        return pltpu.make_async_remote_copy(
            src_ref=self.own.at[self.slot(b)], dst_ref=self.got.at[self.slot(b)],
            send_sem=self.send1.at[b], recv_sem=self.got_in.at[b], device_id={"head": to}, device_id_type=MESH)

    def cross_copy(self, b):
        return pltpu.make_async_remote_copy(
            src_ref=self.own.at[self.slot(b)], dst_ref=self.total.at[self.rows(b)],
            send_sem=self.send1.at[b], recv_sem=self.got_total.at[b],
            device_id={"head": self.inner}, device_id_type=MESH)

    def out_copy(self, b, to):
        return pltpu.make_async_remote_copy(
            src_ref=self.total.at[self.rows(b)], dst_ref=self.total.at[self.rows(b)],
            send_sem=self.send2.at[b], recv_sem=self.got_total.at[b],
            device_id={"head": to}, device_id_type=MESH)

    def store(self, b):
        return pltpu.make_async_copy(
            self.total.at[self.rows(b)], self.out.at[self.rows(self.place(b))], self.stored.at[b])

    def inward(self, b):
        rows = self.slot(b)
        self.in_copy(b, self.outer).wait_recv()
        self.own[rows] = self.got[rows] + self.own[rows]

        @pl.when(self.mid)
        def _():
            self.cross_copy(b).start()

        @pl.when(jnp.logical_not(self.mid))
        def _():
            self.in_copy(b, self.inner).start()

    def outward(self, b):
        rows = self.rows(b)
        self.cross_copy(b).wait_recv()

        @pl.when(self.has_outer)
        def _():
            self.cross_copy(b).wait_send()

        @pl.when(self.mid)
        def _():
            self.total[rows] = self.own[self.slot(b)] + self.total[rows]

        @pl.when(self.has_outer)
        def _():
            self.out_copy(b, self.outer).start()
        self.store(b).start()

    def serve(self, first, last, lag):
        @pl.when(self.has_outer)
        def _():
            @pl.loop(first, last)
            def _(b):
                @pl.when(b < self.count)
                def _():
                    self.inward(b)

                @pl.when(b >= lag)
                def _():
                    self.outward(b - lag)

    def send(self, first, last):
        @pl.when(jnp.logical_not(self.has_outer))
        def _():
            @pl.loop(first, last)
            def _(b):
                @pl.when(b >= self.AHEAD)
                def _():
                    self.in_copy(b - self.AHEAD, self.inner).wait_send()

                @pl.when(b >= self.half)
                def _():
                    self.outward(b - self.half)
                self.in_copy(b, self.inner).start()

    def finish(self):
        @pl.when(jnp.logical_not(self.has_outer))
        def _():
            pl.loop(self.half, self.count)(self.outward)

            @pl.loop(self.count - self.AHEAD, self.count)
            def _(b):
                self.in_copy(b, self.inner).wait_send()

        @pl.loop(0, self.count)
        def _(b):
            self.store(b).wait()

            @pl.when(self.has_outer)
            def _():
                self.out_copy(b, self.outer).wait_send()


class PairedSum:
    def __init__(self, own, pair, mine, slots, theirs, sems):
        self.own, self.pair, self.mine, self.slots, self.theirs = own, pair, mine, slots, theirs
        self.sems = sems
        self.me = lax.axis_index("seq")
        self.chip, self.odd = self.me // 2, lax.rem(self.me, 2)
        self.partner = self.me + 1 - 2 * self.odd
        self.chips, self.piece = own.shape[0], own.shape[1] // 2

    @staticmethod
    def scratch(rows, width):
        seq = lax.axis_size("seq")
        piece = max(16, rows // seq)
        part = pltpu.VMEM((seq // 2, piece, width), bf16)
        return [pltpu.VMEM((seq // 2, 2 * piece, width), bf16)] + [part] * 4 + [DMA((8, seq // 2))]

    def half(self, odd):
        return pl.ds(pl.multiple_of(odd * self.piece, self.piece), self.piece)

    def swap_copy(self):
        return pltpu.make_async_remote_copy(
            src_ref=self.own.at[:, self.half(1 - self.odd)], dst_ref=self.pair,
            send_sem=self.sems.at[0, 0], recv_sem=self.sems.at[1, 0],
            device_id={"seq": self.partner}, device_id_type=MESH)

    def back_copy(self):
        return pltpu.make_async_remote_copy(
            src_ref=self.pair, dst_ref=self.theirs,
            send_sem=self.sems.at[0, 1], recv_sem=self.sems.at[1, 1],
            device_id={"seq": self.partner}, device_id_type=MESH)

    def scatter_copy(self, to, source):
        return pltpu.make_async_remote_copy(
            src_ref=self.mine.at[to], dst_ref=self.slots.at[source],
            send_sem=self.sems.at[2, to], recv_sem=self.sems.at[3, source],
            device_id={"seq": 2 * to + self.odd}, device_id_type=MESH)

    def gather_copy(self, owner, to):
        return pltpu.make_async_remote_copy(
            src_ref=self.pair.at[owner], dst_ref=self.pair.at[owner],
            send_sem=self.sems.at[4, to], recv_sem=self.sems.at[5, owner],
            device_id={"seq": 2 * to + self.odd}, device_id_type=MESH)

    def release(self, free):
        pl.semaphore_signal(free, inc=1, device_id={"seq": self.partner}, device_id_type=MESH)

    def others(self, do):
        @pl.loop(1, self.chips)
        def _(k):
            do(lax.rem(self.chip + k, self.chips))

    def swap(self):
        self.swap_copy().start()

    def scatter(self):
        self.swap_copy().wait()
        self.mine[...] = (self.own[:, self.half(self.odd)].astype(f32) + self.pair[...].astype(f32)).astype(bf16)
        self.others(lambda other: self.scatter_copy(other, self.chip).start())

    def gather(self):
        self.others(lambda other: self.scatter_copy(self.chip, other).wait_recv())
        self.others(lambda other: self.scatter_copy(other, self.chip).wait_send())
        self.slots[self.chip] = self.mine[self.chip]
        total = self.slots[0].astype(f32)
        for k in range(1, self.chips):
            total = total + self.slots[k].astype(f32)
        self.pair[self.chip] = total.astype(bf16)
        self.others(lambda other: self.gather_copy(self.chip, other).start())

    def back(self):
        self.others(lambda other: self.gather_copy(other, self.chip).wait_recv())
        self.back_copy().start()

    def stores(self, out):
        for k in range(min(self.chips, out.shape[0] // (2 * self.piece))):
            for n, (odd, ref) in enumerate(((self.odd, self.pair), (1 - self.odd, self.theirs))):
                start = pl.multiple_of((2 * k + odd) * self.piece, self.piece)
                yield pltpu.make_async_copy(
                    ref.at[k], out.at[pl.ds(start, self.piece)], self.sems.at[6 + n, k])

    def finish(self, out):
        self.back_copy().wait()
        self.others(lambda other: self.gather_copy(self.chip, other).wait_send())
        for copy in self.stores(out):
            copy.start()

    def stored(self, out):
        for copy in self.stores(out):
            copy.wait()


class Swap:
    def __init__(self, axis, own, slots, sems):
        self.axis, self.own, self.slots = axis, own, slots
        self.send, self.got = sems.at[0], sems.at[1]
        self.size, self.me = lax.axis_size(axis), lax.axis_index(axis)

    def copy(self, to, source):
        return pltpu.make_async_remote_copy(
            src_ref=self.own, dst_ref=self.slots.at[source],
            send_sem=self.send.at[to], recv_sem=self.got.at[source],
            device_id={self.axis: to}, device_id_type=MESH)

    def start(self):
        @pl.loop(1, self.size)
        def _(k):
            self.copy(other_of(self.axis, k), self.me).start()
        self.slots[self.me] = self.own[...]

    def wait(self):
        @pl.loop(1, self.size)
        def _(k):
            self.copy(self.me, other_of(self.axis, k)).wait_recv()

    def total(self):
        out = self.slots[0]
        for k in range(1, self.size):
            out = out + self.slots[k]
        return out

    def finish(self):
        @pl.loop(1, self.size)
        def _(k):
            self.copy(other_of(self.axis, k), self.me).wait_send()


class DeviceScan:
    def __init__(self, backward, total, fade, lead, out, got, got_fade, sent, sent_fade, sems):
        self.backward, self.total, self.fade, self.lead, self.out = backward, total, fade, lead, out
        self.got, self.got_fade, self.sent, self.sent_fade, self.sems = got, got_fade, sent, sent_fade, sems
        self.me = lax.axis_index("seq")
        self.rounds = lax.axis_size("seq").bit_length() - 1

    @staticmethod
    def scratch(state, fade):
        rounds = lax.axis_size("seq").bit_length() - 1
        return [pltpu.VMEM(fade, f32), pltpu.VMEM(fade, f32)] + [
            pltpu.VMEM((rounds,) + state, bf16), pltpu.VMEM((rounds,) + fade, f32)] * 2 + [DMA((4, rounds))]

    def copies(self, k):
        return [
            pltpu.make_async_remote_copy(
                src_ref=src.at[k], dst_ref=dst.at[k],
                send_sem=self.sems.at[i, k], recv_sem=self.sems.at[i + 1, k],
                device_id={"seq": jnp.bitwise_xor(self.me, 1 << k)}, device_id_type=MESH)
            for src, dst, i in ((self.sent, self.got, 0), (self.sent_fade, self.got_fade, 2))]

    def begin(self, decay):
        self.fade[...] = decay
        self.out[...] = jnp.zeros_like(self.out)
        self.lead[...] = jnp.ones_like(self.lead)

    def start(self, k):
        self.sent[k] = self.total[...].astype(bf16)
        self.sent_fade[k] = self.fade[...]
        for copy in self.copies(k):
            copy.start()

    def finish(self, k):
        for copy in self.copies(k):
            copy.wait()
        later = lax.rem(self.me // (1 << k), 2) == (0 if self.backward else 1)

        @pl.when(later)
        def _():
            theirs = self.got[k].astype(f32)
            self.out[...] = self.out[...] + self.lead[0:1] * theirs
            self.total[...] = self.total[...] + self.fade[0:1] * theirs
            self.lead[...] = self.lead[...] * self.got_fade[k]

        @pl.when(jnp.logical_not(later))
        def _():
            self.total[...] = self.got[k].astype(f32) + self.got_fade[k, 0:1] * self.total[...]
        self.fade[...] = self.fade[...] * self.got_fade[k]

    def run(self, between=None):
        for k in range(self.rounds):
            self.start(k)
            if between is not None:
                between(k)
            self.finish(k)


GROUP = 256
STRIP = 128
GAP = 200.0
epsilon = 1e-05
LIMIT = 56 * 2**20


def dot(a, b):
    return jnp.dot(a, b, preferred_element_type=f32)


def dot_nt(a, b):
    return lax.dot_general(a, b, (((1,), (1,)), ((), ())), preferred_element_type=f32)


def dot_tn(a, b):
    return lax.dot_general(a, b, (((0,), (0,)), ((), ())), preferred_element_type=f32)


def split3(v):
    one = v.astype(bf16)
    rest = v - one.astype(f32)
    two = rest.astype(bf16)
    return one, two, (rest - two.astype(f32)).astype(bf16)


def exact_left(ones, v):
    width = v.shape[1]
    out = dot(ones, jnp.concatenate(split3(v), axis=1))
    return out[:, :width] + out[:, width : 2 * width] + out[:, 2 * width :]


def head_sum(v, group_ones):
    high = v.astype(bf16)
    low = (v - high.astype(f32)).astype(bf16)
    return dot(high, group_ones) + dot(low, group_ones)


def sigmoid(v):
    return 1.0 / (1.0 + jnp.exp(-v))


def softplus(v):
    return jnp.maximum(v, 0.0) + jnp.log1p(jnp.exp(-jnp.abs(v)))


def spread(cols, first, heads, head_dim):
    rows = cols.shape[0]
    per = 128 // head_dim
    lane = lax.broadcasted_iota(jnp.int32, (rows, 128), 1)
    tiles = []
    for at in range(0, heads, per):
        tile = cols[:, first + at : first + at + 1]
        for k in range(1, per):
            tile = jnp.where(lane < k * head_dim, tile, cols[:, first + at + k : first + at + k + 1])
        tiles.append(jnp.broadcast_to(tile, (rows, 128)))
    return jnp.concatenate(tiles, axis=1)


def norm_rows(block, gain):
    value = block.astype(f32)
    inv = lax.rsqrt(jnp.mean(value * value, axis=1, keepdims=True) + epsilon)
    return (value * inv * gain).astype(bf16)


def whole(shape):
    return pl.BlockSpec(shape, lambda g: (0,) * len(shape))


def lane_groups(rows, *parts):
    lane = lax.broadcasted_iota(jnp.int32, (rows, 128), 1)
    out = parts[-1]
    for k in range(len(parts) - 2, -1, -1):
        out = jnp.where(lane < 8 * (k + 1), parts[k], out)
    return out


RAW, STEP, CUM, DEV, KEEP = 0, 8, 16, 24, 32


def head_lanes(row, heads, lane):
    out = jnp.zeros(lane.shape, f32)
    for k in range(heads):
        out = jnp.where(lane % 8 == k, row[:, k : k + 1], out)
    return out


def loads_of(source, target, sems, first):
    parts = sems.shape[0]
    rows = source.shape[0] // parts
    return [pltpu.make_async_copy(source.at[pl.ds(k * rows, rows), pl.ds(first, target.shape[1])],
                                  target.at[pl.ds(k * rows, rows)], sems.at[k]) for k in range(parts)]


def front_kernel(heads, head_dim, state_dim, count,
                 tokens, last_tokens, zx, flags, gain, proj_bc, proj_dt, conv_x_weight, conv_x_bias,
                 conv_bc_weight, conv_bc_bias, dt_bias, a_log, skip, norm_gain,
                 normed_out, x_in_out, x_conv_out, bc_in_out, bc_conv_out, heads_out, entering, decay_out,
                 halo_out, weights_out, conv_w_out, params, gains_out, mask_out,
                 normed, x_active, tail_rows, landed, head_low, proj_all, conv_bc, conv_all, flag_cols, flag_ext,
                 x_ext, bc_ext, state, running, x_weights, lead, fade,
                 scan_got, scan_got_fade, scan_sent, scan_sent_fade, scan_sems, proj_sems, conv_sems, row_sems, load_sems):
    at = pl.program_id(0)
    rows = tokens.shape[0]
    inner = heads * head_dim
    bc_width = 2 * state_dim
    bc_part = proj_bc.shape[0]
    seq, me = lax.axis_size("seq"), lax.axis_index("seq")
    block = lax.rem(at, count)
    mine = pl.ds(pl.multiple_of(block * rows, rows), rows)
    swaps = [Swap("head", proj_bc, proj_all, proj_sems), Swap("head", conv_bc, conv_all, conv_sems)]
    row_copy = pltpu.make_async_remote_copy(
        src_ref=tail_rows, dst_ref=landed, send_sem=row_sems.at[0], recv_sem=row_sems.at[1],
        device_id={"seq": lax.rem(me + 1, seq)}, device_id_type=MESH)
    lane_row = lax.broadcasted_iota(jnp.int32, (1, 128), 1)
    loads = loads_of(zx, x_weights, load_sems, inner)

    @pl.when(at == 0)
    def _():
        for copy in loads:
            copy.start()
        final = 1.0 - flags[flags.shape[0] - 1 :].astype(f32)
        one, two = final[:, 127:128], final[:, 126:127]
        row = lax.broadcasted_iota(jnp.int32, (16, 128), 0)
        mask = jnp.where(row == 15, 1.0, jnp.where(row == 14, one, jnp.where(row == 13, one * two, 0.0)))
        mask_out[...] = mask
        tail_rows[...] = (last_tokens[...].astype(f32) * mask[:, 0:1]).astype(bf16)
        conv_bc[...] = jnp.zeros_like(conv_bc)
        conv_bc[0:4, :bc_part] = conv_bc_weight[...].astype(f32)
        conv_bc[4:5, :bc_part] = conv_bc_bias[...]
        greet("head", "seq")
        row_copy.start()
        for each in swaps:
            each.start()
        params[...] = jnp.zeros_like(params)
        params[0:1] = head_lanes(dt_bias[...], heads, lane_row)
        params[1:2] = -jnp.exp(head_lanes(a_log[...], heads, lane_row))
        gains_out[...] = jnp.zeros_like(gains_out)
        gains_out[0:1] = norm_gain[...]
        gains_out[1:2] = spread(head_lanes(skip[...], heads, lane_row), 0, heads, head_dim)
        flat = flags[...].astype(f32)
        turned = jnp.concatenate([flat, jnp.zeros((128 - flat.shape[0], 128), f32)], axis=0).T
        conv_w_out[...] = jnp.zeros_like(conv_w_out)
        conv_w_out[0:4, :inner] = conv_x_weight[...].astype(f32)
        conv_w_out[4:5, :inner] = conv_x_bias[...]
        for k in range(flat.shape[0]):
            flag_cols[k * 128 : (k + 1) * 128] = jnp.broadcast_to(turned[:, k : k + 1], (128, 128))
        flag_ext[0:8] = jnp.zeros((8, 128), f32)

    def keeps(flag):
        flag_ext[8:] = flag
        one = 1.0 - flag
        two = one * (1.0 - flag_ext[7 : 7 + rows])
        three = two * (1.0 - flag_ext[6 : 6 + rows])
        flag_ext[0:8] = flag_ext[rows:]
        return one, two, three

    def convolve(ext, current, keep, first, last):
        ext[8:] = current
        total = conv_w_out[4:5, first:last] + conv_w_out[0:1, first:last] * current
        for j in range(1, 4):
            total = total + conv_w_out[j : j + 1, first:last] * ext[pl.ds(8 - j, rows)] * keep[j - 1][:, 0:1]
        ext[0:8] = ext[rows:]
        return total

    @pl.when(at < count)
    def _():
        low = norm_rows(tokens[...], gain[...])
        normed[mine] = low
        normed_out[...] = low

        @pl.when(at == 0)
        def _():
            for copy in loads:
                copy.wait()
        x_in = dot(low, x_weights[...]).astype(bf16)
        x_in_out[...] = x_in

        @pl.when(at == 0)
        def _():
            row_copy.wait()
            head_low[...] = norm_rows(landed[...], gain[...])
            ahead = jnp.where(me > 0, dot(head_low[...], x_weights[...]), 0.0).astype(bf16)
            halo_out[:, :inner] = ahead
            x_ext[0:8] = ahead[8:].astype(f32)
        total = convolve(x_ext, x_in.astype(f32), keeps(flag_cols[mine]), 0, inner)
        x_conv_out[...] = total
        x_active[mine] = total * sigmoid(total)

    @pl.when(at == count)
    def _():
        for each in swaps:
            each.wait()
            each.finish()
        heads_there = proj_all.shape[0]
        for k in range(heads_there):
            weights_out[k * bc_part : (k + 1) * bc_part] = proj_all[k]
        eight = jnp.concatenate([proj_dt[...].astype(f32)] + (
            [jnp.zeros((8 - heads, proj_dt.shape[1]), f32)] if heads < 8 else []), axis=0)
        weights_out[bc_width:] = jnp.concatenate([eight] * 16, axis=0).astype(bf16)
        conv_w_out[:, inner:] = jnp.concatenate([conv_all[k, :, :bc_part] for k in range(heads_there)], axis=1)
        ahead = jnp.where(me > 0, dot_nt(head_low[...], weights_out[:bc_width]), 0.0).astype(bf16)
        halo_out[:, inner:] = ahead
        bc_ext[0:8] = ahead[8:].astype(f32)
        state[...] = jnp.zeros_like(state)
        running[...] = jnp.zeros_like(running)
        flag_ext[0:8] = jnp.zeros((8, 128), f32)

    @pl.when(at >= count)
    def _():
        raw = dot_nt(normed[mine], weights_out[...])
        bc_in = raw[:, :bc_width].astype(bf16)
        bc_in_out[...] = bc_in
        flag = flag_cols[mine]
        keep = keeps(flag)
        total = convolve(bc_ext, bc_in.astype(f32), keep, inner, inner + bc_width)
        bc_conv_out[...] = total
        b_proj = (total[:, :state_dim] * sigmoid(total[:, :state_dim])).astype(bf16)

        step_raw = raw[:, bc_width:]
        step = softplus(step_raw + params[0:1])
        log_decay = step * params[1:2] - GAP * flag
        order_r = lax.broadcasted_iota(jnp.int32, (rows, rows), 0)
        order_c = lax.broadcasted_iota(jnp.int32, (rows, rows), 1)
        cum = exact_left((order_r >= order_c).astype(bf16), log_decay)
        lane = lax.broadcasted_iota(jnp.int32, (rows, 128), 1)
        kept = jnp.where(lane < KEEP + 1, keep[0], jnp.where(lane < KEEP + 2, keep[1], keep[2]))
        heads_out[...] = lane_groups(rows, step_raw, step, cum, cum + running[0:1], kept)
        end = cum[rows - 1 : rows]
        running[...] = running[...] + end
        weight = step * jnp.exp(end - cum)
        scaled = (x_active[mine] * spread(weight, 0, heads, head_dim)).astype(bf16)
        state[...] = state[...] * spread(jnp.exp(end), 0, heads, head_dim) + dot_tn(b_proj, scaled)

    @pl.when(at == 2 * count - 1)
    def _():
        decay = spread(jnp.exp(running[...]), 0, heads, head_dim)
        decay_out[...] = decay
        scan = DeviceScan(False, state, fade, lead, entering, scan_got, scan_got_fade, scan_sent,
                          scan_sent_fade, scan_sems)
        scan.begin(decay)
        scan.run()


def front(tokens, zx, flags, gain, proj_bc, proj_dt, conv_x_weight, conv_x_bias, conv_bc_weight, conv_bc_bias,
          dt_bias, a_log, skip, norm_gain, heads, head_dim, state_dim):
    length, width = tokens.shape
    count = length // GROUP
    inner = heads * head_dim
    conv = inner + 2 * state_dim
    head_count = lax.axis_size("head")

    def early(cols):
        return pl.BlockSpec((GROUP, cols), lambda g: (jnp.minimum(g, count - 1), 0))

    def late(cols):
        return pl.BlockSpec((GROUP, cols), lambda g: (jnp.maximum(g - count, 0), 0))
    shape = jax.ShapeDtypeStruct
    state, fade = (state_dim, inner), (8, inner)
    rest = 2 * state_dim + 128
    return pl.pallas_call(
        functools.partial(front_kernel, heads, head_dim, state_dim, count),
        grid=(2 * count,),
        out_shape=(shape((length, width), bf16), shape((length, inner), bf16), shape((length, inner), f32),
                   shape((length, conv - inner), bf16), shape((length, conv - inner), f32),
                   shape((length, 128), f32), shape(state, f32),
                   shape(fade, f32), shape((16, conv), bf16), shape((rest, width), bf16),
                   shape((8, conv), f32), shape((8, 128), f32), shape((8, inner), f32), shape((16, 128), f32)),
        in_specs=[early(width), pl.BlockSpec((16, width), lambda g: (length // 16 - 1, 0)), HBM] + [VMEM] * 12,
        out_specs=(early(width), early(inner), early(inner), late(conv - inner), late(conv - inner), late(128))
        + (VMEM,) * 8,
        scratch_shapes=[
            pltpu.VMEM((length, width), bf16), pltpu.VMEM((length, inner), f32),
            pltpu.VMEM((16, width), bf16), pltpu.VMEM((16, width), bf16), pltpu.VMEM((16, width), bf16),
            pltpu.VMEM((head_count,) + proj_bc.shape, bf16), pltpu.VMEM((8, 128), f32),
            pltpu.VMEM((head_count, 8, 128), f32), pltpu.VMEM((length, 128), f32),
            pltpu.VMEM((GROUP + 8, 128), f32), pltpu.VMEM((GROUP + 8, inner), f32),
            pltpu.VMEM((GROUP + 8, conv - inner), f32), pltpu.VMEM(state, f32), pltpu.VMEM((8, 128), f32),
            pltpu.VMEM((width, inner), bf16)]
        + DeviceScan.scratch(state, fade) + [DMA((2, head_count)), DMA((2, head_count)), DMA((2,)), DMA((4,))],
        compiler_params=pltpu.CompilerParams(
            dimension_semantics=("arbitrary",), collective_id=3, has_side_effects=True,
            vmem_limit_bytes=LIMIT),
        name="front",
    )(tokens, tokens, zx, flags, gain, proj_bc, proj_dt, conv_x_weight, conv_x_bias, conv_bc_weight,
      conv_bc_bias, dt_bias, a_log, skip, norm_gain)


def strips(rows):
    return [(lo, lo + STRIP) for lo in range(0, rows, STRIP)]


def mix_step(heads, head_dim, state_dim, at,
             x_conv, bc_conv, heads_in, normed, zx, cot, out_proj, gains, entering,
             ssm_out, d_normed_out, partial_out, sums_out, starts_out, state, between):
    rows = x_conv.shape[0]
    inner = heads * head_dim
    per = 128 // head_dim

    @pl.when(at == 0)
    def _():
        state[...] = entering[...]

    values = jnp.concatenate([x_conv[...], bc_conv[...]], axis=1)
    active = values * sigmoid(values)
    x = active[:, :inner]
    b_proj = active[:, inner : inner + state_dim].astype(bf16)
    c_proj = active[:, inner + state_dim :].astype(bf16)
    info = heads_in[...]
    flipped = info.T
    stepped = x * spread(info, STEP, heads, head_dim)
    low = stepped.astype(bf16)
    scores = dot_nt(c_proj, b_proj)
    lane = lax.broadcasted_iota(jnp.int32, (rows, 128), 1)
    tiles = []
    for pair in range(heads // per):
        tile = low[:, pair * 128 : (pair + 1) * 128]
        weights, masked = [], []
        for k in range(per):
            head = pair * per + k
            masked.append(jnp.where((lane >= k * head_dim) & (lane < (k + 1) * head_dim), tile,
                                    jnp.zeros_like(tile)))
            parts = []
            for lo, hi in strips(rows):
                gap = info[lo:hi, CUM + head : CUM + head + 1] - flipped[CUM + head : CUM + head + 1, :hi]
                ok = (lax.broadcasted_iota(jnp.int32, (STRIP, hi), 0) + lo
                      >= lax.broadcasted_iota(jnp.int32, (STRIP, hi), 1))
                part = (jnp.exp(jnp.where(ok, gap, -1e30)) * scores[lo:hi, :hi]).astype(bf16)
                if hi < rows:
                    part = jnp.concatenate([part, jnp.zeros((STRIP, rows - hi), bf16)], axis=1)
                parts.append(part)
            weights.append(jnp.concatenate(parts, axis=0))
        tiles.append(dot(jnp.concatenate(weights, axis=1), jnp.concatenate(masked, axis=0)))
        if pair == heads // per // 2 - 1:
            between()
    inside = jnp.concatenate(tiles, axis=1)
    cum = info[:, CUM : CUM + 8]
    end = info[rows - 1 : rows]
    start = state[...]
    starts_out[at] = start.astype(bf16)
    grown = spread(jnp.exp(info), CUM, heads, head_dim)
    result = inside + grown * dot(c_proj, start.astype(bf16)) + gains[1:2] * x
    fade = spread(jnp.exp(end - info), CUM, heads, head_dim)
    state[...] = start * spread(jnp.exp(end), CUM, heads, head_dim) + dot_tn(b_proj, (stepped * fade).astype(bf16))
    ssm_out[...] = result
    z = dot(normed[...], zx[:, :inner])
    gated = result * (z * sigmoid(z))
    d_normed = dot_nt(cot[...], out_proj[...])
    d_normed_out[...] = d_normed.astype(bf16)
    scaled = gated * gains[0:1]
    partial_out[...] = dot(scaled.astype(bf16), out_proj[...]).astype(bf16)
    squares = jnp.sum(gated * gated, axis=1, keepdims=True)
    cross = jnp.sum(d_normed * scaled, axis=1, keepdims=True)
    turned = jnp.where(lane == 0, squares, cross).T
    sums_out[0, pl.ds(at, 1)] = turned[0:1]
    sums_out[1, pl.ds(at, 1)] = turned[1:2]


def gate_step(heads, head_dim, state_dim, all_channels, at,
              ssm, d_normed, sums, x_conv, bc_conv, heads_in, normed, zx, cot, gains,
              d_ssm_out, d_gate_out, grad_out, rows_out, total_out):
    rows = ssm.shape[0]
    inner = heads * head_dim

    @pl.when(at == 0)
    def _():
        grad_out[...] = jnp.zeros_like(grad_out)
        rows_out[...] = jnp.zeros_like(rows_out)
        total_out[...] = jnp.zeros_like(total_out)

    tall = jnp.concatenate([sums[0, pl.ds(at, 1)], sums[1, pl.ds(at, 1)], jnp.zeros((126, rows), f32)], axis=0).T
    inv = lax.rsqrt(tall[:, 0:1] / all_channels + epsilon)
    cross = tall[:, 1:2] / all_channels
    z = dot(normed[...], zx[:, :inner])
    s = sigmoid(z)
    y = ssm[...]
    gated = y * (z * s)
    gain = gains[0:1]
    back = d_normed[...].astype(f32)
    unit = gated * inv
    d_gated = inv * (back * gain - unit * (inv * cross))
    grad_out[:, : cot.shape[1]] += dot_tn((unit * gain).astype(bf16), cot[...])
    d_ssm = d_gated * (z * s)
    d_ssm_out[...] = d_ssm
    d_gate_out[...] = (d_gated * y * (s * (1.0 + z * (1.0 - s)))).astype(bf16)
    x_values, c_values = x_conv[...], bc_conv[:, state_dim:]
    rows_out[0:1] += jnp.sum(back * unit, axis=0, keepdims=True)
    rows_out[1:2] += jnp.sum(d_ssm * (x_values * sigmoid(x_values)), axis=0, keepdims=True)
    c_proj = (c_values * sigmoid(c_values)).astype(bf16)
    grown = spread(jnp.exp(heads_in[...]), DEV, heads, head_dim)
    total_out[...] += dot_tn(c_proj, (grown * d_ssm).astype(bf16))


def back_step(heads, head_dim, state_dim, first_step, last_step,
              d_ssm, x_conv, bc_conv, x_in, bc_in, heads_in, start, entering, conv_w, params, skip, conv_halo,
              d_conv_in_out, d_step_out, conv_grads, head_grads, halo_out,
              lam, later, later_info, between):
    rows = d_ssm.shape[0]
    inner = heads * head_dim
    per = 128 // head_dim

    @pl.when(first_step)
    def _():
        lam[...] = entering[...]
        conv_grads[...] = jnp.zeros_like(conv_grads)
        head_grads[...] = jnp.zeros_like(head_grads)
        for each in (later, later_info):
            each[rows:] = jnp.zeros((8, each.shape[1]), f32)

    values = jnp.concatenate([x_conv[...], bc_conv[...]], axis=1)
    gates = sigmoid(values)
    active = values * gates
    x = active[:, :inner]
    b_proj = active[:, inner : inner + state_dim].astype(bf16)
    c_proj = active[:, inner + state_dim :].astype(bf16)
    info = heads_in[...]
    flipped = info.T
    step = spread(info, STEP, heads, head_dim)
    stepped = x * step
    low = stepped.astype(bf16)
    dy = d_ssm[...]
    dy_low = dy.astype(bf16)
    scores = dot_nt(b_proj, c_proj)
    lane = lax.broadcasted_iota(jnp.int32, (rows, 128), 1)
    lane_one = lax.broadcasted_iota(jnp.int32, (STRIP, 128), 1)
    cuts = strips(rows)
    d_scores = [jnp.zeros((STRIP, rows - lo), f32) for lo, _ in cuts]
    d_rows = []
    d_cols = [jnp.zeros((STRIP, 128), f32) for _ in cuts]
    tiles = []
    for pair in range(heads // per):
        tile = low[:, pair * 128 : (pair + 1) * 128]
        dy_tile = dy_low[:, pair * 128 : (pair + 1) * 128]
        owns = [(lane >= k * head_dim) & (lane < (k + 1) * head_dim) for k in range(per)]
        stacked = jnp.concatenate([jnp.where(own, tile, jnp.zeros_like(tile)) for own in owns], axis=0)
        all_pairs = dot_nt(stacked, dy_tile)
        weights = []
        for k in range(per):
            head = pair * per + k
            row_total = jnp.zeros((1, rows), f32)
            parts = []
            for n, (lo, hi) in enumerate(cuts):
                gap = flipped[CUM + head : CUM + head + 1, lo:] - info[lo:hi, CUM + head : CUM + head + 1]
                ok = (lax.broadcasted_iota(jnp.int32, (STRIP, rows - lo), 1)
                      >= lax.broadcasted_iota(jnp.int32, (STRIP, rows - lo), 0))
                decay = jnp.exp(jnp.where(ok, gap, -1e30))
                weight = decay * scores[lo:hi, lo:]
                part = weight.astype(bf16)
                if lo:
                    part = jnp.concatenate([jnp.zeros((STRIP, lo), bf16), part], axis=1)
                parts.append(part)
                pairs = all_pairs[k * rows + lo : k * rows + hi, lo:]
                d_scores[n] = d_scores[n] + pairs * decay
                moved = pairs * weight
                d_cols[n] = d_cols[n] - jnp.where(lane_one == head, jnp.sum(moved, axis=1, keepdims=True), 0.0)
                col = jnp.sum(moved, axis=0, keepdims=True)
                if lo:
                    col = jnp.concatenate([jnp.zeros((1, lo), f32), col], axis=1)
                row_total = row_total + col
            weights.append(jnp.concatenate(parts, axis=0))
            d_rows.append(row_total)
        dy_stack = jnp.concatenate([jnp.where(own, dy_tile, jnp.zeros_like(dy_tile)) for own in owns], axis=0)
        tiles.append(dot(jnp.concatenate(weights, axis=1), dy_stack))
        between(pair + 1)
    d_stepped = jnp.concatenate(tiles, axis=1)
    d_cum = jnp.concatenate(d_cols, axis=0)
    d_cum = d_cum + jnp.concatenate(d_rows + [jnp.zeros((128 - heads, rows), f32)], axis=0).T
    full = jnp.concatenate(
        [jnp.concatenate([jnp.zeros((STRIP, lo), f32), part], axis=1) if lo else part
         for part, (lo, _) in zip(d_scores, cuts)], axis=0).astype(bf16)
    d_b = dot(full, c_proj)
    d_c = dot_tn(full, b_proj)

    group_ones = (lax.broadcasted_iota(jnp.int32, (inner, 128), 0) // head_dim
                  == lax.broadcasted_iota(jnp.int32, (inner, 128), 1)).astype(bf16)
    after = lam[...]
    after_low = after.astype(bf16)
    end = info[rows - 1 : rows]
    grown = spread(jnp.exp(info), CUM, heads, head_dim)
    fade = spread(jnp.exp(end - info), CUM, heads, head_dim)
    end_grown = spread(jnp.exp(end), CUM, heads, head_dim)
    from_after = fade * dot(b_proj, after_low)
    d_stepped = d_stepped + from_after
    grown_dy = grown * dy
    grown_low = grown_dy.astype(bf16)
    left = stepped * from_after
    to_cum = head_sum(grown_dy * dot(c_proj, start) - left, group_ones)
    kept = jnp.sum(after * start.astype(f32), axis=0, keepdims=True) * end_grown
    kept = kept + jnp.sum(left, axis=0, keepdims=True)
    last = head_sum(jnp.broadcast_to(kept, (8, inner)), group_ones)[0:1]
    row_id = lax.broadcasted_iota(jnp.int32, (rows, 128), 0)
    d_cum = d_cum + to_cum + jnp.where(row_id == rows - 1, last, 0.0)
    d_c = d_c + dot_nt(grown_low, start)
    d_b = d_b + dot_nt((fade * stepped).astype(bf16), after_low)
    lam[...] = end_grown * after + dot_tn(c_proj, grown_low)
    d_step = dot((d_stepped * x).astype(bf16), group_ones)
    d_x = step * d_stepped + skip[0:1] * dy
    between(heads // per + 1)

    order_r = lax.broadcasted_iota(jnp.int32, (rows, rows), 0)
    order_c = lax.broadcasted_iota(jnp.int32, (rows, rows), 1)
    d_decay = exact_left((order_r <= order_c).astype(bf16), d_cum) * info[:, KEEP : KEEP + 1]
    rate = params[1:2]
    real = lane < heads
    step_raw = jnp.where(real, info, 0.0) + params[0:1]
    slope = sigmoid(step_raw)
    d_pre = jnp.where(real, (d_step + d_decay * rate) * slope, 0.0)
    d_step_out[...] = d_pre.astype(bf16)
    head_grads[0:1] += jnp.sum(d_pre, axis=0, keepdims=True)
    head_grads[1:2] += jnp.sum(jnp.where(real, d_decay * softplus(step_raw) * rate, 0.0), axis=0, keepdims=True)

    d_active = jnp.concatenate([d_x, d_b, d_c], axis=1)
    d_conv = d_active * (gates * (1.0 + values * (1.0 - gates)))
    taken = jnp.concatenate([x_in[...], bc_in[...]], axis=1).astype(f32)
    total = d_conv * conv_w[0:1]
    conv_grads[0:1] += jnp.sum(d_conv * taken, axis=0, keepdims=True)
    conv_grads[4:5] += jnp.sum(d_conv, axis=0, keepdims=True)
    later[0:rows] = d_conv
    later_info[0:rows] = info
    for j in range(1, 4):
        moved = later[pl.ds(j, rows)] * later_info[pl.ds(j, rows)][:, KEEP + j - 1 : KEEP + j]
        total = total + moved * conv_w[j : j + 1]
        conv_grads[j : j + 1] += jnp.sum(moved * taken, axis=0, keepdims=True)
    d_conv_in_out[...] = total.astype(bf16)

    @pl.when(last_step)
    def _():
        ahead = conv_halo[...].astype(f32)
        halo_out[...] = jnp.zeros_like(halo_out)
        for j in range(1, 4):
            first = later[0:8] * later_info[0:8, KEEP + j - 1 : KEEP + j]
            for t in range(j):
                row = 16 + t - j
                conv_grads[j : j + 1] += first[t : t + 1] * ahead[row : row + 1]
                halo_out[row - 8 : row - 7] += first[t : t + 1] * conv_w[j : j + 1]
    for each in (later, later_info):
        each[rows:] = each[0:8]


def block_place(per, blocks):
    def place(b):
        late = b - blocks - (per - 1)
        group = 2 * blocks - 2 * per - late // per * per + late % per
        second = jnp.where(b < blocks + per - 1, b + blocks - per, group)
        return jnp.where((b < blocks) | (b == 2 * blocks - 1), b, second)
    return place


def layer_kernel(heads, head_dim, state_dim, all_channels, count, block, lag, plans, steps, owners, taps,
                 x_conv, bc_conv, x_in, bc_in, heads_in, cot, normed, last_normed, out_proj, gains, entering, decay,
                 conv_w, params, conv_halo, zx_hbm, weights, gain, tail_mask,
                 totals_out, sums_out, zx_out, op_out, bc_out, small_out,
                 own, got, total, held, ssm, d_normed, starts, state, leaving, later, later_info,
                 sums, sum_slots, lead, fade,
                 scan_got, scan_got_fade, scan_sent, scan_sent_fade, scan_sems,
                 grad, sum_own, sum_pair, sum_mine, sum_slot, sum_theirs, sum_sems, grad_bc,
                 bc_slots, bc_z, bc_res, small, small_slots, small_own, small_z,
                 d_conv, d_step, gate_rows, conv_grads, head_grads, halo_rows, landed,
                 line_sems, swap_sems, bc_sems, bcz_sems, small_sems, smallz_sems, row_sems, free_sem, zx,
                 load_sems):
    at = pl.program_id(0)
    rows, width = cot.shape
    inner = heads * head_dim
    bc_width = 2 * state_dim
    seq, head_count = lax.axis_size("seq"), lax.axis_size("head")
    me, my_head = lax.axis_index("seq"), lax.axis_index("head")
    per = rows // block
    line = LineSum(own, got, total, totals_out, block_place(per, count * per), line_sems, block)
    swap = Swap("head", sums, sum_slots, swap_sems)
    scan = DeviceScan(True, state, fade, lead, leaving, scan_got, scan_got_fade, scan_sent, scan_sent_fade,
                      scan_sems)
    op_rows = max(16, inner // seq)
    sum_refs = (sum_own, sum_pair, sum_mine, sum_slot, sum_theirs)
    op_sum = PairedSum(*(ref.at[:, : op_rows * (2 if ref is sum_own else 1), :width] for ref in sum_refs),
                       sum_sems.at[0])
    zx_sum = PairedSum(*(ref.at[:, :, : 2 * inner] for ref in sum_refs), sum_sems.at[1])
    small_swap = Swap("seq", small, small_slots, small_sems)
    both_swap = Swap("head", small_own, small_z, smallz_sems)
    row_copy = pltpu.make_async_remote_copy(
        src_ref=halo_rows, dst_ref=landed, send_sem=row_sems.at[0], recv_sem=row_sems.at[1],
        device_id={"seq": lax.rem(me + seq - 1, seq)}, device_id_type=MESH)
    served, sent = plans
    back_points = inner // 128 + 3
    back_at = at - 2 * count - 1
    last_step = back_at == count - 1

    def serve(phase, k):
        line.send(*sent.span(phase, k))
        line.serve(*served.span(phase, k), lag)

    def serve_mix(k):
        @pl.when(at > 0)
        def _():
            serve(1, MIX_POINTS * (at - 1) + k)

    loads = loads_of(zx_hbm, zx, load_sems, 0)

    @pl.when(at == 0)
    def _():
        for copy in loads:
            copy.start()
        greet("head", "seq")
        state[...] = entering[...]
        for copy in loads:
            copy.wait()

    @pl.when(at < count)
    def _():
        mine = pl.ds(pl.multiple_of(at * rows, rows), rows)
        serve_mix(0)
        mix_step(heads, head_dim, state_dim, at, x_conv, bc_conv, heads_in, normed, zx, cot, out_proj, gains, entering,
                 ssm.at[mine], d_normed.at[mine], own.at[mine], sums, starts, state,
                 lambda: serve_mix(1))

    @pl.when(at == count - 1)
    def _():
        swap.start()

    @pl.when((at >= count) & (at < 2 * count))
    def _():
        serve(2, at - count)

    @pl.when(at == count)
    def _():
        swap.wait()
        sums_out[...] = swap.total()
        swap.finish()
        grad[...] = jnp.zeros_like(grad)
        gate_rows[...] = jnp.zeros_like(gate_rows)
        state[...] = jnp.zeros_like(state)

    @pl.when((at >= count) & (at < 2 * count))
    def _():
        here = at - count
        mine = pl.ds(pl.multiple_of(here * rows, rows), rows)
        gate_step(heads, head_dim, state_dim, all_channels, here,
                  ssm.at[mine], d_normed.at[mine], sums_out, x_conv, bc_conv, heads_in, normed, zx, cot, gains,
                  ssm.at[mine], d_normed.at[mine], grad.at[:inner], gate_rows, state)

    @pl.when(at == 2 * count)
    def _():
        for k in range(seq // 2):
            lo, hi = min(inner, k * 2 * op_rows), min(inner, (k + 1) * 2 * op_rows)
            if hi > lo:
                sum_own[k, : hi - lo, :width] = grad[lo:hi, :width].astype(bf16)
        scan.begin(decay[...])
        scan.run(lambda k: serve(3, k))
        op_sum.swap()
        grad[...] = jnp.zeros_like(grad)
        grad_bc[...] = jnp.zeros_like(grad_bc)
        small[...] = jnp.zeros_like(small)

    def project(block_low, gate_low, conv_low, rest_low):
        d_rows = dot_nt(conv_low, zx[:, inner:]) + dot(rest_low, weights[...])
        grad[:, inner : 2 * inner] += dot_tn(block_low, conv_low)
        if gate_low is not None:
            d_rows = d_rows + dot_nt(gate_low, zx[:, :inner])
            grad[:, :inner] += dot_tn(block_low, gate_low)
        grad_bc[...] += dot_tn(rest_low, block_low).reshape(grad_bc.shape)
        small[16:17] += jnp.sum(d_rows * block_low.astype(f32), axis=0, keepdims=True) / gain[...]
        return d_rows

    @pl.when(at > 2 * count)
    def _():
        here = 3 * count - at
        mine = pl.ds(pl.multiple_of(here * rows, rows), rows)
        serve(4, back_points * back_at)
        back_step(heads, head_dim, state_dim, back_at == 0, last_step,
                  ssm.at[mine], x_conv, bc_conv, x_in, bc_in, heads_in, starts[here], leaving, conv_w, params,
                  gains[1:2], conv_halo, d_conv, d_step, conv_grads, head_grads, halo_rows,
                  state, later, later_info, lambda k: serve(4, back_points * back_at + k))

        @pl.when(last_step)
        def _():
            row_copy.start()
        serve(4, back_points * back_at + back_points - 1)
        rest_low = jnp.concatenate([d_conv[:, inner:], d_step[...]], axis=1)
        d_rows = project(normed[...], d_normed[mine], d_conv[:, :inner], rest_low).astype(bf16)

        @pl.when(back_at == 0)
        def _():
            own[: rows - block] = d_rows[: rows - block]
            held[...] = d_rows[rows - block :]

        @pl.when(back_at > 0)
        def _():
            start = pl.multiple_of(back_at * rows - block, block)
            own[pl.ds(start, rows)] = d_rows

    @pl.when(back_at == 1)
    def _():
        op_sum.scatter()

    @pl.when(back_at == 3)
    def _():
        op_sum.gather()

    @pl.when(back_at == 5)
    def _():
        op_sum.back()

    piece = grad_bc.shape[1] // owners

    def bc_scatter(to, source):
        return pltpu.make_async_remote_copy(
            src_ref=grad_bc.at[:head_count, pl.ds(pl.multiple_of(to * piece, piece), piece)],
            dst_ref=bc_slots.at[source], send_sem=bc_sems.at[0, to], recv_sem=bc_sems.at[1, source],
            device_id={"seq": to}, device_id_type=MESH)

    def bc_gather(owner, to):
        rows = pl.ds(pl.multiple_of(owner * piece, piece), piece)
        return pltpu.make_async_remote_copy(
            src_ref=bc_res.at[rows], dst_ref=bc_res.at[rows],
            send_sem=bc_sems.at[2, to], recv_sem=bc_sems.at[3, owner],
            device_id={"seq": to}, device_id_type=MESH)

    def bc_swap(to, source):
        return pltpu.make_async_remote_copy(
            src_ref=bc_slots.at[me, to], dst_ref=bc_z.at[source],
            send_sem=bcz_sems.at[0, to], recv_sem=bcz_sems.at[1, source],
            device_id={"head": to}, device_id_type=MESH)

    @pl.when(last_step)
    def _():
        op_sum.finish(op_out)
        at_block = [served.before[-1], sent.before[-1]]

        def go(more):
            until = min(line.count + lag, at_block[0] + more)
            ahead = max(at_block[1], min(line.count - (0 if filled else 1), until + 2))
            line.send(at_block[1], ahead)
            line.serve(at_block[0], until, lag)
            at_block[:] = [until, ahead]
        filled = False
        go(steps[0])
        row_copy.wait()
        extra = jnp.where(me < seq - 1, landed[...] * tail_mask[8:, 0:1], 0.0)
        extra = jnp.concatenate([jnp.zeros_like(extra), extra], axis=0).astype(bf16)
        extra_rest = jnp.concatenate([extra[:, inner:], jnp.zeros((16, 128), bf16)], axis=1)
        more = project(last_normed[...], None, extra[:, :inner], extra_rest)
        final = held[...].astype(f32) + jnp.concatenate([jnp.zeros((block - 16, width), f32), more], axis=0)
        own[count * rows - block :] = final.astype(bf16)
        filled = True
        go(steps[1])

        op_sum.stored(op_out)
        op_sum.release(free_sem)
        pair_rows = sum_own.shape[1]
        for k in range(sum_own.shape[0]):
            sum_own[k, :, : 2 * inner] = grad[k * pair_rows : (k + 1) * pair_rows, : 2 * inner].astype(bf16)
        pl.semaphore_wait(free_sem, 1)
        zx_sum.swap()
        go(steps[2])
        small[0:8] += grad_bc[head_count, 0:8]
        small[8 : 9 + taps, :inner] = conv_grads[: taps + 1, :inner]
        small[8:10, inner : 2 * inner] = gate_rows[0:2]
        small[10:12, inner : inner + 128] = head_grads[0:2]
        small[17 : 18 + taps, :bc_width] = conv_grads[: taps + 1, inner:]
        small_swap.start()

        @pl.loop(1, seq)
        def _(k):
            to = other_of("seq", k)

            @pl.when(to < owners)
            def _():
                bc_scatter(to, me).start()

        go(steps[3])
        zx_sum.scatter()
        go(steps[4])
        small_swap.wait()
        sums_small = small_swap.total()
        lone = small.shape[0] - small_own.shape[0]
        small_out[:lone] = sums_small[:lone]
        small_own[...] = sums_small[lone:]
        both_swap.start()
        go(steps[5])

        @pl.when(me < owners)
        def _():
            @pl.loop(1, seq)
            def _(k):
                bc_scatter(me, other_of("seq", k)).wait_recv()
            bc_slots[me] = grad_bc[:head_count, pl.ds(pl.multiple_of(me * piece, piece), piece)]
            sums_bc = bc_slots[0]
            for k in range(1, seq):
                sums_bc = sums_bc + bc_slots[k]
            bc_slots[me] = sums_bc
            bc_z[my_head] = bc_slots[me, my_head]

            @pl.loop(1, head_count)
            def _(k):
                bc_swap(other_of("head", k), my_head).start()

        go(steps[6])
        zx_sum.gather()
        go(steps[7])
        both_swap.wait()
        small_out[lone:] = both_swap.total()

        @pl.when(me < owners)
        def _():
            @pl.loop(1, head_count)
            def _(k):
                bc_swap(my_head, other_of("head", k)).wait_recv()
            sums_bc = bc_z[0]
            for k in range(1, head_count):
                sums_bc = sums_bc + bc_z[k]
            bc_res[pl.ds(pl.multiple_of(me * piece, piece), piece)] = sums_bc

            @pl.loop(1, seq)
            def _(k):
                bc_gather(me, other_of("seq", k)).start()

        go(steps[8])
        zx_sum.back()
        go(steps[9])
        zx_sum.finish(zx_out)
        go(line.count + lag)
        line.finish()
        zx_sum.stored(zx_out)
        small_swap.finish()
        both_swap.finish()

        @pl.loop(1, seq)
        def _(k):
            other = other_of("seq", k)

            @pl.when(other < owners)
            def _():
                bc_gather(other, me).wait_recv()
                bc_scatter(other, me).wait_send()

            @pl.when(me < owners)
            def _():
                bc_gather(me, other).wait_send()
        bc_out[...] = bc_res[...]

        @pl.when(me < owners)
        def _():
            @pl.loop(1, head_count)
            def _(k):
                bc_swap(other_of("head", k), my_head).wait_send()


def layer(x_conv, bc_conv, x_in, bc_in, heads_in, cot, normed, out_proj, gains, entering, decay, conv_w, params,
          conv_halo, zx, weights, gain, tail_mask, heads, head_dim, state_dim, all_channels, taps):
    length, inner = x_conv.shape
    conv = inner + bc_conv.shape[1]
    count = length // GROUP
    width = cot.shape[1]
    seq, head_count = lax.axis_size("seq"), lax.axis_size("head")
    block = BLOCK
    pace = PACE * block // 64
    blocks = length // block
    per = GROUP // block
    lag = max(LAG, head_count // 2 - 1)
    back_points = inner // 128 + 3
    gate_at = MIX * count + SWAP
    scan_at = gate_at + GATE * count
    back_start = scan_at + SCAN
    rounds = seq.bit_length() - 1
    phases = [(MIX_POINTS, -(10**6), 0), (MIX_POINTS * (count - 1), MIX, MIX // MIX_POINTS), (count, gate_at, GATE),
              (rounds, scan_at, SCAN // rounds), (back_points * count, back_start, BACK // back_points)]
    served = Pace(phases, pace, LATE, 2 * blocks + lag)
    sent = Pace(phases, pace, EARLY, 2 * blocks)
    for k in range(count):
        point = (k + 1) * back_points - 1
        assert served.count(4, point) >= min(blocks, (k + 1) * per) + lag
        assert sent.count(4, point) >= min(blocks, (k + 1) * per) + LineSum.AHEAD
        for each in (served, sent):
            assert each.count(4, point) <= blocks + max(0, k * per - 1)
    steps = [step * 64 // block for step in STEPS]

    def by(cols, first, step):
        def index(g):
            ahead = jnp.where(g < count, g, jnp.where(g < 2 * count, g - count, jnp.minimum(3 * count - g, count - 1)))
            if first == 2:
                ahead = jnp.where(g < 2 * count, count - 1, ahead)
            if step == 1:
                ahead = jnp.where(g < 2 * count, ahead, count - 1)
            return (ahead, 0)
        return pl.BlockSpec((GROUP, cols), index)
    shape = jax.ShapeDtypeStruct
    state, fade = (state_dim, inner), (8, inner)
    bc_rows = (conv - inner) // head_count
    owners = min(seq, bc_rows // 8)
    piece = bc_rows // owners
    vm = pltpu.VMEM
    grad_rows = max(width, inner)
    paired = PairedSum.scratch(width, max(width, 2 * inner))
    return pl.pallas_call(
        functools.partial(layer_kernel, heads, head_dim, state_dim, all_channels, count, block, lag,
                          (served, sent), steps, owners, taps),
        grid=(3 * count + 1,),
        out_shape=(shape((2 * length, width), bf16), shape((2, count, GROUP), f32),
                   shape((width, 2 * inner), bf16), shape((inner, width), bf16), shape((bc_rows, width), f32),
                   shape((24, width), f32)),
        in_specs=[by(inner, 0, 2), by(conv - inner, 0, 2), by(inner, 2, 2), by(conv - inner, 2, 2),
                  by(128, 0, 2), by(width, 0, 1), by(width, 0, 2), pl.BlockSpec((16, width), lambda g: (length // 16 - 1, 0))]
        + [VMEM] * 7 + [HBM] + [VMEM] * 3,
        out_specs=(HBM, VMEM, HBM, HBM, VMEM, VMEM),
        scratch_shapes=[
            vm((length, width), bf16), vm((length, width), bf16), vm((2 * length, width), bf16),
            vm((block, width), bf16), vm((length, inner), f32), vm((length, inner), bf16),
            vm((count,) + state, bf16), vm(state, f32), vm(state, f32)]
        + [vm((GROUP + 8, conv), f32), vm((GROUP + 8, 128), f32)]
        + [vm((2, count, GROUP), f32), vm((head_count, 2, count, GROUP), f32)]
        + DeviceScan.scratch(state, fade)
        + [vm((grad_rows, max(width, 2 * inner)), f32)] + paired[:-1] + [DMA((2,) + (8, seq // 2))]
        + [vm(((conv - inner + 128) // bc_rows, bc_rows, width), f32),
           vm((seq, head_count, piece, width), f32), vm((head_count, piece, width), f32),
           vm((bc_rows, width), f32), vm((24, width), f32), vm((seq, 24, width), f32),
           vm((8, width), f32), vm((head_count, 8, width), f32),
           vm((GROUP, conv), bf16), vm((GROUP, 128), bf16), vm((8, inner), f32), vm((8, conv), f32),
           vm((8, 128), f32), vm((8, conv), f32), vm((8, conv), f32),
           LineSum.sems(length, block), DMA((2, head_count)), DMA((4, seq)), DMA((2, head_count)),
           DMA((2, seq)), DMA((2, head_count)), DMA((2,)), pltpu.SemaphoreType.REGULAR,
           vm((width, 2 * inner), bf16), DMA((4,))],
        compiler_params=pltpu.CompilerParams(
            dimension_semantics=("arbitrary",), collective_id=4, has_side_effects=True,
            vmem_limit_bytes=LAYER_LIMIT),
        name="layer",
    )(x_conv, bc_conv, x_in, bc_in, heads_in, cot, normed, normed, out_proj, gains, entering, decay, conv_w, params,
      conv_halo, zx, weights, gain, tail_mask)


PACE = 28
MIX, SWAP, GATE, SCAN, BACK = 27, 30, 20, 100, 94
MIX_POINTS = 2
EARLY, LATE = -14, 50
BLOCK, LAG = 64, 3
STEPS = (2, 2, 2, 2, 6, 2, 3, 2, 6, 2)
LAYER_LIMIT = 63 * 2**20


def finish_kernel(heads, head_dim, all_channels, taps, count,
                  tokens, cot, mixed, d_normed, sums, gain, zx, op, bc, small,
                  mixed_out, tokens_out, zx_out, op_out, bc_out, dt_out, gain_out, conv_w_out, conv_b_out,
                  bc_w_out, bc_b_out, bias_out, rate_out, skip_out, norm_out, held, sems):
    at = pl.program_id(0)
    rows = tokens.shape[0]
    slot = lax.rem(at, 2)
    part = rows // 4

    def stores(step, slot):
        return [pltpu.make_async_copy(
            held.at[slot, pl.ds(k * part, part)],
            tokens_out.at[pl.ds(pl.multiple_of(step * rows + k * part, part), part)], sems.at[slot, k])
            for k in range(4)]

    @pl.when(at >= 2)
    def _():
        for copy in stores(at - 2, slot):
            copy.wait()
    inner = heads * head_dim
    value = tokens[...].astype(f32)
    tall = jnp.concatenate([sums[0, pl.ds(at, 1)], jnp.zeros((127, rows), f32)], axis=0).T
    inv_rms = lax.rsqrt(tall[:, 0:1] / all_channels + epsilon)
    mixed_out[...] = (value + mixed[...].astype(f32) * inv_rms).astype(bf16)
    inv = lax.rsqrt(jnp.mean(value * value, axis=1, keepdims=True) + epsilon)
    xhat = value * inv
    scaled = d_normed[...].astype(f32) * gain[...]
    held[slot] = cot[...].astype(f32) + inv * (
        scaled - xhat * jnp.mean(scaled * xhat, axis=1, keepdims=True))
    for copy in stores(at, slot):
        copy.start()

    @pl.when(at == count - 1)
    def _():
        for step in (count - 2, count - 1):
            for copy in stores(step, step % 2):
                copy.wait()
    sums_zx = zx[...].astype(f32)
    zx_out[:, 0, :] = sums_zx[:, :inner]
    zx_out[:, 1, :] = sums_zx[:, inner:]
    op_out[...] = op[...].astype(f32)
    @pl.when(at == 0)
    def _():
        bc_out[...] = bc[...]
        dt_out[...] = small[0:heads]
        gain_out[...] = small[16:17]
        conv_w_out[...] = small[8 : 8 + taps, :inner]
        conv_b_out[...] = small[8 + taps : 9 + taps, :inner]
        bias_out[...] = small[10:11, inner : inner + heads]
        rate_out[...] = small[11:12, inner : inner + heads]
        norm_out[...] = small[8:9, inner : 2 * inner]
        group_ones = (lax.broadcasted_iota(jnp.int32, (inner, 128), 0) // head_dim
                      == lax.broadcasted_iota(jnp.int32, (inner, 128), 1)).astype(bf16)
        skips = jnp.broadcast_to(small[9:10, inner : 2 * inner], (8, inner))
        total = sum(dot(part, group_ones) for part in split3(skips))
        skip_out[...] = total[0:1, :heads]
        part = bc_w_out.shape[1]
        mine_bc = small[17 : 18 + taps, : part * lax.axis_size("head")]
        chosen = mine_bc[:, :part]
        for k in range(1, lax.axis_size("head")):
            chosen = jnp.where(lax.axis_index("head") == k, mine_bc[:, k * part : (k + 1) * part], chosen)
        bc_w_out[...] = chosen[:taps]
        bc_b_out[...] = chosen[taps : taps + 1]


def finish(tokens, cot, totals, sums, gain, zx, op, bc, small, heads, head_dim, taps):
    length, width = tokens.shape
    count = length // GROUP
    inner = heads * head_dim
    part = bc.shape[0]

    def by(rows, cols):
        return pl.BlockSpec((rows, cols), lambda g: (g, 0))
    shape = jax.ShapeDtypeStruct
    tall = by(GROUP, width)
    lone = [(1, width), (taps, inner), (1, inner), (taps, part), (1, part), (1, heads), (1, heads), (1, heads),
            (1, inner)]
    cols = width // count
    return pl.pallas_call(
        functools.partial(finish_kernel, heads, head_dim, inner * lax.axis_size("head"), taps, count),
        grid=(count,),
        out_shape=(shape((length, width), bf16), shape((length, width), f32), shape((width, 2, inner), f32),
                   shape((inner, width), f32), shape((part, width), f32), shape((heads, width), f32))
        + tuple(shape(each, f32) for each in lone),
        in_specs=[tall] * 3 + [pl.BlockSpec((GROUP, width), lambda g: (count + g, 0)), VMEM, VMEM, by(cols, 2 * inner), by(inner // count, width),
                               VMEM, VMEM],
        out_specs=(tall, HBM, pl.BlockSpec((cols, 2, inner), lambda g: (g, 0, 0)), by(inner // count, width),
                   VMEM, VMEM) + (VMEM,) * len(lone),
        scratch_shapes=[pltpu.VMEM((2, GROUP, width), f32), DMA((2, 4))],
        compiler_params=pltpu.CompilerParams(dimension_semantics=("arbitrary",), vmem_limit_bytes=LIMIT),
        name="finish",
    )(tokens, cot, totals, totals, sums, gain, zx, op, bc, small)


def shards(
    tokens, start_flags, in_gain, proj_zx, proj_bc, proj_dt, conv_x_weight, conv_x_bias,
    conv_bc_weight, conv_bc_bias, dt_bias, a_log, skip_scale, norm_gain, out_proj, cotangent,
):
    length, width = tokens.shape
    heads = a_log.shape[0]
    inner = proj_zx.shape[2]
    head_dim = inner // heads
    taps = conv_x_weight.shape[0]
    head_count = lax.axis_size("head")
    bc_part = conv_bc_bias.shape[0]
    bc_width = bc_part * head_count
    state_dim = bc_width // 2
    zx = proj_zx.reshape(width, 2 * inner)
    gain = in_gain[None]
    (normed, x_in, x_conv, bc_in, bc_conv, info, entering, decay, conv_halo, weights, conv_w, params, gains,
     tail_mask) = front(
        tokens, zx, start_flags.reshape(length // 128, 128), gain, proj_bc.T, proj_dt.T, conv_x_weight,
        conv_x_bias[None], conv_bc_weight, conv_bc_bias[None], dt_bias[None], a_log[None], skip_scale[None],
        norm_gain[None], heads, head_dim, state_dim)
    all_channels = inner * head_count
    totals, sums, zx_sum, op_sum, bc_sum, small_sum = layer(
        x_conv, bc_conv, x_in, bc_in, info, cotangent, normed, out_proj, gains, entering, decay, conv_w, params,
        conv_halo, zx, weights, gain, tail_mask, heads, head_dim, state_dim, all_channels, taps)
    (mixed_out, grad_tokens, grad_zx, grad_op, grad_bc, grad_dt, grad_gain, grad_conv_w, grad_conv_b,
     grad_bc_w, grad_bc_b, grad_bias, grad_rate, grad_skip, grad_norm) = finish(
        tokens, cotangent, totals, sums, gain, zx_sum, op_sum, bc_sum, small_sum, heads, head_dim, taps)
    return (
        mixed_out, grad_tokens, grad_gain[0], grad_zx, grad_bc.T, grad_dt.T, grad_conv_w, grad_conv_b[0],
        grad_bc_w, grad_bc_b[0], grad_bias[0], grad_rate[0], grad_skip[0], grad_norm[0], grad_op,
    )


def solution(mesh):
    in_specs = (
        P("seq", None),
        P("seq"),
        P(),
        P(None, None, "head"),
        P(None, "head"),
        P(None, "head"),
        P(None, "head"),
        P("head"),
        P(None, "head"),
        P("head"),
        P("head"),
        P("head"),
        P("head"),
        P("head"),
        P("head", None),
        P("seq", None),
    )
    out_specs = (
        P("seq", None),
        P("seq", None),
        P(),
        P(None, None, "head"),
        P(None, "head"),
        P(None, "head"),
        P(None, "head"),
        P("head"),
        P(None, "head"),
        P("head"),
        P("head"),
        P("head"),
        P("head"),
        P("head"),
        P("head", None),
    )
    return jax.shard_map(shards, mesh=mesh, in_specs=in_specs, out_specs=out_specs, check_vma=False)
```

```python
import functools

import jax
import jax.numpy as jnp
from jax import lax
from jax.experimental import pallas as pl
from jax.experimental.pallas import tpu as pltpu
from jax.sharding import PartitionSpec as P

MESH = pl.DeviceIdType.MESH
f32 = jnp.float32
bf16 = jnp.bfloat16
VMEM = pl.BlockSpec(memory_space=pltpu.VMEM)
HBM = pl.BlockSpec(memory_space=pl.ANY)
DMA = pltpu.SemaphoreType.DMA


def rows_of(ref, start, size):
    return ref.at[pl.ds(pl.multiple_of(start, size), size)]


def other_of(axis, k):
    size = lax.axis_size(axis)
    return lax.rem(lax.axis_index(axis) + k, size)


def greet(*axes):
    barrier = pltpu.get_barrier_semaphore()
    count = 0
    for axis in axes:
        size = lax.axis_size(axis)
        count += size - 1

        @pl.loop(1, size)
        def _(k):
            pl.semaphore_signal(barrier, inc=1, device_id={axis: other_of(axis, k)}, device_id_type=MESH)
    pl.semaphore_wait(barrier, count)


class Pace:
    def __init__(self, phases, pace, behind, most):
        self.phases, self.pace, self.behind, self.most = phases, pace, behind, most
        self.before = [0]
        for n, (points, _, _) in enumerate(phases):
            self.before.append(self.count(n, points - 1) if points else self.before[-1])

    def count(self, phase, k):
        _, start, step = self.phases[phase]
        low, top = self.before[phase], self.most
        value = (start + k * step - self.behind) // self.pace
        if isinstance(value, int):
            return max(low, min(top, value))
        return jnp.clip(value, low, top)

    def span(self, phase, k):
        if isinstance(k, int):
            return (self.count(phase, k - 1) if k else self.before[phase]), self.count(phase, k)
        return jnp.where(k == 0, self.before[phase], self.count(phase, k - 1)), self.count(phase, k)


class LineSum:
    AHEAD = 3

    def __init__(self, own, got, total, out, place, sems, block):
        self.own, self.got, self.total, self.out, self.place = own, got, total, out, place
        self.send1, self.got_in, self.got_total, self.send2, self.stored = (sems.at[i] for i in range(5))
        self.block = block
        self.half = own.shape[0] // block
        self.count = 2 * self.half
        size, me = lax.axis_size("head"), lax.axis_index("head")
        left = me < size // 2
        self.mid = (me == size // 2 - 1) | (me == size // 2)
        self.has_outer = (me > 0) & (me < size - 1)
        self.inner = jnp.where(left, me + 1, me - 1)
        self.outer = jnp.clip(jnp.where(left, me - 1, me + 1), 0, size - 1)

    @staticmethod
    def sems(rows, block):
        return DMA((5, 2 * rows // block))

    def rows(self, b):
        return pl.ds(pl.multiple_of(b * self.block, self.block), self.block)

    def slot(self, b):
        return self.rows(lax.rem(b, self.half))

    def in_copy(self, b, to):
        return pltpu.make_async_remote_copy(
            src_ref=self.own.at[self.slot(b)], dst_ref=self.got.at[self.slot(b)],
            send_sem=self.send1.at[b], recv_sem=self.got_in.at[b], device_id={"head": to}, device_id_type=MESH)

    def cross_copy(self, b):
        return pltpu.make_async_remote_copy(
            src_ref=self.own.at[self.slot(b)], dst_ref=self.total.at[self.rows(b)],
            send_sem=self.send1.at[b], recv_sem=self.got_total.at[b],
            device_id={"head": self.inner}, device_id_type=MESH)

    def out_copy(self, b, to):
        return pltpu.make_async_remote_copy(
            src_ref=self.total.at[self.rows(b)], dst_ref=self.total.at[self.rows(b)],
            send_sem=self.send2.at[b], recv_sem=self.got_total.at[b],
            device_id={"head": to}, device_id_type=MESH)

    def store(self, b):
        return pltpu.make_async_copy(
            self.total.at[self.rows(b)], self.out.at[self.rows(self.place(b))], self.stored.at[b])

    def inward(self, b):
        rows = self.slot(b)
        self.in_copy(b, self.outer).wait_recv()
        self.own[rows] = self.got[rows] + self.own[rows]

        @pl.when(self.mid)
        def _():
            self.cross_copy(b).start()

        @pl.when(jnp.logical_not(self.mid))
        def _():
            self.in_copy(b, self.inner).start()

    def outward(self, b):
        rows = self.rows(b)
        self.cross_copy(b).wait_recv()

        @pl.when(self.has_outer)
        def _():
            self.cross_copy(b).wait_send()

        @pl.when(self.mid)
        def _():
            self.total[rows] = self.own[self.slot(b)] + self.total[rows]

        @pl.when(self.has_outer)
        def _():
            self.out_copy(b, self.outer).start()
        self.store(b).start()

    def serve(self, first, last, lag):
        @pl.when(self.has_outer)
        def _():
            @pl.loop(first, last)
            def _(b):
                @pl.when(b < self.count)
                def _():
                    self.inward(b)

                @pl.when(b >= lag)
                def _():
                    self.outward(b - lag)

    def send(self, first, last):
        @pl.when(jnp.logical_not(self.has_outer))
        def _():
            @pl.loop(first, last)
            def _(b):
                @pl.when(b >= self.AHEAD)
                def _():
                    self.in_copy(b - self.AHEAD, self.inner).wait_send()

                @pl.when(b >= self.half)
                def _():
                    self.outward(b - self.half)
                self.in_copy(b, self.inner).start()

    def finish(self):
        @pl.when(jnp.logical_not(self.has_outer))
        def _():
            pl.loop(self.half, self.count)(self.outward)

            @pl.loop(self.count - self.AHEAD, self.count)
            def _(b):
                self.in_copy(b, self.inner).wait_send()

        @pl.loop(0, self.count)
        def _(b):
            self.store(b).wait()

            @pl.when(self.has_outer)
            def _():
                self.out_copy(b, self.outer).wait_send()


class PairedSum:
    def __init__(self, own, pair, mine, slots, theirs, sems):
        self.own, self.pair, self.mine, self.slots, self.theirs = own, pair, mine, slots, theirs
        self.sems = sems
        self.me = lax.axis_index("seq")
        self.chip, self.odd = self.me // 2, lax.rem(self.me, 2)
        self.partner = self.me + 1 - 2 * self.odd
        self.chips, self.piece = own.shape[0], own.shape[1] // 2

    @staticmethod
    def scratch(rows, width):
        seq = lax.axis_size("seq")
        piece = max(16, rows // seq)
        part = pltpu.VMEM((seq // 2, piece, width), bf16)
        return [pltpu.VMEM((seq // 2, 2 * piece, width), bf16)] + [part] * 4 + [DMA((8, seq // 2))]

    def half(self, odd):
        return pl.ds(pl.multiple_of(odd * self.piece, self.piece), self.piece)

    def swap_copy(self):
        return pltpu.make_async_remote_copy(
            src_ref=self.own.at[:, self.half(1 - self.odd)], dst_ref=self.pair,
            send_sem=self.sems.at[0, 0], recv_sem=self.sems.at[1, 0],
            device_id={"seq": self.partner}, device_id_type=MESH)

    def back_copy(self):
        return pltpu.make_async_remote_copy(
            src_ref=self.pair, dst_ref=self.theirs,
            send_sem=self.sems.at[0, 1], recv_sem=self.sems.at[1, 1],
            device_id={"seq": self.partner}, device_id_type=MESH)

    def scatter_copy(self, to, source):
        return pltpu.make_async_remote_copy(
            src_ref=self.mine.at[to], dst_ref=self.slots.at[source],
            send_sem=self.sems.at[2, to], recv_sem=self.sems.at[3, source],
            device_id={"seq": 2 * to + self.odd}, device_id_type=MESH)

    def gather_copy(self, owner, to):
        return pltpu.make_async_remote_copy(
            src_ref=self.pair.at[owner], dst_ref=self.pair.at[owner],
            send_sem=self.sems.at[4, to], recv_sem=self.sems.at[5, owner],
            device_id={"seq": 2 * to + self.odd}, device_id_type=MESH)

    def release(self, free):
        pl.semaphore_signal(free, inc=1, device_id={"seq": self.partner}, device_id_type=MESH)

    def others(self, do):
        @pl.loop(1, self.chips)
        def _(k):
            do(lax.rem(self.chip + k, self.chips))

    def swap(self):
        self.swap_copy().start()

    def scatter(self):
        self.swap_copy().wait()
        self.mine[...] = (self.own[:, self.half(self.odd)].astype(f32) + self.pair[...].astype(f32)).astype(bf16)
        self.others(lambda other: self.scatter_copy(other, self.chip).start())

    def gather(self):
        self.others(lambda other: self.scatter_copy(self.chip, other).wait_recv())
        self.others(lambda other: self.scatter_copy(other, self.chip).wait_send())
        self.slots[self.chip] = self.mine[self.chip]
        total = self.slots[0].astype(f32)
        for k in range(1, self.chips):
            total = total + self.slots[k].astype(f32)
        self.pair[self.chip] = total.astype(bf16)
        self.others(lambda other: self.gather_copy(self.chip, other).start())

    def back(self):
        self.others(lambda other: self.gather_copy(other, self.chip).wait_recv())
        self.back_copy().start()

    def stores(self, out):
        for k in range(min(self.chips, out.shape[0] // (2 * self.piece))):
            for n, (odd, ref) in enumerate(((self.odd, self.pair), (1 - self.odd, self.theirs))):
                start = pl.multiple_of((2 * k + odd) * self.piece, self.piece)
                yield pltpu.make_async_copy(
                    ref.at[k], out.at[pl.ds(start, self.piece)], self.sems.at[6 + n, k])

    def finish(self, out):
        self.back_copy().wait()
        self.others(lambda other: self.gather_copy(self.chip, other).wait_send())
        for copy in self.stores(out):
            copy.start()

    def stored(self, out):
        for copy in self.stores(out):
            copy.wait()


class Swap:
    def __init__(self, axis, own, slots, sems):
        self.axis, self.own, self.slots = axis, own, slots
        self.send, self.got = sems.at[0], sems.at[1]
        self.size, self.me = lax.axis_size(axis), lax.axis_index(axis)

    def copy(self, to, source):
        return pltpu.make_async_remote_copy(
            src_ref=self.own, dst_ref=self.slots.at[source],
            send_sem=self.send.at[to], recv_sem=self.got.at[source],
            device_id={self.axis: to}, device_id_type=MESH)

    def start(self):
        @pl.loop(1, self.size)
        def _(k):
            self.copy(other_of(self.axis, k), self.me).start()
        self.slots[self.me] = self.own[...]

    def wait(self):
        @pl.loop(1, self.size)
        def _(k):
            self.copy(self.me, other_of(self.axis, k)).wait_recv()

    def total(self):
        out = self.slots[0]
        for k in range(1, self.size):
            out = out + self.slots[k]
        return out

    def finish(self):
        @pl.loop(1, self.size)
        def _(k):
            self.copy(other_of(self.axis, k), self.me).wait_send()


class DeviceScan:
    def __init__(self, backward, total, fade, lead, out, got, got_fade, sent, sent_fade, sems):
        self.backward, self.total, self.fade, self.lead, self.out = backward, total, fade, lead, out
        self.got, self.got_fade, self.sent, self.sent_fade, self.sems = got, got_fade, sent, sent_fade, sems
        self.me = lax.axis_index("seq")
        self.rounds = lax.axis_size("seq").bit_length() - 1

    @staticmethod
    def scratch(state, fade):
        rounds = lax.axis_size("seq").bit_length() - 1
        return [pltpu.VMEM(fade, f32), pltpu.VMEM(fade, f32)] + [
            pltpu.VMEM((rounds,) + state, bf16), pltpu.VMEM((rounds,) + fade, f32)] * 2 + [DMA((4, rounds))]

    def copies(self, k):
        return [
            pltpu.make_async_remote_copy(
                src_ref=src.at[k], dst_ref=dst.at[k],
                send_sem=self.sems.at[i, k], recv_sem=self.sems.at[i + 1, k],
                device_id={"seq": jnp.bitwise_xor(self.me, 1 << k)}, device_id_type=MESH)
            for src, dst, i in ((self.sent, self.got, 0), (self.sent_fade, self.got_fade, 2))]

    def begin(self, decay):
        self.fade[...] = decay
        self.out[...] = jnp.zeros_like(self.out)
        self.lead[...] = jnp.ones_like(self.lead)

    def start(self, k):
        self.sent[k] = self.total[...].astype(bf16)
        self.sent_fade[k] = self.fade[...]
        for copy in self.copies(k):
            copy.start()

    def finish(self, k):
        for copy in self.copies(k):
            copy.wait()
        later = lax.rem(self.me // (1 << k), 2) == (0 if self.backward else 1)

        @pl.when(later)
        def _():
            theirs = self.got[k].astype(f32)
            self.out[...] = self.out[...] + self.lead[0:1] * theirs
            self.total[...] = self.total[...] + self.fade[0:1] * theirs
            self.lead[...] = self.lead[...] * self.got_fade[k]

        @pl.when(jnp.logical_not(later))
        def _():
            self.total[...] = self.got[k].astype(f32) + self.got_fade[k, 0:1] * self.total[...]
        self.fade[...] = self.fade[...] * self.got_fade[k]

    def run(self, between=None):
        for k in range(self.rounds):
            self.start(k)
            if between is not None:
                between(k)
            self.finish(k)


GROUP = 256
STRIP = 128
GAP = 200.0
epsilon = 1e-05
LIMIT = 56 * 2**20


def dot(a, b):
    return jnp.dot(a, b, preferred_element_type=f32)


def dot_nt(a, b):
    return lax.dot_general(a, b, (((1,), (1,)), ((), ())), preferred_element_type=f32)


def dot_tn(a, b):
    return lax.dot_general(a, b, (((0,), (0,)), ((), ())), preferred_element_type=f32)


def split3(v):
    one = v.astype(bf16)
    rest = v - one.astype(f32)
    two = rest.astype(bf16)
    return one, two, (rest - two.astype(f32)).astype(bf16)


def exact_left(ones, v):
    width = v.shape[1]
    out = dot(ones, jnp.concatenate(split3(v), axis=1))
    return out[:, :width] + out[:, width : 2 * width] + out[:, 2 * width :]


def head_sum(v, group_ones):
    high = v.astype(bf16)
    low = (v - high.astype(f32)).astype(bf16)
    return dot(high, group_ones) + dot(low, group_ones)


def sigmoid(v):
    return 1.0 / (1.0 + jnp.exp(-v))


def softplus(v):
    return jnp.maximum(v, 0.0) + jnp.log1p(jnp.exp(-jnp.abs(v)))


def spread(cols, first, heads, head_dim):
    rows = cols.shape[0]
    per = 128 // head_dim
    lane = lax.broadcasted_iota(jnp.int32, (rows, 128), 1)
    tiles = []
    for at in range(0, heads, per):
        tile = cols[:, first + at : first + at + 1]
        for k in range(1, per):
            tile = jnp.where(lane < k * head_dim, tile, cols[:, first + at + k : first + at + k + 1])
        tiles.append(jnp.broadcast_to(tile, (rows, 128)))
    return jnp.concatenate(tiles, axis=1)


def norm_rows(block, gain):
    value = block.astype(f32)
    inv = lax.rsqrt(jnp.mean(value * value, axis=1, keepdims=True) + epsilon)
    return (value * inv * gain).astype(bf16)


def whole(shape):
    return pl.BlockSpec(shape, lambda g: (0,) * len(shape))


def lane_groups(rows, *parts):
    lane = lax.broadcasted_iota(jnp.int32, (rows, 128), 1)
    out = parts[-1]
    for k in range(len(parts) - 2, -1, -1):
        out = jnp.where(lane < 8 * (k + 1), parts[k], out)
    return out


FRONT = 512
RAW, STEP, CUM, DEV, KEEP = 0, 8, 16, 24, 32


def head_lanes(row, heads, lane):
    out = jnp.zeros(lane.shape, f32)
    for k in range(heads):
        out = jnp.where(lane % 8 == k, row[:, k : k + 1], out)
    return out


def loads_of(source, target, sems, first):
    parts = sems.shape[0]
    rows = source.shape[0] // parts
    return [pltpu.make_async_copy(source.at[pl.ds(k * rows, rows), pl.ds(first, target.shape[1])],
                                  target.at[pl.ds(k * rows, rows)], sems.at[k]) for k in range(parts)]


def front_kernel(heads, head_dim, state_dim, count,
                 tokens, last_tokens, zx, flags, gain, proj_bc, proj_dt, conv_x_weight, conv_x_bias,
                 conv_bc_weight, conv_bc_bias, dt_bias, a_log, skip, norm_gain,
                 normed_out, x_in_out, x_conv_out, bc_in_out, bc_conv_out, heads_out, entering, decay_out,
                 halo_out, weights_hbm, conv_w_out, params, gains_out, mask_out,
                 normed, x_active, tail_rows, landed, head_low, proj_all, conv_bc, conv_all, flag_cols, flag_ext,
                 x_ext, bc_ext, state, running, x_weights, weights_out, lead, fade,
                 scan_got, scan_got_fade, scan_sent, scan_sent_fade, scan_sems, proj_sems, conv_sems, row_sems, load_sems,
                 store_sem):
    at = pl.program_id(0)
    rows = tokens.shape[0]
    inner = heads * head_dim
    bc_width = 2 * state_dim
    bc_part = proj_bc.shape[0]
    seq, me = lax.axis_size("seq"), lax.axis_index("seq")
    block = lax.rem(at, count)
    mine = pl.ds(pl.multiple_of(block * rows, rows), rows)
    swaps = [Swap("head", proj_bc, proj_all, proj_sems), Swap("head", conv_bc, conv_all, conv_sems)]
    row_copy = pltpu.make_async_remote_copy(
        src_ref=tail_rows, dst_ref=landed, send_sem=row_sems.at[0], recv_sem=row_sems.at[1],
        device_id={"seq": lax.rem(me + 1, seq)}, device_id_type=MESH)
    lane_row = lax.broadcasted_iota(jnp.int32, (1, 128), 1)
    loads = loads_of(zx, x_weights, load_sems, inner)
    weights_store = pltpu.make_async_copy(weights_out, weights_hbm, store_sem.at[0])

    @pl.when(at == 0)
    def _():
        for copy in loads:
            copy.start()
        final = 1.0 - flags[flags.shape[0] - 1 :].astype(f32)
        one, two = final[:, 127:128], final[:, 126:127]
        row = lax.broadcasted_iota(jnp.int32, (16, 128), 0)
        mask = jnp.where(row == 15, 1.0, jnp.where(row == 14, one, jnp.where(row == 13, one * two, 0.0)))
        mask_out[...] = mask
        tail_rows[...] = (last_tokens[...].astype(f32) * mask[:, 0:1]).astype(bf16)
        conv_bc[...] = jnp.zeros_like(conv_bc)
        conv_bc[0:4, :bc_part] = conv_bc_weight[...].astype(f32)
        conv_bc[4:5, :bc_part] = conv_bc_bias[...]
        greet("head", "seq")
        row_copy.start()
        for each in swaps:
            each.start()
        params[...] = jnp.zeros_like(params)
        params[0:1] = head_lanes(dt_bias[...], heads, lane_row)
        params[1:2] = -jnp.exp(head_lanes(a_log[...], heads, lane_row))
        gains_out[...] = jnp.zeros_like(gains_out)
        gains_out[0:1] = norm_gain[...]
        gains_out[1:2] = spread(head_lanes(skip[...], heads, lane_row), 0, heads, head_dim)
        flat = flags[...].astype(f32)
        turned = jnp.concatenate([flat, jnp.zeros((128 - flat.shape[0], 128), f32)], axis=0).T
        conv_w_out[...] = jnp.zeros_like(conv_w_out)
        conv_w_out[0:4, :inner] = conv_x_weight[...].astype(f32)
        conv_w_out[4:5, :inner] = conv_x_bias[...]
        for k in range(flat.shape[0]):
            flag_cols[k * 128 : (k + 1) * 128] = jnp.broadcast_to(turned[:, k : k + 1], (128, 128))
        flag_ext[0:8] = jnp.zeros((8, 128), f32)

    def keeps(flag):
        flag_ext[8:] = flag
        one = 1.0 - flag
        two = one * (1.0 - flag_ext[7 : 7 + rows])
        three = two * (1.0 - flag_ext[6 : 6 + rows])
        flag_ext[0:8] = flag_ext[rows:]
        return one, two, three

    def convolve(ext, current, keep, first, last):
        ext[8:] = current
        total = conv_w_out[4:5, first:last] + conv_w_out[0:1, first:last] * current
        for j in range(1, 4):
            total = total + conv_w_out[j : j + 1, first:last] * ext[pl.ds(8 - j, rows)] * keep[j - 1][:, 0:1]
        ext[0:8] = ext[rows:]
        return total

    @pl.when(at < count)
    def _():
        low = norm_rows(tokens[...], gain[...])
        normed[mine] = low
        normed_out[...] = low

        @pl.when(at == 0)
        def _():
            for copy in loads:
                copy.wait()
        x_in = dot(low, x_weights[...]).astype(bf16)
        x_in_out[...] = x_in

        @pl.when(at == 0)
        def _():
            row_copy.wait()
            head_low[...] = norm_rows(landed[...], gain[...])
            ahead = jnp.where(me > 0, dot(head_low[...], x_weights[...]), 0.0).astype(bf16)
            halo_out[:, :inner] = ahead
            x_ext[0:8] = ahead[8:].astype(f32)
        total = convolve(x_ext, x_in.astype(f32), keeps(flag_cols[mine]), 0, inner)
        x_conv_out[...] = total
        x_active[mine] = total * sigmoid(total)

    @pl.when(at == count)
    def _():
        for each in swaps:
            each.wait()
            each.finish()
        heads_there = proj_all.shape[0]
        for k in range(heads_there):
            weights_out[k * bc_part : (k + 1) * bc_part] = proj_all[k]
        eight = jnp.concatenate([proj_dt[...].astype(f32)] + (
            [jnp.zeros((8 - heads, proj_dt.shape[1]), f32)] if heads < 8 else []), axis=0)
        weights_out[bc_width:] = jnp.concatenate([eight] * 16, axis=0).astype(bf16)
        conv_w_out[:, inner:] = jnp.concatenate([conv_all[k, :, :bc_part] for k in range(heads_there)], axis=1)
        weights_store.start()
        ahead = jnp.where(me > 0, dot_nt(head_low[...], weights_out[:bc_width]), 0.0).astype(bf16)
        halo_out[:, inner:] = ahead
        bc_ext[0:8] = ahead[8:].astype(f32)
        state[...] = jnp.zeros_like(state)
        running[...] = jnp.zeros_like(running)
        flag_ext[0:8] = jnp.zeros((8, 128), f32)

    @pl.when(at >= count)
    def _():
        raw = dot_nt(normed[mine], weights_out[...])
        bc_in = raw[:, :bc_width].astype(bf16)
        bc_in_out[...] = bc_in
        flag = flag_cols[mine]
        keep = keeps(flag)
        total = convolve(bc_ext, bc_in.astype(f32), keep, inner, inner + bc_width)
        bc_conv_out[...] = total
        b_proj = (total[:, :state_dim] * sigmoid(total[:, :state_dim])).astype(bf16)

        order_r = lax.broadcasted_iota(jnp.int32, (GROUP, GROUP), 0)
        order_c = lax.broadcasted_iota(jnp.int32, (GROUP, GROUP), 1)
        lower = (order_r >= order_c).astype(bf16)
        lane = lax.broadcasted_iota(jnp.int32, (GROUP, 128), 1)
        for lo in range(0, rows, GROUP):
            part = slice(lo, lo + GROUP)
            step_raw = raw[part, bc_width:]
            step = softplus(step_raw + params[0:1])
            log_decay = step * params[1:2] - GAP * flag[part]
            cum = exact_left(lower, log_decay)
            kept = jnp.where(lane < KEEP + 1, keep[0][part], jnp.where(lane < KEEP + 2, keep[1][part], keep[2][part]))
            heads_out[part] = lane_groups(GROUP, step_raw, step, cum, cum + running[0:1], kept)
            end = cum[GROUP - 1 :]
            running[...] = running[...] + end
            weight = step * jnp.exp(end - cum)
            x_part = x_active[pl.ds(pl.multiple_of(block * rows + lo, GROUP), GROUP)]
            scaled = (x_part * spread(weight, 0, heads, head_dim)).astype(bf16)
            state[...] = state[...] * spread(jnp.exp(end), 0, heads, head_dim) + dot_tn(b_proj[part], scaled)

    @pl.when(at == 2 * count - 1)
    def _():
        decay = spread(jnp.exp(running[...]), 0, heads, head_dim)
        decay_out[...] = decay
        scan = DeviceScan(False, state, fade, lead, entering, scan_got, scan_got_fade, scan_sent,
                          scan_sent_fade, scan_sems)
        scan.begin(decay)
        scan.run()
        weights_store.wait()


def front(tokens, zx, flags, gain, proj_bc, proj_dt, conv_x_weight, conv_x_bias, conv_bc_weight, conv_bc_bias,
          dt_bias, a_log, skip, norm_gain, heads, head_dim, state_dim):
    length, width = tokens.shape
    block = FRONT
    count = length // block
    inner = heads * head_dim
    conv = inner + 2 * state_dim
    head_count = lax.axis_size("head")

    def early(cols):
        return pl.BlockSpec((block, cols), lambda g: (jnp.minimum(g, count - 1), 0))

    def late(cols):
        return pl.BlockSpec((block, cols), lambda g: (jnp.maximum(g - count, 0), 0))
    shape = jax.ShapeDtypeStruct
    state, fade = (state_dim, inner), (8, inner)
    rest = 2 * state_dim + 128
    return pl.pallas_call(
        functools.partial(front_kernel, heads, head_dim, state_dim, count),
        grid=(2 * count,),
        out_shape=(shape((length, width), bf16), shape((length, inner), bf16), shape((length, inner), f32),
                   shape((length, conv - inner), bf16), shape((length, conv - inner), f32),
                   shape((length, 128), f32), shape(state, f32),
                   shape(fade, f32), shape((16, conv), bf16), shape((rest, width), bf16),
                   shape((8, conv), f32), shape((8, 128), f32), shape((8, inner), f32), shape((16, 128), f32)),
        in_specs=[early(width), pl.BlockSpec((16, width), lambda g: (length // 16 - 1, 0)), HBM] + [VMEM] * 12,
        out_specs=(early(width), early(inner), early(inner), late(conv - inner), late(conv - inner), late(128))
        + (VMEM,) * 3 + (HBM,) + (VMEM,) * 4,
        scratch_shapes=[
            pltpu.VMEM((length, width), bf16), pltpu.VMEM((length, inner), f32),
            pltpu.VMEM((16, width), bf16), pltpu.VMEM((16, width), bf16), pltpu.VMEM((16, width), bf16),
            pltpu.VMEM((head_count,) + proj_bc.shape, bf16), pltpu.VMEM((8, 128), f32),
            pltpu.VMEM((head_count, 8, 128), f32), pltpu.VMEM((length, 128), f32),
            pltpu.VMEM((block + 8, 128), f32), pltpu.VMEM((block + 8, inner), f32),
            pltpu.VMEM((block + 8, conv - inner), f32), pltpu.VMEM(state, f32), pltpu.VMEM((8, 128), f32),
            pltpu.VMEM((width, inner), bf16), pltpu.VMEM((rest, width), bf16)]
        + DeviceScan.scratch(state, fade) + [DMA((2, head_count)), DMA((2, head_count)), DMA((2,)), DMA((4,)), DMA((1,))],
        compiler_params=pltpu.CompilerParams(
            dimension_semantics=("arbitrary",), collective_id=3, has_side_effects=True,
            vmem_limit_bytes=LIMIT),
        name="front",
    )(tokens, tokens, zx, flags, gain, proj_bc, proj_dt, conv_x_weight, conv_x_bias, conv_bc_weight,
      conv_bc_bias, dt_bias, a_log, skip, norm_gain)


def strips(rows):
    return [(lo, lo + STRIP) for lo in range(0, rows, STRIP)]


def mix_step(heads, head_dim, state_dim, at,
             x_conv, bc_conv, heads_in, normed, zx, cot, out_proj, gains, entering,
             ssm_out, d_normed_out, partial_out, sums_out, starts_out, state, between):
    rows = x_conv.shape[0]
    inner = heads * head_dim
    per = 128 // head_dim

    @pl.when(at == 0)
    def _():
        state[...] = entering[...]

    values = jnp.concatenate([x_conv[...], bc_conv[...]], axis=1)
    active = values * sigmoid(values)
    x = active[:, :inner]
    b_proj = active[:, inner : inner + state_dim].astype(bf16)
    c_proj = active[:, inner + state_dim :].astype(bf16)
    info = heads_in[...]
    flipped = info.T
    stepped = x * spread(info, STEP, heads, head_dim)
    low = stepped.astype(bf16)
    scores = dot_nt(c_proj, b_proj)
    lane = lax.broadcasted_iota(jnp.int32, (rows, 128), 1)
    tiles = []
    for pair in range(heads // per):
        tile = low[:, pair * 128 : (pair + 1) * 128]
        weights, masked = [], []
        for k in range(per):
            head = pair * per + k
            masked.append(jnp.where((lane >= k * head_dim) & (lane < (k + 1) * head_dim), tile,
                                    jnp.zeros_like(tile)))
            parts = []
            for lo, hi in strips(rows):
                gap = info[lo:hi, CUM + head : CUM + head + 1] - flipped[CUM + head : CUM + head + 1, :hi]
                ok = (lax.broadcasted_iota(jnp.int32, (STRIP, hi), 0) + lo
                      >= lax.broadcasted_iota(jnp.int32, (STRIP, hi), 1))
                part = (jnp.exp(jnp.where(ok, gap, -1e30)) * scores[lo:hi, :hi]).astype(bf16)
                if hi < rows:
                    part = jnp.concatenate([part, jnp.zeros((STRIP, rows - hi), bf16)], axis=1)
                parts.append(part)
            weights.append(jnp.concatenate(parts, axis=0))
        tiles.append(dot(jnp.concatenate(weights, axis=1), jnp.concatenate(masked, axis=0)))
        if pair == heads // per // 2 - 1:
            between()
    inside = jnp.concatenate(tiles, axis=1)
    cum = info[:, CUM : CUM + 8]
    end = info[rows - 1 : rows]
    start = state[...]
    starts_out[at] = start.astype(bf16)
    grown = spread(jnp.exp(info), CUM, heads, head_dim)
    result = inside + grown * dot(c_proj, start.astype(bf16)) + gains[1:2] * x
    fade = spread(jnp.exp(end - info), CUM, heads, head_dim)
    state[...] = start * spread(jnp.exp(end), CUM, heads, head_dim) + dot_tn(b_proj, (stepped * fade).astype(bf16))
    ssm_out[...] = result
    z = dot(normed[...], zx[:, :inner])
    gated = result * (z * sigmoid(z))
    d_normed = dot_nt(cot[...], out_proj[...])
    d_normed_out[...] = d_normed.astype(bf16)
    scaled = gated * gains[0:1]
    partial_out[...] = dot(scaled.astype(bf16), out_proj[...]).astype(bf16)
    squares = jnp.sum(gated * gated, axis=1, keepdims=True)
    cross = jnp.sum(d_normed * scaled, axis=1, keepdims=True)
    turned = jnp.where(lane == 0, squares, cross).T
    sums_out[0, pl.ds(at, 1)] = turned[0:1]
    sums_out[1, pl.ds(at, 1)] = turned[1:2]


def gate_step(heads, head_dim, state_dim, all_channels, at,
              ssm, d_normed, sums, x_conv, bc_conv, heads_in, normed, zx, cot, gains,
              d_ssm_out, d_gate_out, grad_out, rows_out, total_out):
    rows = ssm.shape[0]
    inner = heads * head_dim

    @pl.when(at == 0)
    def _():
        grad_out[...] = jnp.zeros_like(grad_out)
        rows_out[...] = jnp.zeros_like(rows_out)
        total_out[...] = jnp.zeros_like(total_out)

    tall = jnp.concatenate([sums[0, pl.ds(at, 1)], sums[1, pl.ds(at, 1)], jnp.zeros((126, rows), f32)], axis=0).T
    inv = lax.rsqrt(tall[:, 0:1] / all_channels + epsilon)
    cross = tall[:, 1:2] / all_channels
    z = dot(normed[...], zx[:, :inner])
    s = sigmoid(z)
    y = ssm[...]
    gated = y * (z * s)
    gain = gains[0:1]
    back = d_normed[...].astype(f32)
    unit = gated * inv
    d_gated = inv * (back * gain - unit * (inv * cross))
    grad_out[:, : cot.shape[1]] += dot_tn((unit * gain).astype(bf16), cot[...])
    d_ssm = d_gated * (z * s)
    d_ssm_out[...] = d_ssm
    d_gate_out[...] = (d_gated * y * (s * (1.0 + z * (1.0 - s)))).astype(bf16)
    x_values, c_values = x_conv[...], bc_conv[:, state_dim:]
    rows_out[0:1] += jnp.sum(back * unit, axis=0, keepdims=True)
    rows_out[1:2] += jnp.sum(d_ssm * (x_values * sigmoid(x_values)), axis=0, keepdims=True)
    c_proj = (c_values * sigmoid(c_values)).astype(bf16)
    grown = spread(jnp.exp(heads_in[...]), DEV, heads, head_dim)
    total_out[...] += dot_tn(c_proj, (grown * d_ssm).astype(bf16))


def back_step(heads, head_dim, state_dim, first_step, last_step,
              d_ssm, x_conv, bc_conv, x_in, bc_in, heads_in, start, entering, conv_w, params, skip, conv_halo,
              d_conv_in_out, d_step_out, conv_grads, head_grads, halo_out,
              lam, later, later_info, between):
    rows = d_ssm.shape[0]
    inner = heads * head_dim
    per = 128 // head_dim

    @pl.when(first_step)
    def _():
        lam[...] = entering[...]
        conv_grads[...] = jnp.zeros_like(conv_grads)
        head_grads[...] = jnp.zeros_like(head_grads)
        for each in (later, later_info):
            each[rows:] = jnp.zeros((8, each.shape[1]), f32)

    values = jnp.concatenate([x_conv[...], bc_conv[...]], axis=1)
    gates = sigmoid(values)
    active = values * gates
    x = active[:, :inner]
    b_proj = active[:, inner : inner + state_dim].astype(bf16)
    c_proj = active[:, inner + state_dim :].astype(bf16)
    info = heads_in[...]
    flipped = info.T
    step = spread(info, STEP, heads, head_dim)
    stepped = x * step
    low = stepped.astype(bf16)
    dy = d_ssm[...]
    dy_low = dy.astype(bf16)
    scores = dot_nt(b_proj, c_proj)
    lane = lax.broadcasted_iota(jnp.int32, (rows, 128), 1)
    lane_one = lax.broadcasted_iota(jnp.int32, (STRIP, 128), 1)
    cuts = strips(rows)
    d_scores = [jnp.zeros((STRIP, rows - lo), f32) for lo, _ in cuts]
    d_rows = []
    d_cols = [jnp.zeros((STRIP, 128), f32) for _ in cuts]
    tiles = []
    for pair in range(heads // per):
        tile = low[:, pair * 128 : (pair + 1) * 128]
        dy_tile = dy_low[:, pair * 128 : (pair + 1) * 128]
        owns = [(lane >= k * head_dim) & (lane < (k + 1) * head_dim) for k in range(per)]
        stacked = jnp.concatenate([jnp.where(own, tile, jnp.zeros_like(tile)) for own in owns], axis=0)
        all_pairs = dot_nt(stacked, dy_tile)
        weights = []
        for k in range(per):
            head = pair * per + k
            row_total = jnp.zeros((1, rows), f32)
            parts = []
            for n, (lo, hi) in enumerate(cuts):
                gap = flipped[CUM + head : CUM + head + 1, lo:] - info[lo:hi, CUM + head : CUM + head + 1]
                ok = (lax.broadcasted_iota(jnp.int32, (STRIP, rows - lo), 1)
                      >= lax.broadcasted_iota(jnp.int32, (STRIP, rows - lo), 0))
                decay = jnp.exp(jnp.where(ok, gap, -1e30))
                weight = decay * scores[lo:hi, lo:]
                part = weight.astype(bf16)
                if lo:
                    part = jnp.concatenate([jnp.zeros((STRIP, lo), bf16), part], axis=1)
                parts.append(part)
                pairs = all_pairs[k * rows + lo : k * rows + hi, lo:]
                d_scores[n] = d_scores[n] + pairs * decay
                moved = pairs * weight
                d_cols[n] = d_cols[n] - jnp.where(lane_one == head, jnp.sum(moved, axis=1, keepdims=True), 0.0)
                col = jnp.sum(moved, axis=0, keepdims=True)
                if lo:
                    col = jnp.concatenate([jnp.zeros((1, lo), f32), col], axis=1)
                row_total = row_total + col
            weights.append(jnp.concatenate(parts, axis=0))
            d_rows.append(row_total)
        dy_stack = jnp.concatenate([jnp.where(own, dy_tile, jnp.zeros_like(dy_tile)) for own in owns], axis=0)
        tiles.append(dot(jnp.concatenate(weights, axis=1), dy_stack))
        between(pair + 1)
    d_stepped = jnp.concatenate(tiles, axis=1)
    d_cum = jnp.concatenate(d_cols, axis=0)
    d_cum = d_cum + jnp.concatenate(d_rows + [jnp.zeros((128 - heads, rows), f32)], axis=0).T
    full = jnp.concatenate(
        [jnp.concatenate([jnp.zeros((STRIP, lo), f32), part], axis=1) if lo else part
         for part, (lo, _) in zip(d_scores, cuts)], axis=0).astype(bf16)
    d_b = dot(full, c_proj)
    d_c = dot_tn(full, b_proj)

    group_ones = (lax.broadcasted_iota(jnp.int32, (inner, 128), 0) // head_dim
                  == lax.broadcasted_iota(jnp.int32, (inner, 128), 1)).astype(bf16)
    after = lam[...]
    after_low = after.astype(bf16)
    end = info[rows - 1 : rows]
    grown = spread(jnp.exp(info), CUM, heads, head_dim)
    fade = spread(jnp.exp(end - info), CUM, heads, head_dim)
    end_grown = spread(jnp.exp(end), CUM, heads, head_dim)
    from_after = fade * dot(b_proj, after_low)
    d_stepped = d_stepped + from_after
    grown_dy = grown * dy
    grown_low = grown_dy.astype(bf16)
    left = stepped * from_after
    to_cum = head_sum(grown_dy * dot(c_proj, start) - left, group_ones)
    kept = jnp.sum(after * start.astype(f32), axis=0, keepdims=True) * end_grown
    kept = kept + jnp.sum(left, axis=0, keepdims=True)
    last = head_sum(jnp.broadcast_to(kept, (8, inner)), group_ones)[0:1]
    row_id = lax.broadcasted_iota(jnp.int32, (rows, 128), 0)
    d_cum = d_cum + to_cum + jnp.where(row_id == rows - 1, last, 0.0)
    d_c = d_c + dot_nt(grown_low, start)
    d_b = d_b + dot_nt((fade * stepped).astype(bf16), after_low)
    lam[...] = end_grown * after + dot_tn(c_proj, grown_low)
    d_step = dot((d_stepped * x).astype(bf16), group_ones)
    d_x = step * d_stepped + skip[0:1] * dy
    between(heads // per + 1)

    order_r = lax.broadcasted_iota(jnp.int32, (rows, rows), 0)
    order_c = lax.broadcasted_iota(jnp.int32, (rows, rows), 1)
    d_decay = exact_left((order_r <= order_c).astype(bf16), d_cum) * info[:, KEEP : KEEP + 1]
    rate = params[1:2]
    real = lane < heads
    step_raw = jnp.where(real, info, 0.0) + params[0:1]
    slope = sigmoid(step_raw)
    d_pre = jnp.where(real, (d_step + d_decay * rate) * slope, 0.0)
    d_step_out[...] = d_pre.astype(bf16)
    head_grads[0:1] += jnp.sum(d_pre, axis=0, keepdims=True)
    head_grads[1:2] += jnp.sum(jnp.where(real, d_decay * softplus(step_raw) * rate, 0.0), axis=0, keepdims=True)

    d_active = jnp.concatenate([d_x, d_b, d_c], axis=1)
    d_conv = d_active * (gates * (1.0 + values * (1.0 - gates)))
    taken = jnp.concatenate([x_in[...], bc_in[...]], axis=1).astype(f32)
    total = d_conv * conv_w[0:1]
    conv_grads[0:1] += jnp.sum(d_conv * taken, axis=0, keepdims=True)
    conv_grads[4:5] += jnp.sum(d_conv, axis=0, keepdims=True)
    later[0:rows] = d_conv
    later_info[0:rows] = info
    for j in range(1, 4):
        moved = later[pl.ds(j, rows)] * later_info[pl.ds(j, rows)][:, KEEP + j - 1 : KEEP + j]
        total = total + moved * conv_w[j : j + 1]
        conv_grads[j : j + 1] += jnp.sum(moved * taken, axis=0, keepdims=True)
    d_conv_in_out[...] = total.astype(bf16)

    @pl.when(last_step)
    def _():
        ahead = conv_halo[...].astype(f32)
        halo_out[...] = jnp.zeros_like(halo_out)
        for j in range(1, 4):
            first = later[0:8] * later_info[0:8, KEEP + j - 1 : KEEP + j]
            for t in range(j):
                row = 16 + t - j
                conv_grads[j : j + 1] += first[t : t + 1] * ahead[row : row + 1]
                halo_out[row - 8 : row - 7] += first[t : t + 1] * conv_w[j : j + 1]
    for each in (later, later_info):
        each[rows:] = each[0:8]


def block_place(per, blocks):
    def place(b):
        late = b - blocks - (per - 1)
        group = 2 * blocks - 2 * per - late // per * per + late % per
        second = jnp.where(b < blocks + per - 1, b + blocks - per, group)
        return jnp.where((b < blocks) | (b == 2 * blocks - 1), b, second)
    return place


def layer_kernel(heads, head_dim, state_dim, all_channels, count, block, lag, plans, steps, owners, taps,
                 x_conv, bc_conv, x_in, bc_in, heads_in, cot, normed, last_normed, op_hbm, gains, entering, decay,
                 conv_w, params, conv_halo, zx_hbm, weights, gain, tail_mask,
                 totals_out, sums_out, zx_out, op_out, bc_out, small_out,
                 own, got, total, held, ssm, d_normed, starts, state, leaving, later, later_info,
                 sums, sum_slots, lead, fade,
                 scan_got, scan_got_fade, scan_sent, scan_sent_fade, scan_sems,
                 grad, sum_own, sum_pair, sum_mine, sum_slot, sum_theirs, sum_sems, grad_bc,
                 bc_slots, bc_z, bc_res, small, small_slots, small_own, small_z,
                 d_conv, d_step, gate_rows, conv_grads, head_grads, halo_rows, landed,
                 line_sems, swap_sems, bc_sems, bcz_sems, small_sems, smallz_sems, row_sems, free_sem, zx,
                 out_proj, load_sems, op_load_sems):
    at = pl.program_id(0)
    rows, width = cot.shape
    inner = heads * head_dim
    bc_width = 2 * state_dim
    seq, head_count = lax.axis_size("seq"), lax.axis_size("head")
    me, my_head = lax.axis_index("seq"), lax.axis_index("head")
    per = rows // block
    line = LineSum(own, got, total, totals_out, block_place(per, count * per), line_sems, block)
    swap = Swap("head", sums, sum_slots, swap_sems)
    scan = DeviceScan(True, state, fade, lead, leaving, scan_got, scan_got_fade, scan_sent, scan_sent_fade,
                      scan_sems)
    op_rows = max(16, inner // seq)
    sum_refs = (sum_own, sum_pair, sum_mine, sum_slot, sum_theirs)
    op_sum = PairedSum(*(ref.at[:, : op_rows * (2 if ref is sum_own else 1), :width] for ref in sum_refs),
                       sum_sems.at[0])
    zx_sum = PairedSum(*(ref.at[:, :, : 2 * inner] for ref in sum_refs), sum_sems.at[1])
    small_swap = Swap("seq", small, small_slots, small_sems)
    both_swap = Swap("head", small_own, small_z, smallz_sems)
    row_copy = pltpu.make_async_remote_copy(
        src_ref=halo_rows, dst_ref=landed, send_sem=row_sems.at[0], recv_sem=row_sems.at[1],
        device_id={"seq": lax.rem(me + seq - 1, seq)}, device_id_type=MESH)
    served, sent = plans
    back_points = inner // 128 + 3
    back_at = at - 2 * count - 1
    last_step = back_at == count - 1

    def serve(phase, k):
        line.send(*sent.span(phase, k))
        line.serve(*served.span(phase, k), lag)

    def serve_mix(k):
        @pl.when(at > 0)
        def _():
            serve(1, MIX_POINTS * (at - 1) + k)

    loads = loads_of(zx_hbm, zx, load_sems, 0) + loads_of(op_hbm, out_proj, op_load_sems, 0)

    @pl.when(at == 0)
    def _():
        for copy in loads:
            copy.start()
        greet("head", "seq")
        state[...] = entering[...]
        for copy in loads:
            copy.wait()

    @pl.when(at < count)
    def _():
        mine = pl.ds(pl.multiple_of(at * rows, rows), rows)
        serve_mix(0)
        mix_step(heads, head_dim, state_dim, at, x_conv, bc_conv, heads_in, normed, zx, cot, out_proj, gains, entering,
                 ssm.at[mine], d_normed.at[mine], own.at[mine], sums, starts, state,
                 lambda: serve_mix(1))

    @pl.when(at == count - 1)
    def _():
        swap.start()

    @pl.when((at >= count) & (at < 2 * count))
    def _():
        serve(2, at - count)

    @pl.when(at == count)
    def _():
        swap.wait()
        sums_out[...] = swap.total()
        swap.finish()
        grad[...] = jnp.zeros_like(grad)
        gate_rows[...] = jnp.zeros_like(gate_rows)
        state[...] = jnp.zeros_like(state)

    @pl.when((at >= count) & (at < 2 * count))
    def _():
        here = at - count
        mine = pl.ds(pl.multiple_of(here * rows, rows), rows)
        gate_step(heads, head_dim, state_dim, all_channels, here,
                  ssm.at[mine], d_normed.at[mine], sums_out, x_conv, bc_conv, heads_in, normed, zx, cot, gains,
                  ssm.at[mine], d_normed.at[mine], grad.at[:inner], gate_rows, state)

    @pl.when(at == 2 * count)
    def _():
        for k in range(seq // 2):
            lo, hi = min(inner, k * 2 * op_rows), min(inner, (k + 1) * 2 * op_rows)
            if hi > lo:
                sum_own[k, : hi - lo, :width] = grad[lo:hi, :width].astype(bf16)
        scan.begin(decay[...])
        scan.run(lambda k: serve(3, k))
        op_sum.swap()
        grad[...] = jnp.zeros_like(grad)
        grad_bc[...] = jnp.zeros_like(grad_bc)
        small[...] = jnp.zeros_like(small)

    def project(block_low, gate_low, conv_low, rest_low):
        d_rows = dot_nt(conv_low, zx[:, inner:]) + dot(rest_low, weights[...])
        grad[:, inner : 2 * inner] += dot_tn(block_low, conv_low)
        if gate_low is not None:
            d_rows = d_rows + dot_nt(gate_low, zx[:, :inner])
            grad[:, :inner] += dot_tn(block_low, gate_low)
        grad_bc[...] += dot_tn(rest_low, block_low).reshape(grad_bc.shape)
        small[16:17] += jnp.sum(d_rows * block_low.astype(f32), axis=0, keepdims=True) / gain[...]
        return d_rows

    @pl.when(at > 2 * count)
    def _():
        here = 3 * count - at
        mine = pl.ds(pl.multiple_of(here * rows, rows), rows)
        serve(4, back_points * back_at)
        back_step(heads, head_dim, state_dim, back_at == 0, last_step,
                  ssm.at[mine], x_conv, bc_conv, x_in, bc_in, heads_in, starts[here], leaving, conv_w, params,
                  gains[1:2], conv_halo, d_conv, d_step, conv_grads, head_grads, halo_rows,
                  state, later, later_info, lambda k: serve(4, back_points * back_at + k))

        @pl.when(last_step)
        def _():
            row_copy.start()
        serve(4, back_points * back_at + back_points - 1)
        rest_low = jnp.concatenate([d_conv[:, inner:], d_step[...]], axis=1)
        d_rows = project(normed[...], d_normed[mine], d_conv[:, :inner], rest_low).astype(bf16)

        @pl.when(back_at == 0)
        def _():
            own[: rows - block] = d_rows[: rows - block]
            held[...] = d_rows[rows - block :]

        @pl.when(back_at > 0)
        def _():
            start = pl.multiple_of(back_at * rows - block, block)
            own[pl.ds(start, rows)] = d_rows

    @pl.when(back_at == 1)
    def _():
        op_sum.scatter()

    @pl.when(back_at == 3)
    def _():
        op_sum.gather()

    @pl.when(back_at == 5)
    def _():
        op_sum.back()

    piece = grad_bc.shape[1] // owners

    def bc_scatter(to, source):
        return pltpu.make_async_remote_copy(
            src_ref=grad_bc.at[:head_count, pl.ds(pl.multiple_of(to * piece, piece), piece)],
            dst_ref=bc_slots.at[source], send_sem=bc_sems.at[0, to], recv_sem=bc_sems.at[1, source],
            device_id={"seq": to}, device_id_type=MESH)

    def bc_gather(owner, to):
        rows = pl.ds(pl.multiple_of(owner * piece, piece), piece)
        return pltpu.make_async_remote_copy(
            src_ref=bc_res.at[rows], dst_ref=bc_res.at[rows],
            send_sem=bc_sems.at[2, to], recv_sem=bc_sems.at[3, owner],
            device_id={"seq": to}, device_id_type=MESH)

    def bc_swap(to, source):
        return pltpu.make_async_remote_copy(
            src_ref=bc_slots.at[me, to], dst_ref=bc_z.at[source],
            send_sem=bcz_sems.at[0, to], recv_sem=bcz_sems.at[1, source],
            device_id={"head": to}, device_id_type=MESH)

    @pl.when(last_step)
    def _():
        op_sum.finish(op_out)
        at_block = [served.before[-1], sent.before[-1]]

        def go(more):
            until = min(line.count + lag, at_block[0] + more)
            ahead = max(at_block[1], min(line.count - (0 if filled else 1), until + 2))
            line.send(at_block[1], ahead)
            line.serve(at_block[0], until, lag)
            at_block[:] = [until, ahead]
        filled = False
        go(steps[0])
        row_copy.wait()
        extra = jnp.where(me < seq - 1, landed[...] * tail_mask[8:, 0:1], 0.0)
        extra = jnp.concatenate([jnp.zeros_like(extra), extra], axis=0).astype(bf16)
        extra_rest = jnp.concatenate([extra[:, inner:], jnp.zeros((16, 128), bf16)], axis=1)
        more = project(last_normed[...], None, extra[:, :inner], extra_rest)
        final = held[...].astype(f32) + jnp.concatenate([jnp.zeros((block - 16, width), f32), more], axis=0)
        own[count * rows - block :] = final.astype(bf16)
        filled = True
        go(steps[1])

        op_sum.stored(op_out)
        op_sum.release(free_sem)
        pair_rows = sum_own.shape[1]
        for k in range(sum_own.shape[0]):
            sum_own[k, :, : 2 * inner] = grad[k * pair_rows : (k + 1) * pair_rows, : 2 * inner].astype(bf16)
        pl.semaphore_wait(free_sem, 1)
        zx_sum.swap()
        go(steps[2])
        small[0:8] += grad_bc[head_count, 0:8]
        small[8 : 9 + taps, :inner] = conv_grads[: taps + 1, :inner]
        small[8:10, inner : 2 * inner] = gate_rows[0:2]
        small[10:12, inner : inner + 128] = head_grads[0:2]
        small[17 : 18 + taps, :bc_width] = conv_grads[: taps + 1, inner:]
        small_swap.start()

        @pl.loop(1, seq)
        def _(k):
            to = other_of("seq", k)

            @pl.when(to < owners)
            def _():
                bc_scatter(to, me).start()

        go(steps[3])
        zx_sum.scatter()
        go(steps[4])
        small_swap.wait()
        sums_small = small_swap.total()
        lone = small.shape[0] - small_own.shape[0]
        small_out[:lone] = sums_small[:lone]
        small_own[...] = sums_small[lone:]
        both_swap.start()
        go(steps[5])

        @pl.when(me < owners)
        def _():
            @pl.loop(1, seq)
            def _(k):
                bc_scatter(me, other_of("seq", k)).wait_recv()
            bc_slots[me] = grad_bc[:head_count, pl.ds(pl.multiple_of(me * piece, piece), piece)]
            sums_bc = bc_slots[0]
            for k in range(1, seq):
                sums_bc = sums_bc + bc_slots[k]
            bc_slots[me] = sums_bc
            bc_z[my_head] = bc_slots[me, my_head]

            @pl.loop(1, head_count)
            def _(k):
                bc_swap(other_of("head", k), my_head).start()

        go(steps[6])
        zx_sum.gather()
        go(steps[7])
        both_swap.wait()
        small_out[lone:] = both_swap.total()

        @pl.when(me < owners)
        def _():
            @pl.loop(1, head_count)
            def _(k):
                bc_swap(my_head, other_of("head", k)).wait_recv()
            sums_bc = bc_z[0]
            for k in range(1, head_count):
                sums_bc = sums_bc + bc_z[k]
            bc_res[pl.ds(pl.multiple_of(me * piece, piece), piece)] = sums_bc

            @pl.loop(1, seq)
            def _(k):
                bc_gather(me, other_of("seq", k)).start()

        go(steps[8])
        zx_sum.back()
        go(steps[9])
        zx_sum.finish(zx_out)
        go(line.count + lag)
        line.finish()
        zx_sum.stored(zx_out)
        small_swap.finish()
        both_swap.finish()

        @pl.loop(1, seq)
        def _(k):
            other = other_of("seq", k)

            @pl.when(other < owners)
            def _():
                bc_gather(other, me).wait_recv()
                bc_scatter(other, me).wait_send()

            @pl.when(me < owners)
            def _():
                bc_gather(me, other).wait_send()
        bc_out[...] = bc_res[...]

        @pl.when(me < owners)
        def _():
            @pl.loop(1, head_count)
            def _(k):
                bc_swap(other_of("head", k), my_head).wait_send()


def layer(x_conv, bc_conv, x_in, bc_in, heads_in, cot, normed, out_proj, gains, entering, decay, conv_w, params,
          conv_halo, zx, weights, gain, tail_mask, heads, head_dim, state_dim, all_channels, taps):
    length, inner = x_conv.shape
    conv = inner + bc_conv.shape[1]
    count = length // GROUP
    width = cot.shape[1]
    seq, head_count = lax.axis_size("seq"), lax.axis_size("head")
    block = BLOCK
    pace = PACE * block // 64
    blocks = length // block
    per = GROUP // block
    lag = max(LAG, head_count // 2 - 1)
    back_points = inner // 128 + 3
    gate_at = MIX * count + SWAP
    scan_at = gate_at + GATE * count
    back_start = scan_at + SCAN
    rounds = seq.bit_length() - 1
    phases = [(MIX_POINTS, -(10**6), 0), (MIX_POINTS * (count - 1), MIX, MIX // MIX_POINTS), (count, gate_at, GATE),
              (rounds, scan_at, SCAN // rounds), (back_points * count, back_start, BACK // back_points)]
    served = Pace(phases, pace, LATE, 2 * blocks + lag)
    sent = Pace(phases, pace, EARLY, 2 * blocks)
    for k in range(count):
        point = (k + 1) * back_points - 1
        assert served.count(4, point) >= min(blocks, (k + 1) * per) + lag
        assert sent.count(4, point) >= min(blocks, (k + 1) * per) + LineSum.AHEAD
        for each in (served, sent):
            assert each.count(4, point) <= blocks + max(0, k * per - 1)
    steps = [step * 64 // block for step in STEPS]

    def by(cols, first, step):
        def index(g):
            ahead = jnp.where(g < count, g, jnp.where(g < 2 * count, g - count, jnp.minimum(3 * count - g, count - 1)))
            if first == 2:
                ahead = jnp.where(g < 2 * count, count - 1, ahead)
            if step == 1:
                ahead = jnp.where(g < 2 * count, ahead, count - 1)
            return (ahead, 0)
        return pl.BlockSpec((GROUP, cols), index)
    shape = jax.ShapeDtypeStruct
    state, fade = (state_dim, inner), (8, inner)
    bc_rows = (conv - inner) // head_count
    owners = min(seq, bc_rows // 8)
    piece = bc_rows // owners
    vm = pltpu.VMEM
    grad_rows = max(width, inner)
    paired = PairedSum.scratch(width, max(width, 2 * inner))
    return pl.pallas_call(
        functools.partial(layer_kernel, heads, head_dim, state_dim, all_channels, count, block, lag,
                          (served, sent), steps, owners, taps),
        grid=(3 * count + 1,),
        out_shape=(shape((2 * length, width), bf16), shape((2, count, GROUP), f32),
                   shape((width, 2 * inner), bf16), shape((inner, width), bf16), shape((bc_rows, width), f32),
                   shape((24, width), f32)),
        in_specs=[by(inner, 0, 2), by(conv - inner, 0, 2), by(inner, 2, 2), by(conv - inner, 2, 2),
                  by(128, 0, 2), by(width, 0, 1), by(width, 0, 2), pl.BlockSpec((16, width), lambda g: (length // 16 - 1, 0))]
        + [HBM] + [VMEM] * 6 + [HBM] + [VMEM] * 3,
        out_specs=(HBM, VMEM, HBM, HBM, VMEM, VMEM),
        scratch_shapes=[
            vm((length, width), bf16), vm((length, width), bf16), vm((2 * length, width), bf16),
            vm((block, width), bf16), vm((length, inner), f32), vm((length, inner), bf16),
            vm((count,) + state, bf16), vm(state, f32), vm(state, f32)]
        + [vm((GROUP + 8, conv), f32), vm((GROUP + 8, 128), f32)]
        + [vm((2, count, GROUP), f32), vm((head_count, 2, count, GROUP), f32)]
        + DeviceScan.scratch(state, fade)
        + [vm((grad_rows, max(width, 2 * inner)), f32)] + paired[:-1] + [DMA((2,) + (8, seq // 2))]
        + [vm(((conv - inner + 128) // bc_rows, bc_rows, width), f32),
           vm((seq, head_count, piece, width), f32), vm((head_count, piece, width), f32),
           vm((bc_rows, width), f32), vm((24, width), f32), vm((seq, 24, width), f32),
           vm((8, width), f32), vm((head_count, 8, width), f32),
           vm((GROUP, conv), bf16), vm((GROUP, 128), bf16), vm((8, inner), f32), vm((8, conv), f32),
           vm((8, 128), f32), vm((8, conv), f32), vm((8, conv), f32),
           LineSum.sems(length, block), DMA((2, head_count)), DMA((4, seq)), DMA((2, head_count)),
           DMA((2, seq)), DMA((2, head_count)), DMA((2,)), pltpu.SemaphoreType.REGULAR,
           vm((width, 2 * inner), bf16), vm((inner, width), bf16), DMA((4,)), DMA((4,))],
        compiler_params=pltpu.CompilerParams(
            dimension_semantics=("arbitrary",), collective_id=4, has_side_effects=True,
            vmem_limit_bytes=LAYER_LIMIT),
        name="layer",
    )(x_conv, bc_conv, x_in, bc_in, heads_in, cot, normed, normed, out_proj, gains, entering, decay, conv_w, params,
      conv_halo, zx, weights, gain, tail_mask)


PACE = 28
MIX, SWAP, GATE, SCAN, BACK = 27, 30, 20, 100, 94
MIX_POINTS = 2
EARLY, LATE = -14, 50
BLOCK, LAG = 64, 3
STEPS = (2, 2, 2, 2, 6, 2, 3, 2, 6, 2)
LAYER_LIMIT = 63 * 2**20


def finish_kernel(heads, head_dim, all_channels, taps, count,
                  tokens, cot, mixed, d_normed, sums, gain, zx, op, bc, small,
                  mixed_out, tokens_out, zx_out, op_out, bc_out, dt_out, gain_out, conv_w_out, conv_b_out,
                  bc_w_out, bc_b_out, bias_out, rate_out, skip_out, norm_out, held, sems):
    at = pl.program_id(0)
    rows = tokens.shape[0]
    slot = lax.rem(at, 2)
    part = rows // 4

    def stores(step, slot):
        return [pltpu.make_async_copy(
            held.at[slot, pl.ds(k * part, part)],
            tokens_out.at[pl.ds(pl.multiple_of(step * rows + k * part, part), part)], sems.at[slot, k])
            for k in range(4)]

    @pl.when(at >= 2)
    def _():
        for copy in stores(at - 2, slot):
            copy.wait()
    inner = heads * head_dim
    value = tokens[...].astype(f32)
    tall = jnp.concatenate([sums[0, pl.ds(at, 1)], jnp.zeros((127, rows), f32)], axis=0).T
    inv_rms = lax.rsqrt(tall[:, 0:1] / all_channels + epsilon)
    mixed_out[...] = (value + mixed[...].astype(f32) * inv_rms).astype(bf16)
    inv = lax.rsqrt(jnp.mean(value * value, axis=1, keepdims=True) + epsilon)
    xhat = value * inv
    scaled = d_normed[...].astype(f32) * gain[...]
    held[slot] = cot[...].astype(f32) + inv * (
        scaled - xhat * jnp.mean(scaled * xhat, axis=1, keepdims=True))
    for copy in stores(at, slot):
        copy.start()

    @pl.when(at == count - 1)
    def _():
        for step in (count - 2, count - 1):
            for copy in stores(step, step % 2):
                copy.wait()
    sums_zx = zx[...].astype(f32)
    zx_out[:, 0, :] = sums_zx[:, :inner]
    zx_out[:, 1, :] = sums_zx[:, inner:]
    op_out[...] = op[...].astype(f32)
    @pl.when(at == 0)
    def _():
        bc_out[...] = bc[...]
        dt_out[...] = small[0:heads]
        gain_out[...] = small[16:17]
        conv_w_out[...] = small[8 : 8 + taps, :inner]
        conv_b_out[...] = small[8 + taps : 9 + taps, :inner]
        bias_out[...] = small[10:11, inner : inner + heads]
        rate_out[...] = small[11:12, inner : inner + heads]
        norm_out[...] = small[8:9, inner : 2 * inner]
        group_ones = (lax.broadcasted_iota(jnp.int32, (inner, 128), 0) // head_dim
                      == lax.broadcasted_iota(jnp.int32, (inner, 128), 1)).astype(bf16)
        skips = jnp.broadcast_to(small[9:10, inner : 2 * inner], (8, inner))
        total = sum(dot(part, group_ones) for part in split3(skips))
        skip_out[...] = total[0:1, :heads]
        part = bc_w_out.shape[1]
        mine_bc = small[17 : 18 + taps, : part * lax.axis_size("head")]
        chosen = mine_bc[:, :part]
        for k in range(1, lax.axis_size("head")):
            chosen = jnp.where(lax.axis_index("head") == k, mine_bc[:, k * part : (k + 1) * part], chosen)
        bc_w_out[...] = chosen[:taps]
        bc_b_out[...] = chosen[taps : taps + 1]


def finish(tokens, cot, totals, sums, gain, zx, op, bc, small, heads, head_dim, taps):
    length, width = tokens.shape
    count = length // GROUP
    inner = heads * head_dim
    part = bc.shape[0]

    def by(rows, cols):
        return pl.BlockSpec((rows, cols), lambda g: (g, 0))
    shape = jax.ShapeDtypeStruct
    tall = by(GROUP, width)
    lone = [(1, width), (taps, inner), (1, inner), (taps, part), (1, part), (1, heads), (1, heads), (1, heads),
            (1, inner)]
    cols = width // count
    return pl.pallas_call(
        functools.partial(finish_kernel, heads, head_dim, inner * lax.axis_size("head"), taps, count),
        grid=(count,),
        out_shape=(shape((length, width), bf16), shape((length, width), f32), shape((width, 2, inner), f32),
                   shape((inner, width), f32), shape((part, width), f32), shape((heads, width), f32))
        + tuple(shape(each, f32) for each in lone),
        in_specs=[tall] * 3 + [pl.BlockSpec((GROUP, width), lambda g: (count + g, 0)), VMEM, VMEM, by(cols, 2 * inner), by(inner // count, width),
                               VMEM, VMEM],
        out_specs=(tall, HBM, pl.BlockSpec((cols, 2, inner), lambda g: (g, 0, 0)), by(inner // count, width),
                   VMEM, VMEM) + (VMEM,) * len(lone),
        scratch_shapes=[pltpu.VMEM((2, GROUP, width), f32), DMA((2, 4))],
        compiler_params=pltpu.CompilerParams(dimension_semantics=("arbitrary",), vmem_limit_bytes=LIMIT),
        name="finish",
    )(tokens, cot, totals, totals, sums, gain, zx, op, bc, small)


def shards(
    tokens, start_flags, in_gain, proj_zx, proj_bc, proj_dt, conv_x_weight, conv_x_bias,
    conv_bc_weight, conv_bc_bias, dt_bias, a_log, skip_scale, norm_gain, out_proj, cotangent,
):
    length, width = tokens.shape
    heads = a_log.shape[0]
    inner = proj_zx.shape[2]
    head_dim = inner // heads
    taps = conv_x_weight.shape[0]
    head_count = lax.axis_size("head")
    bc_part = conv_bc_bias.shape[0]
    bc_width = bc_part * head_count
    state_dim = bc_width // 2
    zx = proj_zx.reshape(width, 2 * inner)
    gain = in_gain[None]
    (normed, x_in, x_conv, bc_in, bc_conv, info, entering, decay, conv_halo, weights, conv_w, params, gains,
     tail_mask) = front(
        tokens, zx, start_flags.reshape(length // 128, 128), gain, proj_bc.T, proj_dt.T, conv_x_weight,
        conv_x_bias[None], conv_bc_weight, conv_bc_bias[None], dt_bias[None], a_log[None], skip_scale[None],
        norm_gain[None], heads, head_dim, state_dim)
    all_channels = inner * head_count
    totals, sums, zx_sum, op_sum, bc_sum, small_sum = layer(
        x_conv, bc_conv, x_in, bc_in, info, cotangent, normed, out_proj, gains, entering, decay, conv_w, params,
        conv_halo, zx, weights, gain, tail_mask, heads, head_dim, state_dim, all_channels, taps)
    (mixed_out, grad_tokens, grad_zx, grad_op, grad_bc, grad_dt, grad_gain, grad_conv_w, grad_conv_b,
     grad_bc_w, grad_bc_b, grad_bias, grad_rate, grad_skip, grad_norm) = finish(
        tokens, cotangent, totals, sums, gain, zx_sum, op_sum, bc_sum, small_sum, heads, head_dim, taps)
    return (
        mixed_out, grad_tokens, grad_gain[0], grad_zx, grad_bc.T, grad_dt.T, grad_conv_w, grad_conv_b[0],
        grad_bc_w, grad_bc_b[0], grad_bias[0], grad_rate[0], grad_skip[0], grad_norm[0], grad_op,
    )


def solution(mesh):
    in_specs = (
        P("seq", None),
        P("seq"),
        P(),
        P(None, None, "head"),
        P(None, "head"),
        P(None, "head"),
        P(None, "head"),
        P("head"),
        P(None, "head"),
        P("head"),
        P("head"),
        P("head"),
        P("head"),
        P("head"),
        P("head", None),
        P("seq", None),
    )
    out_specs = (
        P("seq", None),
        P("seq", None),
        P(),
        P(None, None, "head"),
        P(None, "head"),
        P(None, "head"),
        P(None, "head"),
        P("head"),
        P(None, "head"),
        P("head"),
        P("head"),
        P("head"),
        P("head"),
        P("head"),
        P("head", None),
    )
    return jax.shard_map(shards, mesh=mesh, in_specs=in_specs, out_specs=out_specs, check_vma=False)
```

```python
import functools

import jax
import jax.numpy as jnp
from jax import lax
from jax.experimental import pallas as pl
from jax.experimental.pallas import tpu as pltpu
from jax.sharding import PartitionSpec as P

MESH = pl.DeviceIdType.MESH
f32 = jnp.float32
bf16 = jnp.bfloat16
VMEM = pl.BlockSpec(memory_space=pltpu.VMEM)
HBM = pl.BlockSpec(memory_space=pl.ANY)
DMA = pltpu.SemaphoreType.DMA


def rows_of(ref, start, size):
    return ref.at[pl.ds(pl.multiple_of(start, size), size)]


def other_of(axis, k):
    size = lax.axis_size(axis)
    return lax.rem(lax.axis_index(axis) + k, size)


def greet(*axes):
    barrier = pltpu.get_barrier_semaphore()
    count = 0
    for axis in axes:
        size = lax.axis_size(axis)
        count += size - 1

        @pl.loop(1, size)
        def _(k):
            pl.semaphore_signal(barrier, inc=1, device_id={axis: other_of(axis, k)}, device_id_type=MESH)
    pl.semaphore_wait(barrier, count)


class Pace:
    def __init__(self, phases, pace, behind, most):
        self.phases, self.pace, self.behind, self.most = phases, pace, behind, most
        self.before = [0]
        for n, (points, _, _) in enumerate(phases):
            self.before.append(self.count(n, points - 1) if points else self.before[-1])

    def count(self, phase, k):
        _, start, step = self.phases[phase]
        low, top = self.before[phase], self.most
        value = (start + k * step - self.behind) // self.pace
        if isinstance(value, int):
            return max(low, min(top, value))
        return jnp.clip(value, low, top)

    def span(self, phase, k):
        if isinstance(k, int):
            return (self.count(phase, k - 1) if k else self.before[phase]), self.count(phase, k)
        return jnp.where(k == 0, self.before[phase], self.count(phase, k - 1)), self.count(phase, k)


class LineSum:
    AHEAD = 3

    def __init__(self, own, got, total, out, place, sems, block):
        self.own, self.got, self.total, self.out, self.place = own, got, total, out, place
        self.send1, self.got_in, self.got_total, self.send2, self.stored = (sems.at[i] for i in range(5))
        self.block = block
        self.half = own.shape[0] // block
        self.count = 2 * self.half
        size, me = lax.axis_size("head"), lax.axis_index("head")
        left = me < size // 2
        self.mid = (me == size // 2 - 1) | (me == size // 2)
        self.has_outer = (me > 0) & (me < size - 1)
        self.inner = jnp.where(left, me + 1, me - 1)
        self.outer = jnp.clip(jnp.where(left, me - 1, me + 1), 0, size - 1)

    @staticmethod
    def sems(rows, block):
        return DMA((5, 2 * rows // block))

    def rows(self, b):
        return pl.ds(pl.multiple_of(b * self.block, self.block), self.block)

    def slot(self, b):
        return self.rows(lax.rem(b, self.half))

    def in_copy(self, b, to):
        return pltpu.make_async_remote_copy(
            src_ref=self.own.at[self.slot(b)], dst_ref=self.got.at[self.slot(b)],
            send_sem=self.send1.at[b], recv_sem=self.got_in.at[b], device_id={"head": to}, device_id_type=MESH)

    def cross_copy(self, b):
        return pltpu.make_async_remote_copy(
            src_ref=self.own.at[self.slot(b)], dst_ref=self.total.at[self.rows(b)],
            send_sem=self.send1.at[b], recv_sem=self.got_total.at[b],
            device_id={"head": self.inner}, device_id_type=MESH)

    def out_copy(self, b, to):
        return pltpu.make_async_remote_copy(
            src_ref=self.total.at[self.rows(b)], dst_ref=self.total.at[self.rows(b)],
            send_sem=self.send2.at[b], recv_sem=self.got_total.at[b],
            device_id={"head": to}, device_id_type=MESH)

    def store(self, b):
        return pltpu.make_async_copy(
            self.total.at[self.rows(b)], self.out.at[self.rows(self.place(b))], self.stored.at[b])

    def inward(self, b):
        rows = self.slot(b)
        self.in_copy(b, self.outer).wait_recv()
        self.own[rows] = self.got[rows] + self.own[rows]

        @pl.when(self.mid)
        def _():
            self.cross_copy(b).start()

        @pl.when(jnp.logical_not(self.mid))
        def _():
            self.in_copy(b, self.inner).start()

    def outward(self, b):
        rows = self.rows(b)
        self.cross_copy(b).wait_recv()

        @pl.when(self.has_outer)
        def _():
            self.cross_copy(b).wait_send()

        @pl.when(self.mid)
        def _():
            self.total[rows] = self.own[self.slot(b)] + self.total[rows]

        @pl.when(self.has_outer)
        def _():
            self.out_copy(b, self.outer).start()
        self.store(b).start()

    def serve(self, first, last, lag):
        @pl.when(self.has_outer)
        def _():
            @pl.loop(first, last)
            def _(b):
                @pl.when(b < self.count)
                def _():
                    self.inward(b)

                @pl.when(b >= lag)
                def _():
                    self.outward(b - lag)

    def send(self, first, last):
        @pl.when(jnp.logical_not(self.has_outer))
        def _():
            @pl.loop(first, last)
            def _(b):
                @pl.when(b >= self.AHEAD)
                def _():
                    self.in_copy(b - self.AHEAD, self.inner).wait_send()

                @pl.when(b >= self.half)
                def _():
                    self.outward(b - self.half)
                self.in_copy(b, self.inner).start()

    def finish(self):
        @pl.when(jnp.logical_not(self.has_outer))
        def _():
            pl.loop(self.half, self.count)(self.outward)

            @pl.loop(self.count - self.AHEAD, self.count)
            def _(b):
                self.in_copy(b, self.inner).wait_send()

        @pl.loop(0, self.count)
        def _(b):
            self.store(b).wait()

            @pl.when(self.has_outer)
            def _():
                self.out_copy(b, self.outer).wait_send()


class PairedSum:
    def __init__(self, own, pair, mine, slots, theirs, sems):
        self.own, self.pair, self.mine, self.slots, self.theirs = own, pair, mine, slots, theirs
        self.sems = sems
        self.me = lax.axis_index("seq")
        self.chip, self.odd = self.me // 2, lax.rem(self.me, 2)
        self.partner = self.me + 1 - 2 * self.odd
        self.chips, self.piece = own.shape[0], own.shape[1] // 2

    @staticmethod
    def scratch(rows, width):
        seq = lax.axis_size("seq")
        piece = max(16, rows // seq)
        part = pltpu.VMEM((seq // 2, piece, width), bf16)
        return [pltpu.VMEM((seq // 2, 2 * piece, width), bf16)] + [part] * 4 + [DMA((8, seq // 2))]

    def half(self, odd):
        return pl.ds(pl.multiple_of(odd * self.piece, self.piece), self.piece)

    def swap_copy(self):
        return pltpu.make_async_remote_copy(
            src_ref=self.own.at[:, self.half(1 - self.odd)], dst_ref=self.pair,
            send_sem=self.sems.at[0, 0], recv_sem=self.sems.at[1, 0],
            device_id={"seq": self.partner}, device_id_type=MESH)

    def back_copy(self):
        return pltpu.make_async_remote_copy(
            src_ref=self.pair, dst_ref=self.theirs,
            send_sem=self.sems.at[0, 1], recv_sem=self.sems.at[1, 1],
            device_id={"seq": self.partner}, device_id_type=MESH)

    def scatter_copy(self, to, source):
        return pltpu.make_async_remote_copy(
            src_ref=self.mine.at[to], dst_ref=self.slots.at[source],
            send_sem=self.sems.at[2, to], recv_sem=self.sems.at[3, source],
            device_id={"seq": 2 * to + self.odd}, device_id_type=MESH)

    def gather_copy(self, owner, to):
        return pltpu.make_async_remote_copy(
            src_ref=self.pair.at[owner], dst_ref=self.pair.at[owner],
            send_sem=self.sems.at[4, to], recv_sem=self.sems.at[5, owner],
            device_id={"seq": 2 * to + self.odd}, device_id_type=MESH)

    def release(self, free):
        pl.semaphore_signal(free, inc=1, device_id={"seq": self.partner}, device_id_type=MESH)

    def others(self, do):
        @pl.loop(1, self.chips)
        def _(k):
            do(lax.rem(self.chip + k, self.chips))

    def swap(self):
        self.swap_copy().start()

    def scatter(self):
        self.swap_copy().wait()
        self.mine[...] = (self.own[:, self.half(self.odd)].astype(f32) + self.pair[...].astype(f32)).astype(bf16)
        self.others(lambda other: self.scatter_copy(other, self.chip).start())

    def gather(self):
        self.others(lambda other: self.scatter_copy(self.chip, other).wait_recv())
        self.others(lambda other: self.scatter_copy(other, self.chip).wait_send())
        self.slots[self.chip] = self.mine[self.chip]
        total = self.slots[0].astype(f32)
        for k in range(1, self.chips):
            total = total + self.slots[k].astype(f32)
        self.pair[self.chip] = total.astype(bf16)
        self.others(lambda other: self.gather_copy(self.chip, other).start())

    def back(self):
        self.others(lambda other: self.gather_copy(other, self.chip).wait_recv())
        self.back_copy().start()

    def stores(self, out):
        for k in range(min(self.chips, out.shape[0] // (2 * self.piece))):
            for n, (odd, ref) in enumerate(((self.odd, self.pair), (1 - self.odd, self.theirs))):
                start = pl.multiple_of((2 * k + odd) * self.piece, self.piece)
                yield pltpu.make_async_copy(
                    ref.at[k], out.at[pl.ds(start, self.piece)], self.sems.at[6 + n, k])

    def finish(self, out):
        self.back_copy().wait()
        self.others(lambda other: self.gather_copy(self.chip, other).wait_send())
        for copy in self.stores(out):
            copy.start()

    def stored(self, out):
        for copy in self.stores(out):
            copy.wait()


class Swap:
    def __init__(self, axis, own, slots, sems):
        self.axis, self.own, self.slots = axis, own, slots
        self.send, self.got = sems.at[0], sems.at[1]
        self.size, self.me = lax.axis_size(axis), lax.axis_index(axis)

    def copy(self, to, source):
        return pltpu.make_async_remote_copy(
            src_ref=self.own, dst_ref=self.slots.at[source],
            send_sem=self.send.at[to], recv_sem=self.got.at[source],
            device_id={self.axis: to}, device_id_type=MESH)

    def start(self):
        @pl.loop(1, self.size)
        def _(k):
            self.copy(other_of(self.axis, k), self.me).start()
        self.slots[self.me] = self.own[...]

    def wait(self):
        @pl.loop(1, self.size)
        def _(k):
            self.copy(self.me, other_of(self.axis, k)).wait_recv()

    def total(self):
        out = self.slots[0]
        for k in range(1, self.size):
            out = out + self.slots[k]
        return out

    def finish(self):
        @pl.loop(1, self.size)
        def _(k):
            self.copy(other_of(self.axis, k), self.me).wait_send()


class DeviceScan:
    def __init__(self, backward, total, fade, lead, out, got, got_fade, sent, sent_fade, sems):
        self.backward, self.total, self.fade, self.lead, self.out = backward, total, fade, lead, out
        self.got, self.got_fade, self.sent, self.sent_fade, self.sems = got, got_fade, sent, sent_fade, sems
        self.me = lax.axis_index("seq")
        self.rounds = lax.axis_size("seq").bit_length() - 1

    @staticmethod
    def scratch(state, fade):
        rounds = lax.axis_size("seq").bit_length() - 1
        return [pltpu.VMEM(fade, f32), pltpu.VMEM(fade, f32)] + [
            pltpu.VMEM((rounds,) + state, bf16), pltpu.VMEM((rounds,) + fade, f32)] * 2 + [DMA((4, rounds))]

    def copies(self, k):
        return [
            pltpu.make_async_remote_copy(
                src_ref=src.at[k], dst_ref=dst.at[k],
                send_sem=self.sems.at[i, k], recv_sem=self.sems.at[i + 1, k],
                device_id={"seq": jnp.bitwise_xor(self.me, 1 << k)}, device_id_type=MESH)
            for src, dst, i in ((self.sent, self.got, 0), (self.sent_fade, self.got_fade, 2))]

    def begin(self, decay):
        self.fade[...] = decay
        self.out[...] = jnp.zeros_like(self.out)
        self.lead[...] = jnp.ones_like(self.lead)

    def start(self, k):
        self.sent[k] = self.total[...].astype(bf16)
        self.sent_fade[k] = self.fade[...]
        for copy in self.copies(k):
            copy.start()

    def finish(self, k):
        for copy in self.copies(k):
            copy.wait()
        later = lax.rem(self.me // (1 << k), 2) == (0 if self.backward else 1)

        @pl.when(later)
        def _():
            theirs = self.got[k].astype(f32)
            self.out[...] = self.out[...] + self.lead[0:1] * theirs
            self.total[...] = self.total[...] + self.fade[0:1] * theirs
            self.lead[...] = self.lead[...] * self.got_fade[k]

        @pl.when(jnp.logical_not(later))
        def _():
            self.total[...] = self.got[k].astype(f32) + self.got_fade[k, 0:1] * self.total[...]
        self.fade[...] = self.fade[...] * self.got_fade[k]

    def run(self, between=None):
        for k in range(self.rounds):
            self.start(k)
            if between is not None:
                between(k)
            self.finish(k)


GROUP = 256
STRIP = 128
GAP = 200.0
epsilon = 1e-05
LIMIT = 56 * 2**20


def dot(a, b):
    return jnp.dot(a, b, preferred_element_type=f32)


def dot_nt(a, b):
    return lax.dot_general(a, b, (((1,), (1,)), ((), ())), preferred_element_type=f32)


def dot_tn(a, b):
    return lax.dot_general(a, b, (((0,), (0,)), ((), ())), preferred_element_type=f32)


def split3(v):
    one = v.astype(bf16)
    rest = v - one.astype(f32)
    two = rest.astype(bf16)
    return one, two, (rest - two.astype(f32)).astype(bf16)


def exact_left(ones, v):
    width = v.shape[1]
    out = dot(ones, jnp.concatenate(split3(v), axis=1))
    return out[:, :width] + out[:, width : 2 * width] + out[:, 2 * width :]


def head_sum(v, group_ones):
    high = v.astype(bf16)
    low = (v - high.astype(f32)).astype(bf16)
    return dot(high, group_ones) + dot(low, group_ones)


def sigmoid(v):
    return 1.0 / (1.0 + jnp.exp(-v))


def softplus(v):
    return jnp.maximum(v, 0.0) + jnp.log1p(jnp.exp(-jnp.abs(v)))


def spread(cols, first, heads, head_dim):
    rows = cols.shape[0]
    per = 128 // head_dim
    lane = lax.broadcasted_iota(jnp.int32, (rows, 128), 1)
    tiles = []
    for at in range(0, heads, per):
        tile = cols[:, first + at : first + at + 1]
        for k in range(1, per):
            tile = jnp.where(lane < k * head_dim, tile, cols[:, first + at + k : first + at + k + 1])
        tiles.append(jnp.broadcast_to(tile, (rows, 128)))
    return jnp.concatenate(tiles, axis=1)


def norm_rows(block, gain):
    value = block.astype(f32)
    inv = lax.rsqrt(jnp.mean(value * value, axis=1, keepdims=True) + epsilon)
    return (value * inv * gain).astype(bf16)


def whole(shape):
    return pl.BlockSpec(shape, lambda g: (0,) * len(shape))


def lane_groups(rows, *parts):
    lane = lax.broadcasted_iota(jnp.int32, (rows, 128), 1)
    out = parts[-1]
    for k in range(len(parts) - 2, -1, -1):
        out = jnp.where(lane < 8 * (k + 1), parts[k], out)
    return out


FRONT = 512
RAW, STEP, CUM, DEV, KEEP = 0, 8, 16, 24, 32


def head_lanes(row, heads, lane):
    out = jnp.zeros(lane.shape, f32)
    for k in range(heads):
        out = jnp.where(lane % 8 == k, row[:, k : k + 1], out)
    return out


def loads_of(source, target, sems, first):
    parts = sems.shape[0]
    rows = source.shape[0] // parts
    return [pltpu.make_async_copy(source.at[pl.ds(k * rows, rows), pl.ds(first, target.shape[1])],
                                  target.at[pl.ds(k * rows, rows)], sems.at[k]) for k in range(parts)]


def front_kernel(heads, head_dim, state_dim, count,
                 tokens, last_tokens, pairs_hbm, flags, gain, proj_bc, proj_dt, conv_x_weight, conv_x_bias,
                 conv_bc_weight, conv_bc_bias, dt_bias, a_log, skip, norm_gain,
                 normed_out, x_in_out, x_conv_out, bc_in_out, bc_conv_out, heads_out, entering, decay_out,
                 halo_out, weights_hbm, zx_hbm, conv_w_out, params, gains_out, mask_out,
                 normed, x_active, tail_rows, landed, head_low, proj_all, conv_bc, conv_all, flag_cols, flag_ext,
                 x_ext, bc_ext, state, running, pairs, zx, weights_out, lead, fade,
                 scan_got, scan_got_fade, scan_sent, scan_sent_fade, scan_sems, proj_sems, conv_sems, row_sems, load_sems,
                 store_sem):
    at = pl.program_id(0)
    rows = tokens.shape[0]
    inner = heads * head_dim
    bc_width = 2 * state_dim
    bc_part = proj_bc.shape[0]
    seq, me = lax.axis_size("seq"), lax.axis_index("seq")
    block = lax.rem(at, count)
    mine = pl.ds(pl.multiple_of(block * rows, rows), rows)
    swaps = [Swap("head", proj_bc, proj_all, proj_sems), Swap("head", conv_bc, conv_all, conv_sems)]
    row_copy = pltpu.make_async_remote_copy(
        src_ref=tail_rows, dst_ref=landed, send_sem=row_sems.at[0], recv_sem=row_sems.at[1],
        device_id={"seq": lax.rem(me + 1, seq)}, device_id_type=MESH)
    lane_row = lax.broadcasted_iota(jnp.int32, (1, 128), 1)
    quarter = pairs.shape[0] // 4
    quarters = [pl.ds(k * quarter, quarter) for k in range(4)]
    loads = [pltpu.make_async_copy(pairs_hbm.at[each], pairs.at[each], load_sems.at[k])
             for k, each in enumerate(quarters)]
    zx_stores = [pltpu.make_async_copy(zx.at[each], zx_hbm.at[each], store_sem.at[1 + k])
                 for k, each in enumerate(quarters)]
    weights_store = pltpu.make_async_copy(weights_out, weights_hbm, store_sem.at[0])

    @pl.when(at == 0)
    def _():
        for copy in loads:
            copy.start()
        final = 1.0 - flags[flags.shape[0] - 1 :].astype(f32)
        one, two = final[:, 127:128], final[:, 126:127]
        row = lax.broadcasted_iota(jnp.int32, (16, 128), 0)
        mask = jnp.where(row == 15, 1.0, jnp.where(row == 14, one, jnp.where(row == 13, one * two, 0.0)))
        mask_out[...] = mask
        tail_rows[...] = (last_tokens[...].astype(f32) * mask[:, 0:1]).astype(bf16)
        conv_bc[...] = jnp.zeros_like(conv_bc)
        conv_bc[0:4, :bc_part] = conv_bc_weight[...].astype(f32)
        conv_bc[4:5, :bc_part] = conv_bc_bias[...]
        greet("head", "seq")
        row_copy.start()
        for each in swaps:
            each.start()
        params[...] = jnp.zeros_like(params)
        params[0:1] = head_lanes(dt_bias[...], heads, lane_row)
        params[1:2] = -jnp.exp(head_lanes(a_log[...], heads, lane_row))
        gains_out[...] = jnp.zeros_like(gains_out)
        gains_out[0:1] = norm_gain[...]
        gains_out[1:2] = spread(head_lanes(skip[...], heads, lane_row), 0, heads, head_dim)
        flat = flags[...].astype(f32)
        turned = jnp.concatenate([flat, jnp.zeros((128 - flat.shape[0], 128), f32)], axis=0).T
        conv_w_out[...] = jnp.zeros_like(conv_w_out)
        conv_w_out[0:4, :inner] = conv_x_weight[...].astype(f32)
        conv_w_out[4:5, :inner] = conv_x_bias[...]
        for k in range(flat.shape[0]):
            flag_cols[k * 128 : (k + 1) * 128] = jnp.broadcast_to(turned[:, k : k + 1], (128, 128))
        flag_ext[0:8] = jnp.zeros((8, 128), f32)

    def keeps(flag):
        flag_ext[8:] = flag
        one = 1.0 - flag
        two = one * (1.0 - flag_ext[7 : 7 + rows])
        three = two * (1.0 - flag_ext[6 : 6 + rows])
        flag_ext[0:8] = flag_ext[rows:]
        return one, two, three

    def convolve(ext, current, keep, first, last):
        ext[8:] = current
        total = conv_w_out[4:5, first:last] + conv_w_out[0:1, first:last] * current
        for j in range(1, 4):
            total = total + conv_w_out[j : j + 1, first:last] * ext[pl.ds(8 - j, rows)] * keep[j - 1][:, 0:1]
        ext[0:8] = ext[rows:]
        return total

    @pl.when(at < count)
    def _():
        low = norm_rows(tokens[...], gain[...])
        normed[mine] = low
        normed_out[...] = low

        @pl.when(at == 0)
        def _():
            for copy in loads:
                copy.wait()
            zx[:, :inner] = pairs[:, 0, :]
            zx[:, inner:] = pairs[:, 1, :]
            for copy in zx_stores:
                copy.start()
        x_in = dot(low, zx[:, inner:]).astype(bf16)
        x_in_out[...] = x_in

        @pl.when(at == 0)
        def _():
            row_copy.wait()
            head_low[...] = norm_rows(landed[...], gain[...])
            ahead = jnp.where(me > 0, dot(head_low[...], zx[:, inner:]), 0.0).astype(bf16)
            halo_out[:, :inner] = ahead
            x_ext[0:8] = ahead[8:].astype(f32)
        total = convolve(x_ext, x_in.astype(f32), keeps(flag_cols[mine]), 0, inner)
        x_conv_out[...] = total
        x_active[mine] = total * sigmoid(total)

    @pl.when(at == count)
    def _():
        for each in swaps:
            each.wait()
            each.finish()
        heads_there = proj_all.shape[0]
        for k in range(heads_there):
            weights_out[k * bc_part : (k + 1) * bc_part] = proj_all[k]
        eight = jnp.concatenate([proj_dt[...].astype(f32)] + (
            [jnp.zeros((8 - heads, proj_dt.shape[1]), f32)] if heads < 8 else []), axis=0)
        weights_out[bc_width:] = jnp.concatenate([eight] * 16, axis=0).astype(bf16)
        conv_w_out[:, inner:] = jnp.concatenate([conv_all[k, :, :bc_part] for k in range(heads_there)], axis=1)
        weights_store.start()
        ahead = jnp.where(me > 0, dot_nt(head_low[...], weights_out[:bc_width]), 0.0).astype(bf16)
        halo_out[:, inner:] = ahead
        bc_ext[0:8] = ahead[8:].astype(f32)
        state[...] = jnp.zeros_like(state)
        running[...] = jnp.zeros_like(running)
        flag_ext[0:8] = jnp.zeros((8, 128), f32)

    @pl.when(at >= count)
    def _():
        raw = dot_nt(normed[mine], weights_out[...])
        bc_in = raw[:, :bc_width].astype(bf16)
        bc_in_out[...] = bc_in
        flag = flag_cols[mine]
        keep = keeps(flag)
        total = convolve(bc_ext, bc_in.astype(f32), keep, inner, inner + bc_width)
        bc_conv_out[...] = total
        b_proj = (total[:, :state_dim] * sigmoid(total[:, :state_dim])).astype(bf16)

        order_r = lax.broadcasted_iota(jnp.int32, (GROUP, GROUP), 0)
        order_c = lax.broadcasted_iota(jnp.int32, (GROUP, GROUP), 1)
        lower = (order_r >= order_c).astype(bf16)
        lane = lax.broadcasted_iota(jnp.int32, (GROUP, 128), 1)
        for lo in range(0, rows, GROUP):
            part = slice(lo, lo + GROUP)
            step_raw = raw[part, bc_width:]
            step = softplus(step_raw + params[0:1])
            log_decay = step * params[1:2] - GAP * flag[part]
            cum = exact_left(lower, log_decay)
            kept = jnp.where(lane < KEEP + 1, keep[0][part], jnp.where(lane < KEEP + 2, keep[1][part], keep[2][part]))
            heads_out[part] = lane_groups(GROUP, step_raw, step, cum, cum + running[0:1], kept)
            end = cum[GROUP - 1 :]
            running[...] = running[...] + end
            weight = step * jnp.exp(end - cum)
            x_part = x_active[pl.ds(pl.multiple_of(block * rows + lo, GROUP), GROUP)]
            scaled = (x_part * spread(weight, 0, heads, head_dim)).astype(bf16)
            state[...] = state[...] * spread(jnp.exp(end), 0, heads, head_dim) + dot_tn(b_proj[part], scaled)

    @pl.when(at == 2 * count - 1)
    def _():
        decay = spread(jnp.exp(running[...]), 0, heads, head_dim)
        decay_out[...] = decay
        scan = DeviceScan(False, state, fade, lead, entering, scan_got, scan_got_fade, scan_sent,
                          scan_sent_fade, scan_sems)
        scan.begin(decay)
        scan.run()
        for copy in [weights_store] + zx_stores:
            copy.wait()


def front(tokens, proj_zx, flags, gain, proj_bc, proj_dt, conv_x_weight, conv_x_bias, conv_bc_weight, conv_bc_bias,
          dt_bias, a_log, skip, norm_gain, heads, head_dim, state_dim):
    length, width = tokens.shape
    block = FRONT
    count = length // block
    inner = heads * head_dim
    conv = inner + 2 * state_dim
    head_count = lax.axis_size("head")

    def early(cols):
        return pl.BlockSpec((block, cols), lambda g: (jnp.minimum(g, count - 1), 0))

    def late(cols):
        return pl.BlockSpec((block, cols), lambda g: (jnp.maximum(g - count, 0), 0))
    shape = jax.ShapeDtypeStruct
    state, fade = (state_dim, inner), (8, inner)
    rest = 2 * state_dim + 128
    return pl.pallas_call(
        functools.partial(front_kernel, heads, head_dim, state_dim, count),
        grid=(2 * count,),
        out_shape=(shape((length, width), bf16), shape((length, inner), bf16), shape((length, inner), f32),
                   shape((length, conv - inner), bf16), shape((length, conv - inner), f32),
                   shape((length, 128), f32), shape(state, f32),
                   shape(fade, f32), shape((16, conv), bf16), shape((rest, width), bf16), shape((width, 2 * inner), bf16),
                   shape((8, conv), f32), shape((8, 128), f32), shape((8, inner), f32), shape((16, 128), f32)),
        in_specs=[early(width), pl.BlockSpec((16, width), lambda g: (length // 16 - 1, 0)), HBM] + [VMEM] * 12,
        out_specs=(early(width), early(inner), early(inner), late(conv - inner), late(conv - inner), late(128))
        + (VMEM,) * 3 + (HBM,) * 2 + (VMEM,) * 4,
        scratch_shapes=[
            pltpu.VMEM((length, width), bf16), pltpu.VMEM((length, inner), f32),
            pltpu.VMEM((16, width), bf16), pltpu.VMEM((16, width), bf16), pltpu.VMEM((16, width), bf16),
            pltpu.VMEM((head_count,) + proj_bc.shape, bf16), pltpu.VMEM((8, 128), f32),
            pltpu.VMEM((head_count, 8, 128), f32), pltpu.VMEM((length, 128), f32),
            pltpu.VMEM((block + 8, 128), f32), pltpu.VMEM((block + 8, inner), f32),
            pltpu.VMEM((block + 8, conv - inner), f32), pltpu.VMEM(state, f32), pltpu.VMEM((8, 128), f32),
            pltpu.VMEM(proj_zx.shape, bf16), pltpu.VMEM((width, 2 * inner), bf16), pltpu.VMEM((rest, width), bf16)]
        + DeviceScan.scratch(state, fade) + [DMA((2, head_count)), DMA((2, head_count)), DMA((2,)), DMA((4,)), DMA((5,))],
        compiler_params=pltpu.CompilerParams(
            dimension_semantics=("arbitrary",), collective_id=3, has_side_effects=True,
            vmem_limit_bytes=LIMIT),
        name="front",
    )(tokens, tokens, proj_zx, flags, gain, proj_bc, proj_dt, conv_x_weight, conv_x_bias, conv_bc_weight,
      conv_bc_bias, dt_bias, a_log, skip, norm_gain)


def strips(rows):
    return [(lo, lo + STRIP) for lo in range(0, rows, STRIP)]


def mix_step(heads, head_dim, state_dim, at,
             x_conv, bc_conv, heads_in, normed, zx, cot, out_proj, gains, entering,
             ssm_out, d_normed_out, partial_out, sums_out, starts_out, state, between):
    rows = x_conv.shape[0]
    inner = heads * head_dim
    per = 128 // head_dim

    @pl.when(at == 0)
    def _():
        state[...] = entering[...]

    values = jnp.concatenate([x_conv[...], bc_conv[...]], axis=1)
    active = values * sigmoid(values)
    x = active[:, :inner]
    b_proj = active[:, inner : inner + state_dim].astype(bf16)
    c_proj = active[:, inner + state_dim :].astype(bf16)
    info = heads_in[...]
    flipped = info.T
    stepped = x * spread(info, STEP, heads, head_dim)
    low = stepped.astype(bf16)
    scores = dot_nt(c_proj, b_proj)
    lane = lax.broadcasted_iota(jnp.int32, (rows, 128), 1)
    tiles = []
    for pair in range(heads // per):
        tile = low[:, pair * 128 : (pair + 1) * 128]
        weights, masked = [], []
        for k in range(per):
            head = pair * per + k
            masked.append(jnp.where((lane >= k * head_dim) & (lane < (k + 1) * head_dim), tile,
                                    jnp.zeros_like(tile)))
            parts = []
            for lo, hi in strips(rows):
                gap = info[lo:hi, CUM + head : CUM + head + 1] - flipped[CUM + head : CUM + head + 1, :hi]
                ok = (lax.broadcasted_iota(jnp.int32, (STRIP, hi), 0) + lo
                      >= lax.broadcasted_iota(jnp.int32, (STRIP, hi), 1))
                part = (jnp.exp(jnp.where(ok, gap, -1e30)) * scores[lo:hi, :hi]).astype(bf16)
                if hi < rows:
                    part = jnp.concatenate([part, jnp.zeros((STRIP, rows - hi), bf16)], axis=1)
                parts.append(part)
            weights.append(jnp.concatenate(parts, axis=0))
        tiles.append(dot(jnp.concatenate(weights, axis=1), jnp.concatenate(masked, axis=0)))
        if pair == heads // per // 2 - 1:
            between()
    inside = jnp.concatenate(tiles, axis=1)
    cum = info[:, CUM : CUM + 8]
    end = info[rows - 1 : rows]
    start = state[...]
    starts_out[at] = start.astype(bf16)
    grown = spread(jnp.exp(info), CUM, heads, head_dim)
    result = inside + grown * dot(c_proj, start.astype(bf16)) + gains[1:2] * x
    fade = spread(jnp.exp(end - info), CUM, heads, head_dim)
    state[...] = start * spread(jnp.exp(end), CUM, heads, head_dim) + dot_tn(b_proj, (stepped * fade).astype(bf16))
    ssm_out[...] = result
    z = dot(normed[...], zx[:, :inner])
    gated = result * (z * sigmoid(z))
    d_normed = dot_nt(cot[...], out_proj[...])
    d_normed_out[...] = d_normed.astype(bf16)
    scaled = gated * gains[0:1]
    partial_out[...] = dot(scaled.astype(bf16), out_proj[...]).astype(bf16)
    squares = jnp.sum(gated * gated, axis=1, keepdims=True)
    cross = jnp.sum(d_normed * scaled, axis=1, keepdims=True)
    turned = jnp.where(lane == 0, squares, cross).T
    sums_out[0, pl.ds(at, 1)] = turned[0:1]
    sums_out[1, pl.ds(at, 1)] = turned[1:2]


def gate_step(heads, head_dim, state_dim, all_channels, at,
              ssm, d_normed, sums, x_conv, bc_conv, heads_in, normed, zx, cot, gains,
              d_ssm_out, d_gate_out, grad_out, rows_out, total_out):
    rows = ssm.shape[0]
    inner = heads * head_dim

    @pl.when(at == 0)
    def _():
        grad_out[...] = jnp.zeros_like(grad_out)
        rows_out[...] = jnp.zeros_like(rows_out)
        total_out[...] = jnp.zeros_like(total_out)

    tall = jnp.concatenate([sums[0, pl.ds(at, 1)], sums[1, pl.ds(at, 1)], jnp.zeros((126, rows), f32)], axis=0).T
    inv = lax.rsqrt(tall[:, 0:1] / all_channels + epsilon)
    cross = tall[:, 1:2] / all_channels
    z = dot(normed[...], zx[:, :inner])
    s = sigmoid(z)
    y = ssm[...]
    gated = y * (z * s)
    gain = gains[0:1]
    back = d_normed[...].astype(f32)
    unit = gated * inv
    d_gated = inv * (back * gain - unit * (inv * cross))
    grad_out[:, : cot.shape[1]] += dot_tn((unit * gain).astype(bf16), cot[...])
    d_ssm = d_gated * (z * s)
    d_ssm_out[...] = d_ssm
    d_gate_out[...] = (d_gated * y * (s * (1.0 + z * (1.0 - s)))).astype(bf16)
    x_values, c_values = x_conv[...], bc_conv[:, state_dim:]
    rows_out[0:1] += jnp.sum(back * unit, axis=0, keepdims=True)
    rows_out[1:2] += jnp.sum(d_ssm * (x_values * sigmoid(x_values)), axis=0, keepdims=True)
    c_proj = (c_values * sigmoid(c_values)).astype(bf16)
    grown = spread(jnp.exp(heads_in[...]), DEV, heads, head_dim)
    total_out[...] += dot_tn(c_proj, (grown * d_ssm).astype(bf16))


def back_step(heads, head_dim, state_dim, first_step, last_step,
              d_ssm, x_conv, bc_conv, x_in, bc_in, heads_in, start, entering, conv_w, params, skip, conv_halo,
              d_conv_in_out, d_step_out, conv_grads, head_grads, halo_out,
              lam, later, later_info, between):
    rows = d_ssm.shape[0]
    inner = heads * head_dim
    per = 128 // head_dim

    @pl.when(first_step)
    def _():
        lam[...] = entering[...]
        conv_grads[...] = jnp.zeros_like(conv_grads)
        head_grads[...] = jnp.zeros_like(head_grads)
        for each in (later, later_info):
            each[rows:] = jnp.zeros((8, each.shape[1]), f32)

    values = jnp.concatenate([x_conv[...], bc_conv[...]], axis=1)
    gates = sigmoid(values)
    active = values * gates
    x = active[:, :inner]
    b_proj = active[:, inner : inner + state_dim].astype(bf16)
    c_proj = active[:, inner + state_dim :].astype(bf16)
    info = heads_in[...]
    flipped = info.T
    step = spread(info, STEP, heads, head_dim)
    stepped = x * step
    low = stepped.astype(bf16)
    dy = d_ssm[...]
    dy_low = dy.astype(bf16)
    scores = dot_nt(b_proj, c_proj)
    lane = lax.broadcasted_iota(jnp.int32, (rows, 128), 1)
    lane_one = lax.broadcasted_iota(jnp.int32, (STRIP, 128), 1)
    cuts = strips(rows)
    d_scores = [jnp.zeros((STRIP, rows - lo), f32) for lo, _ in cuts]
    d_rows = []
    d_cols = [jnp.zeros((STRIP, 128), f32) for _ in cuts]
    tiles = []
    for pair in range(heads // per):
        tile = low[:, pair * 128 : (pair + 1) * 128]
        dy_tile = dy_low[:, pair * 128 : (pair + 1) * 128]
        owns = [(lane >= k * head_dim) & (lane < (k + 1) * head_dim) for k in range(per)]
        stacked = jnp.concatenate([jnp.where(own, tile, jnp.zeros_like(tile)) for own in owns], axis=0)
        all_pairs = dot_nt(stacked, dy_tile)
        weights = []
        for k in range(per):
            head = pair * per + k
            row_total = jnp.zeros((1, rows), f32)
            parts = []
            for n, (lo, hi) in enumerate(cuts):
                gap = flipped[CUM + head : CUM + head + 1, lo:] - info[lo:hi, CUM + head : CUM + head + 1]
                ok = (lax.broadcasted_iota(jnp.int32, (STRIP, rows - lo), 1)
                      >= lax.broadcasted_iota(jnp.int32, (STRIP, rows - lo), 0))
                decay = jnp.exp(jnp.where(ok, gap, -1e30))
                weight = decay * scores[lo:hi, lo:]
                part = weight.astype(bf16)
                if lo:
                    part = jnp.concatenate([jnp.zeros((STRIP, lo), bf16), part], axis=1)
                parts.append(part)
                pairs = all_pairs[k * rows + lo : k * rows + hi, lo:]
                d_scores[n] = d_scores[n] + pairs * decay
                moved = pairs * weight
                d_cols[n] = d_cols[n] - jnp.where(lane_one == head, jnp.sum(moved, axis=1, keepdims=True), 0.0)
                col = jnp.sum(moved, axis=0, keepdims=True)
                if lo:
                    col = jnp.concatenate([jnp.zeros((1, lo), f32), col], axis=1)
                row_total = row_total + col
            weights.append(jnp.concatenate(parts, axis=0))
            d_rows.append(row_total)
        dy_stack = jnp.concatenate([jnp.where(own, dy_tile, jnp.zeros_like(dy_tile)) for own in owns], axis=0)
        tiles.append(dot(jnp.concatenate(weights, axis=1), dy_stack))
        between(pair + 1)
    d_stepped = jnp.concatenate(tiles, axis=1)
    d_cum = jnp.concatenate(d_cols, axis=0)
    d_cum = d_cum + jnp.concatenate(d_rows + [jnp.zeros((128 - heads, rows), f32)], axis=0).T
    full = jnp.concatenate(
        [jnp.concatenate([jnp.zeros((STRIP, lo), f32), part], axis=1) if lo else part
         for part, (lo, _) in zip(d_scores, cuts)], axis=0).astype(bf16)
    d_b = dot(full, c_proj)
    d_c = dot_tn(full, b_proj)

    group_ones = (lax.broadcasted_iota(jnp.int32, (inner, 128), 0) // head_dim
                  == lax.broadcasted_iota(jnp.int32, (inner, 128), 1)).astype(bf16)
    after = lam[...]
    after_low = after.astype(bf16)
    end = info[rows - 1 : rows]
    grown = spread(jnp.exp(info), CUM, heads, head_dim)
    fade = spread(jnp.exp(end - info), CUM, heads, head_dim)
    end_grown = spread(jnp.exp(end), CUM, heads, head_dim)
    from_after = fade * dot(b_proj, after_low)
    d_stepped = d_stepped + from_after
    grown_dy = grown * dy
    grown_low = grown_dy.astype(bf16)
    left = stepped * from_after
    to_cum = head_sum(grown_dy * dot(c_proj, start) - left, group_ones)
    kept = jnp.sum(after * start.astype(f32), axis=0, keepdims=True) * end_grown
    kept = kept + jnp.sum(left, axis=0, keepdims=True)
    last = head_sum(jnp.broadcast_to(kept, (8, inner)), group_ones)[0:1]
    row_id = lax.broadcasted_iota(jnp.int32, (rows, 128), 0)
    d_cum = d_cum + to_cum + jnp.where(row_id == rows - 1, last, 0.0)
    d_c = d_c + dot_nt(grown_low, start)
    d_b = d_b + dot_nt((fade * stepped).astype(bf16), after_low)
    lam[...] = end_grown * after + dot_tn(c_proj, grown_low)
    d_step = dot((d_stepped * x).astype(bf16), group_ones)
    d_x = step * d_stepped + skip[0:1] * dy
    between(heads // per + 1)

    order_r = lax.broadcasted_iota(jnp.int32, (rows, rows), 0)
    order_c = lax.broadcasted_iota(jnp.int32, (rows, rows), 1)
    d_decay = exact_left((order_r <= order_c).astype(bf16), d_cum) * info[:, KEEP : KEEP + 1]
    rate = params[1:2]
    real = lane < heads
    step_raw = jnp.where(real, info, 0.0) + params[0:1]
    slope = sigmoid(step_raw)
    d_pre = jnp.where(real, (d_step + d_decay * rate) * slope, 0.0)
    d_step_out[...] = d_pre.astype(bf16)
    head_grads[0:1] += jnp.sum(d_pre, axis=0, keepdims=True)
    head_grads[1:2] += jnp.sum(jnp.where(real, d_decay * softplus(step_raw) * rate, 0.0), axis=0, keepdims=True)

    d_active = jnp.concatenate([d_x, d_b, d_c], axis=1)
    d_conv = d_active * (gates * (1.0 + values * (1.0 - gates)))
    taken = jnp.concatenate([x_in[...], bc_in[...]], axis=1).astype(f32)
    total = d_conv * conv_w[0:1]
    conv_grads[0:1] += jnp.sum(d_conv * taken, axis=0, keepdims=True)
    conv_grads[4:5] += jnp.sum(d_conv, axis=0, keepdims=True)
    later[0:rows] = d_conv
    later_info[0:rows] = info
    for j in range(1, 4):
        moved = later[pl.ds(j, rows)] * later_info[pl.ds(j, rows)][:, KEEP + j - 1 : KEEP + j]
        total = total + moved * conv_w[j : j + 1]
        conv_grads[j : j + 1] += jnp.sum(moved * taken, axis=0, keepdims=True)
    d_conv_in_out[...] = total.astype(bf16)

    @pl.when(last_step)
    def _():
        ahead = conv_halo[...].astype(f32)
        halo_out[...] = jnp.zeros_like(halo_out)
        for j in range(1, 4):
            first = later[0:8] * later_info[0:8, KEEP + j - 1 : KEEP + j]
            for t in range(j):
                row = 16 + t - j
                conv_grads[j : j + 1] += first[t : t + 1] * ahead[row : row + 1]
                halo_out[row - 8 : row - 7] += first[t : t + 1] * conv_w[j : j + 1]
    for each in (later, later_info):
        each[rows:] = each[0:8]


def block_place(per, blocks):
    def place(b):
        late = b - blocks - (per - 1)
        group = 2 * blocks - 2 * per - late // per * per + late % per
        second = jnp.where(b < blocks + per - 1, b + blocks - per, group)
        return jnp.where((b < blocks) | (b == 2 * blocks - 1), b, second)
    return place


def layer_kernel(heads, head_dim, state_dim, all_channels, count, block, lag, plans, steps, owners, taps,
                 x_conv, bc_conv, x_in, bc_in, heads_in, cot, normed, last_normed, op_hbm, gains, entering, decay,
                 conv_w, params, conv_halo, zx_hbm, weights, gain, tail_mask,
                 totals_out, sums_out, zx_out, op_out, bc_out, small_out,
                 own, got, total, held, ssm, d_normed, starts, state, leaving, later, later_info,
                 sums, sum_slots, lead, fade,
                 scan_got, scan_got_fade, scan_sent, scan_sent_fade, scan_sems,
                 grad, sum_own, sum_pair, sum_mine, sum_slot, sum_theirs, sum_sems, grad_bc,
                 bc_slots, bc_z, bc_res, small, small_slots, small_own, small_z,
                 d_conv, d_step, gate_rows, conv_grads, head_grads, halo_rows, landed,
                 line_sems, swap_sems, bc_sems, bcz_sems, small_sems, smallz_sems, row_sems, free_sem, zx,
                 out_proj, load_sems, op_load_sems):
    at = pl.program_id(0)
    rows, width = cot.shape
    inner = heads * head_dim
    bc_width = 2 * state_dim
    seq, head_count = lax.axis_size("seq"), lax.axis_size("head")
    me, my_head = lax.axis_index("seq"), lax.axis_index("head")
    per = rows // block
    line = LineSum(own, got, total, totals_out, block_place(per, count * per), line_sems, block)
    swap = Swap("head", sums, sum_slots, swap_sems)
    scan = DeviceScan(True, state, fade, lead, leaving, scan_got, scan_got_fade, scan_sent, scan_sent_fade,
                      scan_sems)
    op_rows = max(16, inner // seq)
    sum_refs = (sum_own, sum_pair, sum_mine, sum_slot, sum_theirs)
    op_sum = PairedSum(*(ref.at[:, : op_rows * (2 if ref is sum_own else 1), :width] for ref in sum_refs),
                       sum_sems.at[0])
    zx_sum = PairedSum(*(ref.at[:, :, : 2 * inner] for ref in sum_refs), sum_sems.at[1])
    small_swap = Swap("seq", small, small_slots, small_sems)
    both_swap = Swap("head", small_own, small_z, smallz_sems)
    row_copy = pltpu.make_async_remote_copy(
        src_ref=halo_rows, dst_ref=landed, send_sem=row_sems.at[0], recv_sem=row_sems.at[1],
        device_id={"seq": lax.rem(me + seq - 1, seq)}, device_id_type=MESH)
    served, sent = plans
    back_points = inner // 128 + 3
    back_at = at - 2 * count - 1
    last_step = back_at == count - 1

    def serve(phase, k):
        line.send(*sent.span(phase, k))
        line.serve(*served.span(phase, k), lag)

    def serve_mix(k):
        @pl.when(at > 0)
        def _():
            serve(1, MIX_POINTS * (at - 1) + k)

    loads = loads_of(zx_hbm, zx, load_sems, 0) + loads_of(op_hbm, out_proj, op_load_sems, 0)

    @pl.when(at == 0)
    def _():
        for copy in loads:
            copy.start()
        greet("head", "seq")
        state[...] = entering[...]
        for copy in loads:
            copy.wait()

    @pl.when(at < count)
    def _():
        mine = pl.ds(pl.multiple_of(at * rows, rows), rows)
        serve_mix(0)
        mix_step(heads, head_dim, state_dim, at, x_conv, bc_conv, heads_in, normed, zx, cot, out_proj, gains, entering,
                 ssm.at[mine], d_normed.at[mine], own.at[mine], sums, starts, state,
                 lambda: serve_mix(1))

    @pl.when(at == count - 1)
    def _():
        swap.start()

    @pl.when((at >= count) & (at < 2 * count))
    def _():
        serve(2, at - count)

    @pl.when(at == count)
    def _():
        swap.wait()
        sums_out[...] = swap.total()
        swap.finish()
        grad[...] = jnp.zeros_like(grad)
        gate_rows[...] = jnp.zeros_like(gate_rows)
        state[...] = jnp.zeros_like(state)

    @pl.when((at >= count) & (at < 2 * count))
    def _():
        here = at - count
        mine = pl.ds(pl.multiple_of(here * rows, rows), rows)
        gate_step(heads, head_dim, state_dim, all_channels, here,
                  ssm.at[mine], d_normed.at[mine], sums_out, x_conv, bc_conv, heads_in, normed, zx, cot, gains,
                  ssm.at[mine], d_normed.at[mine], grad.at[:inner], gate_rows, state)

    @pl.when(at == 2 * count)
    def _():
        for k in range(seq // 2):
            lo, hi = min(inner, k * 2 * op_rows), min(inner, (k + 1) * 2 * op_rows)
            if hi > lo:
                sum_own[k, : hi - lo, :width] = grad[lo:hi, :width].astype(bf16)
        scan.begin(decay[...])
        scan.run(lambda k: serve(3, k))
        op_sum.swap()
        grad[...] = jnp.zeros_like(grad)
        grad_bc[...] = jnp.zeros_like(grad_bc)
        small[...] = jnp.zeros_like(small)

    def project(block_low, gate_low, conv_low, rest_low):
        d_rows = dot_nt(conv_low, zx[:, inner:]) + dot(rest_low, weights[...])
        grad[:, inner : 2 * inner] += dot_tn(block_low, conv_low)
        if gate_low is not None:
            d_rows = d_rows + dot_nt(gate_low, zx[:, :inner])
            grad[:, :inner] += dot_tn(block_low, gate_low)
        grad_bc[...] += dot_tn(rest_low, block_low).reshape(grad_bc.shape)
        small[16:17] += jnp.sum(d_rows * block_low.astype(f32), axis=0, keepdims=True) / gain[...]
        return d_rows

    @pl.when(at > 2 * count)
    def _():
        here = 3 * count - at
        mine = pl.ds(pl.multiple_of(here * rows, rows), rows)
        serve(4, back_points * back_at)
        back_step(heads, head_dim, state_dim, back_at == 0, last_step,
                  ssm.at[mine], x_conv, bc_conv, x_in, bc_in, heads_in, starts[here], leaving, conv_w, params,
                  gains[1:2], conv_halo, d_conv, d_step, conv_grads, head_grads, halo_rows,
                  state, later, later_info, lambda k: serve(4, back_points * back_at + k))

        @pl.when(last_step)
        def _():
            row_copy.start()
        serve(4, back_points * back_at + back_points - 1)
        rest_low = jnp.concatenate([d_conv[:, inner:], d_step[...]], axis=1)
        d_rows = project(normed[...], d_normed[mine], d_conv[:, :inner], rest_low).astype(bf16)

        @pl.when(back_at == 0)
        def _():
            own[: rows - block] = d_rows[: rows - block]
            held[...] = d_rows[rows - block :]

        @pl.when(back_at > 0)
        def _():
            start = pl.multiple_of(back_at * rows - block, block)
            own[pl.ds(start, rows)] = d_rows

    @pl.when(back_at == 1)
    def _():
        op_sum.scatter()

    @pl.when(back_at == 3)
    def _():
        op_sum.gather()

    @pl.when(back_at == 5)
    def _():
        op_sum.back()

    piece = grad_bc.shape[1] // owners

    def bc_scatter(to, source):
        return pltpu.make_async_remote_copy(
            src_ref=grad_bc.at[:head_count, pl.ds(pl.multiple_of(to * piece, piece), piece)],
            dst_ref=bc_slots.at[source], send_sem=bc_sems.at[0, to], recv_sem=bc_sems.at[1, source],
            device_id={"seq": to}, device_id_type=MESH)

    def bc_gather(owner, to):
        rows = pl.ds(pl.multiple_of(owner * piece, piece), piece)
        return pltpu.make_async_remote_copy(
            src_ref=bc_res.at[rows], dst_ref=bc_res.at[rows],
            send_sem=bc_sems.at[2, to], recv_sem=bc_sems.at[3, owner],
            device_id={"seq": to}, device_id_type=MESH)

    def bc_swap(to, source):
        return pltpu.make_async_remote_copy(
            src_ref=bc_slots.at[me, to], dst_ref=bc_z.at[source],
            send_sem=bcz_sems.at[0, to], recv_sem=bcz_sems.at[1, source],
            device_id={"head": to}, device_id_type=MESH)

    @pl.when(last_step)
    def _():
        op_sum.finish(op_out)
        at_block = [served.before[-1], sent.before[-1]]

        def go(more):
            until = min(line.count + lag, at_block[0] + more)
            ahead = max(at_block[1], min(line.count - (0 if filled else 1), until + 2))
            line.send(at_block[1], ahead)
            line.serve(at_block[0], until, lag)
            at_block[:] = [until, ahead]
        filled = False
        go(steps[0])
        row_copy.wait()
        extra = jnp.where(me < seq - 1, landed[...] * tail_mask[8:, 0:1], 0.0)
        extra = jnp.concatenate([jnp.zeros_like(extra), extra], axis=0).astype(bf16)
        extra_rest = jnp.concatenate([extra[:, inner:], jnp.zeros((16, 128), bf16)], axis=1)
        more = project(last_normed[...], None, extra[:, :inner], extra_rest)
        final = held[...].astype(f32) + jnp.concatenate([jnp.zeros((block - 16, width), f32), more], axis=0)
        own[count * rows - block :] = final.astype(bf16)
        filled = True
        go(steps[1])

        op_sum.stored(op_out)
        op_sum.release(free_sem)
        pair_rows = sum_own.shape[1]
        for k in range(sum_own.shape[0]):
            sum_own[k, :, : 2 * inner] = grad[k * pair_rows : (k + 1) * pair_rows, : 2 * inner].astype(bf16)
        pl.semaphore_wait(free_sem, 1)
        zx_sum.swap()
        go(steps[2])
        small[0:8] += grad_bc[head_count, 0:8]
        small[8 : 9 + taps, :inner] = conv_grads[: taps + 1, :inner]
        small[8:10, inner : 2 * inner] = gate_rows[0:2]
        small[10:12, inner : inner + 128] = head_grads[0:2]
        small[17 : 18 + taps, :bc_width] = conv_grads[: taps + 1, inner:]
        small_swap.start()

        @pl.loop(1, seq)
        def _(k):
            to = other_of("seq", k)

            @pl.when(to < owners)
            def _():
                bc_scatter(to, me).start()

        go(steps[3])
        zx_sum.scatter()
        go(steps[4])
        small_swap.wait()
        sums_small = small_swap.total()
        lone = small.shape[0] - small_own.shape[0]
        small_out[:lone] = sums_small[:lone]
        small_own[...] = sums_small[lone:]
        both_swap.start()
        go(steps[5])

        @pl.when(me < owners)
        def _():
            @pl.loop(1, seq)
            def _(k):
                bc_scatter(me, other_of("seq", k)).wait_recv()
            bc_slots[me] = grad_bc[:head_count, pl.ds(pl.multiple_of(me * piece, piece), piece)]
            sums_bc = bc_slots[0]
            for k in range(1, seq):
                sums_bc = sums_bc + bc_slots[k]
            bc_slots[me] = sums_bc
            bc_z[my_head] = bc_slots[me, my_head]

            @pl.loop(1, head_count)
            def _(k):
                bc_swap(other_of("head", k), my_head).start()

        go(steps[6])
        zx_sum.gather()
        go(steps[7])
        both_swap.wait()
        small_out[lone:] = both_swap.total()

        @pl.when(me < owners)
        def _():
            @pl.loop(1, head_count)
            def _(k):
                bc_swap(my_head, other_of("head", k)).wait_recv()
            sums_bc = bc_z[0]
            for k in range(1, head_count):
                sums_bc = sums_bc + bc_z[k]
            bc_res[pl.ds(pl.multiple_of(me * piece, piece), piece)] = sums_bc

            @pl.loop(1, seq)
            def _(k):
                bc_gather(me, other_of("seq", k)).start()

        go(steps[8])
        zx_sum.back()
        go(steps[9])
        zx_sum.finish(zx_out)
        go(line.count + lag)
        line.finish()
        zx_sum.stored(zx_out)
        small_swap.finish()
        both_swap.finish()

        @pl.loop(1, seq)
        def _(k):
            other = other_of("seq", k)

            @pl.when(other < owners)
            def _():
                bc_gather(other, me).wait_recv()
                bc_scatter(other, me).wait_send()

            @pl.when(me < owners)
            def _():
                bc_gather(me, other).wait_send()
        bc_out[...] = bc_res[...]

        @pl.when(me < owners)
        def _():
            @pl.loop(1, head_count)
            def _(k):
                bc_swap(other_of("head", k), my_head).wait_send()


def layer(x_conv, bc_conv, x_in, bc_in, heads_in, cot, normed, out_proj, gains, entering, decay, conv_w, params,
          conv_halo, zx, weights, gain, tail_mask, heads, head_dim, state_dim, all_channels, taps):
    length, inner = x_conv.shape
    conv = inner + bc_conv.shape[1]
    count = length // GROUP
    width = cot.shape[1]
    seq, head_count = lax.axis_size("seq"), lax.axis_size("head")
    block = BLOCK
    pace = PACE * block // 64
    blocks = length // block
    per = GROUP // block
    lag = max(LAG, head_count // 2 - 1)
    back_points = inner // 128 + 3
    gate_at = MIX * count + SWAP
    scan_at = gate_at + GATE * count
    back_start = scan_at + SCAN
    rounds = seq.bit_length() - 1
    phases = [(MIX_POINTS, -(10**6), 0), (MIX_POINTS * (count - 1), MIX, MIX // MIX_POINTS), (count, gate_at, GATE),
              (rounds, scan_at, SCAN // rounds), (back_points * count, back_start, BACK // back_points)]
    served = Pace(phases, pace, LATE, 2 * blocks + lag)
    sent = Pace(phases, pace, EARLY, 2 * blocks)
    for k in range(count):
        point = (k + 1) * back_points - 1
        assert served.count(4, point) >= min(blocks, (k + 1) * per) + lag
        assert sent.count(4, point) >= min(blocks, (k + 1) * per) + LineSum.AHEAD
        for each in (served, sent):
            assert each.count(4, point) <= blocks + max(0, k * per - 1)
    steps = [step * 64 // block for step in STEPS]

    def by(cols, first, step):
        def index(g):
            ahead = jnp.where(g < count, g, jnp.where(g < 2 * count, g - count, jnp.minimum(3 * count - g, count - 1)))
            if first == 2:
                ahead = jnp.where(g < 2 * count, count - 1, ahead)
            if step == 1:
                ahead = jnp.where(g < 2 * count, ahead, count - 1)
            return (ahead, 0)
        return pl.BlockSpec((GROUP, cols), index)
    shape = jax.ShapeDtypeStruct
    state, fade = (state_dim, inner), (8, inner)
    bc_rows = (conv - inner) // head_count
    owners = min(seq, bc_rows // 8)
    piece = bc_rows // owners
    vm = pltpu.VMEM
    grad_rows = max(width, inner)
    paired = PairedSum.scratch(width, max(width, 2 * inner))
    return pl.pallas_call(
        functools.partial(layer_kernel, heads, head_dim, state_dim, all_channels, count, block, lag,
                          (served, sent), steps, owners, taps),
        grid=(3 * count + 1,),
        out_shape=(shape((2 * length, width), bf16), shape((2, count, GROUP), f32),
                   shape((width, 2 * inner), bf16), shape((inner, width), bf16), shape((bc_rows, width), f32),
                   shape((24, width), f32)),
        in_specs=[by(inner, 0, 2), by(conv - inner, 0, 2), by(inner, 2, 2), by(conv - inner, 2, 2),
                  by(128, 0, 2), by(width, 0, 1), by(width, 0, 2), pl.BlockSpec((16, width), lambda g: (length // 16 - 1, 0))]
        + [HBM] + [VMEM] * 6 + [HBM] + [VMEM] * 3,
        out_specs=(HBM, VMEM, HBM, HBM, VMEM, VMEM),
        scratch_shapes=[
            vm((length, width), bf16), vm((length, width), bf16), vm((2 * length, width), bf16),
            vm((block, width), bf16), vm((length, inner), f32), vm((length, inner), bf16),
            vm((count,) + state, bf16), vm(state, f32), vm(state, f32)]
        + [vm((GROUP + 8, conv), f32), vm((GROUP + 8, 128), f32)]
        + [vm((2, count, GROUP), f32), vm((head_count, 2, count, GROUP), f32)]
        + DeviceScan.scratch(state, fade)
        + [vm((grad_rows, max(width, 2 * inner)), f32)] + paired[:-1] + [DMA((2,) + (8, seq // 2))]
        + [vm(((conv - inner + 128) // bc_rows, bc_rows, width), f32),
           vm((seq, head_count, piece, width), f32), vm((head_count, piece, width), f32),
           vm((bc_rows, width), f32), vm((24, width), f32), vm((seq, 24, width), f32),
           vm((8, width), f32), vm((head_count, 8, width), f32),
           vm((GROUP, conv), bf16), vm((GROUP, 128), bf16), vm((8, inner), f32), vm((8, conv), f32),
           vm((8, 128), f32), vm((8, conv), f32), vm((8, conv), f32),
           LineSum.sems(length, block), DMA((2, head_count)), DMA((4, seq)), DMA((2, head_count)),
           DMA((2, seq)), DMA((2, head_count)), DMA((2,)), pltpu.SemaphoreType.REGULAR,
           vm((width, 2 * inner), bf16), vm((inner, width), bf16), DMA((4,)), DMA((4,))],
        compiler_params=pltpu.CompilerParams(
            dimension_semantics=("arbitrary",), collective_id=4, has_side_effects=True,
            vmem_limit_bytes=LAYER_LIMIT),
        name="layer",
    )(x_conv, bc_conv, x_in, bc_in, heads_in, cot, normed, normed, out_proj, gains, entering, decay, conv_w, params,
      conv_halo, zx, weights, gain, tail_mask)


PACE = 28
MIX, SWAP, GATE, SCAN, BACK = 27, 30, 20, 100, 94
MIX_POINTS = 2
EARLY, LATE = -14, 50
BLOCK, LAG = 64, 3
STEPS = (2, 2, 2, 2, 6, 2, 3, 2, 6, 2)
LAYER_LIMIT = 63 * 2**20


def finish_kernel(heads, head_dim, all_channels, taps, count,
                  tokens, cot, mixed, d_normed, sums, gain, zx, op, bc, small,
                  mixed_out, tokens_out, zx_out, op_out, bc_out, dt_out, gain_out, conv_w_out, conv_b_out,
                  bc_w_out, bc_b_out, bias_out, rate_out, skip_out, norm_out, held, sems):
    at = pl.program_id(0)
    rows = tokens.shape[0]
    slot = lax.rem(at, 2)
    part = rows // 4

    def stores(step, slot):
        return [pltpu.make_async_copy(
            held.at[slot, pl.ds(k * part, part)],
            tokens_out.at[pl.ds(pl.multiple_of(step * rows + k * part, part), part)], sems.at[slot, k])
            for k in range(4)]

    @pl.when(at >= 2)
    def _():
        for copy in stores(at - 2, slot):
            copy.wait()
    inner = heads * head_dim
    value = tokens[...].astype(f32)
    tall = jnp.concatenate([sums[0, pl.ds(at, 1)], jnp.zeros((127, rows), f32)], axis=0).T
    inv_rms = lax.rsqrt(tall[:, 0:1] / all_channels + epsilon)
    mixed_out[...] = (value + mixed[...].astype(f32) * inv_rms).astype(bf16)
    inv = lax.rsqrt(jnp.mean(value * value, axis=1, keepdims=True) + epsilon)
    xhat = value * inv
    scaled = d_normed[...].astype(f32) * gain[...]
    held[slot] = cot[...].astype(f32) + inv * (
        scaled - xhat * jnp.mean(scaled * xhat, axis=1, keepdims=True))
    for copy in stores(at, slot):
        copy.start()

    @pl.when(at == count - 1)
    def _():
        for step in (count - 2, count - 1):
            for copy in stores(step, step % 2):
                copy.wait()
    sums_zx = zx[...].astype(f32)
    zx_out[:, 0, :] = sums_zx[:, :inner]
    zx_out[:, 1, :] = sums_zx[:, inner:]
    op_out[...] = op[...].astype(f32)
    @pl.when(at == 0)
    def _():
        bc_out[...] = bc[...]
        dt_out[...] = small[0:heads]
        gain_out[...] = small[16:17]
        conv_w_out[...] = small[8 : 8 + taps, :inner]
        conv_b_out[...] = small[8 + taps : 9 + taps, :inner]
        bias_out[...] = small[10:11, inner : inner + heads]
        rate_out[...] = small[11:12, inner : inner + heads]
        norm_out[...] = small[8:9, inner : 2 * inner]
        group_ones = (lax.broadcasted_iota(jnp.int32, (inner, 128), 0) // head_dim
                      == lax.broadcasted_iota(jnp.int32, (inner, 128), 1)).astype(bf16)
        skips = jnp.broadcast_to(small[9:10, inner : 2 * inner], (8, inner))
        total = sum(dot(part, group_ones) for part in split3(skips))
        skip_out[...] = total[0:1, :heads]
        part = bc_w_out.shape[1]
        mine_bc = small[17 : 18 + taps, : part * lax.axis_size("head")]
        chosen = mine_bc[:, :part]
        for k in range(1, lax.axis_size("head")):
            chosen = jnp.where(lax.axis_index("head") == k, mine_bc[:, k * part : (k + 1) * part], chosen)
        bc_w_out[...] = chosen[:taps]
        bc_b_out[...] = chosen[taps : taps + 1]


def finish(tokens, cot, totals, sums, gain, zx, op, bc, small, heads, head_dim, taps):
    length, width = tokens.shape
    count = length // GROUP
    inner = heads * head_dim
    part = bc.shape[0]

    def by(rows, cols):
        return pl.BlockSpec((rows, cols), lambda g: (g, 0))
    shape = jax.ShapeDtypeStruct
    tall = by(GROUP, width)
    lone = [(1, width), (taps, inner), (1, inner), (taps, part), (1, part), (1, heads), (1, heads), (1, heads),
            (1, inner)]
    cols = width // count
    return pl.pallas_call(
        functools.partial(finish_kernel, heads, head_dim, inner * lax.axis_size("head"), taps, count),
        grid=(count,),
        out_shape=(shape((length, width), bf16), shape((length, width), f32), shape((width, 2, inner), f32),
                   shape((inner, width), f32), shape((part, width), f32), shape((heads, width), f32))
        + tuple(shape(each, f32) for each in lone),
        in_specs=[tall] * 3 + [pl.BlockSpec((GROUP, width), lambda g: (count + g, 0)), VMEM, VMEM, by(cols, 2 * inner), by(inner // count, width),
                               VMEM, VMEM],
        out_specs=(tall, HBM, pl.BlockSpec((cols, 2, inner), lambda g: (g, 0, 0)), by(inner // count, width),
                   VMEM, VMEM) + (VMEM,) * len(lone),
        scratch_shapes=[pltpu.VMEM((2, GROUP, width), f32), DMA((2, 4))],
        compiler_params=pltpu.CompilerParams(dimension_semantics=("arbitrary",), vmem_limit_bytes=LIMIT),
        name="finish",
    )(tokens, cot, totals, totals, sums, gain, zx, op, bc, small)


def shards(
    tokens, start_flags, in_gain, proj_zx, proj_bc, proj_dt, conv_x_weight, conv_x_bias,
    conv_bc_weight, conv_bc_bias, dt_bias, a_log, skip_scale, norm_gain, out_proj, cotangent,
):
    length, width = tokens.shape
    heads = a_log.shape[0]
    inner = proj_zx.shape[2]
    head_dim = inner // heads
    taps = conv_x_weight.shape[0]
    head_count = lax.axis_size("head")
    bc_part = conv_bc_bias.shape[0]
    bc_width = bc_part * head_count
    state_dim = bc_width // 2
    gain = in_gain[None]
    (normed, x_in, x_conv, bc_in, bc_conv, info, entering, decay, conv_halo, weights, zx, conv_w, params, gains,
     tail_mask) = front(
        tokens, proj_zx, start_flags.reshape(length // 128, 128), gain, proj_bc.T, proj_dt.T, conv_x_weight,
        conv_x_bias[None], conv_bc_weight, conv_bc_bias[None], dt_bias[None], a_log[None], skip_scale[None],
        norm_gain[None], heads, head_dim, state_dim)
    all_channels = inner * head_count
    totals, sums, zx_sum, op_sum, bc_sum, small_sum = layer(
        x_conv, bc_conv, x_in, bc_in, info, cotangent, normed, out_proj, gains, entering, decay, conv_w, params,
        conv_halo, zx, weights, gain, tail_mask, heads, head_dim, state_dim, all_channels, taps)
    (mixed_out, grad_tokens, grad_zx, grad_op, grad_bc, grad_dt, grad_gain, grad_conv_w, grad_conv_b,
     grad_bc_w, grad_bc_b, grad_bias, grad_rate, grad_skip, grad_norm) = finish(
        tokens, cotangent, totals, sums, gain, zx_sum, op_sum, bc_sum, small_sum, heads, head_dim, taps)
    return (
        mixed_out, grad_tokens, grad_gain[0], grad_zx, grad_bc.T, grad_dt.T, grad_conv_w, grad_conv_b[0],
        grad_bc_w, grad_bc_b[0], grad_bias[0], grad_rate[0], grad_skip[0], grad_norm[0], grad_op,
    )


def solution(mesh):
    in_specs = (
        P("seq", None),
        P("seq"),
        P(),
        P(None, None, "head"),
        P(None, "head"),
        P(None, "head"),
        P(None, "head"),
        P("head"),
        P(None, "head"),
        P("head"),
        P("head"),
        P("head"),
        P("head"),
        P("head"),
        P("head", None),
        P("seq", None),
    )
    out_specs = (
        P("seq", None),
        P("seq", None),
        P(),
        P(None, None, "head"),
        P(None, "head"),
        P(None, "head"),
        P(None, "head"),
        P("head"),
        P(None, "head"),
        P("head"),
        P("head"),
        P("head"),
        P("head"),
        P("head"),
        P("head", None),
    )
    return jax.shard_map(shards, mesh=mesh, in_specs=in_specs, out_specs=out_specs, check_vma=False)
```

```python
import functools

import jax
import jax.numpy as jnp
from jax import lax
from jax.experimental import pallas as pl
from jax.experimental.pallas import tpu as pltpu
from jax.sharding import PartitionSpec as P

MESH = pl.DeviceIdType.MESH
f32 = jnp.float32
bf16 = jnp.bfloat16
VMEM = pl.BlockSpec(memory_space=pltpu.VMEM)
HBM = pl.BlockSpec(memory_space=pl.ANY)
DMA = pltpu.SemaphoreType.DMA


def rows_of(ref, start, size):
    return ref.at[pl.ds(pl.multiple_of(start, size), size)]


def other_of(axis, k):
    size = lax.axis_size(axis)
    return lax.rem(lax.axis_index(axis) + k, size)


def greet(*axes):
    barrier = pltpu.get_barrier_semaphore()
    count = 0
    for axis in axes:
        size = lax.axis_size(axis)
        count += size - 1

        @pl.loop(1, size)
        def _(k):
            pl.semaphore_signal(barrier, inc=1, device_id={axis: other_of(axis, k)}, device_id_type=MESH)
    pl.semaphore_wait(barrier, count)


class Pace:
    def __init__(self, phases, pace, behind, most):
        self.phases, self.pace, self.behind, self.most = phases, pace, behind, most
        self.before = [0]
        for n, (points, _, _) in enumerate(phases):
            self.before.append(self.count(n, points - 1) if points else self.before[-1])

    def count(self, phase, k):
        _, start, step = self.phases[phase]
        low, top = self.before[phase], self.most
        value = (start + k * step - self.behind) // self.pace
        if isinstance(value, int):
            return max(low, min(top, value))
        return jnp.clip(value, low, top)

    def span(self, phase, k):
        if isinstance(k, int):
            return (self.count(phase, k - 1) if k else self.before[phase]), self.count(phase, k)
        return jnp.where(k == 0, self.before[phase], self.count(phase, k - 1)), self.count(phase, k)


class LineSum:
    AHEAD = 3

    def __init__(self, own, got, total, out, place, sems, block):
        self.own, self.got, self.total, self.out, self.place = own, got, total, out, place
        self.send1, self.got_in, self.got_total, self.send2, self.stored = (sems.at[i] for i in range(5))
        self.block = block
        self.half = own.shape[0] // block
        self.count = 2 * self.half
        size, me = lax.axis_size("head"), lax.axis_index("head")
        left = me < size // 2
        self.mid = (me == size // 2 - 1) | (me == size // 2)
        self.has_outer = (me > 0) & (me < size - 1)
        self.inner = jnp.where(left, me + 1, me - 1)
        self.outer = jnp.clip(jnp.where(left, me - 1, me + 1), 0, size - 1)

    @staticmethod
    def sems(rows, block):
        return DMA((5, 2 * rows // block))

    def rows(self, b):
        return pl.ds(pl.multiple_of(b * self.block, self.block), self.block)

    def slot(self, b):
        return self.rows(lax.rem(b, self.half))

    def in_copy(self, b, to):
        return pltpu.make_async_remote_copy(
            src_ref=self.own.at[self.slot(b)], dst_ref=self.got.at[self.slot(b)],
            send_sem=self.send1.at[b], recv_sem=self.got_in.at[b], device_id={"head": to}, device_id_type=MESH)

    def cross_copy(self, b):
        return pltpu.make_async_remote_copy(
            src_ref=self.own.at[self.slot(b)], dst_ref=self.total.at[self.rows(b)],
            send_sem=self.send1.at[b], recv_sem=self.got_total.at[b],
            device_id={"head": self.inner}, device_id_type=MESH)

    def out_copy(self, b, to):
        return pltpu.make_async_remote_copy(
            src_ref=self.total.at[self.rows(b)], dst_ref=self.total.at[self.rows(b)],
            send_sem=self.send2.at[b], recv_sem=self.got_total.at[b],
            device_id={"head": to}, device_id_type=MESH)

    def store(self, b):
        return pltpu.make_async_copy(
            self.total.at[self.rows(b)], self.out.at[self.rows(self.place(b))], self.stored.at[b])

    def inward(self, b):
        rows = self.slot(b)
        self.in_copy(b, self.outer).wait_recv()
        self.own[rows] = self.got[rows] + self.own[rows]

        @pl.when(self.mid)
        def _():
            self.cross_copy(b).start()

        @pl.when(jnp.logical_not(self.mid))
        def _():
            self.in_copy(b, self.inner).start()

    def outward(self, b):
        rows = self.rows(b)
        self.cross_copy(b).wait_recv()

        @pl.when(self.has_outer)
        def _():
            self.cross_copy(b).wait_send()

        @pl.when(self.mid)
        def _():
            self.total[rows] = self.own[self.slot(b)] + self.total[rows]

        @pl.when(self.has_outer)
        def _():
            self.out_copy(b, self.outer).start()
        self.store(b).start()

    def serve(self, first, last, lag):
        @pl.when(self.has_outer)
        def _():
            @pl.loop(first, last)
            def _(b):
                @pl.when(b < self.count)
                def _():
                    self.inward(b)

                @pl.when(b >= lag)
                def _():
                    self.outward(b - lag)

    def send(self, first, last):
        @pl.when(jnp.logical_not(self.has_outer))
        def _():
            @pl.loop(first, last)
            def _(b):
                @pl.when(b >= self.AHEAD)
                def _():
                    self.in_copy(b - self.AHEAD, self.inner).wait_send()

                @pl.when(b >= self.half)
                def _():
                    self.outward(b - self.half)
                self.in_copy(b, self.inner).start()

    def drain(self, first, last):
        @pl.loop(first, last)
        def _(b):
            self.store(b).wait()

            @pl.when(self.has_outer)
            def _():
                self.out_copy(b, self.outer).wait_send()

    def finish(self):
        last = self.count - 4

        @pl.when(jnp.logical_not(self.has_outer))
        def _():
            pl.loop(self.half, last)(self.outward)

            @pl.loop(self.count - self.AHEAD, self.count)
            def _(b):
                self.in_copy(b, self.inner).wait_send()
            self.drain(0, last)
            pl.loop(last, self.count)(self.outward)
            self.drain(last, self.count)

        @pl.when(self.has_outer)
        def _():
            self.drain(0, self.count)


class PairedSum:
    def __init__(self, own, pair, mine, slots, theirs, sems):
        self.own, self.pair, self.mine, self.slots, self.theirs = own, pair, mine, slots, theirs
        self.sems = sems
        self.me = lax.axis_index("seq")
        self.chip, self.odd = self.me // 2, lax.rem(self.me, 2)
        self.partner = self.me + 1 - 2 * self.odd
        self.chips, self.piece = own.shape[0], own.shape[1] // 2

    @staticmethod
    def scratch(rows, width):
        seq = lax.axis_size("seq")
        piece = max(16, rows // seq)
        part = pltpu.VMEM((seq // 2, piece, width), bf16)
        return [pltpu.VMEM((seq // 2, 2 * piece, width), bf16)] + [part] * 4 + [DMA((8, seq // 2))]

    def half(self, odd):
        return pl.ds(pl.multiple_of(odd * self.piece, self.piece), self.piece)

    def swap_copy(self):
        return pltpu.make_async_remote_copy(
            src_ref=self.own.at[:, self.half(1 - self.odd)], dst_ref=self.pair,
            send_sem=self.sems.at[0, 0], recv_sem=self.sems.at[1, 0],
            device_id={"seq": self.partner}, device_id_type=MESH)

    def back_copy(self):
        return pltpu.make_async_remote_copy(
            src_ref=self.pair, dst_ref=self.theirs,
            send_sem=self.sems.at[0, 1], recv_sem=self.sems.at[1, 1],
            device_id={"seq": self.partner}, device_id_type=MESH)

    def scatter_copy(self, to, source):
        return pltpu.make_async_remote_copy(
            src_ref=self.mine.at[to], dst_ref=self.slots.at[source],
            send_sem=self.sems.at[2, to], recv_sem=self.sems.at[3, source],
            device_id={"seq": 2 * to + self.odd}, device_id_type=MESH)

    def gather_copy(self, owner, to):
        return pltpu.make_async_remote_copy(
            src_ref=self.pair.at[owner], dst_ref=self.pair.at[owner],
            send_sem=self.sems.at[4, to], recv_sem=self.sems.at[5, owner],
            device_id={"seq": 2 * to + self.odd}, device_id_type=MESH)

    def release(self, free):
        pl.semaphore_signal(free, inc=1, device_id={"seq": self.partner}, device_id_type=MESH)

    def others(self, do):
        @pl.loop(1, self.chips)
        def _(k):
            do(lax.rem(self.chip + k, self.chips))

    def swap(self):
        self.swap_copy().start()

    def scatter(self):
        self.swap_copy().wait()
        self.mine[...] = (self.own[:, self.half(self.odd)].astype(f32) + self.pair[...].astype(f32)).astype(bf16)
        self.others(lambda other: self.scatter_copy(other, self.chip).start())

    def gather(self):
        self.others(lambda other: self.scatter_copy(self.chip, other).wait_recv())
        self.others(lambda other: self.scatter_copy(other, self.chip).wait_send())
        self.slots[self.chip] = self.mine[self.chip]
        total = self.slots[0].astype(f32)
        for k in range(1, self.chips):
            total = total + self.slots[k].astype(f32)
        self.pair[self.chip] = total.astype(bf16)
        self.others(lambda other: self.gather_copy(self.chip, other).start())

    def back(self):
        self.others(lambda other: self.gather_copy(other, self.chip).wait_recv())
        self.back_copy().start()

    def stores(self, out):
        for k in range(min(self.chips, out.shape[0] // (2 * self.piece))):
            for n, (odd, ref) in enumerate(((self.odd, self.pair), (1 - self.odd, self.theirs))):
                start = pl.multiple_of((2 * k + odd) * self.piece, self.piece)
                yield pltpu.make_async_copy(
                    ref.at[k], out.at[pl.ds(start, self.piece)], self.sems.at[6 + n, k])

    def finish(self, out):
        self.back_copy().wait()
        self.others(lambda other: self.gather_copy(self.chip, other).wait_send())
        for copy in self.stores(out):
            copy.start()

    def stored(self, out):
        for copy in self.stores(out):
            copy.wait()


class Swap:
    def __init__(self, axis, own, slots, sems):
        self.axis, self.own, self.slots = axis, own, slots
        self.send, self.got = sems.at[0], sems.at[1]
        self.size, self.me = lax.axis_size(axis), lax.axis_index(axis)

    def copy(self, to, source):
        return pltpu.make_async_remote_copy(
            src_ref=self.own, dst_ref=self.slots.at[source],
            send_sem=self.send.at[to], recv_sem=self.got.at[source],
            device_id={self.axis: to}, device_id_type=MESH)

    def start(self):
        @pl.loop(1, self.size)
        def _(k):
            self.copy(other_of(self.axis, k), self.me).start()
        self.slots[self.me] = self.own[...]

    def wait(self):
        @pl.loop(1, self.size)
        def _(k):
            self.copy(self.me, other_of(self.axis, k)).wait_recv()

    def total(self):
        out = self.slots[0]
        for k in range(1, self.size):
            out = out + self.slots[k]
        return out

    def finish(self):
        @pl.loop(1, self.size)
        def _(k):
            self.copy(other_of(self.axis, k), self.me).wait_send()


class DeviceScan:
    def __init__(self, backward, total, fade, lead, out, got, got_fade, sent, sent_fade, sems):
        self.backward, self.total, self.fade, self.lead, self.out = backward, total, fade, lead, out
        self.got, self.got_fade, self.sent, self.sent_fade, self.sems = got, got_fade, sent, sent_fade, sems
        self.me = lax.axis_index("seq")
        self.rounds = lax.axis_size("seq").bit_length() - 1

    @staticmethod
    def scratch(state, fade):
        rounds = lax.axis_size("seq").bit_length() - 1
        return [pltpu.VMEM(fade, f32), pltpu.VMEM(fade, f32)] + [
            pltpu.VMEM((rounds,) + state, bf16), pltpu.VMEM((rounds,) + fade, f32)] * 2 + [DMA((4, rounds))]

    def copies(self, k):
        return [
            pltpu.make_async_remote_copy(
                src_ref=src.at[k], dst_ref=dst.at[k],
                send_sem=self.sems.at[i, k], recv_sem=self.sems.at[i + 1, k],
                device_id={"seq": jnp.bitwise_xor(self.me, 1 << k)}, device_id_type=MESH)
            for src, dst, i in ((self.sent, self.got, 0), (self.sent_fade, self.got_fade, 2))]

    def begin(self, decay):
        self.fade[...] = decay
        self.out[...] = jnp.zeros_like(self.out)
        self.lead[...] = jnp.ones_like(self.lead)

    def start(self, k):
        self.sent[k] = self.total[...].astype(bf16)
        self.sent_fade[k] = self.fade[...]
        for copy in self.copies(k):
            copy.start()

    def finish(self, k):
        for copy in self.copies(k):
            copy.wait()
        later = lax.rem(self.me // (1 << k), 2) == (0 if self.backward else 1)

        @pl.when(later)
        def _():
            theirs = self.got[k].astype(f32)
            self.out[...] = self.out[...] + self.lead[0:1] * theirs
            self.total[...] = self.total[...] + self.fade[0:1] * theirs
            self.lead[...] = self.lead[...] * self.got_fade[k]

        @pl.when(jnp.logical_not(later))
        def _():
            self.total[...] = self.got[k].astype(f32) + self.got_fade[k, 0:1] * self.total[...]
        self.fade[...] = self.fade[...] * self.got_fade[k]

    def run(self, between=None):
        for k in range(self.rounds):
            self.start(k)
            if between is not None:
                between(k)
            self.finish(k)


GROUP = 256
STRIP = 128
GAP = 200.0
epsilon = 1e-05
LIMIT = 56 * 2**20


def dot(a, b):
    return jnp.dot(a, b, preferred_element_type=f32)


def dot_nt(a, b):
    return lax.dot_general(a, b, (((1,), (1,)), ((), ())), preferred_element_type=f32)


def dot_tn(a, b):
    return lax.dot_general(a, b, (((0,), (0,)), ((), ())), preferred_element_type=f32)


def split3(v):
    one = v.astype(bf16)
    rest = v - one.astype(f32)
    two = rest.astype(bf16)
    return one, two, (rest - two.astype(f32)).astype(bf16)


def exact_left(ones, v):
    width = v.shape[1]
    out = dot(ones, jnp.concatenate(split3(v), axis=1))
    return out[:, :width] + out[:, width : 2 * width] + out[:, 2 * width :]


def head_sum(v, group_ones):
    high = v.astype(bf16)
    low = (v - high.astype(f32)).astype(bf16)
    return dot(high, group_ones) + dot(low, group_ones)


def sigmoid(v):
    return 1.0 / (1.0 + jnp.exp(-v))


def softplus(v):
    return jnp.maximum(v, 0.0) + jnp.log1p(jnp.exp(-jnp.abs(v)))


def spread(cols, first, heads, head_dim):
    rows = cols.shape[0]
    per = 128 // head_dim
    lane = lax.broadcasted_iota(jnp.int32, (rows, 128), 1)
    tiles = []
    for at in range(0, heads, per):
        tile = cols[:, first + at : first + at + 1]
        for k in range(1, per):
            tile = jnp.where(lane < k * head_dim, tile, cols[:, first + at + k : first + at + k + 1])
        tiles.append(jnp.broadcast_to(tile, (rows, 128)))
    return jnp.concatenate(tiles, axis=1)


def norm_rows(block, gain):
    value = block.astype(f32)
    inv = lax.rsqrt(jnp.mean(value * value, axis=1, keepdims=True) + epsilon)
    return (value * inv * gain).astype(bf16)


def whole(shape):
    return pl.BlockSpec(shape, lambda g: (0,) * len(shape))


def lane_groups(rows, *parts):
    lane = lax.broadcasted_iota(jnp.int32, (rows, 128), 1)
    out = parts[-1]
    for k in range(len(parts) - 2, -1, -1):
        out = jnp.where(lane < 8 * (k + 1), parts[k], out)
    return out


FRONT = 512
RAW, STEP, CUM, DEV, KEEP = 0, 8, 16, 24, 32


def head_lanes(row, heads, lane):
    out = jnp.zeros(lane.shape, f32)
    for k in range(heads):
        out = jnp.where(lane % 8 == k, row[:, k : k + 1], out)
    return out


def loads_of(source, target, sems, first):
    parts = sems.shape[0]
    rows = source.shape[0] // parts
    return [pltpu.make_async_copy(source.at[pl.ds(k * rows, rows), pl.ds(first, target.shape[1])],
                                  target.at[pl.ds(k * rows, rows)], sems.at[k]) for k in range(parts)]


def front_kernel(heads, head_dim, state_dim, count,
                 tokens, last_tokens, pairs_hbm, flags, gain, proj_bc, proj_dt, conv_x_weight, conv_x_bias,
                 conv_bc_weight, conv_bc_bias, dt_bias, a_log, skip, norm_gain,
                 normed_out, x_in_out, x_conv_out, bc_in_out, bc_conv_out, heads_out, entering, decay_out,
                 halo_out, weights_hbm, zx_hbm, conv_w_out, params, gains_out, mask_out,
                 normed, x_active, tail_rows, landed, head_low, proj_all, conv_bc, conv_all, flag_cols, flag_ext,
                 x_ext, bc_ext, state, running, pairs, zx, weights_out, lead, fade,
                 scan_got, scan_got_fade, scan_sent, scan_sent_fade, scan_sems, proj_sems, conv_sems, row_sems, load_sems,
                 store_sem):
    at = pl.program_id(0)
    rows = tokens.shape[0]
    inner = heads * head_dim
    bc_width = 2 * state_dim
    bc_part = proj_bc.shape[0]
    seq, me = lax.axis_size("seq"), lax.axis_index("seq")
    block = lax.rem(at, count)
    mine = pl.ds(pl.multiple_of(block * rows, rows), rows)
    swaps = [Swap("head", proj_bc, proj_all, proj_sems), Swap("head", conv_bc, conv_all, conv_sems)]
    row_copy = pltpu.make_async_remote_copy(
        src_ref=tail_rows, dst_ref=landed, send_sem=row_sems.at[0], recv_sem=row_sems.at[1],
        device_id={"seq": lax.rem(me + 1, seq)}, device_id_type=MESH)
    lane_row = lax.broadcasted_iota(jnp.int32, (1, 128), 1)
    quarter = pairs.shape[0] // 4
    quarters = [pl.ds(k * quarter, quarter) for k in range(4)]
    loads = [pltpu.make_async_copy(pairs_hbm.at[each], pairs.at[each], load_sems.at[k])
             for k, each in enumerate(quarters)]
    zx_stores = [pltpu.make_async_copy(zx.at[each], zx_hbm.at[each], store_sem.at[1 + k])
                 for k, each in enumerate(quarters)]
    weights_store = pltpu.make_async_copy(weights_out, weights_hbm, store_sem.at[0])

    @pl.when(at == 0)
    def _():
        for copy in loads:
            copy.start()
        final = 1.0 - flags[flags.shape[0] - 1 :].astype(f32)
        one, two = final[:, 127:128], final[:, 126:127]
        row = lax.broadcasted_iota(jnp.int32, (16, 128), 0)
        mask = jnp.where(row == 15, 1.0, jnp.where(row == 14, one, jnp.where(row == 13, one * two, 0.0)))
        mask_out[...] = mask
        tail_rows[...] = (last_tokens[...].astype(f32) * mask[:, 0:1]).astype(bf16)
        conv_bc[...] = jnp.zeros_like(conv_bc)
        conv_bc[0:4, :bc_part] = conv_bc_weight[...].astype(f32)
        conv_bc[4:5, :bc_part] = conv_bc_bias[...]
        greet("head", "seq")
        row_copy.start()
        for each in swaps:
            each.start()
        params[...] = jnp.zeros_like(params)
        params[0:1] = head_lanes(dt_bias[...], heads, lane_row)
        params[1:2] = -jnp.exp(head_lanes(a_log[...], heads, lane_row))
        gains_out[...] = jnp.zeros_like(gains_out)
        gains_out[0:1] = norm_gain[...]
        gains_out[1:2] = spread(head_lanes(skip[...], heads, lane_row), 0, heads, head_dim)
        flat = flags[...].astype(f32)
        turned = jnp.concatenate([flat, jnp.zeros((128 - flat.shape[0], 128), f32)], axis=0).T
        conv_w_out[...] = jnp.zeros_like(conv_w_out)
        conv_w_out[0:4, :inner] = conv_x_weight[...].astype(f32)
        conv_w_out[4:5, :inner] = conv_x_bias[...]
        for k in range(flat.shape[0]):
            flag_cols[k * 128 : (k + 1) * 128] = jnp.broadcast_to(turned[:, k : k + 1], (128, 128))
        flag_ext[0:8] = jnp.zeros((8, 128), f32)

    def keeps(flag):
        flag_ext[8:] = flag
        one = 1.0 - flag
        two = one * (1.0 - flag_ext[7 : 7 + rows])
        three = two * (1.0 - flag_ext[6 : 6 + rows])
        flag_ext[0:8] = flag_ext[rows:]
        return one, two, three

    def convolve(ext, current, keep, first, last):
        ext[8:] = current
        total = conv_w_out[4:5, first:last] + conv_w_out[0:1, first:last] * current
        for j in range(1, 4):
            total = total + conv_w_out[j : j + 1, first:last] * ext[pl.ds(8 - j, rows)] * keep[j - 1][:, 0:1]
        ext[0:8] = ext[rows:]
        return total

    @pl.when(at < count)
    def _():
        low = norm_rows(tokens[...], gain[...])
        normed[mine] = low
        normed_out[...] = low

        @pl.when(at == 0)
        def _():
            for copy in loads:
                copy.wait()
            zx[:, :inner] = pairs[:, 0, :]
            zx[:, inner:] = pairs[:, 1, :]
            for copy in zx_stores:
                copy.start()
        x_in = dot(low, zx[:, inner:]).astype(bf16)
        x_in_out[...] = x_in

        @pl.when(at == 0)
        def _():
            row_copy.wait()
            head_low[...] = norm_rows(landed[...], gain[...])
            ahead = jnp.where(me > 0, dot(head_low[...], zx[:, inner:]), 0.0).astype(bf16)
            halo_out[:, :inner] = ahead
            x_ext[0:8] = ahead[8:].astype(f32)
        total = convolve(x_ext, x_in.astype(f32), keeps(flag_cols[mine]), 0, inner)
        x_conv_out[...] = total
        x_active[mine] = total * sigmoid(total)

    @pl.when(at == count)
    def _():
        for each in swaps:
            each.wait()
            each.finish()
        heads_there = proj_all.shape[0]
        for k in range(heads_there):
            weights_out[k * bc_part : (k + 1) * bc_part] = proj_all[k]
        eight = jnp.concatenate([proj_dt[...].astype(f32)] + (
            [jnp.zeros((8 - heads, proj_dt.shape[1]), f32)] if heads < 8 else []), axis=0)
        weights_out[bc_width:] = jnp.concatenate([eight] * 16, axis=0).astype(bf16)
        conv_w_out[:, inner:] = jnp.concatenate([conv_all[k, :, :bc_part] for k in range(heads_there)], axis=1)
        weights_store.start()
        ahead = jnp.where(me > 0, dot_nt(head_low[...], weights_out[:bc_width]), 0.0).astype(bf16)
        halo_out[:, inner:] = ahead
        bc_ext[0:8] = ahead[8:].astype(f32)
        state[...] = jnp.zeros_like(state)
        running[...] = jnp.zeros_like(running)
        flag_ext[0:8] = jnp.zeros((8, 128), f32)

    @pl.when(at >= count)
    def _():
        raw = dot_nt(normed[mine], weights_out[...])
        bc_in = raw[:, :bc_width].astype(bf16)
        bc_in_out[...] = bc_in
        flag = flag_cols[mine]
        keep = keeps(flag)
        total = convolve(bc_ext, bc_in.astype(f32), keep, inner, inner + bc_width)
        bc_conv_out[...] = total
        b_proj = (total[:, :state_dim] * sigmoid(total[:, :state_dim])).astype(bf16)

        order_r = lax.broadcasted_iota(jnp.int32, (GROUP, GROUP), 0)
        order_c = lax.broadcasted_iota(jnp.int32, (GROUP, GROUP), 1)
        lower = (order_r >= order_c).astype(bf16)
        lane = lax.broadcasted_iota(jnp.int32, (GROUP, 128), 1)
        for lo in range(0, rows, GROUP):
            part = slice(lo, lo + GROUP)
            step_raw = raw[part, bc_width:]
            step = softplus(step_raw + params[0:1])
            log_decay = step * params[1:2] - GAP * flag[part]
            cum = exact_left(lower, log_decay)
            kept = jnp.where(lane < KEEP + 1, keep[0][part], jnp.where(lane < KEEP + 2, keep[1][part], keep[2][part]))
            heads_out[part] = lane_groups(GROUP, step_raw, step, cum, cum + running[0:1], kept)
            end = cum[GROUP - 1 :]
            running[...] = running[...] + end
            weight = step * jnp.exp(end - cum)
            x_part = x_active[pl.ds(pl.multiple_of(block * rows + lo, GROUP), GROUP)]
            scaled = (x_part * spread(weight, 0, heads, head_dim)).astype(bf16)
            state[...] = state[...] * spread(jnp.exp(end), 0, heads, head_dim) + dot_tn(b_proj[part], scaled)

    @pl.when(at == 2 * count - 1)
    def _():
        decay = spread(jnp.exp(running[...]), 0, heads, head_dim)
        decay_out[...] = decay
        scan = DeviceScan(False, state, fade, lead, entering, scan_got, scan_got_fade, scan_sent,
                          scan_sent_fade, scan_sems)
        scan.begin(decay)
        scan.run()
        for copy in [weights_store] + zx_stores:
            copy.wait()


def front(tokens, proj_zx, flags, gain, proj_bc, proj_dt, conv_x_weight, conv_x_bias, conv_bc_weight, conv_bc_bias,
          dt_bias, a_log, skip, norm_gain, heads, head_dim, state_dim):
    length, width = tokens.shape
    block = FRONT
    count = length // block
    inner = heads * head_dim
    conv = inner + 2 * state_dim
    head_count = lax.axis_size("head")

    def early(cols):
        return pl.BlockSpec((block, cols), lambda g: (jnp.minimum(g, count - 1), 0))

    def late(cols):
        return pl.BlockSpec((block, cols), lambda g: (jnp.maximum(g - count, 0), 0))
    shape = jax.ShapeDtypeStruct
    state, fade = (state_dim, inner), (8, inner)
    rest = 2 * state_dim + 128
    return pl.pallas_call(
        functools.partial(front_kernel, heads, head_dim, state_dim, count),
        grid=(2 * count,),
        out_shape=(shape((length, width), bf16), shape((length, inner), bf16), shape((length, inner), f32),
                   shape((length, conv - inner), bf16), shape((length, conv - inner), f32),
                   shape((length, 128), f32), shape(state, f32),
                   shape(fade, f32), shape((16, conv), bf16), shape((rest, width), bf16), shape((width, 2 * inner), bf16),
                   shape((8, conv), f32), shape((8, 128), f32), shape((8, inner), f32), shape((16, 128), f32)),
        in_specs=[early(width), pl.BlockSpec((16, width), lambda g: (length // 16 - 1, 0)), HBM] + [VMEM] * 12,
        out_specs=(early(width), early(inner), early(inner), late(conv - inner), late(conv - inner), late(128))
        + (VMEM,) * 3 + (HBM,) * 2 + (VMEM,) * 4,
        scratch_shapes=[
            pltpu.VMEM((length, width), bf16), pltpu.VMEM((length, inner), f32),
            pltpu.VMEM((16, width), bf16), pltpu.VMEM((16, width), bf16), pltpu.VMEM((16, width), bf16),
            pltpu.VMEM((head_count,) + proj_bc.shape, bf16), pltpu.VMEM((8, 128), f32),
            pltpu.VMEM((head_count, 8, 128), f32), pltpu.VMEM((length, 128), f32),
            pltpu.VMEM((block + 8, 128), f32), pltpu.VMEM((block + 8, inner), f32),
            pltpu.VMEM((block + 8, conv - inner), f32), pltpu.VMEM(state, f32), pltpu.VMEM((8, 128), f32),
            pltpu.VMEM(proj_zx.shape, bf16), pltpu.VMEM((width, 2 * inner), bf16), pltpu.VMEM((rest, width), bf16)]
        + DeviceScan.scratch(state, fade) + [DMA((2, head_count)), DMA((2, head_count)), DMA((2,)), DMA((4,)), DMA((5,))],
        compiler_params=pltpu.CompilerParams(
            dimension_semantics=("arbitrary",), collective_id=3, has_side_effects=True,
            vmem_limit_bytes=LIMIT),
        name="front",
    )(tokens, tokens, proj_zx, flags, gain, proj_bc, proj_dt, conv_x_weight, conv_x_bias, conv_bc_weight,
      conv_bc_bias, dt_bias, a_log, skip, norm_gain)


def strips(rows):
    return [(lo, lo + STRIP) for lo in range(0, rows, STRIP)]


def mix_step(heads, head_dim, state_dim, at,
             x_conv, bc_conv, heads_in, normed, zx, cot, out_proj, gains, entering,
             ssm_out, d_normed_out, partial_out, sums_out, starts_out, state, between):
    rows = x_conv.shape[0]
    inner = heads * head_dim
    per = 128 // head_dim

    @pl.when(at == 0)
    def _():
        state[...] = entering[...]

    values = jnp.concatenate([x_conv[...], bc_conv[...]], axis=1)
    active = values * sigmoid(values)
    x = active[:, :inner]
    b_proj = active[:, inner : inner + state_dim].astype(bf16)
    c_proj = active[:, inner + state_dim :].astype(bf16)
    info = heads_in[...]
    flipped = info.T
    stepped = x * spread(info, STEP, heads, head_dim)
    low = stepped.astype(bf16)
    scores = dot_nt(c_proj, b_proj)
    lane = lax.broadcasted_iota(jnp.int32, (rows, 128), 1)
    tiles = []
    for pair in range(heads // per):
        tile = low[:, pair * 128 : (pair + 1) * 128]
        weights, masked = [], []
        for k in range(per):
            head = pair * per + k
            masked.append(jnp.where((lane >= k * head_dim) & (lane < (k + 1) * head_dim), tile,
                                    jnp.zeros_like(tile)))
            parts = []
            for lo, hi in strips(rows):
                gap = info[lo:hi, CUM + head : CUM + head + 1] - flipped[CUM + head : CUM + head + 1, :hi]
                ok = (lax.broadcasted_iota(jnp.int32, (STRIP, hi), 0) + lo
                      >= lax.broadcasted_iota(jnp.int32, (STRIP, hi), 1))
                part = (jnp.exp(jnp.where(ok, gap, -1e30)) * scores[lo:hi, :hi]).astype(bf16)
                if hi < rows:
                    part = jnp.concatenate([part, jnp.zeros((STRIP, rows - hi), bf16)], axis=1)
                parts.append(part)
            weights.append(jnp.concatenate(parts, axis=0))
        tiles.append(dot(jnp.concatenate(weights, axis=1), jnp.concatenate(masked, axis=0)))
        if pair == heads // per // 2 - 1:
            between()
    inside = jnp.concatenate(tiles, axis=1)
    cum = info[:, CUM : CUM + 8]
    end = info[rows - 1 : rows]
    start = state[...]
    starts_out[at] = start.astype(bf16)
    grown = spread(jnp.exp(info), CUM, heads, head_dim)
    result = inside + grown * dot(c_proj, start.astype(bf16)) + gains[1:2] * x
    fade = spread(jnp.exp(end - info), CUM, heads, head_dim)
    state[...] = start * spread(jnp.exp(end), CUM, heads, head_dim) + dot_tn(b_proj, (stepped * fade).astype(bf16))
    ssm_out[...] = result
    z = dot(normed[...], zx[:, :inner])
    gated = result * (z * sigmoid(z))
    d_normed = dot_nt(cot[...], out_proj[...])
    d_normed_out[...] = d_normed.astype(bf16)
    scaled = gated * gains[0:1]
    partial_out[...] = dot(scaled.astype(bf16), out_proj[...]).astype(bf16)
    squares = jnp.sum(gated * gated, axis=1, keepdims=True)
    cross = jnp.sum(d_normed * scaled, axis=1, keepdims=True)
    turned = jnp.where(lane == 0, squares, cross).T
    sums_out[0, pl.ds(at, 1)] = turned[0:1]
    sums_out[1, pl.ds(at, 1)] = turned[1:2]


def gate_step(heads, head_dim, state_dim, all_channels, at,
              ssm, d_normed, sums, x_conv, bc_conv, heads_in, normed, zx, cot, gains,
              d_ssm_out, d_gate_out, grad_out, rows_out, total_out):
    rows = ssm.shape[0]
    inner = heads * head_dim

    @pl.when(at == 0)
    def _():
        grad_out[...] = jnp.zeros_like(grad_out)
        rows_out[...] = jnp.zeros_like(rows_out)
        total_out[...] = jnp.zeros_like(total_out)

    tall = jnp.concatenate([sums[0, pl.ds(at, 1)], sums[1, pl.ds(at, 1)], jnp.zeros((126, rows), f32)], axis=0).T
    inv = lax.rsqrt(tall[:, 0:1] / all_channels + epsilon)
    cross = tall[:, 1:2] / all_channels
    z = dot(normed[...], zx[:, :inner])
    s = sigmoid(z)
    y = ssm[...]
    gated = y * (z * s)
    gain = gains[0:1]
    back = d_normed[...].astype(f32)
    unit = gated * inv
    d_gated = inv * (back * gain - unit * (inv * cross))
    grad_out[:, : cot.shape[1]] += dot_tn((unit * gain).astype(bf16), cot[...])
    d_ssm = d_gated * (z * s)
    d_ssm_out[...] = d_ssm
    d_gate_out[...] = (d_gated * y * (s * (1.0 + z * (1.0 - s)))).astype(bf16)
    x_values, c_values = x_conv[...], bc_conv[:, state_dim:]
    rows_out[0:1] += jnp.sum(back * unit, axis=0, keepdims=True)
    rows_out[1:2] += jnp.sum(d_ssm * (x_values * sigmoid(x_values)), axis=0, keepdims=True)
    c_proj = (c_values * sigmoid(c_values)).astype(bf16)
    grown = spread(jnp.exp(heads_in[...]), DEV, heads, head_dim)
    total_out[...] += dot_tn(c_proj, (grown * d_ssm).astype(bf16))


def back_step(heads, head_dim, state_dim, first_step, last_step,
              d_ssm, x_conv, bc_conv, x_in, bc_in, heads_in, start, entering, conv_w, params, skip, conv_halo,
              d_conv_in_out, d_step_out, conv_grads, head_grads, halo_out,
              lam, later, later_info, between):
    rows = d_ssm.shape[0]
    inner = heads * head_dim
    per = 128 // head_dim

    @pl.when(first_step)
    def _():
        lam[...] = entering[...]
        conv_grads[...] = jnp.zeros_like(conv_grads)
        head_grads[...] = jnp.zeros_like(head_grads)
        for each in (later, later_info):
            each[rows:] = jnp.zeros((8, each.shape[1]), f32)

    values = jnp.concatenate([x_conv[...], bc_conv[...]], axis=1)
    gates = sigmoid(values)
    active = values * gates
    x = active[:, :inner]
    b_proj = active[:, inner : inner + state_dim].astype(bf16)
    c_proj = active[:, inner + state_dim :].astype(bf16)
    info = heads_in[...]
    flipped = info.T
    step = spread(info, STEP, heads, head_dim)
    stepped = x * step
    low = stepped.astype(bf16)
    dy = d_ssm[...]
    dy_low = dy.astype(bf16)
    scores = dot_nt(b_proj, c_proj)
    lane = lax.broadcasted_iota(jnp.int32, (rows, 128), 1)
    lane_one = lax.broadcasted_iota(jnp.int32, (STRIP, 128), 1)
    cuts = strips(rows)
    d_scores = [jnp.zeros((STRIP, rows - lo), f32) for lo, _ in cuts]
    d_rows = []
    d_cols = [jnp.zeros((STRIP, 128), f32) for _ in cuts]
    tiles = []
    for pair in range(heads // per):
        tile = low[:, pair * 128 : (pair + 1) * 128]
        dy_tile = dy_low[:, pair * 128 : (pair + 1) * 128]
        owns = [(lane >= k * head_dim) & (lane < (k + 1) * head_dim) for k in range(per)]
        stacked = jnp.concatenate([jnp.where(own, tile, jnp.zeros_like(tile)) for own in owns], axis=0)
        all_pairs = dot_nt(stacked, dy_tile)
        weights = []
        for k in range(per):
            head = pair * per + k
            row_total = jnp.zeros((1, rows), f32)
            parts = []
            for n, (lo, hi) in enumerate(cuts):
                gap = flipped[CUM + head : CUM + head + 1, lo:] - info[lo:hi, CUM + head : CUM + head + 1]
                ok = (lax.broadcasted_iota(jnp.int32, (STRIP, rows - lo), 1)
                      >= lax.broadcasted_iota(jnp.int32, (STRIP, rows - lo), 0))
                decay = jnp.exp(jnp.where(ok, gap, -1e30))
                weight = decay * scores[lo:hi, lo:]
                part = weight.astype(bf16)
                if lo:
                    part = jnp.concatenate([jnp.zeros((STRIP, lo), bf16), part], axis=1)
                parts.append(part)
                pairs = all_pairs[k * rows + lo : k * rows + hi, lo:]
                d_scores[n] = d_scores[n] + pairs * decay
                moved = pairs * weight
                d_cols[n] = d_cols[n] - jnp.where(lane_one == head, jnp.sum(moved, axis=1, keepdims=True), 0.0)
                col = jnp.sum(moved, axis=0, keepdims=True)
                if lo:
                    col = jnp.concatenate([jnp.zeros((1, lo), f32), col], axis=1)
                row_total = row_total + col
            weights.append(jnp.concatenate(parts, axis=0))
            d_rows.append(row_total)
        dy_stack = jnp.concatenate([jnp.where(own, dy_tile, jnp.zeros_like(dy_tile)) for own in owns], axis=0)
        tiles.append(dot(jnp.concatenate(weights, axis=1), dy_stack))
        between(pair + 1)
    d_stepped = jnp.concatenate(tiles, axis=1)
    d_cum = jnp.concatenate(d_cols, axis=0)
    d_cum = d_cum + jnp.concatenate(d_rows + [jnp.zeros((128 - heads, rows), f32)], axis=0).T
    full = jnp.concatenate(
        [jnp.concatenate([jnp.zeros((STRIP, lo), f32), part], axis=1) if lo else part
         for part, (lo, _) in zip(d_scores, cuts)], axis=0).astype(bf16)
    d_b = dot(full, c_proj)
    d_c = dot_tn(full, b_proj)

    group_ones = (lax.broadcasted_iota(jnp.int32, (inner, 128), 0) // head_dim
                  == lax.broadcasted_iota(jnp.int32, (inner, 128), 1)).astype(bf16)
    after = lam[...]
    after_low = after.astype(bf16)
    end = info[rows - 1 : rows]
    grown = spread(jnp.exp(info), CUM, heads, head_dim)
    fade = spread(jnp.exp(end - info), CUM, heads, head_dim)
    end_grown = spread(jnp.exp(end), CUM, heads, head_dim)
    from_after = fade * dot(b_proj, after_low)
    d_stepped = d_stepped + from_after
    grown_dy = grown * dy
    grown_low = grown_dy.astype(bf16)
    left = stepped * from_after
    to_cum = head_sum(grown_dy * dot(c_proj, start) - left, group_ones)
    kept = jnp.sum(after * start.astype(f32), axis=0, keepdims=True) * end_grown
    kept = kept + jnp.sum(left, axis=0, keepdims=True)
    last = head_sum(jnp.broadcast_to(kept, (8, inner)), group_ones)[0:1]
    row_id = lax.broadcasted_iota(jnp.int32, (rows, 128), 0)
    d_cum = d_cum + to_cum + jnp.where(row_id == rows - 1, last, 0.0)
    d_c = d_c + dot_nt(grown_low, start)
    d_b = d_b + dot_nt((fade * stepped).astype(bf16), after_low)
    lam[...] = end_grown * after + dot_tn(c_proj, grown_low)
    d_step = dot((d_stepped * x).astype(bf16), group_ones)
    d_x = step * d_stepped + skip[0:1] * dy
    between(heads // per + 1)

    order_r = lax.broadcasted_iota(jnp.int32, (rows, rows), 0)
    order_c = lax.broadcasted_iota(jnp.int32, (rows, rows), 1)
    d_decay = exact_left((order_r <= order_c).astype(bf16), d_cum) * info[:, KEEP : KEEP + 1]
    rate = params[1:2]
    real = lane < heads
    step_raw = jnp.where(real, info, 0.0) + params[0:1]
    slope = sigmoid(step_raw)
    d_pre = jnp.where(real, (d_step + d_decay * rate) * slope, 0.0)
    d_step_out[...] = d_pre.astype(bf16)
    head_grads[0:1] += jnp.sum(d_pre, axis=0, keepdims=True)
    head_grads[1:2] += jnp.sum(jnp.where(real, d_decay * softplus(step_raw) * rate, 0.0), axis=0, keepdims=True)

    d_active = jnp.concatenate([d_x, d_b, d_c], axis=1)
    d_conv = d_active * (gates * (1.0 + values * (1.0 - gates)))
    taken = jnp.concatenate([x_in[...], bc_in[...]], axis=1).astype(f32)
    total = d_conv * conv_w[0:1]
    conv_grads[0:1] += jnp.sum(d_conv * taken, axis=0, keepdims=True)
    conv_grads[4:5] += jnp.sum(d_conv, axis=0, keepdims=True)
    later[0:rows] = d_conv
    later_info[0:rows] = info
    for j in range(1, 4):
        moved = later[pl.ds(j, rows)] * later_info[pl.ds(j, rows)][:, KEEP + j - 1 : KEEP + j]
        total = total + moved * conv_w[j : j + 1]
        conv_grads[j : j + 1] += jnp.sum(moved * taken, axis=0, keepdims=True)
    d_conv_in_out[...] = total.astype(bf16)

    @pl.when(last_step)
    def _():
        ahead = conv_halo[...].astype(f32)
        halo_out[...] = jnp.zeros_like(halo_out)
        for j in range(1, 4):
            first = later[0:8] * later_info[0:8, KEEP + j - 1 : KEEP + j]
            for t in range(j):
                row = 16 + t - j
                conv_grads[j : j + 1] += first[t : t + 1] * ahead[row : row + 1]
                halo_out[row - 8 : row - 7] += first[t : t + 1] * conv_w[j : j + 1]
    for each in (later, later_info):
        each[rows:] = each[0:8]


def block_place(per, blocks):
    def place(b):
        late = b - blocks - (per - 1)
        group = 2 * blocks - 2 * per - late // per * per + late % per
        second = jnp.where(b < blocks + per - 1, b + blocks - per, group)
        return jnp.where((b < blocks) | (b == 2 * blocks - 1), b, second)
    return place


def layer_kernel(heads, head_dim, state_dim, all_channels, count, block, lag, plans, steps, owners, taps,
                 x_conv, bc_conv, x_in, bc_in, heads_in, cot, normed, last_normed, op_hbm, gains, entering, decay,
                 conv_w, params, conv_halo, zx_hbm, weights, gain, tail_mask,
                 totals_out, sums_out, zx_out, op_out, bc_out, small_out,
                 own, got, total, held, ssm, d_normed, starts, state, leaving, later, later_info,
                 sums, sum_slots, lead, fade,
                 scan_got, scan_got_fade, scan_sent, scan_sent_fade, scan_sems,
                 grad, sum_own, sum_pair, sum_mine, sum_slot, sum_theirs, sum_sems, grad_bc,
                 bc_slots, bc_z, bc_res, small, small_slots, small_own, small_z,
                 d_conv, d_step, gate_rows, conv_grads, head_grads, halo_rows, landed,
                 line_sems, swap_sems, bc_sems, bcz_sems, small_sems, smallz_sems, row_sems, free_sem, zx,
                 out_proj, load_sems, op_load_sems):
    at = pl.program_id(0)
    rows, width = cot.shape
    inner = heads * head_dim
    bc_width = 2 * state_dim
    seq, head_count = lax.axis_size("seq"), lax.axis_size("head")
    me, my_head = lax.axis_index("seq"), lax.axis_index("head")
    per = rows // block
    line = LineSum(own, got, total, totals_out, block_place(per, count * per), line_sems, block)
    swap = Swap("head", sums, sum_slots, swap_sems)
    scan = DeviceScan(True, state, fade, lead, leaving, scan_got, scan_got_fade, scan_sent, scan_sent_fade,
                      scan_sems)
    op_rows = max(16, inner // seq)
    sum_refs = (sum_own, sum_pair, sum_mine, sum_slot, sum_theirs)
    op_sum = PairedSum(*(ref.at[:, : op_rows * (2 if ref is sum_own else 1), :width] for ref in sum_refs),
                       sum_sems.at[0])
    zx_sum = PairedSum(*(ref.at[:, :, : 2 * inner] for ref in sum_refs), sum_sems.at[1])
    small_swap = Swap("seq", small, small_slots, small_sems)
    both_swap = Swap("head", small_own, small_z, smallz_sems)
    row_copy = pltpu.make_async_remote_copy(
        src_ref=halo_rows, dst_ref=landed, send_sem=row_sems.at[0], recv_sem=row_sems.at[1],
        device_id={"seq": lax.rem(me + seq - 1, seq)}, device_id_type=MESH)
    served, sent = plans
    back_points = inner // 128 + 3
    back_at = at - 2 * count - 1
    last_step = back_at == count - 1

    def serve(phase, k):
        line.send(*sent.span(phase, k))
        line.serve(*served.span(phase, k), lag)

    def serve_mix(k):
        @pl.when(at > 0)
        def _():
            serve(1, MIX_POINTS * (at - 1) + k)

    loads = loads_of(zx_hbm, zx, load_sems, 0) + loads_of(op_hbm, out_proj, op_load_sems, 0)

    @pl.when(at == 0)
    def _():
        for copy in loads:
            copy.start()
        greet("head", "seq")
        state[...] = entering[...]
        for copy in loads:
            copy.wait()

    @pl.when(at < count)
    def _():
        mine = pl.ds(pl.multiple_of(at * rows, rows), rows)
        serve_mix(0)
        mix_step(heads, head_dim, state_dim, at, x_conv, bc_conv, heads_in, normed, zx, cot, out_proj, gains, entering,
                 ssm.at[mine], d_normed.at[mine], own.at[mine], sums, starts, state,
                 lambda: serve_mix(1))

    @pl.when(at == count - 1)
    def _():
        swap.start()

    @pl.when((at >= count) & (at < 2 * count))
    def _():
        serve(2, at - count)

    @pl.when(at == count)
    def _():
        swap.wait()
        sums_out[...] = swap.total()
        swap.finish()
        grad[...] = jnp.zeros_like(grad)
        gate_rows[...] = jnp.zeros_like(gate_rows)
        state[...] = jnp.zeros_like(state)

    @pl.when((at >= count) & (at < 2 * count))
    def _():
        here = at - count
        mine = pl.ds(pl.multiple_of(here * rows, rows), rows)
        gate_step(heads, head_dim, state_dim, all_channels, here,
                  ssm.at[mine], d_normed.at[mine], sums_out, x_conv, bc_conv, heads_in, normed, zx, cot, gains,
                  ssm.at[mine], d_normed.at[mine], grad.at[:inner], gate_rows, state)

    @pl.when(at == 2 * count)
    def _():
        for k in range(seq // 2):
            lo, hi = min(inner, k * 2 * op_rows), min(inner, (k + 1) * 2 * op_rows)
            if hi > lo:
                sum_own[k, : hi - lo, :width] = grad[lo:hi, :width].astype(bf16)
        scan.begin(decay[...])
        scan.run(lambda k: serve(3, k))
        op_sum.swap()
        grad[...] = jnp.zeros_like(grad)
        grad_bc[...] = jnp.zeros_like(grad_bc)
        small[...] = jnp.zeros_like(small)

    def project(block_low, gate_low, conv_low, rest_low):
        d_rows = dot_nt(conv_low, zx[:, inner:]) + dot(rest_low, weights[...])
        grad[:, inner : 2 * inner] += dot_tn(block_low, conv_low)
        if gate_low is not None:
            d_rows = d_rows + dot_nt(gate_low, zx[:, :inner])
            grad[:, :inner] += dot_tn(block_low, gate_low)
        grad_bc[...] += dot_tn(rest_low, block_low).reshape(grad_bc.shape)
        small[16:17] += jnp.sum(d_rows * block_low.astype(f32), axis=0, keepdims=True) / gain[...]
        return d_rows

    @pl.when(at > 2 * count)
    def _():
        here = 3 * count - at
        mine = pl.ds(pl.multiple_of(here * rows, rows), rows)
        serve(4, back_points * back_at)
        back_step(heads, head_dim, state_dim, back_at == 0, last_step,
                  ssm.at[mine], x_conv, bc_conv, x_in, bc_in, heads_in, starts[here], leaving, conv_w, params,
                  gains[1:2], conv_halo, d_conv, d_step, conv_grads, head_grads, halo_rows,
                  state, later, later_info, lambda k: serve(4, back_points * back_at + k))

        @pl.when(last_step)
        def _():
            row_copy.start()
        serve(4, back_points * back_at + back_points - 1)
        rest_low = jnp.concatenate([d_conv[:, inner:], d_step[...]], axis=1)
        d_rows = project(normed[...], d_normed[mine], d_conv[:, :inner], rest_low).astype(bf16)

        @pl.when(back_at == 0)
        def _():
            own[: rows - block] = d_rows[: rows - block]
            held[...] = d_rows[rows - block :]

        @pl.when(back_at > 0)
        def _():
            start = pl.multiple_of(back_at * rows - block, block)
            own[pl.ds(start, rows)] = d_rows

    @pl.when(back_at == 1)
    def _():
        op_sum.scatter()

    @pl.when(back_at == 3)
    def _():
        op_sum.gather()

    @pl.when(back_at == 5)
    def _():
        op_sum.back()

    piece = grad_bc.shape[1] // owners

    def bc_scatter(to, source):
        return pltpu.make_async_remote_copy(
            src_ref=grad_bc.at[:head_count, pl.ds(pl.multiple_of(to * piece, piece), piece)],
            dst_ref=bc_slots.at[source], send_sem=bc_sems.at[0, to], recv_sem=bc_sems.at[1, source],
            device_id={"seq": to}, device_id_type=MESH)

    def bc_gather(owner, to):
        rows = pl.ds(pl.multiple_of(owner * piece, piece), piece)
        return pltpu.make_async_remote_copy(
            src_ref=bc_res.at[rows], dst_ref=bc_res.at[rows],
            send_sem=bc_sems.at[2, to], recv_sem=bc_sems.at[3, owner],
            device_id={"seq": to}, device_id_type=MESH)

    def bc_swap(to, source):
        return pltpu.make_async_remote_copy(
            src_ref=bc_slots.at[me, to], dst_ref=bc_z.at[source],
            send_sem=bcz_sems.at[0, to], recv_sem=bcz_sems.at[1, source],
            device_id={"head": to}, device_id_type=MESH)

    @pl.when(last_step)
    def _():
        op_sum.finish(op_out)
        at_block = [served.before[-1], sent.before[-1]]

        def go(more):
            until = min(line.count + lag, at_block[0] + more)
            ahead = max(at_block[1], min(line.count - (0 if filled else 1), until + 2))
            line.send(at_block[1], ahead)
            line.serve(at_block[0], until, lag)
            at_block[:] = [until, ahead]
        filled = False
        go(steps[0])
        row_copy.wait()
        extra = jnp.where(me < seq - 1, landed[...] * tail_mask[8:, 0:1], 0.0)
        extra = jnp.concatenate([jnp.zeros_like(extra), extra], axis=0).astype(bf16)
        extra_rest = jnp.concatenate([extra[:, inner:], jnp.zeros((16, 128), bf16)], axis=1)
        more = project(last_normed[...], None, extra[:, :inner], extra_rest)
        final = held[...].astype(f32) + jnp.concatenate([jnp.zeros((block - 16, width), f32), more], axis=0)
        own[count * rows - block :] = final.astype(bf16)
        filled = True
        go(steps[1])

        op_sum.stored(op_out)
        op_sum.release(free_sem)
        pair_rows = sum_own.shape[1]
        for k in range(sum_own.shape[0]):
            sum_own[k, :, : 2 * inner] = grad[k * pair_rows : (k + 1) * pair_rows, : 2 * inner].astype(bf16)
        pl.semaphore_wait(free_sem, 1)
        zx_sum.swap()
        go(steps[2])
        small[0:8] += grad_bc[head_count, 0:8]
        small[8 : 9 + taps, :inner] = conv_grads[: taps + 1, :inner]
        small[8:10, inner : 2 * inner] = gate_rows[0:2]
        small[10:12, inner : inner + 128] = head_grads[0:2]
        small[17 : 18 + taps, :bc_width] = conv_grads[: taps + 1, inner:]
        small_swap.start()

        @pl.loop(1, seq)
        def _(k):
            to = other_of("seq", k)

            @pl.when(to < owners)
            def _():
                bc_scatter(to, me).start()

        go(steps[3])
        zx_sum.scatter()
        go(steps[4])
        small_swap.wait()
        sums_small = small_swap.total()
        lone = small.shape[0] - small_own.shape[0]
        small_out[:lone] = sums_small[:lone]
        small_own[...] = sums_small[lone:]
        both_swap.start()
        go(steps[5])

        @pl.when(me < owners)
        def _():
            @pl.loop(1, seq)
            def _(k):
                bc_scatter(me, other_of("seq", k)).wait_recv()
            bc_slots[me] = grad_bc[:head_count, pl.ds(pl.multiple_of(me * piece, piece), piece)]
            sums_bc = bc_slots[0]
            for k in range(1, seq):
                sums_bc = sums_bc + bc_slots[k]
            bc_slots[me] = sums_bc
            bc_z[my_head] = bc_slots[me, my_head]

            @pl.loop(1, head_count)
            def _(k):
                bc_swap(other_of("head", k), my_head).start()

        go(steps[6])
        zx_sum.gather()
        go(steps[7])
        both_swap.wait()
        small_out[lone:] = both_swap.total()

        @pl.when(me < owners)
        def _():
            @pl.loop(1, head_count)
            def _(k):
                bc_swap(my_head, other_of("head", k)).wait_recv()
            sums_bc = bc_z[0]
            for k in range(1, head_count):
                sums_bc = sums_bc + bc_z[k]
            bc_res[pl.ds(pl.multiple_of(me * piece, piece), piece)] = sums_bc

            @pl.loop(1, seq)
            def _(k):
                bc_gather(me, other_of("seq", k)).start()

        go(steps[8])
        zx_sum.back()
        go(steps[9])
        zx_sum.finish(zx_out)
        go(line.count + lag)
        line.finish()
        zx_sum.stored(zx_out)
        small_swap.finish()
        both_swap.finish()

        @pl.loop(1, seq)
        def _(k):
            other = other_of("seq", k)

            @pl.when(other < owners)
            def _():
                bc_gather(other, me).wait_recv()
                bc_scatter(other, me).wait_send()

            @pl.when(me < owners)
            def _():
                bc_gather(me, other).wait_send()
        bc_out[...] = bc_res[...]

        @pl.when(me < owners)
        def _():
            @pl.loop(1, head_count)
            def _(k):
                bc_swap(other_of("head", k), my_head).wait_send()


def layer(x_conv, bc_conv, x_in, bc_in, heads_in, cot, normed, out_proj, gains, entering, decay, conv_w, params,
          conv_halo, zx, weights, gain, tail_mask, heads, head_dim, state_dim, all_channels, taps):
    length, inner = x_conv.shape
    conv = inner + bc_conv.shape[1]
    count = length // GROUP
    width = cot.shape[1]
    seq, head_count = lax.axis_size("seq"), lax.axis_size("head")
    block = BLOCK
    pace = PACE * block // 64
    blocks = length // block
    per = GROUP // block
    lag = max(LAG, head_count // 2 - 1)
    back_points = inner // 128 + 3
    gate_at = MIX * count + SWAP
    scan_at = gate_at + GATE * count
    back_start = scan_at + SCAN
    rounds = seq.bit_length() - 1
    phases = [(MIX_POINTS, -(10**6), 0), (MIX_POINTS * (count - 1), MIX, MIX // MIX_POINTS), (count, gate_at, GATE),
              (rounds, scan_at, SCAN // rounds), (back_points * count, back_start, BACK // back_points)]
    served = Pace(phases, pace, LATE, 2 * blocks + lag)
    sent = Pace(phases, pace, EARLY, 2 * blocks)
    for k in range(count):
        point = (k + 1) * back_points - 1
        assert served.count(4, point) >= min(blocks, (k + 1) * per) + lag
        assert sent.count(4, point) >= min(blocks, (k + 1) * per) + LineSum.AHEAD
        for each in (served, sent):
            assert each.count(4, point) <= blocks + max(0, k * per - 1)
    steps = [step * 64 // block for step in STEPS]

    def by(cols, first, step):
        def index(g):
            ahead = jnp.where(g < count, g, jnp.where(g < 2 * count, g - count, jnp.minimum(3 * count - g, count - 1)))
            if first == 2:
                ahead = jnp.where(g < 2 * count, count - 1, ahead)
            if step == 1:
                ahead = jnp.where(g < 2 * count, ahead, count - 1)
            return (ahead, 0)
        return pl.BlockSpec((GROUP, cols), index)
    shape = jax.ShapeDtypeStruct
    state, fade = (state_dim, inner), (8, inner)
    bc_rows = (conv - inner) // head_count
    owners = min(seq, bc_rows // 8)
    piece = bc_rows // owners
    vm = pltpu.VMEM
    grad_rows = max(width, inner)
    paired = PairedSum.scratch(width, max(width, 2 * inner))
    return pl.pallas_call(
        functools.partial(layer_kernel, heads, head_dim, state_dim, all_channels, count, block, lag,
                          (served, sent), steps, owners, taps),
        grid=(3 * count + 1,),
        out_shape=(shape((2 * length, width), bf16), shape((2, count, GROUP), f32),
                   shape((width, 2 * inner), bf16), shape((inner, width), bf16), shape((bc_rows, width), f32),
                   shape((24, width), f32)),
        in_specs=[by(inner, 0, 2), by(conv - inner, 0, 2), by(inner, 2, 2), by(conv - inner, 2, 2),
                  by(128, 0, 2), by(width, 0, 1), by(width, 0, 2), pl.BlockSpec((16, width), lambda g: (length // 16 - 1, 0))]
        + [HBM] + [VMEM] * 6 + [HBM] + [VMEM] * 3,
        out_specs=(HBM, VMEM, HBM, HBM, VMEM, VMEM),
        scratch_shapes=[
            vm((length, width), bf16), vm((length, width), bf16), vm((2 * length, width), bf16),
            vm((block, width), bf16), vm((length, inner), f32), vm((length, inner), bf16),
            vm((count,) + state, bf16), vm(state, f32), vm(state, f32)]
        + [vm((GROUP + 8, conv), f32), vm((GROUP + 8, 128), f32)]
        + [vm((2, count, GROUP), f32), vm((head_count, 2, count, GROUP), f32)]
        + DeviceScan.scratch(state, fade)
        + [vm((grad_rows, max(width, 2 * inner)), f32)] + paired[:-1] + [DMA((2,) + (8, seq // 2))]
        + [vm(((conv - inner + 128) // bc_rows, bc_rows, width), f32),
           vm((seq, head_count, piece, width), f32), vm((head_count, piece, width), f32),
           vm((bc_rows, width), f32), vm((24, width), f32), vm((seq, 24, width), f32),
           vm((8, width), f32), vm((head_count, 8, width), f32),
           vm((GROUP, conv), bf16), vm((GROUP, 128), bf16), vm((8, inner), f32), vm((8, conv), f32),
           vm((8, 128), f32), vm((8, conv), f32), vm((8, conv), f32),
           LineSum.sems(length, block), DMA((2, head_count)), DMA((4, seq)), DMA((2, head_count)),
           DMA((2, seq)), DMA((2, head_count)), DMA((2,)), pltpu.SemaphoreType.REGULAR,
           vm((width, 2 * inner), bf16), vm((inner, width), bf16), DMA((4,)), DMA((4,))],
        compiler_params=pltpu.CompilerParams(
            dimension_semantics=("arbitrary",), collective_id=4, has_side_effects=True,
            vmem_limit_bytes=LAYER_LIMIT),
        name="layer",
    )(x_conv, bc_conv, x_in, bc_in, heads_in, cot, normed, normed, out_proj, gains, entering, decay, conv_w, params,
      conv_halo, zx, weights, gain, tail_mask)


PACE = 27
MIX, SWAP, GATE, SCAN, BACK = 27, 30, 20, 100, 94
MIX_POINTS = 2
EARLY, LATE = -14, 50
BLOCK, LAG = 64, 3
STEPS = (2, 2, 2, 2, 6, 2, 3, 2, 6, 2)
LAYER_LIMIT = 63 * 2**20


def finish_kernel(heads, head_dim, all_channels, taps, count,
                  tokens, cot, mixed, d_normed, sums, gain, zx, op, bc, small,
                  mixed_out, tokens_out, zx_out, op_out, bc_out, dt_out, gain_out, conv_w_out, conv_b_out,
                  bc_w_out, bc_b_out, bias_out, rate_out, skip_out, norm_out, held, sems):
    at = pl.program_id(0)
    rows = tokens.shape[0]
    slot = lax.rem(at, 2)
    part = rows // 4

    def stores(step, slot):
        return [pltpu.make_async_copy(
            held.at[slot, pl.ds(k * part, part)],
            tokens_out.at[pl.ds(pl.multiple_of(step * rows + k * part, part), part)], sems.at[slot, k])
            for k in range(4)]

    @pl.when(at >= 2)
    def _():
        for copy in stores(at - 2, slot):
            copy.wait()
    inner = heads * head_dim
    value = tokens[...].astype(f32)
    tall = jnp.concatenate([sums[0, pl.ds(at, 1)], jnp.zeros((127, rows), f32)], axis=0).T
    inv_rms = lax.rsqrt(tall[:, 0:1] / all_channels + epsilon)
    mixed_out[...] = (value + mixed[...].astype(f32) * inv_rms).astype(bf16)
    inv = lax.rsqrt(jnp.mean(value * value, axis=1, keepdims=True) + epsilon)
    xhat = value * inv
    scaled = d_normed[...].astype(f32) * gain[...]
    held[slot] = cot[...].astype(f32) + inv * (
        scaled - xhat * jnp.mean(scaled * xhat, axis=1, keepdims=True))
    for copy in stores(at, slot):
        copy.start()

    @pl.when(at == count - 1)
    def _():
        for step in (count - 2, count - 1):
            for copy in stores(step, step % 2):
                copy.wait()
    sums_zx = zx[...].astype(f32)
    zx_out[:, 0, :] = sums_zx[:, :inner]
    zx_out[:, 1, :] = sums_zx[:, inner:]
    op_out[...] = op[...].astype(f32)
    @pl.when(at == 0)
    def _():
        bc_out[...] = bc[...]
        dt_out[...] = small[0:heads]
        gain_out[...] = small[16:17]
        conv_w_out[...] = small[8 : 8 + taps, :inner]
        conv_b_out[...] = small[8 + taps : 9 + taps, :inner]
        bias_out[...] = small[10:11, inner : inner + heads]
        rate_out[...] = small[11:12, inner : inner + heads]
        norm_out[...] = small[8:9, inner : 2 * inner]
        group_ones = (lax.broadcasted_iota(jnp.int32, (inner, 128), 0) // head_dim
                      == lax.broadcasted_iota(jnp.int32, (inner, 128), 1)).astype(bf16)
        skips = jnp.broadcast_to(small[9:10, inner : 2 * inner], (8, inner))
        total = sum(dot(part, group_ones) for part in split3(skips))
        skip_out[...] = total[0:1, :heads]
        part = bc_w_out.shape[1]
        mine_bc = small[17 : 18 + taps, : part * lax.axis_size("head")]
        chosen = mine_bc[:, :part]
        for k in range(1, lax.axis_size("head")):
            chosen = jnp.where(lax.axis_index("head") == k, mine_bc[:, k * part : (k + 1) * part], chosen)
        bc_w_out[...] = chosen[:taps]
        bc_b_out[...] = chosen[taps : taps + 1]


def finish(tokens, cot, totals, sums, gain, zx, op, bc, small, heads, head_dim, taps):
    length, width = tokens.shape
    count = length // GROUP
    inner = heads * head_dim
    part = bc.shape[0]

    def by(rows, cols):
        return pl.BlockSpec((rows, cols), lambda g: (g, 0))
    shape = jax.ShapeDtypeStruct
    tall = by(GROUP, width)
    lone = [(1, width), (taps, inner), (1, inner), (taps, part), (1, part), (1, heads), (1, heads), (1, heads),
            (1, inner)]
    cols = width // count
    return pl.pallas_call(
        functools.partial(finish_kernel, heads, head_dim, inner * lax.axis_size("head"), taps, count),
        grid=(count,),
        out_shape=(shape((length, width), bf16), shape((length, width), f32), shape((width, 2, inner), f32),
                   shape((inner, width), f32), shape((part, width), f32), shape((heads, width), f32))
        + tuple(shape(each, f32) for each in lone),
        in_specs=[tall] * 3 + [pl.BlockSpec((GROUP, width), lambda g: (count + g, 0)), VMEM, VMEM, by(cols, 2 * inner), by(inner // count, width),
                               VMEM, VMEM],
        out_specs=(tall, HBM, pl.BlockSpec((cols, 2, inner), lambda g: (g, 0, 0)), by(inner // count, width),
                   VMEM, VMEM) + (VMEM,) * len(lone),
        scratch_shapes=[pltpu.VMEM((2, GROUP, width), f32), DMA((2, 4))],
        compiler_params=pltpu.CompilerParams(dimension_semantics=("arbitrary",), vmem_limit_bytes=LIMIT),
        name="finish",
    )(tokens, cot, totals, totals, sums, gain, zx, op, bc, small)


def shards(
    tokens, start_flags, in_gain, proj_zx, proj_bc, proj_dt, conv_x_weight, conv_x_bias,
    conv_bc_weight, conv_bc_bias, dt_bias, a_log, skip_scale, norm_gain, out_proj, cotangent,
):
    length, width = tokens.shape
    heads = a_log.shape[0]
    inner = proj_zx.shape[2]
    head_dim = inner // heads
    taps = conv_x_weight.shape[0]
    head_count = lax.axis_size("head")
    bc_part = conv_bc_bias.shape[0]
    bc_width = bc_part * head_count
    state_dim = bc_width // 2
    gain = in_gain[None]
    (normed, x_in, x_conv, bc_in, bc_conv, info, entering, decay, conv_halo, weights, zx, conv_w, params, gains,
     tail_mask) = front(
        tokens, proj_zx, start_flags.reshape(length // 128, 128), gain, proj_bc.T, proj_dt.T, conv_x_weight,
        conv_x_bias[None], conv_bc_weight, conv_bc_bias[None], dt_bias[None], a_log[None], skip_scale[None],
        norm_gain[None], heads, head_dim, state_dim)
    all_channels = inner * head_count
    totals, sums, zx_sum, op_sum, bc_sum, small_sum = layer(
        x_conv, bc_conv, x_in, bc_in, info, cotangent, normed, out_proj, gains, entering, decay, conv_w, params,
        conv_halo, zx, weights, gain, tail_mask, heads, head_dim, state_dim, all_channels, taps)
    (mixed_out, grad_tokens, grad_zx, grad_op, grad_bc, grad_dt, grad_gain, grad_conv_w, grad_conv_b,
     grad_bc_w, grad_bc_b, grad_bias, grad_rate, grad_skip, grad_norm) = finish(
        tokens, cotangent, totals, sums, gain, zx_sum, op_sum, bc_sum, small_sum, heads, head_dim, taps)
    return (
        mixed_out, grad_tokens, grad_gain[0], grad_zx, grad_bc.T, grad_dt.T, grad_conv_w, grad_conv_b[0],
        grad_bc_w, grad_bc_b[0], grad_bias[0], grad_rate[0], grad_skip[0], grad_norm[0], grad_op,
    )


def solution(mesh):
    in_specs = (
        P("seq", None),
        P("seq"),
        P(),
        P(None, None, "head"),
        P(None, "head"),
        P(None, "head"),
        P(None, "head"),
        P("head"),
        P(None, "head"),
        P("head"),
        P("head"),
        P("head"),
        P("head"),
        P("head"),
        P("head", None),
        P("seq", None),
    )
    out_specs = (
        P("seq", None),
        P("seq", None),
        P(),
        P(None, None, "head"),
        P(None, "head"),
        P(None, "head"),
        P(None, "head"),
        P("head"),
        P(None, "head"),
        P("head"),
        P("head"),
        P("head"),
        P("head"),
        P("head"),
        P("head", None),
    )
    return jax.shard_map(shards, mesh=mesh, in_specs=in_specs, out_specs=out_specs, check_vma=False)
```
